32 devices in a mesh: wide: 8 (over z, x), blk: 4 (over y, core).
Axes of the slice: x: 2, y: 2, z: 4, core: 2. Of those that a mesh axis runs over, the one named last changes fastest.
Arguments:
- patches: bfloat16 [32, 256, 768], P('wide', 'blk'), may hold values from -6 to 6
- norm_gain: bfloat16 [2, 768], P(None, ('wide', 'blk')), may hold values from 0.099609375 to 1.8984375
- norm_bias: bfloat16 [2, 768], P(None, ('wide', 'blk')), may hold values from -3 to 3
- qkv_weight: bfloat16 [768, 2304], P(('wide', 'blk')), may hold values from -0.21875 to 0.21875
- qv_bias: bfloat16 [2, 768], P(None, ('wide', 'blk')), may hold values from -3 to 3
- out_weight: bfloat16 [768, 768], P(('wide', 'blk')), may hold values from -0.875 to 0.875
- fc1_weight: bfloat16 [768, 3072], P(('wide', 'blk')), may hold values from -0.21875 to 0.21875
- fc1_bias: bfloat16 [3072], P(('wide', 'blk')), may hold values from -3 to 3
- fc2_weight: bfloat16 [3072, 768], P(('wide', 'blk')), may hold values from -0.109375 to 0.109375
- res_bias: bfloat16 [2, 768], P(None, ('wide', 'blk')), may hold values from -3 to 3
- cotangent: bfloat16 [32, 256, 768], P('wide', 'blk'), may hold values from -6 to 6
- frame_valid: int32 [32], P('wide'), may hold values 0 or 1
Outputs:
- encoded: bfloat16 [32, 256, 768], P('wide', 'blk')
- grad_patches: float32 [32, 256, 768], P('wide', 'blk')
- grad_norm_gain: float32 [2, 768], P(None, ('wide', 'blk'))
- grad_norm_bias: float32 [2, 768], P(None, ('wide', 'blk'))
- grad_qkv_weight: float32 [768, 2304], P(('wide', 'blk'))
- grad_qv_bias: float32 [2, 768], P(None, ('wide', 'blk'))
- grad_out_weight: float32 [768, 768], P(('wide', 'blk'))
- grad_fc1_weight: float32 [768, 3072], P(('wide', 'blk'))
- grad_fc1_bias: float32 [3072], P(('wide', 'blk'))
- grad_fc2_weight: float32 [3072, 768], P(('wide', 'blk'))
- grad_res_bias: float32 [2, 768], P(None, ('wide', 'blk'))
The draws below stay inside these ranges and needn't reach their ends.
All inputs are finite; a program needn't handle non-finite values. No bound on the sum of `frame_valid` on one device may be relied on, other than what follows from the above.
Results may differ from the reference program's by a relative error of at most 0.013.
Values may be sent and summed in bfloat16 or wider, within the bound.
A program may use at most 128 MiB of HBM per device.

```python
import math
import jax
import jax.numpy as jnp
from jax import lax

D = 768
HEADS = 12
HEAD = 64
FF = 3072
PATCHES = 256
SLOTS = 32


def set_ends(values, own_key, low, high):
    longest = values.shape.index(max(values.shape))
    spots = []
    for shift in (0, 1):
        where = [jax.random.randint(jax.random.fold_in(own_key, axis), (), 0, length) for axis, length in enumerate(values.shape)]
        where[longest] = (where[longest] + shift) % values.shape[longest]
        spots.append(tuple(where))
    return values.at[spots[0]].set(low).at[spots[1]].set(high)


def raised(values, stream_key, source, target, parts, factor):
    def block_of(dim):
        return (jnp.arange(values.shape[dim]) // (values.shape[dim] // parts)).reshape((-1,) + (1,) * (values.ndim - 1 - dim))

    first = jax.random.permutation(stream_key, parts)[block_of(target)]
    far = (block_of(target) + parts // 2) % parts
    return jnp.where((block_of(source) == first) | (block_of(source) == far), factor * values, values)


def block_levels(own_key, dims, split, smallest, high):
    level = 1.0
    for position, blocks in split:
        draws = jax.random.uniform(jax.random.fold_in(jax.random.fold_in(own_key, 6), position), (blocks,), jnp.float32, smallest / len(split), high / len(split))
        level = level * jnp.repeat(jnp.exp(draws), dims[position] // blocks).reshape((-1,) + (1,) * (len(dims) - 1 - position))
    return level


def bell_draw(key, extent, deviation, bound, cuts=(), held_as=jnp.bfloat16):
    entries = jax.random.normal(key, extent, jnp.float32) * deviation
    if len(cuts) > 0:
        entries = block_levels(key, extent, cuts, -0.22, 0.18) * entries
    return jnp.clip(entries, min=-bound, max=bound).astype(held_as)


def noise_with(key, extent, scale, bound, split, heavy, dtype=jnp.bfloat16):
    entries = scale * jax.random.normal(key, extent, jnp.float32)
    if split:
        entries = entries * block_levels(key, extent, split, -0.22, 0.18)
    return jnp.clip(raised(entries, jax.random.fold_in(key, 3), *heavy), -bound, bound).astype(dtype)


def setup_inputs(seed: int = 0) -> dict:
    streams_of = jax.random.split(jax.random.key(seed), 13)
    patches = bell_draw(streams_of[0], (SLOTS, PATCHES, D), 1.0, 6.0, ((0, 8), (1, 4)))
    norm_gain = jnp.clip(1.0 + 0.18 * jax.random.normal(streams_of[1], (2, D), jnp.float32), 0.099609375, 1.8984375).astype(jnp.bfloat16)
    norm_bias = bell_draw(streams_of[2], (2, D), 0.5, 3.0, ((1, 32),))
    qkv_weight = bell_draw(streams_of[3], (D, 3 * D), D ** -0.5, 0.21875, ((0, 32),))
    qv_bias = bell_draw(streams_of[4], (2, D), 0.5, 3.0, ((1, 32),))
    out_weight = bell_draw(streams_of[5], (D, D), (D // 16) ** -0.5, 0.875, ((0, 32),))
    fc1_weight = bell_draw(streams_of[6], (D, FF), D ** -0.5, 0.21875, ((0, 32),))
    fc1_bias = bell_draw(streams_of[7], (FF,), 0.5, 3.0, ((0, 32),))
    fc2_weight = bell_draw(streams_of[8], (FF, D), FF ** -0.5, 0.109375, ((0, 32),))
    res_bias = bell_draw(streams_of[9], (2, D), 0.5, 3.0, ((1, 32),))
    cotangent = noise_with(streams_of[10], (SLOTS, PATCHES, D), 1.0, 6.0, ((0, 8), (1, 4)), (0, 2, 8, 2.0))
    frame_valid = set_ends((jax.random.randint(streams_of[11], (SLOTS,), 0, 5) < 3).astype(jnp.int32), jax.random.fold_in(streams_of[11], 1), 0, 1)
    return dict(patches=patches, norm_gain=norm_gain, norm_bias=norm_bias, qkv_weight=qkv_weight, qv_bias=qv_bias, out_weight=out_weight, fc1_weight=fc1_weight, fc1_bias=fc1_bias, fc2_weight=fc2_weight, res_bias=res_bias, cotangent=cotangent, frame_valid=frame_valid)


@jax.custom_vjp
def low(v):
    return lax.optimization_barrier(v.astype(jnp.bfloat16)).astype(jnp.float32)

@jax.custom_vjp
def low_back(v):
    return v

def low_keep(v):
    return (low(v), None)

def low_pass(kept, grad):
    return (grad,)

def back_keep(v):
    return (v, None)

def back_low(kept, grad):
    return (low(grad),)
low.defvjp(low_keep, low_pass)
low_back.defvjp(back_keep, back_low)
EPSILON = 1e-06
HIGHEST = lax.Precision.HIGHEST

def layer_normalize(token_rows, norm_gain_vector, norm_bias_vector):
    row_average = lax.optimization_barrier(jnp.mean(token_rows, axis=-1, keepdims=True))
    centered_rows = token_rows - row_average
    inverse_deviation_scale = lax.rsqrt(lax.optimization_barrier(jnp.mean(centered_rows * centered_rows, axis=-1, keepdims=True)) + EPSILON)
    return centered_rows * inverse_deviation_scale * norm_gain_vector + norm_bias_vector

def project(left, right):
    return jnp.einsum('gpd,de->gpe', left, right, precision=HIGHEST)

def frame_block(token_rows, params):
    norm_gain, norm_bias, qkv_weight, qv_bias, out_weight, fc1_weight, fc1_bias, fc2_weight, res_bias = params
    frames = token_rows.shape[0]
    normed = low(layer_normalize(token_rows, norm_gain[0], norm_bias[0]))
    mixed = project(normed, qkv_weight)
    query = low(low_back((mixed[..., :D] + qv_bias[0]) * 0.125))
    keys = low(low_back(mixed[..., D:2 * D]))
    values = low(low_back(mixed[..., 2 * D:] + qv_bias[1]))
    query = query.reshape(frames, PATCHES, HEADS, HEAD)
    keys = keys.reshape(frames, PATCHES, HEADS, HEAD)
    values = values.reshape(frames, PATCHES, HEADS, HEAD)
    scores = low_back(jnp.einsum('gqhe,gkhe->ghqk', query, keys, precision=HIGHEST))
    probs = low(jax.nn.softmax(scores, axis=-1))
    attended = jnp.einsum('ghqk,gkhe->gqhe', probs, values, precision=HIGHEST).reshape(frames, PATCHES, D)
    attended = low(low_back(attended))
    branch = low_back(project(attended, out_weight) + res_bias[0])
    middle_activation = token_rows + branch
    normed2 = low(layer_normalize(middle_activation, norm_gain[1], norm_bias[1]))
    hidden = low_back(project(normed2, fc1_weight) + fc1_bias)
    active = low(jax.nn.gelu(hidden, approximate=False))
    branch2 = low_back(project(active, fc2_weight) + res_bias[1])
    return middle_activation + branch2

def reference(patches, norm_gain, norm_bias, qkv_weight, qv_bias, out_weight, fc1_weight, fc1_bias, fc2_weight, res_bias, cotangent, frame_valid):
    params = tuple((p.astype(jnp.float32) for p in (norm_gain, norm_bias, qkv_weight, qv_bias, out_weight, fc1_weight, fc1_bias, fc2_weight, res_bias)))
    token_rows = patches.astype(jnp.float32)
    weight = frame_valid.astype(jnp.float32)[:, None, None]
    group_frames = math.gcd(SLOTS, 16)

    def forward(whole, weights):
        blocks = whole.reshape(SLOTS // group_frames, group_frames, PATCHES, D)
        result = lax.map(jax.checkpoint(lambda block: frame_block(block, weights)), blocks)
        return result.reshape(whole.shape) * weight
    encoded, pullback = jax.vjp(forward, token_rows, params)
    grad_rows, grads = pullback(cotangent.astype(jnp.float32))
    return (encoded.astype(jnp.bfloat16), grad_rows, grads[0], grads[1], grads[2], grads[3], grads[4], grads[5], grads[6], grads[7], grads[8])
```

```python
from functools import partial
import math
import types

import jax
import jax.numpy as jnp
from jax import lax
from jax.experimental import pallas as pl
from jax.experimental.pallas import tpu as pltpu
from jax.sharding import PartitionSpec as P

D = 768
HEADS = 12
HEAD = 64


EPSILON = 1e-06


def layer_normalize(token_rows, norm_gain_vector, norm_bias_vector):
    row_average = jnp.mean(token_rows, axis=-1, keepdims=True)
    centered_rows = token_rows - row_average
    inverse_deviation_scale = lax.rsqrt(
        jnp.mean(centered_rows * centered_rows, axis=-1, keepdims=True) + EPSILON
    )
    standardized_rows = centered_rows * inverse_deviation_scale
    return (
        standardized_rows * norm_gain_vector + norm_bias_vector,
        standardized_rows,
        inverse_deviation_scale,
    )


def layer_normalize_backward(
    incoming_gradient, standardized_rows, inverse_deviation_scale, norm_gain_vector
):
    gain_weighted_gradient = incoming_gradient * norm_gain_vector
    inner_product_sum = (
        gain_weighted_gradient
        - jnp.mean(gain_weighted_gradient, axis=-1, keepdims=True)
        - standardized_rows
        * jnp.mean(gain_weighted_gradient * standardized_rows, axis=-1, keepdims=True)
    )
    return (
        inverse_deviation_scale * inner_product_sum,
        jnp.sum(incoming_gradient * standardized_rows, axis=0),
        jnp.sum(incoming_gradient, axis=0),
    )


def frame_groups(array, count):
    return array.reshape((array.shape[0] // count, count) + array.shape[1:])


def attend_forward(query, keys, values):
    scores = jnp.einsum("gqhe,gkhe->ghqk", query, keys, preferred_element_type=jnp.float32)
    top = jnp.max(scores, axis=-1, keepdims=True)
    expo = jnp.exp(scores - top)
    total = jnp.sum(expo, axis=-1, keepdims=True)
    probs = (expo / total).astype(jnp.bfloat16)
    attended = jnp.einsum("ghqk,gkhe->gqhe", probs, values, preferred_element_type=jnp.float32)
    return (attended, top + jnp.log(total))


def attend_back(query, keys, values, logsum, grad_out):
    scores = jnp.einsum("gqhe,gkhe->ghqk", query, keys, preferred_element_type=jnp.float32)
    probs = jnp.exp(scores - logsum)
    grad_probs = jnp.einsum("gqhe,gkhe->ghqk", grad_out, values, preferred_element_type=jnp.float32)
    grad_values = jnp.einsum(
        "ghqk,gqhe->gkhe", probs.astype(jnp.bfloat16), grad_out, preferred_element_type=jnp.float32
    )
    grad_scores = (
        probs * (grad_probs - jnp.sum(probs * grad_probs, axis=-1, keepdims=True))
    ).astype(jnp.bfloat16)
    grad_query = jnp.einsum(
        "ghqk,gkhe->gqhe", grad_scores, keys, preferred_element_type=jnp.float32
    )
    grad_keys = jnp.einsum(
        "ghqk,gqhe->gkhe", grad_scores, query, preferred_element_type=jnp.float32
    )
    return (grad_query, grad_keys, grad_values)


def local(
    patches,
    norm_gain,
    norm_bias,
    qkv_weight,
    qv_bias,
    out_weight,
    fc1_weight,
    fc1_bias,
    fc2_weight,
    res_bias,
    cotangent,
    frame_valid,
):
    frames, frame_rows, width = patches.shape
    count = frames * frame_rows
    group = math.gcd(frames, 8)
    params = (
        lax.all_gather(norm_gain, ("wide", "blk"), axis=1, tiled=True),
        lax.all_gather(norm_bias, ("wide", "blk"), axis=1, tiled=True),
        lax.all_gather(qkv_weight, ("wide", "blk"), axis=0, tiled=True),
        lax.all_gather(qv_bias, ("wide", "blk"), axis=1, tiled=True),
        lax.all_gather(out_weight, ("wide", "blk"), axis=0, tiled=True),
        lax.all_gather(fc1_weight, ("wide", "blk"), axis=0, tiled=True),
        lax.all_gather(fc1_bias, ("wide", "blk"), axis=0, tiled=True),
        lax.all_gather(fc2_weight, ("wide", "blk"), axis=0, tiled=True),
        lax.all_gather(res_bias, ("wide", "blk"), axis=1, tiled=True),
    )
    norm_gain_pair = params[0].astype(jnp.float32)
    norm_bias_pair = params[1].astype(jnp.float32)
    biases_qv = params[3].astype(jnp.float32)
    bias_fc1 = params[6].astype(jnp.float32)
    biases_res = params[8].astype(jnp.float32)
    token_rows = patches.reshape(count, width).astype(jnp.float32)
    valid = jnp.repeat(frame_valid.astype(jnp.float32), frame_rows)[:, None]
    first_branch, first_standardized_rows, first_norm_scale = layer_normalize(
        token_rows, norm_gain_pair[0], norm_bias_pair[0]
    )
    normed = first_branch.astype(jnp.bfloat16)
    mixed = jnp.dot(normed, params[2], preferred_element_type=jnp.float32)
    query = ((mixed[:, :D] + biases_qv[0]) * 0.125).astype(jnp.bfloat16)
    keys = mixed[:, D : 2 * D].astype(jnp.bfloat16).reshape(frames, frame_rows, width)
    values = (
        (mixed[:, 2 * D :] + biases_qv[1]).astype(jnp.bfloat16).reshape(frames, frame_rows, width)
    )
    keys_all, values_all = (
        lax.all_gather(keys, "blk", axis=1, tiled=True),
        lax.all_gather(values, "blk", axis=1, tiled=True),
    )
    query_heads = frame_groups(query.reshape(frames, frame_rows, HEADS, HEAD), group)
    keys_heads = frame_groups(keys_all.reshape(frames, -1, HEADS, HEAD), group)
    values_heads = frame_groups(values_all.reshape(frames, -1, HEADS, HEAD), group)
    attended, logsum = lax.map(
        lambda item: attend_forward(item[0], item[1], item[2]),
        (query_heads, keys_heads, values_heads),
    )
    attended = attended.reshape(count, width).astype(jnp.bfloat16)
    middle_activation = (
        token_rows
        + jnp.dot(attended, params[4], preferred_element_type=jnp.float32)
        + biases_res[0]
    )
    second_branch, second_standardized_rows, second_norm_scale = layer_normalize(
        middle_activation, norm_gain_pair[1], norm_bias_pair[1]
    )
    normed2 = second_branch.astype(jnp.bfloat16)
    hidden = jnp.dot(normed2, params[5], preferred_element_type=jnp.float32) + bias_fc1
    active = jax.nn.gelu(hidden, approximate=False).astype(jnp.bfloat16)
    branch2 = jnp.dot(active, params[7], preferred_element_type=jnp.float32) + biases_res[1]
    encoded = (
        ((middle_activation + branch2) * valid)
        .astype(jnp.bfloat16)
        .reshape(frames, frame_rows, width)
    )
    params = (
        lax.all_gather(norm_gain, ("wide", "blk"), axis=1, tiled=True),
        lax.all_gather(norm_bias, ("wide", "blk"), axis=1, tiled=True),
        lax.all_gather(qkv_weight, ("wide", "blk"), axis=0, tiled=True),
        lax.all_gather(qv_bias, ("wide", "blk"), axis=1, tiled=True),
        lax.all_gather(out_weight, ("wide", "blk"), axis=0, tiled=True),
        lax.all_gather(fc1_weight, ("wide", "blk"), axis=0, tiled=True),
        lax.all_gather(fc1_bias, ("wide", "blk"), axis=0, tiled=True),
        lax.all_gather(fc2_weight, ("wide", "blk"), axis=0, tiled=True),
        lax.all_gather(res_bias, ("wide", "blk"), axis=1, tiled=True),
    )
    grad_out = cotangent.reshape(count, width).astype(jnp.float32) * valid
    grad_branch2 = grad_out.astype(jnp.bfloat16)
    grad_fc2 = jnp.dot(active.T, grad_branch2, preferred_element_type=jnp.float32)
    grad_res_two = jnp.sum(grad_branch2.astype(jnp.float32), axis=0)
    grad_active = jnp.dot(grad_branch2, params[7].T, preferred_element_type=jnp.float32)
    gelu_back = jax.vjp(partial(jax.nn.gelu, approximate=False), hidden)[1]
    grad_hidden = gelu_back(grad_active)[0].astype(jnp.bfloat16)
    grad_fc1 = jnp.dot(normed2.T, grad_hidden, preferred_element_type=jnp.float32)
    grad_bias_fc1 = jnp.sum(grad_hidden.astype(jnp.float32), axis=0)
    normed_input_gradient2 = jnp.dot(grad_hidden, params[5].T, preferred_element_type=jnp.float32)
    second_norm_gradient, second_norm_gain, second_norm_bias = layer_normalize_backward(
        normed_input_gradient2, second_standardized_rows, second_norm_scale, norm_gain_pair[1]
    )
    grad_middle = grad_out + second_norm_gradient
    grad_branch = grad_middle.astype(jnp.bfloat16)
    grad_out_proj = jnp.dot(attended.T, grad_branch, preferred_element_type=jnp.float32)
    grad_res_one = jnp.sum(grad_branch.astype(jnp.float32), axis=0)
    grad_attended = jnp.dot(grad_branch, params[4].T, preferred_element_type=jnp.float32).astype(
        jnp.bfloat16
    )
    grad_heads = frame_groups(grad_attended.reshape(frames, frame_rows, HEADS, HEAD), group)
    grad_query, grad_keys, grad_values = lax.map(
        lambda item: attend_back(item[0], item[1], item[2], item[3], item[4]),
        (query_heads, keys_heads, values_heads, logsum, grad_heads),
    )
    grad_keys, grad_values = (
        lax.psum_scatter(
            grad_keys.reshape(frames, -1, width).astype(jnp.bfloat16),
            "blk",
            scatter_dimension=1,
            tiled=True,
        ).astype(jnp.float32),
        lax.psum_scatter(
            grad_values.reshape(frames, -1, width).astype(jnp.bfloat16),
            "blk",
            scatter_dimension=1,
            tiled=True,
        ).astype(jnp.float32),
    )
    grad_query = grad_query.reshape(count, width).astype(jnp.bfloat16) * 0.125
    grad_keys = grad_keys.reshape(count, width).astype(jnp.bfloat16)
    grad_values = grad_values.reshape(count, width).astype(jnp.bfloat16)
    grad_mixed = jnp.concatenate([grad_query, grad_keys, grad_values], axis=1)
    grad_qkv = jnp.dot(normed.T, grad_mixed, preferred_element_type=jnp.float32)
    grad_qv = jnp.stack(
        [
            jnp.sum(grad_query.astype(jnp.float32), axis=0),
            jnp.sum(grad_values.astype(jnp.float32), axis=0),
        ]
    )
    normed_input_gradient = jnp.dot(grad_mixed, params[2].T, preferred_element_type=jnp.float32)
    first_norm_gradient, first_norm_gain, first_norm_bias = layer_normalize_backward(
        normed_input_gradient, first_standardized_rows, first_norm_scale, norm_gain_pair[0]
    )
    grad_rows = (grad_middle + first_norm_gradient).reshape(frames, frame_rows, width)
    grad_gain = jnp.stack([first_norm_gain, second_norm_gain])
    grad_shift = jnp.stack([first_norm_bias, second_norm_bias])
    grad_res = jnp.stack([grad_res_one, grad_res_two])
    summed = (
        lax.psum_scatter(grad_gain, ("wide", "blk"), scatter_dimension=1, tiled=True),
        lax.psum_scatter(grad_shift, ("wide", "blk"), scatter_dimension=1, tiled=True),
        lax.psum_scatter(grad_qkv, ("wide", "blk"), scatter_dimension=0, tiled=True),
        lax.psum_scatter(grad_qv, ("wide", "blk"), scatter_dimension=1, tiled=True),
        lax.psum_scatter(grad_out_proj, ("wide", "blk"), scatter_dimension=0, tiled=True),
        lax.psum_scatter(grad_fc1, ("wide", "blk"), scatter_dimension=0, tiled=True),
        lax.psum_scatter(grad_bias_fc1, ("wide", "blk"), scatter_dimension=0, tiled=True),
        lax.psum_scatter(grad_fc2, ("wide", "blk"), scatter_dimension=0, tiled=True),
        lax.psum_scatter(grad_res, ("wide", "blk"), scatter_dimension=1, tiled=True),
    )
    return (
        encoded,
        grad_rows,
        summed[0],
        summed[1],
        summed[2],
        summed[3],
        summed[4],
        summed[5],
        summed[6],
        summed[7],
        summed[8],
    )


MESH_ID = pl.DeviceIdType.MESH
BF16 = jnp.bfloat16
F32 = jnp.float32
FF = 3072
TOKENS = 256
ROWS = 64
ALL, LOW, HIGH = pl.ds(0, 4), pl.ds(0, 2), pl.ds(2, 2)


def dot(left, right):
    return lax.dot_general(left, right, (((1,), (0,)), ((), ())), preferred_element_type=F32)


def dot_nt(left, right):
    return lax.dot_general(left, right, (((1,), (1,)), ((), ())), preferred_element_type=F32)


def dot_tn(left, right):
    return lax.dot_general(left, right, (((0,), (0,)), ((), ())), preferred_element_type=F32)


COPIES = 300


def scratch_shapes():
    def vm(*shape, dtype=BF16):
        return pltpu.VMEM(shape, dtype)

    return dict(
        w_small=vm(4, 4, 16, 256),
        w_qkv=vm(4, 4, 48, 2304),
        w_out=vm(4, 4, 48, 768),
        w_fc1=vm(4, 4, 48, 3072),
        w_fc2=vm(4, 4, 2, 96, 768),
        own_small=vm(16, 128, dtype=F32),
        pair_rows=vm(48, 3072, dtype=F32),
        pair_send=vm(24, 3072, dtype=F32),
        par=vm(16, 768, dtype=F32),
        par_fc1=vm(8, 3072, dtype=F32),
        rows_in=vm(256, 768),
        cot_in=vm(256, 768),
        normed=vm(256, 768),
        normed_t=vm(768, 256),
        mixed=vm(256, 2304),
        attended=vm(256, 768),
        attended_t=vm(768, 256),
        middle=vm(256, 768, dtype=F32),
        normed2=vm(256, 768),
        normed2_t=vm(768, 256),
        slope=vm(256, 3072, dtype=F32),
        active=vm(256, 3072),
        active_t=vm(32, 96, 256),
        g_branch2=vm(256, 768),
        total=vm(256, 768, dtype=F32),
        g_middle=vm(256, 768, dtype=F32),
        g_branch=vm(256, 768),
        g_attended=vm(256, 768),
        g_mixed=vm(256, 2304),
        enc_send=vm(256, 768),
        gx_send=vm(256, 768),
        gx_recv=vm(4, 64, 768),
        sums=vm(16, 768, dtype=F32),
        sums_fc1=vm(8, 3072, dtype=F32),
        g_small=vm(4, 4, 16, 256),
        g_fc1=vm(4, 4, 48, 3072),
        g_fc2=vm(4, 4, 2, 96, 768),
        pr_small=vm(4, 4, 16, 128),
        pr_a=vm(4, 4, 48, 3072),
        pr_fc2=vm(4, 4, 2, 96, 384),
        dx_small=vm(2, 16, 128),
        dx_a=vm(2, 48, 3072),
        dx_fc2=vm(2, 2, 96, 384),
        dy_small=vm(2, 16, 128),
        dy_a=vm(2, 48, 3072),
        dy_fc2=vm(2, 2, 96, 384),
        px_small=vm(4, 16, 128),
        px_a=vm(4, 48, 3072),
        px_fc2=vm(4, 2, 96, 384),
        py_small=vm(4, 16, 128),
        py_a=vm(4, 48, 3072),
        py_fc2=vm(4, 2, 96, 384),
        pz_small=vm(3, 16, 128),
        pz_a=vm(3, 48, 3072),
        pz_fc2=vm(3, 2, 96, 384),
        last_a=vm(48, 3072, dtype=F32),
        last_fc2=vm(96, 384, dtype=F32),
        send_sem=pltpu.SemaphoreType.DMA((COPIES,)),
        recv_sem=pltpu.SemaphoreType.DMA((COPIES,)),
    )


def layer_kernel(
    patches,
    norm_gain,
    norm_bias,
    qkv_weight,
    qv_bias,
    out_weight,
    fc1_weight,
    fc1_bias,
    fc2_weight,
    res_bias,
    cotangent,
    frame_valid,
    encoded,
    grad_patches,
    grad_gain,
    grad_shift,
    grad_qkv,
    grad_qv,
    grad_out,
    grad_fc1,
    grad_fc1_bias,
    grad_fc2,
    grad_res,
    *scratch,
):
    s = types.SimpleNamespace(**dict(zip(scratch_shapes(), scratch)))
    wide, blk = lax.axis_index("wide"), lax.axis_index("blk")
    z, x = lax.div(wide, 2), lax.rem(wide, 2)
    y, core = lax.div(blk, 2), lax.rem(blk, 2)
    here, at_x, at_y, at_d = 2 * x + y, 2 * (1 - x) + y, 2 * x + 1 - y, 2 * (1 - x) + 1 - y
    sibling = (wide, 2 * y + 1 - core)
    x_peer = (2 * z + 1 - x, blk)
    y_peer = (wide, 2 * (1 - y) + core)
    y_cross = (wide, 2 * (1 - y) + 1 - core)
    z_of = [lax.rem(z + step, 4) for step in range(4)]
    z_peers = [(2 * z_of[step] + x, blk) for step in range(4)]
    blk_peers = [(y, 1 - core), (1 - y, core), (1 - y, 1 - core)]

    barrier = pltpu.get_barrier_semaphore()
    peers = [sibling, x_peer, y_peer, y_cross] + z_peers[1:]
    for peer in peers:
        pl.semaphore_signal(barrier, inc=1, device_id=peer, device_id_type=MESH_ID)

    started, waited = [], set()

    def sent(copies):
        for copy in copies:
            if id(copy) not in waited:
                waited.add(id(copy))
                copy.wait_send()

    def remote(source, target, peer):
        spot = len(started)
        copy = pltpu.make_async_remote_copy(
            src_ref=source,
            dst_ref=target,
            send_sem=s.send_sem.at[spot],
            recv_sem=s.recv_sem.at[spot],
            device_id=peer,
            device_id_type=MESH_ID,
        )
        copy.start()
        started.append(copy)
        return copy

    def lanes(start, size):
        return pl.ds(pl.multiple_of(start, 128), size)

    s.own_small[...] = jnp.zeros((16, 128), F32)
    s.sums[...] = jnp.zeros((16, D), F32)
    s.own_small[0:2, 0:24] = norm_gain[...].astype(F32)
    s.own_small[2:4, 0:24] = norm_bias[...].astype(F32)
    s.own_small[4:6, 0:24] = qv_bias[...].astype(F32)
    s.own_small[6:8, 0:24] = res_bias[...].astype(F32)
    s.own_small[8:9, 0:96] = fc1_bias[...].astype(F32)
    s.w_small[z, here, :, lanes(128 * core, 128)] = s.own_small[...].astype(BF16)
    own_rows = pl.ds(pl.multiple_of(24 * core, 8), 24)
    for ref, half, start in ((qkv_weight, 1152, 0), (out_weight, 384, 1152), (fc1_weight, 1536, 1536)):
        s.pair_send[:, start : start + half] = ref[:, lanes((1 - core) * half, half)].astype(F32)
        s.pair_rows[own_rows, start : start + half] = ref[:, lanes(core * half, half)].astype(F32)
    s.w_fc2[z, here, core] = fc2_weight[...]

    pl.semaphore_wait(barrier, len(peers))

    pair = remote(s.pair_send, s.pair_rows.at[own_rows, :], sibling)

    mine = pl.ds(pl.multiple_of(64 * blk, 64), 64)

    def to_frames(source, target):
        return [remote(source.at[2 * py + pc], target.at[mine, :], (wide, 2 * py + pc)) for py, pc in blk_peers]

    rows_moved = to_frames(patches, s.rows_in)
    s.rows_in[mine, :] = patches[blk]
    s.cot_in[mine, :] = cotangent[blk]

    class Gather:
        def __init__(self, part):
            self.part = part

        def along_z(self):
            own = self.part(z, here)
            self.z = [remote(own, own, z_peers[step]) for step in (1, 2, 3)]

        def to_plane(self):
            for copy in self.z:
                copy.wait_recv()
            column = self.part(ALL, here)
            self.x, self.y = remote(column, column, x_peer), remote(column, column, y_peer)
            self.pair = [remote(column, column, sibling)]

        def forward(self):
            self.x.wait_recv()
            some = self.part(LOW, at_x)
            self.dy = remote(some, some, y_peer)
            self.y.wait_recv()
            some = self.part(HIGH, at_y)
            self.dx = remote(some, some, x_peer)
            for column in (self.part(ALL, at_x), self.part(ALL, at_y)):
                self.pair.append(remote(column, column, sibling))

        def last(self):
            self.dy.wait_recv()
            self.dx.wait_recv()
            column = self.part(ALL, at_d)
            self.pair.append(remote(column, column, sibling))

        def done(self):
            for copy in self.pair:
                copy.wait_recv()

        def copies(self):
            return self.z + self.pair + [self.x, self.y, self.dx, self.dy]

    def column_part(ref, half, start, size):
        return lambda levels, place: ref.at[levels, place, :, lanes(half * core + start, size)]

    def row_part(ref, start, size):
        return lambda levels, place: ref.at[levels, place, core, pl.ds(start, size), :]

    gathers = [Gather(column_part(s.w_small, 128, 0, 128))]
    gathers += [Gather(column_part(s.w_qkv, 1152, 384 * j, 384)) for j in range(3)]
    gathers += [Gather(column_part(s.w_out, 384, 0, 384))]
    gathers += [Gather(column_part(s.w_fc1, 1536, 384 * j, 384)) for j in range(4)]
    gathers += [Gather(row_part(s.w_fc2, 32 * j, 32)) for j in range(3)]

    gathers[0].along_z()
    pair.wait_recv()
    for ref, half, start in ((s.w_qkv, 1152, 0), (s.w_out, 384, 1152), (s.w_fc1, 1536, 1536)):
        ref[z, here, :, lanes(core * half, half)] = s.pair_rows[:, start : start + half].astype(BF16)
    for gather in gathers[1:3]:
        gather.along_z()
    gathers[0].to_plane()


    def by_rows(body, carry=None):
        def step(i, held):
            return body(pl.ds(pl.multiple_of(ROWS * i, ROWS), ROWS), held)

        return lax.fori_loop(0, TOKENS // ROWS, step, carry)

    def over(shape, axis):
        return lax.broadcasted_iota(jnp.int32, shape, axis)

    def piece24(columns):
        return lax.shift_right_logical(columns * 43691, 20)

    def piece96(columns):
        return lax.shift_right_logical(columns * 10923, 20)

    def spread24():
        columns = over((128, D), 1)
        return (columns - 24 * piece24(columns) == over((128, D), 0)).astype(F32).astype(BF16)

    def spread96():
        columns = over((128, FF), 1)
        return (columns - 96 * piece96(columns) == over((128, FF), 0)).astype(F32).astype(BF16)

    def unpack_small():
        flat = s.w_small[...].reshape(256, 256)
        chips = lax.shift_right_logical(over((256, D), 0), 4)
        pieces = piece24(over((256, D), 1))
        spread = spread24()
        found = jnp.zeros((16, D), F32)
        for side in (0, 1):
            wide_rows = dot(flat[:, 128 * side : 128 * side + 128], spread)
            wide_rows = jnp.where(pieces == 2 * chips + side, wide_rows, 0.0)
            found = found + jnp.sum(wide_rows.reshape(16, 16, D), axis=0)
        s.par[...] = found
        pick = (over((16, 256), 1) == 16 * over((16, 256), 0) + 8).astype(F32).astype(BF16)
        spread = spread96()
        pieces = piece96(over((16, FF), 1))
        found = jnp.zeros((16, FF), F32)
        for side in (0, 1):
            rows = dot(pick, flat[:, 128 * side : 128 * side + 128]).astype(BF16)
            found = found + jnp.where(pieces == 2 * over((16, FF), 0) + side, dot(rows, spread), 0.0)
        s.par_fc1[0:1, :] = jnp.sum(found, axis=0, keepdims=True)

    def standardized(rows):
        centered = rows - jnp.mean(rows, axis=-1, keepdims=True)
        scale = lax.rsqrt(jnp.mean(centered * centered, axis=-1, keepdims=True) + EPSILON)
        return centered * scale, scale

    def first_norm():
        def body(rows, _):
            found, _ = standardized(s.rows_in[rows, :].astype(F32))
            s.normed[rows, :] = (found * s.par[0:1, :] + s.par[2:3, :]).astype(BF16)
            return 0

        by_rows(body, 0)
        s.normed_t[...] = s.normed[...].T

    def project_qkv(tile):
        start = 384 * tile
        found = dot(s.normed[...], s.w_qkv[:, :, :, start : start + 384].reshape(D, 384))
        if tile < 2:
            found = (found + s.par[4:5, start : start + 384]) * 0.125
        if tile >= 4:
            found = found + s.par[5:6, start - 1536 : start - 1152]
        s.mixed[:, start : start + 384] = found.astype(BF16)

    def head_masks():
        first = (over((TOKENS, 128), 1) < 64).astype(F32)
        return first.astype(BF16), (1.0 - first).astype(BF16)

    def softmax(scores):
        expo = jnp.exp(scores - jnp.max(scores, axis=-1, keepdims=True))
        return expo * (1.0 / jnp.sum(expo, axis=-1, keepdims=True))

    def attend():
        def body(two, _):
            query, key, value = (s.mixed[:, lanes(128 * two + part, 128)] for part in (0, D, 2 * D))
            found = jnp.zeros((TOKENS, 128), F32)
            for mask in head_masks():
                probs = softmax(dot_nt(query * mask, key)).astype(BF16)
                found = found + dot(probs, value * mask)
            s.attended[:, lanes(128 * two, 128)] = found.astype(BF16)
            return 0

        lax.fori_loop(0, HEADS // 2, body, 0)

    def project_out():
        s.middle[...] = dot(s.attended[...], s.w_out[...].reshape(D, D))

        def body(rows, _):
            middle = s.rows_in[rows, :].astype(F32) + (s.middle[rows, :] + s.par[6:7, :])
            s.middle[rows, :] = middle
            found, _ = standardized(middle)
            s.normed2[rows, :] = (found * s.par[1:2, :] + s.par[3:4, :]).astype(BF16)
            return 0

        by_rows(body, 0)
        s.attended_t[...] = s.attended[...].T
        s.normed2_t[...] = s.normed2[...].T

    def feed(j):
        def body(side, _):
            start = 1536 * side + 384 * j
            columns = lanes(start, 384)
            s.total[:, 0:384] = dot(s.normed2[...], s.w_fc1[:, :, :, columns].reshape(D, 384))

            def gelu(rows, _):
                hidden = s.total[rows, 0:384] + s.par_fc1[0:1, columns]
                normal = 0.5 + 0.5 * lax.erf(hidden * (1.0 / math.sqrt(2.0)))
                bell = jnp.exp(-0.5 * hidden * hidden) * (1.0 / math.sqrt(2.0 * math.pi))
                s.slope[rows, columns] = normal + hidden * bell
                s.active[rows, columns] = (hidden * normal).astype(BF16)
                return 0

            by_rows(gelu, 0)
            s.active_t[pl.ds(16 * side + 4 * j, 4)] = s.active[:, columns].T.reshape(4, 96, 256)
            return 0

        lax.fori_loop(0, 2, body, 0)

    def gather_step(at):
        if at + 3 < len(gathers):
            gathers[at + 3].along_z()
        if at + 1 < len(gathers):
            gathers[at + 1].to_plane()
        if at < len(gathers):
            gathers[at].forward()
        if 0 <= at - 1 < len(gathers):
            gathers[at - 1].last()
        if 0 <= at - 2 < len(gathers):
            gathers[at - 2].done()

    gathers_at = [0]

    def next_gather():
        gather_step(gathers_at[0])
        gathers_at[0] += 1

    next_gather()
    next_gather()
    next_gather()
    unpack_small()
    for copy in rows_moved:
        copy.wait_recv()
    first_norm()
    cot_moved = to_frames(cotangent, s.cot_in)
    for j in range(3):
        next_gather()
        project_qkv(j)
        project_qkv(j + 3)
    attend()
    next_gather()
    project_out()
    for j in range(4):
        next_gather()
        feed(j)

    for copy in cot_moved:
        copy.wait_recv()
    valid = frame_valid[blk].astype(F32)

    def mask_cotangent(rows, _):
        s.g_branch2[rows, :] = (s.cot_in[rows, :].astype(F32) * valid).astype(BF16)
        return 0

    by_rows(mask_cotangent, 0)

    class Scatter:
        def __init__(self, own, other, pr, dx, dy, px, py, pz, finish):
            self.own, self.other, self.finish = own, other, finish
            self.pr, self.dx, self.dy, self.px, self.py, self.pz = pr, dx, dy, px, py, pz

        def pair(self):
            self.s = remote(self.other(), self.pr(ALL, ALL), sibling)

        def plane(self):
            self.s.wait_recv()

            def add(level, _):
                ref = self.own(level, ALL)
                ref[...] = ref[...] + self.pr(level, ALL)[...]
                return 0

            lax.fori_loop(0, 4, add, 0)
            self.a = remote(self.own(LOW, at_d), self.dx(), x_peer)
            self.b = remote(self.own(HIGH, at_d), self.dy(), y_peer)
            self.c = remote(self.own(LOW, at_x), self.px(LOW), x_peer)
            self.d = remote(self.own(HIGH, at_y), self.py(HIGH), y_peer)

        def plane2(self):
            self.a.wait_recv()
            ref = self.own(LOW, at_y)
            ref[...] = ref[...] + self.dx()[...]
            self.e = remote(ref, self.py(LOW), y_peer)
            self.b.wait_recv()
            ref = self.own(HIGH, at_x)
            ref[...] = ref[...] + self.dy()[...]
            self.f = remote(ref, self.px(HIGH), x_peer)

        def along_z(self):
            for copy in (self.c, self.d, self.e, self.f):
                copy.wait_recv()

            def add(level, _):
                ref = self.own(level, here)
                ref[...] = (
                    ref[...].astype(F32)
                    + self.px(level)[...].astype(F32)
                    + self.py(level)[...].astype(F32)
                ).astype(BF16)
                return 0

            lax.fori_loop(0, 4, add, 0)
            self.z = [remote(self.own(z_of[step], here), self.pz(step - 1), z_peers[step]) for step in (1, 2, 3)]

        def last(self):
            for copy in self.z:
                copy.wait_recv()
            self.finish(self)

        def summed(self, view):
            found = view(self.own(z, here))[...].astype(F32)
            for i in range(3):
                found = found + view(self.pz(i))[...].astype(F32)
            return found

    def columns_of(ref, base, half, start, size):
        def own(levels, places):
            return ref.at[levels, places, :, lanes(base + half * core + start, size)]

        def other():
            return ref.at[:, :, :, lanes(base + half * (1 - core) + start, size)]

        return own, other

    def column_scatter(ref, base, half, start, size, spot, output):
        at = pl.ds(spot, size)

        def finish(scatter):
            s.last_a[:, at] = scatter.summed(lambda ref: ref)
            target = lanes(half * core + start, size)
            other_rows = pl.ds(pl.multiple_of(24 * (1 - core), 8), 24)
            finals.append(remote(s.last_a.at[other_rows, at], output.at[:, target], sibling))
            output[:, target] = s.last_a[own_rows, at]

        return Scatter(
            *columns_of(ref, base, half, start, size),
            lambda levels, places: s.pr_a.at[levels, places, :, at],
            lambda: s.dx_a.at[:, :, at],
            lambda: s.dy_a.at[:, :, at],
            lambda levels: s.px_a.at[levels, :, at],
            lambda levels: s.py_a.at[levels, :, at],
            lambda i: s.pz_a.at[i, :, at],
            finish,
        )

    def fc2_scatter(j):
        rows = pl.ds(32 * j, 32)
        half = lanes(384 * core, 384)

        def finish(scatter):
            s.last_fc2[rows, :] = scatter.summed(lambda ref: ref.at[1 - core])
            finals.append(remote(s.last_fc2.at[rows, :], grad_fc2.at[rows, half], sibling))
            grad_fc2[rows, half] = scatter.summed(lambda ref: ref.at[core])

        return Scatter(
            lambda levels, places: s.g_fc2.at[levels, places, :, rows, half],
            lambda: s.g_fc2.at[:, :, :, rows, lanes(384 * (1 - core), 384)],
            lambda levels, places: s.pr_fc2.at[levels, places, :, rows, :],
            lambda: s.dx_fc2.at[:, :, rows, :],
            lambda: s.dy_fc2.at[:, :, rows, :],
            lambda levels: s.px_fc2.at[levels, :, rows, :],
            lambda levels: s.py_fc2.at[levels, :, rows, :],
            lambda i: s.pz_fc2.at[i, :, rows, :],
            finish,
        )

    def small_finish(scatter):
        found = scatter.summed(lambda ref: ref)
        grad_gain[...] = found[0:2, 0:24]
        grad_shift[...] = found[2:4, 0:24]
        grad_qv[...] = found[4:6, 0:24]
        grad_res[...] = found[6:8, 0:24]
        grad_fc1_bias[...] = found[8:9, 0:96]

    finals = []
    scatters = [fc2_scatter(j) for j in range(3)]
    scatters += [column_scatter(s.g_fc1, 0, 1536, 384 * j, 384, 384 * j, grad_fc1) for j in range(4)]
    scatters += [column_scatter(s.w_fc1, 0, 384, 0, 384, 1536, grad_out)]
    scatters += [column_scatter(s.w_fc1, 768, 1152, 384 * j, 384, 1920 + 384 * j, grad_qkv) for j in range(3)]
    scatters += [
        Scatter(
            *columns_of(s.g_small, 0, 128, 0, 128),
            lambda levels, places: s.pr_small.at[levels, places],
            lambda: s.dx_small,
            lambda: s.dy_small,
            lambda levels: s.px_small.at[levels],
            lambda levels: s.py_small.at[levels],
            lambda i: s.pz_small.at[i],
            small_finish,
        )
    ]

    def scatter_step(at):
        if at < len(scatters):
            scatters[at].plane()
        if 0 <= at - 1 < len(scatters):
            scatters[at - 1].plane2()
        if 0 <= at - 2 < len(scatters):
            scatters[at - 2].along_z()
        if 0 <= at - 3 < len(scatters):
            scatters[at - 3].last()

    scatters_at = [0]

    def next_scatter():
        scatter_step(scatters_at[0])
        scatters_at[0] += 1

    def weight_grad_fc2(j):
        def body(turn, _):
            columns = lanes(384 * (turn * core + (1 - turn) * (1 - core)), 384)
            found = dot(s.active_t[:, 32 * j : 32 * j + 32, :].reshape(1024, 256), s.g_branch2[:, columns])
            s.g_fc2[:, :, :, 32 * j : 32 * j + 32, columns] = found.astype(BF16).reshape(4, 4, 2, 32, 384)
            return 0

        lax.fori_loop(0, 2, body, 0)

    def column_grad(left, right, start, ref, base, half, size):
        def body(turn, _):
            side = turn * core + (1 - turn) * (1 - core)
            found = dot(left[...], right[:, lanes(half * side + start, size)])
            ref[:, :, :, lanes(base + half * side + start, size)] = found.astype(BF16).reshape(4, 4, 48, size)
            return 0

        lax.fori_loop(0, 2, body, 0)

    def column_sums(ref, width):
        return jnp.sum(ref[...].astype(F32), axis=0, keepdims=True)

    def feed_back():
        s.total[...] = jnp.zeros((TOKENS, D), F32)

        def body(level, _):
            columns = lanes(D * level, D)
            weight = s.w_fc2[level].reshape(D, D)
            s.total[...] += dot(s.active[:, columns], weight)
            s.g_middle[...] = dot_nt(s.g_branch2[...], weight)

            def slope(rows, sums):
                found = (s.g_middle[rows, :] * s.slope[rows, columns]).astype(BF16)
                s.active[rows, columns] = found
                return sums + jnp.sum(found.astype(F32), axis=0, keepdims=True)

            s.sums_fc1[0:1, columns] = by_rows(slope, jnp.zeros((1, D), F32))
            return 0

        lax.fori_loop(0, 4, body, 0)

        def finish(rows, sums):
            found = valid * (s.middle[rows, :] + (s.total[rows, :] + s.par[7:8, :]))
            s.enc_send[rows, :] = found.astype(BF16)
            return sums + jnp.sum(s.g_branch2[rows, :].astype(F32), axis=0, keepdims=True)

        s.sums[7:8, :] = by_rows(finish, jnp.zeros((1, D), F32))

    def norm_back(upstream, found, scale, gain):
        weighted = upstream * gain
        return scale * (
            weighted
            - jnp.mean(weighted, axis=-1, keepdims=True)
            - found * jnp.mean(weighted * found, axis=-1, keepdims=True)
        )

    def column_sum(values):
        return jnp.sum(values, axis=0, keepdims=True)

    def second_norm_back():
        s.total[...] = jnp.zeros((TOKENS, D), F32)

        def body(level, _):
            columns = lanes(D * level, D)
            s.total[...] += dot_nt(s.active[:, columns], s.w_fc1[:, :, :, columns].reshape(D, D))
            return 0

        lax.fori_loop(0, 4, body, 0)

        def rows_back(rows, sums):
            upstream = s.total[rows, :]
            found, scale = standardized(s.middle[rows, :])
            middle = s.g_branch2[rows, :].astype(F32) + norm_back(upstream, found, scale, s.par[1:2, :])
            s.g_middle[rows, :] = middle
            branch = middle.astype(BF16)
            s.g_branch[rows, :] = branch
            return (
                sums[0] + column_sum(upstream * found),
                sums[1] + column_sum(upstream),
                sums[2] + column_sum(branch.astype(F32)),
            )

        empty = jnp.zeros((1, D), F32)
        s.sums[1:2, :], s.sums[3:4, :], s.sums[6:7, :] = by_rows(rows_back, (empty, empty, empty))

    def attend_back():
        def body(two, _):
            spots = [lanes(128 * two + part, 128) for part in (0, D, 2 * D)]
            query, key, value = (s.mixed[:, spot] for spot in spots)
            upstream = s.g_attended[:, spots[0]]
            g_query, g_key, g_value = (jnp.zeros((TOKENS, 128), F32) for _ in range(3))
            for mask in head_masks():
                probs = softmax(dot_nt(query * mask, key))
                g_probs = dot_nt(upstream * mask, value)
                g_value = g_value + dot_tn(probs.astype(BF16), upstream * mask)
                inner = jnp.sum(probs * g_probs, axis=-1, keepdims=True)
                g_scores = (probs * (g_probs - inner)).astype(BF16)
                g_query = g_query + dot(g_scores, key * mask)
                g_key = g_key + dot_tn(g_scores, query * mask)
            g_query = 0.125 * g_query.astype(BF16).astype(F32)
            g_value = g_value.astype(BF16)
            s.g_mixed[:, spots[0]] = g_query.astype(BF16)
            s.g_mixed[:, spots[1]] = g_key.astype(BF16)
            s.g_mixed[:, spots[2]] = g_value
            s.sums[4:5, spots[0]] = column_sum(g_query)
            s.sums[5:6, spots[0]] = column_sum(g_value.astype(F32))
            return 0

        lax.fori_loop(0, HEADS // 2, body, 0)

    def first_norm_back():
        s.total[...] = jnp.zeros((TOKENS, D), F32)

        def body(level, _):
            columns = lanes(D * level, D)
            s.total[...] += dot_nt(s.g_mixed[:, columns], s.w_qkv[:, :, :, columns].reshape(D, D))
            return 0

        lax.fori_loop(0, 3, body, 0)

        def rows_back(rows, sums):
            upstream = s.total[rows, :]
            found, scale = standardized(s.rows_in[rows, :].astype(F32))
            result = s.g_middle[rows, :] + norm_back(upstream, found, scale, s.par[0:1, :])
            s.gx_send[rows, :] = result.astype(BF16)
            return (sums[0] + column_sum(upstream * found), sums[1] + column_sum(upstream))

        empty = jnp.zeros((1, D), F32)
        s.sums[0:1, :], s.sums[2:3, :] = by_rows(rows_back, (empty, empty))

    def pack_small():
        chips = lax.shift_right_logical(over((256, D), 0), 4)
        pieces = piece24(over((256, D), 1))
        spread = spread24()
        rows = jnp.broadcast_to(s.sums[...][None], (16, 16, D)).reshape(256, D)
        for side in (0, 1):
            placed = dot_nt(jnp.where(pieces == 2 * chips + side, rows, 0.0).astype(BF16), spread)
            s.g_small[:, :, :, 128 * side : 128 * side + 128] = placed.astype(BF16).reshape(4, 4, 16, 128)
        put = (over((256, 16), 0) == 16 * over((256, 16), 1) + 8).astype(F32).astype(BF16)
        spread = spread96()
        pieces = piece96(over((16, FF), 1))
        row = s.sums_fc1[0:1, :]
        for side in (0, 1):
            mine = pieces == 2 * over((16, FF), 0) + side
            placed = dot_nt(jnp.where(mine, row, 0.0).astype(BF16), spread).astype(BF16)
            here_ = s.g_small.at[:, :, :, pl.ds(128 * side, 128)]
            here_[...] = here_[...] + dot(put, placed).astype(BF16).reshape(4, 4, 16, 128)

    for j in range(3):
        weight_grad_fc2(j)
        scatters[j].pair()
    next_gather()
    next_scatter()
    next_gather()
    next_scatter()
    next_gather()
    next_scatter()
    feed_back()

    def to_patches(source, target):
        return [
            remote(
                source.at[pl.ds(pl.multiple_of(64 * (2 * py + pc), 64), 64), :],
                target.at[blk],
                (wide, 2 * py + pc),
            )
            for py, pc in blk_peers
        ]

    moved = to_patches(s.enc_send, encoded)
    encoded[blk] = s.enc_send[mine, :]
    for j in range(4):
        column_grad(s.normed2_t, s.active, 384 * j, s.g_fc1, 0, 1536, 384)
        scatters[3 + j].pair()
    next_scatter()
    second_norm_back()
    next_scatter()
    for gather in gathers[5:9]:
        sent(gather.copies())
    column_grad(s.attended_t, s.g_branch, 0, s.w_fc1, 0, 384, 384)
    scatters[7].pair()
    s.g_attended[...] = dot_nt(s.g_branch[...], s.w_out[...].reshape(D, D)).astype(BF16)
    next_scatter()
    attend_back()
    next_scatter()
    for j in range(3):
        column_grad(s.normed_t, s.g_mixed, 384 * j, s.w_fc1, D, 1152, 384)
        scatters[8 + j].pair()
    next_scatter()
    first_norm_back()
    moved += to_patches(s.gx_send, s.gx_recv)
    s.gx_recv[blk] = s.gx_send[mine, :]
    next_scatter()
    pack_small()
    scatters[11].pair()
    while scatters_at[0] < len(scatters) + 3:
        next_scatter()
    for copy in moved + finals:
        copy.wait_recv()
    grad_patches[...] = s.gx_recv[...].astype(F32)
    sent(started)


def fast(
    patches,
    norm_gain,
    norm_bias,
    qkv_weight,
    qv_bias,
    out_weight,
    fc1_weight,
    fc1_bias,
    fc2_weight,
    res_bias,
    cotangent,
    frame_valid,
):
    outputs = [
        ((4, 64, D), BF16),
        ((4, 64, D), F32),
        ((2, 24), F32),
        ((2, 24), F32),
        ((24, 3 * D), F32),
        ((2, 24), F32),
        ((24, D), F32),
        ((24, FF), F32),
        ((1, 96), F32),
        ((96, D), F32),
        ((2, 24), F32),
    ]
    vmem = pl.BlockSpec(memory_space=pltpu.VMEM)
    found = list(pl.pallas_call(
        layer_kernel,
        out_shape=[jax.ShapeDtypeStruct(shape, dtype) for shape, dtype in outputs],
        in_specs=[vmem] * 11 + [pl.BlockSpec(memory_space=pltpu.SMEM)],
        out_specs=[vmem] * len(outputs),
        scratch_shapes=list(scratch_shapes().values()),
        compiler_params=pltpu.CompilerParams(
            collective_id=0, has_side_effects=True, vmem_limit_bytes=63 * 2**20
        ),
    )(
        patches,
        norm_gain,
        norm_bias,
        qkv_weight,
        qv_bias,
        out_weight,
        fc1_weight,
        fc1_bias.reshape(1, 96),
        fc2_weight,
        res_bias,
        cotangent,
        frame_valid,
    ))
    found[8] = found[8].reshape(96)
    return tuple(found)


def solution(mesh):
    in_specs = (
        P("wide", "blk", None),
        P(None, ("wide", "blk")),
        P(None, ("wide", "blk")),
        P(("wide", "blk"), None),
        P(None, ("wide", "blk")),
        P(("wide", "blk"), None),
        P(("wide", "blk"), None),
        P(("wide", "blk")),
        P(("wide", "blk"), None),
        P(None, ("wide", "blk")),
        P("wide", "blk", None),
        P("wide"),
    )
    out_specs = (
        P("wide", "blk", None),
        P("wide", "blk", None),
        P(None, ("wide", "blk")),
        P(None, ("wide", "blk")),
        P(("wide", "blk"), None),
        P(None, ("wide", "blk")),
        P(("wide", "blk"), None),
        P(("wide", "blk"), None),
        P(("wide", "blk")),
        P(("wide", "blk"), None),
        P(None, ("wide", "blk")),
    )
    body = fast if dict(mesh.shape) == {"wide": 8, "blk": 4} else local
    return jax.shard_map(body, mesh=mesh, in_specs=in_specs, out_specs=out_specs, check_vma=False)
```

```python
from functools import partial
import math
import types

import jax
import jax.numpy as jnp
from jax import lax
from jax.experimental import pallas as pl
from jax.experimental.pallas import tpu as pltpu
from jax.sharding import PartitionSpec as P

D = 768
HEADS = 12
HEAD = 64


EPSILON = 1e-06


def layer_normalize(token_rows, norm_gain_vector, norm_bias_vector):
    row_average = jnp.mean(token_rows, axis=-1, keepdims=True)
    centered_rows = token_rows - row_average
    inverse_deviation_scale = lax.rsqrt(
        jnp.mean(centered_rows * centered_rows, axis=-1, keepdims=True) + EPSILON
    )
    standardized_rows = centered_rows * inverse_deviation_scale
    return (
        standardized_rows * norm_gain_vector + norm_bias_vector,
        standardized_rows,
        inverse_deviation_scale,
    )


def layer_normalize_backward(
    incoming_gradient, standardized_rows, inverse_deviation_scale, norm_gain_vector
):
    gain_weighted_gradient = incoming_gradient * norm_gain_vector
    inner_product_sum = (
        gain_weighted_gradient
        - jnp.mean(gain_weighted_gradient, axis=-1, keepdims=True)
        - standardized_rows
        * jnp.mean(gain_weighted_gradient * standardized_rows, axis=-1, keepdims=True)
    )
    return (
        inverse_deviation_scale * inner_product_sum,
        jnp.sum(incoming_gradient * standardized_rows, axis=0),
        jnp.sum(incoming_gradient, axis=0),
    )


def frame_groups(array, count):
    return array.reshape((array.shape[0] // count, count) + array.shape[1:])


def attend_forward(query, keys, values):
    scores = jnp.einsum("gqhe,gkhe->ghqk", query, keys, preferred_element_type=jnp.float32)
    top = jnp.max(scores, axis=-1, keepdims=True)
    expo = jnp.exp(scores - top)
    total = jnp.sum(expo, axis=-1, keepdims=True)
    probs = (expo / total).astype(jnp.bfloat16)
    attended = jnp.einsum("ghqk,gkhe->gqhe", probs, values, preferred_element_type=jnp.float32)
    return (attended, top + jnp.log(total))


def attend_back(query, keys, values, logsum, grad_out):
    scores = jnp.einsum("gqhe,gkhe->ghqk", query, keys, preferred_element_type=jnp.float32)
    probs = jnp.exp(scores - logsum)
    grad_probs = jnp.einsum("gqhe,gkhe->ghqk", grad_out, values, preferred_element_type=jnp.float32)
    grad_values = jnp.einsum(
        "ghqk,gqhe->gkhe", probs.astype(jnp.bfloat16), grad_out, preferred_element_type=jnp.float32
    )
    grad_scores = (
        probs * (grad_probs - jnp.sum(probs * grad_probs, axis=-1, keepdims=True))
    ).astype(jnp.bfloat16)
    grad_query = jnp.einsum(
        "ghqk,gkhe->gqhe", grad_scores, keys, preferred_element_type=jnp.float32
    )
    grad_keys = jnp.einsum(
        "ghqk,gqhe->gkhe", grad_scores, query, preferred_element_type=jnp.float32
    )
    return (grad_query, grad_keys, grad_values)


def local(
    patches,
    norm_gain,
    norm_bias,
    qkv_weight,
    qv_bias,
    out_weight,
    fc1_weight,
    fc1_bias,
    fc2_weight,
    res_bias,
    cotangent,
    frame_valid,
):
    frames, frame_rows, width = patches.shape
    count = frames * frame_rows
    group = math.gcd(frames, 8)
    params = (
        lax.all_gather(norm_gain, ("wide", "blk"), axis=1, tiled=True),
        lax.all_gather(norm_bias, ("wide", "blk"), axis=1, tiled=True),
        lax.all_gather(qkv_weight, ("wide", "blk"), axis=0, tiled=True),
        lax.all_gather(qv_bias, ("wide", "blk"), axis=1, tiled=True),
        lax.all_gather(out_weight, ("wide", "blk"), axis=0, tiled=True),
        lax.all_gather(fc1_weight, ("wide", "blk"), axis=0, tiled=True),
        lax.all_gather(fc1_bias, ("wide", "blk"), axis=0, tiled=True),
        lax.all_gather(fc2_weight, ("wide", "blk"), axis=0, tiled=True),
        lax.all_gather(res_bias, ("wide", "blk"), axis=1, tiled=True),
    )
    norm_gain_pair = params[0].astype(jnp.float32)
    norm_bias_pair = params[1].astype(jnp.float32)
    biases_qv = params[3].astype(jnp.float32)
    bias_fc1 = params[6].astype(jnp.float32)
    biases_res = params[8].astype(jnp.float32)
    token_rows = patches.reshape(count, width).astype(jnp.float32)
    valid = jnp.repeat(frame_valid.astype(jnp.float32), frame_rows)[:, None]
    first_branch, first_standardized_rows, first_norm_scale = layer_normalize(
        token_rows, norm_gain_pair[0], norm_bias_pair[0]
    )
    normed = first_branch.astype(jnp.bfloat16)
    mixed = jnp.dot(normed, params[2], preferred_element_type=jnp.float32)
    query = ((mixed[:, :D] + biases_qv[0]) * 0.125).astype(jnp.bfloat16)
    keys = mixed[:, D : 2 * D].astype(jnp.bfloat16).reshape(frames, frame_rows, width)
    values = (
        (mixed[:, 2 * D :] + biases_qv[1]).astype(jnp.bfloat16).reshape(frames, frame_rows, width)
    )
    keys_all, values_all = (
        lax.all_gather(keys, "blk", axis=1, tiled=True),
        lax.all_gather(values, "blk", axis=1, tiled=True),
    )
    query_heads = frame_groups(query.reshape(frames, frame_rows, HEADS, HEAD), group)
    keys_heads = frame_groups(keys_all.reshape(frames, -1, HEADS, HEAD), group)
    values_heads = frame_groups(values_all.reshape(frames, -1, HEADS, HEAD), group)
    attended, logsum = lax.map(
        lambda item: attend_forward(item[0], item[1], item[2]),
        (query_heads, keys_heads, values_heads),
    )
    attended = attended.reshape(count, width).astype(jnp.bfloat16)
    middle_activation = (
        token_rows
        + jnp.dot(attended, params[4], preferred_element_type=jnp.float32)
        + biases_res[0]
    )
    second_branch, second_standardized_rows, second_norm_scale = layer_normalize(
        middle_activation, norm_gain_pair[1], norm_bias_pair[1]
    )
    normed2 = second_branch.astype(jnp.bfloat16)
    hidden = jnp.dot(normed2, params[5], preferred_element_type=jnp.float32) + bias_fc1
    active = jax.nn.gelu(hidden, approximate=False).astype(jnp.bfloat16)
    branch2 = jnp.dot(active, params[7], preferred_element_type=jnp.float32) + biases_res[1]
    encoded = (
        ((middle_activation + branch2) * valid)
        .astype(jnp.bfloat16)
        .reshape(frames, frame_rows, width)
    )
    params = (
        lax.all_gather(norm_gain, ("wide", "blk"), axis=1, tiled=True),
        lax.all_gather(norm_bias, ("wide", "blk"), axis=1, tiled=True),
        lax.all_gather(qkv_weight, ("wide", "blk"), axis=0, tiled=True),
        lax.all_gather(qv_bias, ("wide", "blk"), axis=1, tiled=True),
        lax.all_gather(out_weight, ("wide", "blk"), axis=0, tiled=True),
        lax.all_gather(fc1_weight, ("wide", "blk"), axis=0, tiled=True),
        lax.all_gather(fc1_bias, ("wide", "blk"), axis=0, tiled=True),
        lax.all_gather(fc2_weight, ("wide", "blk"), axis=0, tiled=True),
        lax.all_gather(res_bias, ("wide", "blk"), axis=1, tiled=True),
    )
    grad_out = cotangent.reshape(count, width).astype(jnp.float32) * valid
    grad_branch2 = grad_out.astype(jnp.bfloat16)
    grad_fc2 = jnp.dot(active.T, grad_branch2, preferred_element_type=jnp.float32)
    grad_res_two = jnp.sum(grad_branch2.astype(jnp.float32), axis=0)
    grad_active = jnp.dot(grad_branch2, params[7].T, preferred_element_type=jnp.float32)
    gelu_back = jax.vjp(partial(jax.nn.gelu, approximate=False), hidden)[1]
    grad_hidden = gelu_back(grad_active)[0].astype(jnp.bfloat16)
    grad_fc1 = jnp.dot(normed2.T, grad_hidden, preferred_element_type=jnp.float32)
    grad_bias_fc1 = jnp.sum(grad_hidden.astype(jnp.float32), axis=0)
    normed_input_gradient2 = jnp.dot(grad_hidden, params[5].T, preferred_element_type=jnp.float32)
    second_norm_gradient, second_norm_gain, second_norm_bias = layer_normalize_backward(
        normed_input_gradient2, second_standardized_rows, second_norm_scale, norm_gain_pair[1]
    )
    grad_middle = grad_out + second_norm_gradient
    grad_branch = grad_middle.astype(jnp.bfloat16)
    grad_out_proj = jnp.dot(attended.T, grad_branch, preferred_element_type=jnp.float32)
    grad_res_one = jnp.sum(grad_branch.astype(jnp.float32), axis=0)
    grad_attended = jnp.dot(grad_branch, params[4].T, preferred_element_type=jnp.float32).astype(
        jnp.bfloat16
    )
    grad_heads = frame_groups(grad_attended.reshape(frames, frame_rows, HEADS, HEAD), group)
    grad_query, grad_keys, grad_values = lax.map(
        lambda item: attend_back(item[0], item[1], item[2], item[3], item[4]),
        (query_heads, keys_heads, values_heads, logsum, grad_heads),
    )
    grad_keys, grad_values = (
        lax.psum_scatter(
            grad_keys.reshape(frames, -1, width).astype(jnp.bfloat16),
            "blk",
            scatter_dimension=1,
            tiled=True,
        ).astype(jnp.float32),
        lax.psum_scatter(
            grad_values.reshape(frames, -1, width).astype(jnp.bfloat16),
            "blk",
            scatter_dimension=1,
            tiled=True,
        ).astype(jnp.float32),
    )
    grad_query = grad_query.reshape(count, width).astype(jnp.bfloat16) * 0.125
    grad_keys = grad_keys.reshape(count, width).astype(jnp.bfloat16)
    grad_values = grad_values.reshape(count, width).astype(jnp.bfloat16)
    grad_mixed = jnp.concatenate([grad_query, grad_keys, grad_values], axis=1)
    grad_qkv = jnp.dot(normed.T, grad_mixed, preferred_element_type=jnp.float32)
    grad_qv = jnp.stack(
        [
            jnp.sum(grad_query.astype(jnp.float32), axis=0),
            jnp.sum(grad_values.astype(jnp.float32), axis=0),
        ]
    )
    normed_input_gradient = jnp.dot(grad_mixed, params[2].T, preferred_element_type=jnp.float32)
    first_norm_gradient, first_norm_gain, first_norm_bias = layer_normalize_backward(
        normed_input_gradient, first_standardized_rows, first_norm_scale, norm_gain_pair[0]
    )
    grad_rows = (grad_middle + first_norm_gradient).reshape(frames, frame_rows, width)
    grad_gain = jnp.stack([first_norm_gain, second_norm_gain])
    grad_shift = jnp.stack([first_norm_bias, second_norm_bias])
    grad_res = jnp.stack([grad_res_one, grad_res_two])
    summed = (
        lax.psum_scatter(grad_gain, ("wide", "blk"), scatter_dimension=1, tiled=True),
        lax.psum_scatter(grad_shift, ("wide", "blk"), scatter_dimension=1, tiled=True),
        lax.psum_scatter(grad_qkv, ("wide", "blk"), scatter_dimension=0, tiled=True),
        lax.psum_scatter(grad_qv, ("wide", "blk"), scatter_dimension=1, tiled=True),
        lax.psum_scatter(grad_out_proj, ("wide", "blk"), scatter_dimension=0, tiled=True),
        lax.psum_scatter(grad_fc1, ("wide", "blk"), scatter_dimension=0, tiled=True),
        lax.psum_scatter(grad_bias_fc1, ("wide", "blk"), scatter_dimension=0, tiled=True),
        lax.psum_scatter(grad_fc2, ("wide", "blk"), scatter_dimension=0, tiled=True),
        lax.psum_scatter(grad_res, ("wide", "blk"), scatter_dimension=1, tiled=True),
    )
    return (
        encoded,
        grad_rows,
        summed[0],
        summed[1],
        summed[2],
        summed[3],
        summed[4],
        summed[5],
        summed[6],
        summed[7],
        summed[8],
    )


MESH_ID = pl.DeviceIdType.MESH
BF16 = jnp.bfloat16
F32 = jnp.float32
FF = 3072
TOKENS = 256
ROWS = 64
ALL = pl.ds(0, 4)
GATHER_WAYS = dict(q=(2, 2, 2), o=(2,), h=(2, 2, 1, 1), f=(2, 1, 0))
SCATTER_WAYS = dict(f=(0, 3, 2), h=(3, 2, 3, 2), o=(2,), q=(2, 2, 2))


def dot(left, right):
    return lax.dot_general(left, right, (((1,), (0,)), ((), ())), preferred_element_type=F32)


def dot_nt(left, right):
    return lax.dot_general(left, right, (((1,), (1,)), ((), ())), preferred_element_type=F32)


def dot_tn(left, right):
    return lax.dot_general(left, right, (((0,), (0,)), ((), ())), preferred_element_type=F32)


COPIES = 360


def scratch_shapes():
    def vm(*shape, dtype=BF16):
        return pltpu.VMEM(shape, dtype)

    return dict(
        w_small=vm(4, 4, 16, 256),
        w_qkv=vm(4, 4, 48, 2304),
        w_out=vm(4, 4, 48, 768),
        w_fc1=vm(4, 4, 48, 3072),
        w_fc2=vm(4, 4, 2, 96, 768),
        own_small=vm(16, 128, dtype=F32),
        pair_rows=vm(48, 3072, dtype=F32),
        pair_send=vm(24, 3072, dtype=F32),
        par=vm(16, 768, dtype=F32),
        par_fc1=vm(8, 3072, dtype=F32),
        rows_in=vm(256, 768),
        cot_in=vm(256, 768),
        normed=vm(256, 768),
        normed_t=vm(768, 256),
        mixed=vm(256, 2304),
        attended=vm(256, 768),
        attended_t=vm(768, 256),
        middle=vm(256, 768, dtype=F32),
        normed2=vm(256, 768),
        normed2_t=vm(768, 256),
        slope=vm(256, 3072, dtype=F32),
        active=vm(256, 3072),
        active_t=vm(32, 96, 256),
        g_branch2=vm(256, 768),
        total=vm(256, 768, dtype=F32),
        g_middle=vm(256, 768, dtype=F32),
        g_branch=vm(256, 768),
        g_attended=vm(256, 768),
        g_mixed=vm(256, 2304),
        enc_send=vm(256, 768),
        gx_send=vm(256, 768),
        gx_recv=vm(4, 64, 768),
        sums=vm(16, 768, dtype=F32),
        sums_fc1=vm(8, 3072, dtype=F32),
        g_small=vm(4, 4, 16, 256),
        g_fc1=vm(4, 4, 48, 3072),
        g_fc2=vm(4, 4, 2, 96, 768),
        pr_small=vm(4, 4, 16, 128),
        pr_a=vm(4, 4, 48, 3072),
        pr_fc2=vm(4, 4, 2, 96, 384),
        dx_small=vm(4, 16, 128),
        dx_a=vm(4, 48, 3072),
        dx_fc2=vm(4, 2, 96, 384),
        px_small=vm(4, 16, 128),
        px_a=vm(4, 48, 3072),
        px_fc2=vm(4, 2, 96, 384),
        py_small=vm(4, 16, 128),
        py_a=vm(4, 48, 3072),
        py_fc2=vm(4, 2, 96, 384),
        pz_small=vm(3, 16, 128),
        pz_a=vm(3, 48, 3072),
        pz_fc2=vm(3, 2, 96, 384),
        bz_fc2=vm(3, 4, 2, 96, 384),
        last_a=vm(48, 3072, dtype=F32),
        last_fc2=vm(96, 384, dtype=F32),
        send_sem=pltpu.SemaphoreType.DMA((COPIES,)),
        recv_sem=pltpu.SemaphoreType.DMA((COPIES,)),
    )


def layer_kernel(
    patches,
    norm_gain,
    norm_bias,
    qkv_weight,
    qv_bias,
    out_weight,
    fc1_weight,
    fc1_bias,
    fc2_weight,
    res_bias,
    cotangent,
    frame_valid,
    encoded,
    grad_patches,
    grad_gain,
    grad_shift,
    grad_qkv,
    grad_qv,
    grad_out,
    grad_fc1,
    grad_fc1_bias,
    grad_fc2,
    grad_res,
    *scratch,
):
    s = types.SimpleNamespace(**dict(zip(scratch_shapes(), scratch)))
    wide, blk = lax.axis_index("wide"), lax.axis_index("blk")
    z, x = lax.div(wide, 2), lax.rem(wide, 2)
    y, core = lax.div(blk, 2), lax.rem(blk, 2)
    here, at_x, at_y, at_d = 2 * x + y, 2 * (1 - x) + y, 2 * x + 1 - y, 2 * (1 - x) + 1 - y
    sibling = (wide, 2 * y + 1 - core)
    x_peer = (2 * z + 1 - x, blk)
    y_peer = (wide, 2 * (1 - y) + core)
    d_peer = (2 * z + 1 - x, 2 * (1 - y) + core)
    y_cross = (wide, 2 * (1 - y) + 1 - core)
    z_of = [lax.rem(z + step, 4) for step in range(4)]
    z_peers = [(2 * z_of[step] + x, blk) for step in range(4)]
    blk_peers = [(y, 1 - core), (1 - y, core), (1 - y, 1 - core)]

    barrier = pltpu.get_barrier_semaphore()
    peers = [sibling, x_peer, y_peer, d_peer, y_cross] + z_peers[1:]
    for peer in peers:
        pl.semaphore_signal(barrier, inc=1, device_id=peer, device_id_type=MESH_ID)

    started, waited = [], set()

    def sent(copies):
        for copy in copies:
            if id(copy) not in waited:
                waited.add(id(copy))
                copy.wait_send()

    def remote(source, target, peer):
        spot = len(started)
        copy = pltpu.make_async_remote_copy(
            src_ref=source,
            dst_ref=target,
            send_sem=s.send_sem.at[spot],
            recv_sem=s.recv_sem.at[spot],
            device_id=peer,
            device_id_type=MESH_ID,
        )
        copy.start()
        started.append(copy)
        return copy

    def lanes(start, size):
        return pl.ds(pl.multiple_of(start, 128), size)

    s.own_small[...] = jnp.zeros((16, 128), F32)
    s.sums[...] = jnp.zeros((16, D), F32)
    s.own_small[0:2, 0:24] = norm_gain[...].astype(F32)
    s.own_small[2:4, 0:24] = norm_bias[...].astype(F32)
    s.own_small[4:6, 0:24] = qv_bias[...].astype(F32)
    s.own_small[6:8, 0:24] = res_bias[...].astype(F32)
    s.own_small[8:9, 0:96] = fc1_bias[...].astype(F32)
    s.w_small[z, here, :, lanes(128 * core, 128)] = s.own_small[...].astype(BF16)
    own_rows = pl.ds(pl.multiple_of(24 * core, 8), 24)
    for ref, half, start in ((qkv_weight, 1152, 0), (out_weight, 384, 1152), (fc1_weight, 1536, 1536)):
        s.pair_send[:, start : start + half] = ref[:, lanes((1 - core) * half, half)].astype(F32)
        s.pair_rows[own_rows, start : start + half] = ref[:, lanes(core * half, half)].astype(F32)
    s.w_fc2[z, here, core] = fc2_weight[...]

    pl.semaphore_wait(barrier, len(peers))

    pair = remote(s.pair_send, s.pair_rows.at[own_rows, :], sibling)

    mine = pl.ds(pl.multiple_of(64 * blk, 64), 64)

    def to_frames(source, target):
        return [remote(source.at[2 * py + pc], target.at[mine, :], (wide, 2 * py + pc)) for py, pc in blk_peers]

    s.rows_in[mine, :] = patches[blk]
    s.cot_in[mine, :] = cotangent[blk]

    class Gather:
        def __init__(self, part, low):
            self.part, self.low, self.high = part, pl.ds(0, low), pl.ds(low, 4 - low)

        def z(self):
            own = self.part(z, here)
            self.z_copies = [remote(own, own, z_peers[step]) for step in (1, 2, 3)]

        def p(self):
            for copy in self.z_copies:
                copy.wait_recv()
            column = self.part(ALL, here)
            self.x, self.y = remote(column, column, x_peer), remote(column, column, y_peer)
            self.pair = [remote(column, column, sibling)]

        def f(self):
            self.x.wait_recv()
            some = self.part(self.low, at_x)
            self.dy = remote(some, some, y_peer)
            column = self.part(ALL, at_x)
            self.pair.append(remote(column, column, sibling))

        def g(self):
            self.y.wait_recv()
            some = self.part(self.high, at_y)
            self.dx = remote(some, some, x_peer)
            column = self.part(ALL, at_y)
            self.pair.append(remote(column, column, sibling))

        def l(self):
            self.dy.wait_recv()
            self.dx.wait_recv()
            column = self.part(ALL, at_d)
            self.pair.append(remote(column, column, sibling))

        def d(self):
            for copy in self.pair:
                copy.wait_recv()

        def copies(self):
            return self.z_copies + self.pair + [self.x, self.y, self.dx, self.dy]

    class SquareGather:
        def __init__(self, part):
            self.part = part

        def p(self):
            own = self.part(z, here)
            self.square = [remote(own, own, peer) for peer in (x_peer, y_peer, d_peer)]

        def z(self):
            for copy in self.square:
                copy.wait_recv()
            level = self.part(z, ALL)
            self.z_copies = [remote(level, level, z_peers[step]) for step in (1, 2, 3)]
            self.pair = [remote(level, level, sibling)]

        def l(self):
            for step, copy in zip((1, 2, 3), self.z_copies):
                copy.wait_recv()
                level = self.part(z_of[4 - step], ALL)
                self.pair.append(remote(level, level, sibling))

        def d(self):
            for copy in self.pair:
                copy.wait_recv()

        def copies(self):
            return self.square + self.z_copies + self.pair

    def column_part(ref, half, start, size):
        return lambda levels, place: ref.at[levels, place, :, lanes(half * core + start, size)]

    def row_part(ref, start, size):
        return lambda levels, place: ref.at[levels, place, core, pl.ds(start, size), :]

    def gather(part, way):
        return Gather(part, way) if way else SquareGather(part)

    gathers = {"s0": gather(column_part(s.w_small, 128, 0, 128), 2)}
    for name, ref, half in (("q", s.w_qkv, 1152), ("o", s.w_out, 384), ("h", s.w_fc1, 1536)):
        for j in range(half // 384):
            gathers[name + str(j)] = gather(column_part(ref, half, 384 * j, 384), GATHER_WAYS[name][j])
    for j, way in enumerate(GATHER_WAYS["f"]):
        rows = 96 // len(GATHER_WAYS["f"])
        gathers["f" + str(j)] = gather(row_part(s.w_fc2, rows * j, rows), way)


    pair.wait_recv()
    for ref, half, start in ((s.w_qkv, 1152, 0), (s.w_out, 384, 1152), (s.w_fc1, 1536, 1536)):
        ref[z, here, :, lanes(core * half, half)] = s.pair_rows[:, start : start + half].astype(BF16)

    def by_rows(body, carry=None):
        def step(i, held):
            return body(pl.ds(pl.multiple_of(ROWS * i, ROWS), ROWS), held)

        return lax.fori_loop(0, TOKENS // ROWS, step, carry)

    def over(shape, axis):
        return lax.broadcasted_iota(jnp.int32, shape, axis)

    def piece24(columns):
        return lax.shift_right_logical(columns * 43691, 20)

    def piece96(columns):
        return lax.shift_right_logical(columns * 10923, 20)

    def spread24():
        columns = over((128, D), 1)
        return (columns - 24 * piece24(columns) == over((128, D), 0)).astype(F32).astype(BF16)

    def spread96():
        columns = over((128, FF), 1)
        return (columns - 96 * piece96(columns) == over((128, FF), 0)).astype(F32).astype(BF16)

    def unpack_small():
        flat = s.w_small[...].reshape(256, 256)
        chips = lax.shift_right_logical(over((256, D), 0), 4)
        pieces = piece24(over((256, D), 1))
        spread = spread24()
        found = jnp.zeros((16, D), F32)
        for side in (0, 1):
            wide_rows = dot(flat[:, 128 * side : 128 * side + 128], spread)
            wide_rows = jnp.where(pieces == 2 * chips + side, wide_rows, 0.0)
            found = found + jnp.sum(wide_rows.reshape(16, 16, D), axis=0)
        s.par[...] = found
        pick = (over((16, 256), 1) == 16 * over((16, 256), 0) + 8).astype(F32).astype(BF16)
        spread = spread96()
        pieces = piece96(over((16, FF), 1))
        found = jnp.zeros((16, FF), F32)
        for side in (0, 1):
            rows = dot(pick, flat[:, 128 * side : 128 * side + 128]).astype(BF16)
            found = found + jnp.where(pieces == 2 * over((16, FF), 0) + side, dot(rows, spread), 0.0)
        s.par_fc1[0:1, :] = jnp.sum(found, axis=0, keepdims=True)

    def standardized(rows):
        centered = rows - jnp.mean(rows, axis=-1, keepdims=True)
        scale = lax.rsqrt(jnp.mean(centered * centered, axis=-1, keepdims=True) + EPSILON)
        return centered * scale, scale

    def first_norm():
        def body(rows, _):
            found, _ = standardized(s.rows_in[rows, :].astype(F32))
            s.normed[rows, :] = (found * s.par[0:1, :] + s.par[2:3, :]).astype(BF16)
            return 0

        by_rows(body, 0)
        s.normed_t[...] = s.normed[...].T

    def project_qkv(tile):
        start = 384 * tile
        found = dot(s.normed[...], s.w_qkv[:, :, :, start : start + 384].reshape(D, 384))
        if tile < 2:
            found = (found + s.par[4:5, start : start + 384]) * 0.125
        if tile >= 4:
            found = found + s.par[5:6, start - 1536 : start - 1152]
        s.mixed[:, start : start + 384] = found.astype(BF16)

    def head_masks():
        first = (over((TOKENS, 128), 1) < 64).astype(F32)
        return first.astype(BF16), (1.0 - first).astype(BF16)

    def softmax(scores):
        expo = jnp.exp(scores - jnp.max(scores, axis=-1, keepdims=True))
        return expo * (1.0 / jnp.sum(expo, axis=-1, keepdims=True))

    def attend():
        def body(two, _):
            query, key, value = (s.mixed[:, lanes(128 * two + part, 128)] for part in (0, D, 2 * D))
            found = jnp.zeros((TOKENS, 128), F32)
            for mask in head_masks():
                probs = softmax(dot_nt(query * mask, key)).astype(BF16)
                found = found + dot(probs, value * mask)
            s.attended[:, lanes(128 * two, 128)] = found.astype(BF16)
            return 0

        lax.fori_loop(0, HEADS // 2, body, 0)

    def project_out():
        s.middle[...] = dot(s.attended[...], s.w_out[...].reshape(D, D))

        def body(rows, _):
            middle = s.rows_in[rows, :].astype(F32) + (s.middle[rows, :] + s.par[6:7, :])
            s.middle[rows, :] = middle
            found, _ = standardized(middle)
            s.normed2[rows, :] = (found * s.par[1:2, :] + s.par[3:4, :]).astype(BF16)
            return 0

        by_rows(body, 0)
        s.attended_t[...] = s.attended[...].T
        s.normed2_t[...] = s.normed2[...].T

    def feed(j):
        def body(side, _):
            start = 1536 * side + 384 * j
            columns = lanes(start, 384)
            s.total[:, 0:384] = dot(s.normed2[...], s.w_fc1[:, :, :, columns].reshape(D, 384))

            def gelu(rows, _):
                hidden = s.total[rows, 0:384] + s.par_fc1[0:1, columns]
                normal = 0.5 + 0.5 * lax.erf(hidden * (1.0 / math.sqrt(2.0)))
                bell = jnp.exp(-0.5 * hidden * hidden) * (1.0 / math.sqrt(2.0 * math.pi))
                s.slope[rows, columns] = normal + hidden * bell
                s.active[rows, columns] = (hidden * normal).astype(BF16)
                return 0

            by_rows(gelu, 0)
            s.active_t[pl.ds(16 * side + 4 * j, 4)] = s.active[:, columns].T.reshape(4, 96, 256)
            return 0

        lax.fori_loop(0, 2, body, 0)

    valid = frame_valid[blk].astype(F32)

    def mask_cotangent():
        def body(rows, _):
            s.g_branch2[rows, :] = (s.cot_in[rows, :].astype(F32) * valid).astype(BF16)
            return 0

        by_rows(body, 0)


    class Scatter:
        def __init__(self, own, other, pr, dx, dy, px, py, pz, finish, low=2):
            self.own, self.other, self.finish = own, other, finish
            self.pr, self.dx, self.dy, self.px, self.py, self.pz = pr, dx, dy, px, py, pz
            self.low, self.high = pl.ds(0, low), pl.ds(low, 4 - low)

        def s(self):
            self.pair = remote(self.other(), self.pr(ALL, ALL), sibling)

        def add_pair(self):
            self.pair.wait_recv()

            def add(level, _):
                ref = self.own(level, ALL)
                ref[...] = ref[...] + self.pr(level, ALL)[...]
                return 0

            lax.fori_loop(0, 4, add, 0)

        def p(self):
            self.add_pair()
            low, high = self.low, self.high
            self.a = remote(self.own(low, at_d), self.dx(low), x_peer)
            self.b = remote(self.own(high, at_d), self.dy(high), y_peer)
            self.c = remote(self.own(low, at_x), self.px(low), x_peer)
            self.d = remote(self.own(high, at_y), self.py(high), y_peer)

        def f(self):
            self.a.wait_recv()
            ref = self.own(self.low, at_y)
            ref[...] = ref[...] + self.dx(self.low)[...]
            self.e = remote(ref, self.py(self.low), y_peer)

        def g(self):
            self.b.wait_recv()
            ref = self.own(self.high, at_x)
            ref[...] = ref[...] + self.dy(self.high)[...]
            self.f_copy = remote(ref, self.px(self.high), x_peer)

        def z(self):
            for copy in (self.c, self.d, self.e, self.f_copy):
                copy.wait_recv()

            def add(level, _):
                ref = self.own(level, here)
                ref[...] = (
                    ref[...].astype(F32)
                    + self.px(level)[...].astype(F32)
                    + self.py(level)[...].astype(F32)
                ).astype(BF16)
                return 0

            lax.fori_loop(0, 4, add, 0)
            self.z_copies = [
                remote(self.own(z_of[step], here), self.pz(step - 1), z_peers[step]) for step in (1, 2, 3)
            ]

        def l(self):
            for copy in self.z_copies:
                copy.wait_recv()
            self.finish(self)

        def summed(self, view):
            found = view(self.own(z, here))[...].astype(F32)
            for i in range(3):
                found = found + view(self.pz(i))[...].astype(F32)
            return found

    class SquareScatter(Scatter):
        def __init__(self, own, other, pr, bz, pz, finish):
            self.own, self.other, self.finish = own, other, finish
            self.pr, self.bz, self.pz = pr, bz, pz

        def z(self):
            self.add_pair()
            self.z_copies = [
                remote(self.own(z_of[step], ALL), self.bz(step - 1, ALL), z_peers[step]) for step in (1, 2, 3)
            ]

        def p(self):
            for copy in self.z_copies:
                copy.wait_recv()

            def add(place, _):
                ref = self.own(z, place)
                found = ref[...].astype(F32)
                for i in range(3):
                    found = found + self.bz(i, place)[...].astype(F32)
                ref[...] = found.astype(BF16)
                return 0

            lax.fori_loop(0, 4, add, 0)
            targets = ((at_x, x_peer), (at_y, y_peer), (at_d, d_peer))
            self.square = [
                remote(self.own(z, place), self.pz(i), peer) for i, (place, peer) in enumerate(targets)
            ]

        def l(self):
            for copy in self.square:
                copy.wait_recv()
            self.finish(self)

    def columns_of(ref, base, half, start, size):
        def own(levels, places):
            return ref.at[levels, places, :, lanes(base + half * core + start, size)]

        def other():
            return ref.at[:, :, :, lanes(base + half * (1 - core) + start, size)]

        return own, other

    def column_scatter(ref, base, half, start, size, spot, output, way):
        at = pl.ds(spot, size)

        def finish(scatter):
            s.last_a[:, at] = scatter.summed(lambda ref: ref)
            target = lanes(half * core + start, size)
            other_rows = pl.ds(pl.multiple_of(24 * (1 - core), 8), 24)
            finals.append(remote(s.last_a.at[other_rows, at], output.at[:, target], sibling))
            output[:, target] = s.last_a[own_rows, at]

        if not way:
            extra = pl.ds(spot, size)
            return SquareScatter(
                *columns_of(ref, base, half, start, size),
                lambda levels, places: s.pr_a.at[levels, places, :, at],
                lambda i, places: s.bz_a.at[i, places, :, extra],
                lambda i: s.pz_a.at[i, :, at],
                finish,
            )
        return Scatter(
            *columns_of(ref, base, half, start, size),
            lambda levels, places: s.pr_a.at[levels, places, :, at],
            lambda levels: s.dx_a.at[levels, :, at],
            lambda levels: s.dx_a.at[levels, :, at],
            lambda levels: s.px_a.at[levels, :, at],
            lambda levels: s.py_a.at[levels, :, at],
            lambda i: s.pz_a.at[i, :, at],
            finish,
            way,
        )

    def fc2_scatter(j, size, way):
        rows = pl.ds(size * j, size)
        half = lanes(384 * core, 384)

        def finish(scatter):
            s.last_fc2[rows, :] = scatter.summed(lambda ref: ref.at[1 - core])
            finals.append(remote(s.last_fc2.at[rows, :], grad_fc2.at[rows, half], sibling))
            grad_fc2[rows, half] = scatter.summed(lambda ref: ref.at[core])

        own = lambda levels, places: s.g_fc2.at[levels, places, :, rows, half]
        other = lambda: s.g_fc2.at[:, :, :, rows, lanes(384 * (1 - core), 384)]
        pr = lambda levels, places: s.pr_fc2.at[levels, places, :, rows, :]
        pz = lambda i: s.pz_fc2.at[i, :, rows, :]
        if not way:
            return SquareScatter(own, other, pr, lambda i, places: s.bz_fc2.at[i, places, :, rows, :], pz, finish)
        return Scatter(
            own,
            other,
            pr,
            lambda levels: s.dx_fc2.at[levels, :, rows, :],
            lambda levels: s.dx_fc2.at[levels, :, rows, :],
            lambda levels: s.px_fc2.at[levels, :, rows, :],
            lambda levels: s.py_fc2.at[levels, :, rows, :],
            pz,
            finish,
            way,
        )

    def small_finish(scatter):
        found = scatter.summed(lambda ref: ref)
        grad_gain[...] = found[0:2, 0:24]
        grad_shift[...] = found[2:4, 0:24]
        grad_qv[...] = found[4:6, 0:24]
        grad_res[...] = found[6:8, 0:24]
        grad_fc1_bias[...] = found[8:9, 0:96]

    finals = []
    scatters = {}
    for j, way in enumerate(SCATTER_WAYS["f"]):
        scatters["f" + str(j)] = fc2_scatter(j, 96 // len(SCATTER_WAYS["f"]), way)
    for name, ref, base, half, spot, output in (
        ("h", s.g_fc1, 0, 1536, 0, grad_fc1),
        ("o", s.w_fc1, 0, 384, 1536, grad_out),
        ("q", s.w_fc1, D, 1152, 1920, grad_qkv),
    ):
        for j in range(half // 384):
            way = SCATTER_WAYS[name][j]
            scatters[name + str(j)] = column_scatter(
                ref, base, half, 384 * j, 384, spot + 384 * j, output, way
            )
    scatters["s0"] = Scatter(
        *columns_of(s.g_small, 0, 128, 0, 128),
        lambda levels, places: s.pr_small.at[levels, places],
        lambda levels: s.dx_small.at[levels],
        lambda levels: s.dx_small.at[levels],
        lambda levels: s.px_small.at[levels],
        lambda levels: s.py_small.at[levels],
        lambda i: s.pz_small.at[i],
        small_finish,
    )

    def weight_grad_fc2(j):
        size = 96 // len(SCATTER_WAYS["f"])
        rows = pl.ds(size * j, size)

        def body(turn, _):
            columns = lanes(384 * (turn * core + (1 - turn) * (1 - core)), 384)
            found = dot(s.active_t[:, rows, :].reshape(32 * size, 256), s.g_branch2[:, columns])
            s.g_fc2[:, :, :, rows, columns] = found.astype(BF16).reshape(4, 4, 2, size, 384)
            return 0

        lax.fori_loop(0, 2, body, 0)

    def column_grad(left, right, start, ref, base, half, size):
        def body(turn, _):
            side = turn * core + (1 - turn) * (1 - core)
            found = dot(left[...], right[:, lanes(half * side + start, size)])
            ref[:, :, :, lanes(base + half * side + start, size)] = found.astype(BF16).reshape(4, 4, 48, size)
            return 0

        lax.fori_loop(0, 2, body, 0)

    def column_sums(ref, width):
        return jnp.sum(ref[...].astype(F32), axis=0, keepdims=True)

    def feed_back():
        s.total[...] = jnp.zeros((TOKENS, D), F32)

        def body(level, _):
            columns = lanes(D * level, D)
            weight = s.w_fc2[level].reshape(D, D)
            s.total[...] += dot(s.active[:, columns], weight)
            s.g_middle[...] = dot_nt(s.g_branch2[...], weight)

            def slope(rows, sums):
                found = (s.g_middle[rows, :] * s.slope[rows, columns]).astype(BF16)
                s.active[rows, columns] = found
                return sums + jnp.sum(found.astype(F32), axis=0, keepdims=True)

            s.sums_fc1[0:1, columns] = by_rows(slope, jnp.zeros((1, D), F32))
            return 0

        lax.fori_loop(0, 4, body, 0)

        def finish(rows, sums):
            found = valid * (s.middle[rows, :] + (s.total[rows, :] + s.par[7:8, :]))
            s.enc_send[rows, :] = found.astype(BF16)
            return sums + jnp.sum(s.g_branch2[rows, :].astype(F32), axis=0, keepdims=True)

        s.sums[7:8, :] = by_rows(finish, jnp.zeros((1, D), F32))

    def norm_back(upstream, found, scale, gain):
        weighted = upstream * gain
        return scale * (
            weighted
            - jnp.mean(weighted, axis=-1, keepdims=True)
            - found * jnp.mean(weighted * found, axis=-1, keepdims=True)
        )

    def column_sum(values):
        return jnp.sum(values, axis=0, keepdims=True)

    def second_norm_back():
        s.total[...] = jnp.zeros((TOKENS, D), F32)

        def body(level, _):
            columns = lanes(D * level, D)
            s.total[...] += dot_nt(s.active[:, columns], s.w_fc1[:, :, :, columns].reshape(D, D))
            return 0

        lax.fori_loop(0, 4, body, 0)

        def rows_back(rows, sums):
            upstream = s.total[rows, :]
            found, scale = standardized(s.middle[rows, :])
            middle = s.g_branch2[rows, :].astype(F32) + norm_back(upstream, found, scale, s.par[1:2, :])
            s.g_middle[rows, :] = middle
            branch = middle.astype(BF16)
            s.g_branch[rows, :] = branch
            return (
                sums[0] + column_sum(upstream * found),
                sums[1] + column_sum(upstream),
                sums[2] + column_sum(branch.astype(F32)),
            )

        empty = jnp.zeros((1, D), F32)
        s.sums[1:2, :], s.sums[3:4, :], s.sums[6:7, :] = by_rows(rows_back, (empty, empty, empty))

    def attend_back():
        def body(two, _):
            spots = [lanes(128 * two + part, 128) for part in (0, D, 2 * D)]
            query, key, value = (s.mixed[:, spot] for spot in spots)
            upstream = s.g_attended[:, spots[0]]
            g_query, g_key, g_value = (jnp.zeros((TOKENS, 128), F32) for _ in range(3))
            for mask in head_masks():
                probs = softmax(dot_nt(query * mask, key))
                g_probs = dot_nt(upstream * mask, value)
                g_value = g_value + dot_tn(probs.astype(BF16), upstream * mask)
                inner = jnp.sum(probs * g_probs, axis=-1, keepdims=True)
                g_scores = (probs * (g_probs - inner)).astype(BF16)
                g_query = g_query + dot(g_scores, key * mask)
                g_key = g_key + dot_tn(g_scores, query * mask)
            g_query = 0.125 * g_query.astype(BF16).astype(F32)
            g_value = g_value.astype(BF16)
            s.g_mixed[:, spots[0]] = g_query.astype(BF16)
            s.g_mixed[:, spots[1]] = g_key.astype(BF16)
            s.g_mixed[:, spots[2]] = g_value
            s.sums[4:5, spots[0]] = column_sum(g_query)
            s.sums[5:6, spots[0]] = column_sum(g_value.astype(F32))
            return 0

        lax.fori_loop(0, HEADS // 2, body, 0)

    def first_norm_back():
        s.total[...] = jnp.zeros((TOKENS, D), F32)

        def body(level, _):
            columns = lanes(D * level, D)
            s.total[...] += dot_nt(s.g_mixed[:, columns], s.w_qkv[:, :, :, columns].reshape(D, D))
            return 0

        lax.fori_loop(0, 3, body, 0)

        def rows_back(rows, sums):
            upstream = s.total[rows, :]
            found, scale = standardized(s.rows_in[rows, :].astype(F32))
            result = s.g_middle[rows, :] + norm_back(upstream, found, scale, s.par[0:1, :])
            s.gx_send[rows, :] = result.astype(BF16)
            return (sums[0] + column_sum(upstream * found), sums[1] + column_sum(upstream))

        empty = jnp.zeros((1, D), F32)
        s.sums[0:1, :], s.sums[2:3, :] = by_rows(rows_back, (empty, empty))

    def pack_small():
        chips = lax.shift_right_logical(over((256, D), 0), 4)
        pieces = piece24(over((256, D), 1))
        spread = spread24()
        rows = jnp.broadcast_to(s.sums[...][None], (16, 16, D)).reshape(256, D)
        for side in (0, 1):
            placed = dot_nt(jnp.where(pieces == 2 * chips + side, rows, 0.0).astype(BF16), spread)
            s.g_small[:, :, :, 128 * side : 128 * side + 128] = placed.astype(BF16).reshape(4, 4, 16, 128)
        put = (over((256, 16), 0) == 16 * over((256, 16), 1) + 8).astype(F32).astype(BF16)
        spread = spread96()
        pieces = piece96(over((16, FF), 1))
        row = s.sums_fc1[0:1, :]
        for side in (0, 1):
            mine = pieces == 2 * over((16, FF), 0) + side
            placed = dot_nt(jnp.where(mine, row, 0.0).astype(BF16), spread).astype(BF16)
            here_ = s.g_small.at[:, :, :, pl.ds(128 * side, 128)]
            here_[...] = here_[...] + dot(put, placed).astype(BF16).reshape(4, 4, 16, 128)

    def to_patches(source, target):
        return [
            remote(
                source.at[pl.ds(pl.multiple_of(64 * (2 * py + pc), 64), 64), :],
                target.at[blk],
                (wide, 2 * py + pc),
            )
            for py, pc in blk_peers
        ]

    moved = {}

    def send_rows():
        moved["rows"] = to_frames(patches, s.rows_in)

    def send_cotangent():
        moved["cot"] = to_frames(cotangent, s.cot_in)

    def received(name):
        for copy in moved.pop(name):
            copy.wait_recv()

    def start_norm():
        received("rows")
        first_norm()

    def start_cotangent():
        received("cot")
        mask_cotangent()

    def send_encoded():
        moved["enc"] = to_patches(s.enc_send, encoded)
        encoded[blk] = s.enc_send[mine, :]

    def send_grad_rows():
        moved["grad"] = to_patches(s.gx_send, s.gx_recv)
        s.gx_recv[blk] = s.gx_send[mine, :]

    def free_fc1():
        for name in ("h0", "h1", "h2", "h3"):
            sent(gathers[name].copies())

    def project_attended():
        s.g_attended[...] = dot_nt(s.g_branch[...], s.w_out[...].reshape(D, D)).astype(BF16)

    def project_both(j):
        project_qkv(j)
        project_qkv(j + 3)

    def grad_fc1_weight(j):
        column_grad(s.normed2_t, s.active, 384 * j, s.g_fc1, 0, 1536, 384)

    def grad_out_weight():
        column_grad(s.attended_t, s.g_branch, 0, s.w_fc1, 0, 384, 384)

    def grad_qkv_weight(j):
        column_grad(s.normed_t, s.g_mixed, 384 * j, s.w_fc1, D, 1152, 384)

    g, r = types.SimpleNamespace(**gathers), types.SimpleNamespace(**scatters)
    g.f2.p()
    g.s0.z()
    g.q0.z()
    send_rows()
    g.q1.z()
    g.s0.p()
    g.q2.z()
    g.q0.p()
    g.s0.f()
    g.o0.z()
    g.h2.z()
    g.q1.p()
    g.q2.p()
    g.q1.f()
    g.q0.f()
    g.q1.g()
    g.q0.g()
    g.h0.z()
    g.o0.p()
    g.h2.p()
    g.h3.z()
    g.q1.l()
    g.s0.g()
    g.q0.l()
    g.h1.z()
    g.f0.z()
    g.q0.d()
    g.h0.p()
    g.o0.f()
    g.h2.f()
    g.q2.f()
    g.h1.p()
    g.s0.l()
    g.f1.z()
    g.q2.g()
    send_cotangent()
    g.s0.d()
    unpack_small()
    g.h3.p()
    g.o0.g()
    g.h2.g()
    start_norm()
    g.h0.f()
    project_both(0)
    g.f2.z()
    g.h1.f()
    g.f1.p()
    g.h1.g()
    g.h3.f()
    g.q2.l()
    g.o0.l()
    g.h0.g()
    g.q2.d()
    g.f0.p()
    g.q1.d()
    project_both(1)
    project_both(2)
    g.h2.l()
    g.o0.d()
    attend()
    g.h3.g()
    project_out()
    g.h1.l()
    g.h2.d()
    g.h1.d()
    g.h0.l()
    start_cotangent()
    feed(1)
    g.f1.f()
    g.h0.d()
    feed(2)
    g.f1.g()
    g.f0.f()
    g.f2.l()
    feed(0)
    g.h3.l()
    g.h3.d()
    g.f0.g()
    feed(3)
    g.f1.l()
    weight_grad_fc2(1)
    g.f2.d()
    r.f1.s()
    weight_grad_fc2(2)
    r.f2.s()
    weight_grad_fc2(0)
    g.f0.l()
    r.f1.p()
    r.f0.s()
    r.f2.p()
    g.f1.d()
    g.f0.d()
    feed_back()
    send_encoded()
    r.f1.f()
    r.f1.g()
    grad_fc1_weight(0)
    r.f0.z()
    r.h0.s()
    grad_fc1_weight(2)
    grad_fc1_weight(3)
    r.f2.f()
    r.h0.p()
    r.f2.g()
    r.h3.s()
    r.h2.s()
    second_norm_back()
    project_attended()
    r.h3.p()
    r.h2.p()
    free_fc1()
    r.h0.f()
    attend_back()
    r.f2.z()
    r.h3.f()
    r.h0.g()
    r.h3.g()
    grad_qkv_weight(1)
    grad_out_weight()
    r.h2.f()
    r.q1.s()
    r.f1.z()
    r.h2.g()
    grad_qkv_weight(0)
    r.o0.s()
    r.q1.p()
    r.q0.s()
    grad_fc1_weight(1)
    r.q0.p()
    r.h3.z()
    grad_qkv_weight(2)
    r.q1.f()
    r.q2.s()
    r.h1.s()
    r.q1.g()
    r.o0.p()
    r.h0.z()
    r.h1.p()
    r.h2.z()
    first_norm_back()
    r.q1.z()
    pack_small()
    r.f2.l()
    r.s0.s()
    r.h0.l()
    r.o0.f()
    r.o0.g()
    r.s0.p()
    r.h1.f()
    r.q0.f()
    r.f1.l()
    r.h1.g()
    r.q0.g()
    r.o0.z()
    r.s0.f()
    r.q2.p()
    r.h1.z()
    r.q2.f()
    r.h3.l()
    r.q2.g()
    r.h2.l()
    r.q0.z()
    r.f0.p()
    send_grad_rows()
    r.q1.l()
    r.o0.l()
    r.s0.g()
    r.q2.z()
    r.f0.l()
    r.h1.l()
    r.s0.z()
    r.q0.l()
    r.q2.l()
    r.s0.l()
    for name in list(moved):
        received(name)
    for copy in finals:
        copy.wait_recv()
    grad_patches[...] = s.gx_recv[...].astype(F32)
    sent(started)


def emit_kernel(*refs):
    count = len(refs) // 2
    for i in range(count):
        refs[count + i][...] = refs[i][...].astype(refs[count + i].dtype)


def emit(arrays):
    vmem = pl.BlockSpec(memory_space=pltpu.VMEM)
    return list(
        pl.pallas_call(
            emit_kernel,
            out_shape=[jax.ShapeDtypeStruct(a.shape, a.dtype) for a in arrays],
            in_specs=[vmem] * len(arrays),
            out_specs=[vmem] * len(arrays),
        )(*arrays)
    )


def fast(
    patches,
    norm_gain,
    norm_bias,
    qkv_weight,
    qv_bias,
    out_weight,
    fc1_weight,
    fc1_bias,
    fc2_weight,
    res_bias,
    cotangent,
    frame_valid,
):
    outputs = [
        ((4, 64, D), BF16),
        ((4, 64, D), F32),
        ((2, 24), F32),
        ((2, 24), F32),
        ((24, 3 * D), F32),
        ((2, 24), F32),
        ((24, D), F32),
        ((24, FF), F32),
        ((1, 96), F32),
        ((96, D), F32),
        ((2, 24), F32),
    ]
    vmem = pl.BlockSpec(memory_space=pltpu.VMEM)
    found = list(pl.pallas_call(
        layer_kernel,
        out_shape=[jax.ShapeDtypeStruct(shape, dtype) for shape, dtype in outputs],
        in_specs=[vmem] * 11 + [pl.BlockSpec(memory_space=pltpu.SMEM)],
        out_specs=[vmem] * len(outputs),
        scratch_shapes=list(scratch_shapes().values()),
        compiler_params=pltpu.CompilerParams(
            collective_id=0, has_side_effects=True, vmem_limit_bytes=63 * 2**20
        ),
    )(
        patches,
        norm_gain,
        norm_bias,
        qkv_weight,
        qv_bias,
        out_weight,
        fc1_weight,
        fc1_bias.reshape(1, 96),
        fc2_weight,
        res_bias,
        cotangent,
        frame_valid,
    ))
    found = emit(found)
    found[8] = found[8].reshape(96)
    return tuple(found)


def solution(mesh):
    in_specs = (
        P("wide", "blk", None),
        P(None, ("wide", "blk")),
        P(None, ("wide", "blk")),
        P(("wide", "blk"), None),
        P(None, ("wide", "blk")),
        P(("wide", "blk"), None),
        P(("wide", "blk"), None),
        P(("wide", "blk")),
        P(("wide", "blk"), None),
        P(None, ("wide", "blk")),
        P("wide", "blk", None),
        P("wide"),
    )
    out_specs = (
        P("wide", "blk", None),
        P("wide", "blk", None),
        P(None, ("wide", "blk")),
        P(None, ("wide", "blk")),
        P(("wide", "blk"), None),
        P(None, ("wide", "blk")),
        P(("wide", "blk"), None),
        P(("wide", "blk"), None),
        P(("wide", "blk")),
        P(("wide", "blk"), None),
        P(None, ("wide", "blk")),
    )
    body = fast if dict(mesh.shape) == {"wide": 8, "blk": 4} else local
    return jax.shard_map(body, mesh=mesh, in_specs=in_specs, out_specs=out_specs, check_vma=False)
```

```python
from functools import partial
import math
import types

import jax
import jax.numpy as jnp
from jax import lax
from jax.experimental import pallas as pl
from jax.experimental.pallas import tpu as pltpu
from jax.sharding import PartitionSpec as P

D = 768
HEADS = 12
HEAD = 64


EPSILON = 1e-06


def layer_normalize(token_rows, norm_gain_vector, norm_bias_vector):
    row_average = jnp.mean(token_rows, axis=-1, keepdims=True)
    centered_rows = token_rows - row_average
    inverse_deviation_scale = lax.rsqrt(
        jnp.mean(centered_rows * centered_rows, axis=-1, keepdims=True) + EPSILON
    )
    standardized_rows = centered_rows * inverse_deviation_scale
    return (
        standardized_rows * norm_gain_vector + norm_bias_vector,
        standardized_rows,
        inverse_deviation_scale,
    )


def layer_normalize_backward(
    incoming_gradient, standardized_rows, inverse_deviation_scale, norm_gain_vector
):
    gain_weighted_gradient = incoming_gradient * norm_gain_vector
    inner_product_sum = (
        gain_weighted_gradient
        - jnp.mean(gain_weighted_gradient, axis=-1, keepdims=True)
        - standardized_rows
        * jnp.mean(gain_weighted_gradient * standardized_rows, axis=-1, keepdims=True)
    )
    return (
        inverse_deviation_scale * inner_product_sum,
        jnp.sum(incoming_gradient * standardized_rows, axis=0),
        jnp.sum(incoming_gradient, axis=0),
    )


def frame_groups(array, count):
    return array.reshape((array.shape[0] // count, count) + array.shape[1:])


def attend_forward(query, keys, values):
    scores = jnp.einsum("gqhe,gkhe->ghqk", query, keys, preferred_element_type=jnp.float32)
    top = jnp.max(scores, axis=-1, keepdims=True)
    expo = jnp.exp(scores - top)
    total = jnp.sum(expo, axis=-1, keepdims=True)
    probs = (expo / total).astype(jnp.bfloat16)
    attended = jnp.einsum("ghqk,gkhe->gqhe", probs, values, preferred_element_type=jnp.float32)
    return (attended, top + jnp.log(total))


def attend_back(query, keys, values, logsum, grad_out):
    scores = jnp.einsum("gqhe,gkhe->ghqk", query, keys, preferred_element_type=jnp.float32)
    probs = jnp.exp(scores - logsum)
    grad_probs = jnp.einsum("gqhe,gkhe->ghqk", grad_out, values, preferred_element_type=jnp.float32)
    grad_values = jnp.einsum(
        "ghqk,gqhe->gkhe", probs.astype(jnp.bfloat16), grad_out, preferred_element_type=jnp.float32
    )
    grad_scores = (
        probs * (grad_probs - jnp.sum(probs * grad_probs, axis=-1, keepdims=True))
    ).astype(jnp.bfloat16)
    grad_query = jnp.einsum(
        "ghqk,gkhe->gqhe", grad_scores, keys, preferred_element_type=jnp.float32
    )
    grad_keys = jnp.einsum(
        "ghqk,gqhe->gkhe", grad_scores, query, preferred_element_type=jnp.float32
    )
    return (grad_query, grad_keys, grad_values)


def local(
    patches,
    norm_gain,
    norm_bias,
    qkv_weight,
    qv_bias,
    out_weight,
    fc1_weight,
    fc1_bias,
    fc2_weight,
    res_bias,
    cotangent,
    frame_valid,
):
    frames, frame_rows, width = patches.shape
    count = frames * frame_rows
    group = math.gcd(frames, 8)
    params = (
        lax.all_gather(norm_gain, ("wide", "blk"), axis=1, tiled=True),
        lax.all_gather(norm_bias, ("wide", "blk"), axis=1, tiled=True),
        lax.all_gather(qkv_weight, ("wide", "blk"), axis=0, tiled=True),
        lax.all_gather(qv_bias, ("wide", "blk"), axis=1, tiled=True),
        lax.all_gather(out_weight, ("wide", "blk"), axis=0, tiled=True),
        lax.all_gather(fc1_weight, ("wide", "blk"), axis=0, tiled=True),
        lax.all_gather(fc1_bias, ("wide", "blk"), axis=0, tiled=True),
        lax.all_gather(fc2_weight, ("wide", "blk"), axis=0, tiled=True),
        lax.all_gather(res_bias, ("wide", "blk"), axis=1, tiled=True),
    )
    norm_gain_pair = params[0].astype(jnp.float32)
    norm_bias_pair = params[1].astype(jnp.float32)
    biases_qv = params[3].astype(jnp.float32)
    bias_fc1 = params[6].astype(jnp.float32)
    biases_res = params[8].astype(jnp.float32)
    token_rows = patches.reshape(count, width).astype(jnp.float32)
    valid = jnp.repeat(frame_valid.astype(jnp.float32), frame_rows)[:, None]
    first_branch, first_standardized_rows, first_norm_scale = layer_normalize(
        token_rows, norm_gain_pair[0], norm_bias_pair[0]
    )
    normed = first_branch.astype(jnp.bfloat16)
    mixed = jnp.dot(normed, params[2], preferred_element_type=jnp.float32)
    query = ((mixed[:, :D] + biases_qv[0]) * 0.125).astype(jnp.bfloat16)
    keys = mixed[:, D : 2 * D].astype(jnp.bfloat16).reshape(frames, frame_rows, width)
    values = (
        (mixed[:, 2 * D :] + biases_qv[1]).astype(jnp.bfloat16).reshape(frames, frame_rows, width)
    )
    keys_all, values_all = (
        lax.all_gather(keys, "blk", axis=1, tiled=True),
        lax.all_gather(values, "blk", axis=1, tiled=True),
    )
    query_heads = frame_groups(query.reshape(frames, frame_rows, HEADS, HEAD), group)
    keys_heads = frame_groups(keys_all.reshape(frames, -1, HEADS, HEAD), group)
    values_heads = frame_groups(values_all.reshape(frames, -1, HEADS, HEAD), group)
    attended, logsum = lax.map(
        lambda item: attend_forward(item[0], item[1], item[2]),
        (query_heads, keys_heads, values_heads),
    )
    attended = attended.reshape(count, width).astype(jnp.bfloat16)
    middle_activation = (
        token_rows
        + jnp.dot(attended, params[4], preferred_element_type=jnp.float32)
        + biases_res[0]
    )
    second_branch, second_standardized_rows, second_norm_scale = layer_normalize(
        middle_activation, norm_gain_pair[1], norm_bias_pair[1]
    )
    normed2 = second_branch.astype(jnp.bfloat16)
    hidden = jnp.dot(normed2, params[5], preferred_element_type=jnp.float32) + bias_fc1
    active = jax.nn.gelu(hidden, approximate=False).astype(jnp.bfloat16)
    branch2 = jnp.dot(active, params[7], preferred_element_type=jnp.float32) + biases_res[1]
    encoded = (
        ((middle_activation + branch2) * valid)
        .astype(jnp.bfloat16)
        .reshape(frames, frame_rows, width)
    )
    params = (
        lax.all_gather(norm_gain, ("wide", "blk"), axis=1, tiled=True),
        lax.all_gather(norm_bias, ("wide", "blk"), axis=1, tiled=True),
        lax.all_gather(qkv_weight, ("wide", "blk"), axis=0, tiled=True),
        lax.all_gather(qv_bias, ("wide", "blk"), axis=1, tiled=True),
        lax.all_gather(out_weight, ("wide", "blk"), axis=0, tiled=True),
        lax.all_gather(fc1_weight, ("wide", "blk"), axis=0, tiled=True),
        lax.all_gather(fc1_bias, ("wide", "blk"), axis=0, tiled=True),
        lax.all_gather(fc2_weight, ("wide", "blk"), axis=0, tiled=True),
        lax.all_gather(res_bias, ("wide", "blk"), axis=1, tiled=True),
    )
    grad_out = cotangent.reshape(count, width).astype(jnp.float32) * valid
    grad_branch2 = grad_out.astype(jnp.bfloat16)
    grad_fc2 = jnp.dot(active.T, grad_branch2, preferred_element_type=jnp.float32)
    grad_res_two = jnp.sum(grad_branch2.astype(jnp.float32), axis=0)
    grad_active = jnp.dot(grad_branch2, params[7].T, preferred_element_type=jnp.float32)
    gelu_back = jax.vjp(partial(jax.nn.gelu, approximate=False), hidden)[1]
    grad_hidden = gelu_back(grad_active)[0].astype(jnp.bfloat16)
    grad_fc1 = jnp.dot(normed2.T, grad_hidden, preferred_element_type=jnp.float32)
    grad_bias_fc1 = jnp.sum(grad_hidden.astype(jnp.float32), axis=0)
    normed_input_gradient2 = jnp.dot(grad_hidden, params[5].T, preferred_element_type=jnp.float32)
    second_norm_gradient, second_norm_gain, second_norm_bias = layer_normalize_backward(
        normed_input_gradient2, second_standardized_rows, second_norm_scale, norm_gain_pair[1]
    )
    grad_middle = grad_out + second_norm_gradient
    grad_branch = grad_middle.astype(jnp.bfloat16)
    grad_out_proj = jnp.dot(attended.T, grad_branch, preferred_element_type=jnp.float32)
    grad_res_one = jnp.sum(grad_branch.astype(jnp.float32), axis=0)
    grad_attended = jnp.dot(grad_branch, params[4].T, preferred_element_type=jnp.float32).astype(
        jnp.bfloat16
    )
    grad_heads = frame_groups(grad_attended.reshape(frames, frame_rows, HEADS, HEAD), group)
    grad_query, grad_keys, grad_values = lax.map(
        lambda item: attend_back(item[0], item[1], item[2], item[3], item[4]),
        (query_heads, keys_heads, values_heads, logsum, grad_heads),
    )
    grad_keys, grad_values = (
        lax.psum_scatter(
            grad_keys.reshape(frames, -1, width).astype(jnp.bfloat16),
            "blk",
            scatter_dimension=1,
            tiled=True,
        ).astype(jnp.float32),
        lax.psum_scatter(
            grad_values.reshape(frames, -1, width).astype(jnp.bfloat16),
            "blk",
            scatter_dimension=1,
            tiled=True,
        ).astype(jnp.float32),
    )
    grad_query = grad_query.reshape(count, width).astype(jnp.bfloat16) * 0.125
    grad_keys = grad_keys.reshape(count, width).astype(jnp.bfloat16)
    grad_values = grad_values.reshape(count, width).astype(jnp.bfloat16)
    grad_mixed = jnp.concatenate([grad_query, grad_keys, grad_values], axis=1)
    grad_qkv = jnp.dot(normed.T, grad_mixed, preferred_element_type=jnp.float32)
    grad_qv = jnp.stack(
        [
            jnp.sum(grad_query.astype(jnp.float32), axis=0),
            jnp.sum(grad_values.astype(jnp.float32), axis=0),
        ]
    )
    normed_input_gradient = jnp.dot(grad_mixed, params[2].T, preferred_element_type=jnp.float32)
    first_norm_gradient, first_norm_gain, first_norm_bias = layer_normalize_backward(
        normed_input_gradient, first_standardized_rows, first_norm_scale, norm_gain_pair[0]
    )
    grad_rows = (grad_middle + first_norm_gradient).reshape(frames, frame_rows, width)
    grad_gain = jnp.stack([first_norm_gain, second_norm_gain])
    grad_shift = jnp.stack([first_norm_bias, second_norm_bias])
    grad_res = jnp.stack([grad_res_one, grad_res_two])
    summed = (
        lax.psum_scatter(grad_gain, ("wide", "blk"), scatter_dimension=1, tiled=True),
        lax.psum_scatter(grad_shift, ("wide", "blk"), scatter_dimension=1, tiled=True),
        lax.psum_scatter(grad_qkv, ("wide", "blk"), scatter_dimension=0, tiled=True),
        lax.psum_scatter(grad_qv, ("wide", "blk"), scatter_dimension=1, tiled=True),
        lax.psum_scatter(grad_out_proj, ("wide", "blk"), scatter_dimension=0, tiled=True),
        lax.psum_scatter(grad_fc1, ("wide", "blk"), scatter_dimension=0, tiled=True),
        lax.psum_scatter(grad_bias_fc1, ("wide", "blk"), scatter_dimension=0, tiled=True),
        lax.psum_scatter(grad_fc2, ("wide", "blk"), scatter_dimension=0, tiled=True),
        lax.psum_scatter(grad_res, ("wide", "blk"), scatter_dimension=1, tiled=True),
    )
    return (
        encoded,
        grad_rows,
        summed[0],
        summed[1],
        summed[2],
        summed[3],
        summed[4],
        summed[5],
        summed[6],
        summed[7],
        summed[8],
    )


MESH_ID = pl.DeviceIdType.MESH
BF16 = jnp.bfloat16
F32 = jnp.float32
FF = 3072
TOKENS = 256
ROWS = 64
ALL, BOTH = pl.ds(0, 4), pl.ds(0, 2)
GATHER_WAYS = dict(q=(1, 2, 2), o=(2,))
SCATTER_WAYS = dict(o=(2,), q=(2, 2, 3))
FC2_GATHERS, FC2_SCATTERS = 3, 3


def dot(left, right):
    return lax.dot_general(left, right, (((1,), (0,)), ((), ())), preferred_element_type=F32)


def dot_nt(left, right):
    return lax.dot_general(left, right, (((1,), (1,)), ((), ())), preferred_element_type=F32)


def dot_tn(left, right):
    return lax.dot_general(left, right, (((0,), (0,)), ((), ())), preferred_element_type=F32)


COPIES = 360
FC1_OUTPUT = 7


def scratch_shapes():
    def vm(*shape, dtype=BF16):
        return pltpu.VMEM(shape, dtype)

    return dict(
        w_small=vm(4, 4, 16, 256),
        w_qkv=vm(4, 4, 48, 2304),
        w_out=vm(4, 4, 48, 768),
        w_fc1=vm(4, 4, 48, 1536),
        w_fc2=vm(4, 2, 2, 96, 768),
        fc1_other=vm(48, 768),
        own_small=vm(16, 128, dtype=F32),
        pair_rows=vm(48, 3072, dtype=F32),
        pair_send=vm(24, 3072, dtype=F32),
        par=vm(16, 768, dtype=F32),
        par_fc1=vm(8, 1536, dtype=F32),
        rows_in=vm(256, 768),
        cot_in=vm(256, 768),
        normed=vm(256, 768),
        normed_t=vm(768, 256),
        mixed=vm(256, 2304),
        attended=vm(256, 768),
        attended_t=vm(768, 256),
        middle=vm(256, 768, dtype=F32),
        normed2=vm(512, 768),
        normed2_t=vm(768, 512),
        slope=vm(512, 1536, dtype=F32),
        active=vm(512, 1536),
        active_t=vm(16, 96, 512),
        g_branch2=vm(512, 768),
        part_send=vm(2, 256, 768),
        part_recv=vm(2, 256, 768),
        other=vm(256, 768, dtype=F32),
        total=vm(256, 768, dtype=F32),
        g_middle=vm(256, 768, dtype=F32),
        g_branch=vm(256, 768),
        g_attended=vm(256, 768),
        g_mixed=vm(256, 2304),
        enc_send=vm(256, 768),
        gx_send=vm(256, 768),
        gx_recv=vm(4, 64, 768),
        sums=vm(16, 768, dtype=F32),
        sums_fc1=vm(8, 1536, dtype=F32),
        g_small=vm(4, 4, 16, 256),
        g_fc1=vm(4, 4, 48, 1536),
        g_fc2=vm(4, 2, 2, 96, 768),
        g_out=vm(4, 4, 48, 768),
        g_qkv=vm(4, 4, 48, 2304),
        pr_small=vm(4, 4, 16, 128),
        pr_a=vm(4, 4, 48, 1536),
        pr_fc1=vm(4, 4, 48, 768),
        pr_fc2=vm(4, 2, 2, 96, 384),
        dx_small=vm(4, 16, 128),
        dx_a=vm(4, 48, 1536),
        px_small=vm(4, 16, 128),
        px_a=vm(4, 48, 1536),
        px_fc1=vm(4, 2, 48, 768),
        px_fc2=vm(4, 2, 96, 384),
        py_small=vm(4, 16, 128),
        py_a=vm(4, 48, 1536),
        py_fc1=vm(48, 768),
        pz_small=vm(3, 16, 128),
        pz_a=vm(3, 48, 1536),
        pz_fc1=vm(3, 2, 48, 768),
        pz_fc2=vm(3, 2, 96, 384),
        bz_a=vm(3, 4, 48, 1536),
        last_a=vm(48, 1536, dtype=F32),
        last_fc1=vm(2, 48, 768, dtype=F32),
        send_fc1=vm(48, 768),
        last_fc2=vm(96, 384, dtype=F32),
        send_sem=pltpu.SemaphoreType.DMA((COPIES,)),
        recv_sem=pltpu.SemaphoreType.DMA((COPIES,)),
    )


def layer_kernel(
    patches,
    norm_gain,
    norm_bias,
    qkv_weight,
    qv_bias,
    out_weight,
    fc1_weight,
    fc1_bias,
    fc2_weight,
    res_bias,
    cotangent,
    frame_valid,
    encoded,
    grad_patches,
    grad_gain,
    grad_shift,
    grad_qkv,
    grad_qv,
    grad_out,
    grad_fc1,
    grad_fc1_bias,
    grad_fc2,
    grad_res,
    *scratch,
):
    s = types.SimpleNamespace(**dict(zip(scratch_shapes(), scratch)))
    wide, blk = lax.axis_index("wide"), lax.axis_index("blk")
    z, x = lax.div(wide, 2), lax.rem(wide, 2)
    y, core = lax.div(blk, 2), lax.rem(blk, 2)
    here, at_x, at_y, at_d = 2 * x + y, 2 * (1 - x) + y, 2 * x + 1 - y, 2 * (1 - x) + 1 - y
    sibling = (wide, 2 * y + 1 - core)
    x_peer = (2 * z + 1 - x, blk)
    y_peer = (wide, 2 * (1 - y) + core)
    d_peer = (2 * z + 1 - x, 2 * (1 - y) + core)
    y_cross = (wide, 2 * (1 - y) + 1 - core)
    z_of = [lax.rem(z + step, 4) for step in range(4)]
    z_peers = [(2 * z_of[step] + x, blk) for step in range(4)]
    blk_peers = [(y, 1 - core), (1 - y, core), (1 - y, 1 - core)]

    barrier = pltpu.get_barrier_semaphore()
    peers = [sibling, x_peer, y_peer, d_peer, y_cross] + z_peers[1:]
    for peer in peers:
        pl.semaphore_signal(barrier, inc=1, device_id=peer, device_id_type=MESH_ID)

    started, waited = [], set()

    def sent(copies):
        for copy in copies:
            if id(copy) not in waited:
                waited.add(id(copy))
                copy.wait_send()

    def remote(source, target, peer):
        spot = len(started)
        copy = pltpu.make_async_remote_copy(
            src_ref=source,
            dst_ref=target,
            send_sem=s.send_sem.at[spot],
            recv_sem=s.recv_sem.at[spot],
            device_id=peer,
            device_id_type=MESH_ID,
        )
        copy.start()
        started.append(copy)
        return copy

    def lanes(start, size):
        return pl.ds(pl.multiple_of(start, 128), size)

    s.own_small[...] = jnp.zeros((16, 128), F32)
    s.sums[...] = jnp.zeros((16, D), F32)
    s.own_small[0:2, 0:24] = norm_gain[...].astype(F32)
    s.own_small[2:4, 0:24] = norm_bias[...].astype(F32)
    s.own_small[4:6, 0:24] = qv_bias[...].astype(F32)
    s.own_small[6:8, 0:24] = res_bias[...].astype(F32)
    s.own_small[8:9, 0:96] = fc1_bias[...].astype(F32)
    s.w_small[z, here, :, lanes(128 * core, 128)] = s.own_small[...].astype(BF16)
    own_rows = pl.ds(pl.multiple_of(24 * core, 8), 24)
    for ref, half, start in ((qkv_weight, 1152, 0), (out_weight, 384, 1152)):
        s.pair_send[:, start : start + half] = ref[:, lanes((1 - core) * half, half)].astype(F32)
        s.pair_rows[own_rows, start : start + half] = ref[:, lanes(core * half, half)].astype(F32)
    theirs = fc1_weight[:, lanes((1 - core) * 1536, 1536)].astype(F32)
    ours = fc1_weight[:, lanes(core * 1536, 1536)].astype(F32)
    for side in (0, 1):
        for k in range(4):
            at, found = 1536 + 768 * side + 192 * k, 384 * k + 192 * side
            s.pair_send[:, at : at + 192] = theirs[:, found : found + 192]
            s.pair_rows[own_rows, at : at + 192] = ours[:, found : found + 192]
    s.w_fc2[z, x, core] = fc2_weight[...]

    pl.semaphore_wait(barrier, len(peers))

    pair = remote(s.pair_send, s.pair_rows.at[own_rows, :], sibling)

    mine = pl.ds(pl.multiple_of(64 * blk, 64), 64)

    def to_frames(source, target):
        return [remote(source.at[2 * py + pc], target.at[mine, :], (wide, 2 * py + pc)) for py, pc in blk_peers]

    s.rows_in[mine, :] = patches[blk]
    s.cot_in[mine, :] = cotangent[blk]

    class Gather:
        def __init__(self, part, low):
            self.part, self.low, self.high = part, pl.ds(0, low), pl.ds(low, 4 - low)

        def z(self):
            own = self.part(z, here)
            self.z_copies = [remote(own, own, z_peers[step]) for step in (1, 2, 3)]

        def p(self):
            for copy in self.z_copies:
                copy.wait_recv()
            column = self.part(ALL, here)
            self.x, self.y = remote(column, column, x_peer), remote(column, column, y_peer)
            self.pair = [remote(column, column, sibling)]

        def f(self):
            self.x.wait_recv()
            some = self.part(self.low, at_x)
            self.dy = remote(some, some, y_peer)
            column = self.part(ALL, at_x)
            self.pair.append(remote(column, column, sibling))

        def g(self):
            self.y.wait_recv()
            some = self.part(self.high, at_y)
            self.dx = remote(some, some, x_peer)
            column = self.part(ALL, at_y)
            self.pair.append(remote(column, column, sibling))

        def l(self):
            self.dy.wait_recv()
            self.dx.wait_recv()
            column = self.part(ALL, at_d)
            self.pair.append(remote(column, column, sibling))

        def d(self):
            for copy in self.pair:
                copy.wait_recv()

        def copies(self):
            return self.z_copies + self.pair + [self.x, self.y, self.dx, self.dy]

    class SquareGather:
        def __init__(self, part):
            self.part = part

        def p(self):
            own = self.part(z, here)
            self.square = [remote(own, own, peer) for peer in (x_peer, y_peer, d_peer)]

        def z(self):
            for copy in self.square:
                copy.wait_recv()
            level = self.part(z, ALL)
            self.z_copies = [remote(level, level, z_peers[step]) for step in (1, 2, 3)]
            self.pair = [remote(level, level, sibling)]

        def l(self):
            for step, copy in zip((1, 2, 3), self.z_copies):
                copy.wait_recv()
                level = self.part(z_of[4 - step], ALL)
                self.pair.append(remote(level, level, sibling))

        def d(self):
            for copy in self.pair:
                copy.wait_recv()

        def copies(self):
            return self.square + self.z_copies + self.pair

    class PlaneGather:
        def __init__(self, part, across=None):
            self.part, self.across = part, across

        def y(self):
            source, target = self.across
            self.y_copy = remote(source, target, y_peer)

        def z(self):
            if self.across:
                self.y_copy.wait_recv()
            own = self.part(z, x)
            self.z_copies = [remote(own, own, z_peers[step]) for step in (1, 2, 3)]

        def x(self):
            for copy in self.z_copies:
                copy.wait_recv()
            column = self.part(ALL, x)
            self.x_copy = remote(column, column, x_peer)
            self.pair = [remote(column, column, sibling)]

        def l(self):
            self.x_copy.wait_recv()
            column = self.part(ALL, 1 - x)
            self.pair.append(remote(column, column, sibling))

        def d(self):
            for copy in self.pair:
                copy.wait_recv()

    def column_part(ref, half, start, size):
        return lambda levels, place: ref.at[levels, place, :, lanes(half * core + start, size)]

    def gather(part, way):
        return Gather(part, way) if way else SquareGather(part)

    gathers = {"s0": gather(column_part(s.w_small, 128, 0, 128), 2)}
    for name, ref, half in (("q", s.w_qkv, 1152), ("o", s.w_out, 384)):
        for j in range(half // 384):
            gathers[name + str(j)] = gather(column_part(ref, half, 384 * j, 384), GATHER_WAYS[name][j])
    def fc1_gather(j):
        columns = lanes(768 * core + 384 * j, 384)
        return PlaneGather(
            lambda levels, side: s.w_fc1.at[levels, pl.ds(2 * side, 2), :, columns],
            (s.fc1_other.at[:, 384 * j : 384 * j + 384], s.w_fc1.at[z, here, :, columns]),
        )

    def fc2_gather(j, size):
        rows = pl.ds(size * j, size)
        return PlaneGather(lambda levels, side: s.w_fc2.at[levels, side, core, rows, :])

    for j in range(2):
        gathers["h" + str(j)] = fc1_gather(j)
    for j in range(FC2_GATHERS):
        gathers["f" + str(j)] = fc2_gather(j, 96 // FC2_GATHERS)

    pair.wait_recv()
    for ref, half, start in ((s.w_qkv, 1152, 0), (s.w_out, 384, 1152)):
        ref[z, here, :, lanes(core * half, half)] = s.pair_rows[:, start : start + half].astype(BF16)
    halves = lanes(1536 + 768 * y, 768), lanes(1536 + 768 * (1 - y), 768)
    s.w_fc1[z, here, :, lanes(768 * core, 768)] = s.pair_rows[:, halves[0]].astype(BF16)
    s.fc1_other[...] = s.pair_rows[:, halves[1]].astype(BF16)


    def by_rows(body, carry=None):
        def step(i, held):
            return body(pl.ds(pl.multiple_of(ROWS * i, ROWS), ROWS), held)

        return lax.fori_loop(0, TOKENS // ROWS, step, carry)

    def over(shape, axis):
        return lax.broadcasted_iota(jnp.int32, shape, axis)

    def piece24(columns):
        return lax.shift_right_logical(columns * 43691, 20)

    def piece96(columns):
        return lax.shift_right_logical(columns * 10923, 20)

    def spread24():
        columns = over((128, D), 1)
        return (columns - 24 * piece24(columns) == over((128, D), 0)).astype(F32).astype(BF16)

    def hidden_unit(columns):
        return columns + 192 * lax.shift_right_logical(columns * 21846, 22) + 192 * y

    def spread96():
        columns = hidden_unit(over((128, FF // 2), 1))
        return (columns - 96 * piece96(columns) == over((128, FF // 2), 0)).astype(F32).astype(BF16)

    def unpack_small():
        flat = s.w_small[...].reshape(256, 256)
        chips = lax.shift_right_logical(over((256, D), 0), 4)
        pieces = piece24(over((256, D), 1))
        spread = spread24()
        found = jnp.zeros((16, D), F32)
        for side in (0, 1):
            wide_rows = dot(flat[:, 128 * side : 128 * side + 128], spread)
            wide_rows = jnp.where(pieces == 2 * chips + side, wide_rows, 0.0)
            found = found + jnp.sum(wide_rows.reshape(16, 16, D), axis=0)
        s.par[...] = found
        pick = (over((16, 256), 1) == 16 * over((16, 256), 0) + 8).astype(F32).astype(BF16)
        spread = spread96()
        shape = (16, FF // 2)
        pieces = piece96(hidden_unit(over(shape, 1)))
        found = jnp.zeros(shape, F32)
        for side in (0, 1):
            rows = dot(pick, flat[:, 128 * side : 128 * side + 128]).astype(BF16)
            found = found + jnp.where(pieces == 2 * over(shape, 0) + side, dot(rows, spread), 0.0)
        s.par_fc1[0:1, :] = jnp.sum(found, axis=0, keepdims=True)

    def standardized(rows):
        centered = rows - jnp.mean(rows, axis=-1, keepdims=True)
        scale = lax.rsqrt(jnp.mean(centered * centered, axis=-1, keepdims=True) + EPSILON)
        return centered * scale, scale

    def first_norm():
        def body(rows, _):
            found, _ = standardized(s.rows_in[rows, :].astype(F32))
            s.normed[rows, :] = (found * s.par[0:1, :] + s.par[2:3, :]).astype(BF16)
            return 0

        by_rows(body, 0)
        s.normed_t[...] = s.normed[...].T

    def project_qkv(tile):
        start = 384 * tile
        found = dot(s.normed[...], s.w_qkv[:, :, :, start : start + 384].reshape(D, 384))
        if tile < 2:
            found = (found + s.par[4:5, start : start + 384]) * 0.125
        if tile >= 4:
            found = found + s.par[5:6, start - 1536 : start - 1152]
        s.mixed[:, start : start + 384] = found.astype(BF16)

    def head_masks():
        first = (over((TOKENS, 128), 1) < 64).astype(F32)
        return first.astype(BF16), (1.0 - first).astype(BF16)

    def softmax(scores):
        expo = jnp.exp(scores - jnp.max(scores, axis=-1, keepdims=True))
        return expo * (1.0 / jnp.sum(expo, axis=-1, keepdims=True))

    def attend():
        def body(two, _):
            query, key, value = (s.mixed[:, lanes(128 * two + part, 128)] for part in (0, D, 2 * D))
            found = jnp.zeros((TOKENS, 128), F32)
            for mask in head_masks():
                probs = softmax(dot_nt(query * mask, key)).astype(BF16)
                found = found + dot(probs, value * mask)
            s.attended[:, lanes(128 * two, 128)] = found.astype(BF16)
            return 0

        lax.fori_loop(0, HEADS // 2, body, 0)

    def project_out():
        s.middle[...] = dot(s.attended[...], s.w_out[...].reshape(D, D))

        def body(rows, _):
            middle = s.rows_in[rows, :].astype(F32) + (s.middle[rows, :] + s.par[6:7, :])
            s.middle[rows, :] = middle
            found, _ = standardized(middle)
            s.normed2[rows, :] = (found * s.par[1:2, :] + s.par[3:4, :]).astype(BF16)
            return 0

        by_rows(body, 0)

    def transpose_out():
        s.attended_t[...] = s.attended[...].T
        s.normed2_t[:, 0:256] = s.normed2[0:256, :].T

    def feed(j, frame):
        def body(side, _):
            columns = lanes(768 * side + 384 * j, 384)
            tokens = pl.ds(256 * frame, 256)
            s.other[:, 0:384] = dot(s.normed2[tokens, :], s.w_fc1[:, :, :, columns].reshape(D, 384))

            def gelu(rows, _):
                there = pl.ds(pl.multiple_of(rows.start + 256 * frame, ROWS), ROWS)
                hidden = s.other[rows, 0:384] + s.par_fc1[0:1, columns]
                normal = 0.5 + 0.5 * lax.erf(hidden * (1.0 / math.sqrt(2.0)))
                bell = jnp.exp(-0.5 * hidden * hidden) * (1.0 / math.sqrt(2.0 * math.pi))
                s.slope[there, columns] = normal + hidden * bell
                s.active[there, columns] = (hidden * normal).astype(BF16)
                return 0

            by_rows(gelu, 0)
            found = s.active[tokens, columns].T.reshape(4, 96, 256)
            s.active_t[pl.ds(8 * side + 4 * j, 4), :, 256 * frame : 256 * frame + 256] = found
            return 0

        lax.fori_loop(0, 2, body, 0)

    valid = frame_valid[blk].astype(F32)

    def mask_cotangent():
        def body(rows, _):
            s.g_branch2[rows, :] = (s.cot_in[rows, :].astype(F32) * valid).astype(BF16)
            return 0

        by_rows(body, 0)


    class Scatter:
        every = ALL

        def __init__(self, own, other, pr, dx, dy, px, py, pz, finish, low=2):
            self.own, self.other, self.finish = own, other, finish
            self.pr, self.dx, self.dy, self.px, self.py, self.pz = pr, dx, dy, px, py, pz
            self.low, self.high = pl.ds(0, low), pl.ds(low, 4 - low)

        def s(self):
            self.pair = remote(self.other(), self.pr(ALL, self.every), sibling)

        def add_pair(self):
            self.pair.wait_recv()

            def add(level, _):
                ref = self.own(level, self.every)
                ref[...] = ref[...] + self.pr(level, self.every)[...]
                return 0

            lax.fori_loop(0, 4, add, 0)

        def p(self):
            self.add_pair()
            low, high = self.low, self.high
            self.a = remote(self.own(low, at_d), self.dx(low), x_peer)
            self.b = remote(self.own(high, at_d), self.dy(high), y_peer)
            self.c = remote(self.own(low, at_x), self.px(low), x_peer)
            self.d = remote(self.own(high, at_y), self.py(high), y_peer)

        def f(self):
            self.a.wait_recv()
            ref = self.own(self.low, at_y)
            ref[...] = ref[...] + self.dx(self.low)[...]
            self.e = remote(ref, self.py(self.low), y_peer)

        def g(self):
            self.b.wait_recv()
            ref = self.own(self.high, at_x)
            ref[...] = ref[...] + self.dy(self.high)[...]
            self.f_copy = remote(ref, self.px(self.high), x_peer)

        def z(self):
            for copy in (self.c, self.d, self.e, self.f_copy):
                copy.wait_recv()

            def add(level, _):
                ref = self.own(level, here)
                ref[...] = (
                    ref[...].astype(F32)
                    + self.px(level)[...].astype(F32)
                    + self.py(level)[...].astype(F32)
                ).astype(BF16)
                return 0

            lax.fori_loop(0, 4, add, 0)
            self.z_copies = [
                remote(self.own(z_of[step], here), self.pz(step - 1), z_peers[step]) for step in (1, 2, 3)
            ]

        def l(self):
            for copy in self.z_copies:
                copy.wait_recv()
            self.finish(self)

        def summed(self, view):
            found = view(self.own(z, here))[...].astype(F32)
            for i in range(3):
                found = found + view(self.pz(i))[...].astype(F32)
            return found

    class SquareScatter(Scatter):
        def __init__(self, own, other, pr, bz, pz, finish):
            self.own, self.other, self.finish = own, other, finish
            self.pr, self.bz, self.pz = pr, bz, pz

        def z(self):
            self.add_pair()
            self.z_copies = [
                remote(self.own(z_of[step], ALL), self.bz(step - 1, ALL), z_peers[step]) for step in (1, 2, 3)
            ]

        def p(self):
            for copy in self.z_copies:
                copy.wait_recv()

            def add(place, _):
                ref = self.own(z, place)
                found = ref[...].astype(F32)
                for i in range(3):
                    found = found + self.bz(i, place)[...].astype(F32)
                ref[...] = found.astype(BF16)
                return 0

            lax.fori_loop(0, 4, add, 0)
            targets = ((at_x, x_peer), (at_y, y_peer), (at_d, d_peer))
            self.square = [
                remote(self.own(z, place), self.pz(i), peer) for i, (place, peer) in enumerate(targets)
            ]

        def l(self):
            for copy in self.square:
                copy.wait_recv()
            self.finish(self)

    class PlaneScatter(Scatter):
        def __init__(self, own, other, pr, px, pz, finish, across=None):
            self.own, self.other, self.finish, self.across = own, other, finish, across
            self.pr, self.px, self.pz = pr, px, pz

        def x(self):
            self.add_pair()
            self.x_copy = remote(self.own(ALL, 1 - x), self.px(ALL), x_peer)

        def z(self):
            self.x_copy.wait_recv()

            def add(level, _):
                ref = self.own(level, x)
                ref[...] = ref[...] + self.px(level)[...]
                return 0

            lax.fori_loop(0, 4, add, 0)
            self.z_copies = [
                remote(self.own(z_of[step], x), self.pz(step - 1), z_peers[step]) for step in (1, 2, 3)
            ]

        def y(self):
            for copy in self.z_copies:
                copy.wait_recv()
            source, target = self.across(self)
            self.y_copy = remote(source, target, y_peer)

        def l(self):
            for copy in [self.y_copy] if self.across else self.z_copies:
                copy.wait_recv()
            self.finish(self)

        def summed(self, view):
            found = view(self.own(z, x))[...].astype(F32)
            for i in range(3):
                found = found + view(self.pz(i))[...].astype(F32)
            return found

    def columns_of(ref, base, half, start, size):
        def own(levels, places):
            return ref.at[levels, places, :, lanes(base + half * core + start, size)]

        def other():
            return ref.at[:, :, :, lanes(base + half * (1 - core) + start, size)]

        return own, other

    def column_scatter(ref, base, half, start, size, spot, output, way):
        at = pl.ds(spot, size)

        def finish(scatter):
            s.last_a[:, at] = scatter.summed(lambda ref: ref)
            target = lanes(half * core + start, size)
            other_rows = pl.ds(pl.multiple_of(24 * (1 - core), 8), 24)
            finals.append(remote(s.last_a.at[other_rows, at], output.at[:, target], sibling))
            output[:, target] = s.last_a[own_rows, at]

        if not way:
            extra = pl.ds(spot, size)
            return SquareScatter(
                *columns_of(ref, base, half, start, size),
                lambda levels, places: s.pr_a.at[levels, places, :, at],
                lambda i, places: s.bz_a.at[i, places, :, extra],
                lambda i: s.pz_a.at[i, :, at],
                finish,
            )
        return Scatter(
            *columns_of(ref, base, half, start, size),
            lambda levels, places: s.pr_a.at[levels, places, :, at],
            lambda levels: s.dx_a.at[levels, :, at],
            lambda levels: s.dx_a.at[levels, :, at],
            lambda levels: s.px_a.at[levels, :, at],
            lambda levels: s.py_a.at[levels, :, at],
            lambda i: s.pz_a.at[i, :, at],
            finish,
            way,
        )

    def fc1_scatter(j):
        at = slice(384 * j, 384 * j + 384)

        def own_columns(side):
            return lanes(768 * side + 384 * j, 384)

        def own(levels, side):
            places = ALL if side is ALL else pl.ds(2 * side, 2)
            return s.g_fc1.at[levels, places, :, own_columns(core)]

        def across(scatter):
            s.last_fc1[0, :, at] = scatter.summed(lambda ref: ref.at[y])
            s.send_fc1[:, at] = scatter.summed(lambda ref: ref.at[1 - y]).astype(BF16)
            return s.send_fc1.at[:, at], s.py_fc1.at[:, at]

        def finish(scatter):
            s.last_fc1[1, :, at] = s.py_fc1[:, at].astype(F32)
            other_rows = pl.ds(pl.multiple_of(24 * (1 - core), 8), 24)
            for i, half in enumerate((y, 1 - y)):
                target = lanes(1536 * half + 768 * core + 384 * j, 384)
                finals.append(remote(s.last_fc1.at[i, other_rows, at], grad_fc1.at[:, target], sibling))
                grad_fc1[:, target] = s.last_fc1[i, own_rows, at]

        return PlaneScatter(
            own,
            lambda: s.g_fc1.at[:, :, :, own_columns(1 - core)],
            lambda levels, places: s.pr_fc1.at[levels, places, :, at],
            lambda levels: s.px_fc1.at[levels, :, :, at],
            lambda i: s.pz_fc1.at[i, :, :, at],
            finish,
            across,
        )

    def fc2_scatter(j, size):
        rows = pl.ds(size * j, size)
        half = lanes(384 * core, 384)

        def finish(scatter):
            s.last_fc2[rows, :] = scatter.summed(lambda ref: ref.at[1 - core])
            finals.append(remote(s.last_fc2.at[rows, :], grad_fc2.at[rows, half], sibling))
            grad_fc2[rows, half] = scatter.summed(lambda ref: ref.at[core])

        return PlaneScatter(
            lambda levels, side: s.g_fc2.at[levels, side if side is not ALL else BOTH, :, rows, half],
            lambda: s.g_fc2.at[:, :, :, rows, lanes(384 * (1 - core), 384)],
            lambda levels, side: s.pr_fc2.at[levels, side if side is not ALL else BOTH, :, rows, :],
            lambda levels: s.px_fc2.at[levels, :, rows, :],
            lambda i: s.pz_fc2.at[i, :, rows, :],
            finish,
        )

    def small_finish(scatter):
        found = scatter.summed(lambda ref: ref)
        grad_gain[...] = found[0:2, 0:24]
        grad_shift[...] = found[2:4, 0:24]
        grad_qv[...] = found[4:6, 0:24]
        grad_res[...] = found[6:8, 0:24]
        grad_fc1_bias[...] = found[8:9, 0:96]

    finals = []
    scatters = {}
    for j in range(FC2_SCATTERS):
        scatters["f" + str(j)] = fc2_scatter(j, 96 // FC2_SCATTERS)
    for j in range(2):
        scatters["h" + str(j)] = fc1_scatter(j)
    for name, ref, half, spot, output in (
        ("o", s.g_out, 384, 0, grad_out),
        ("q", s.g_qkv, 1152, 384, grad_qkv),
    ):
        for j in range(half // 384):
            way = SCATTER_WAYS[name][j]
            scatters[name + str(j)] = column_scatter(
                ref, 0, half, 384 * j, 384, spot + 384 * j, output, way
            )
    scatters["s0"] = Scatter(
        *columns_of(s.g_small, 0, 128, 0, 128),
        lambda levels, places: s.pr_small.at[levels, places],
        lambda levels: s.dx_small.at[levels],
        lambda levels: s.dx_small.at[levels],
        lambda levels: s.px_small.at[levels],
        lambda levels: s.py_small.at[levels],
        lambda i: s.pz_small.at[i],
        small_finish,
    )

    def weight_grad_fc2(j):
        size = 96 // FC2_SCATTERS
        rows = pl.ds(size * j, size)

        def body(turn, _):
            columns = lanes(384 * (turn * core + (1 - turn) * (1 - core)), 384)
            found = dot(s.active_t[:, rows, :].reshape(16 * size, 512), s.g_branch2[:, columns])
            s.g_fc2[:, :, :, rows, columns] = found.astype(BF16).reshape(4, 2, 2, size, 384)
            return 0

        lax.fori_loop(0, 2, body, 0)

    def column_grad(left, right, start, ref, base, half, size):
        def body(turn, _):
            side = turn * core + (1 - turn) * (1 - core)
            found = dot(left[...], right[:, lanes(half * side + start, size)])
            ref[:, :, :, lanes(base + half * side + start, size)] = found.astype(BF16).reshape(4, 4, 48, size)
            return 0

        lax.fori_loop(0, 2, body, 0)

    def column_sums(ref, width):
        return jnp.sum(ref[...].astype(F32), axis=0, keepdims=True)

    def feed_back(frame):
        tokens = pl.ds(256 * frame, 256)
        s.total[...] = jnp.zeros((TOKENS, D), F32)

        def body(part, _):
            columns = lanes(D * part, D)
            weight = s.w_fc2[pl.ds(2 * part, 2)].reshape(D, D)
            s.total[...] += dot(s.active[tokens, columns], weight)
            s.other[...] = dot_nt(s.g_branch2[tokens, :], weight)

            def slope(rows, sums):
                there = pl.ds(pl.multiple_of(rows.start + 256 * frame, ROWS), ROWS)
                found = (s.other[rows, :] * s.slope[there, columns]).astype(BF16)
                s.active[there, columns] = found
                return sums + jnp.sum(found.astype(F32), axis=0, keepdims=True)

            s.sums_fc1[frame : frame + 1, columns] = by_rows(slope, jnp.zeros((1, D), F32))
            return 0

        lax.fori_loop(0, 2, body, 0)
        if frame:
            s.part_send[0] = s.total[...].astype(BF16)

    def output():
        def finish(rows, sums):
            branch = s.total[rows, :] + s.part_recv[0, rows, :].astype(F32)
            found = valid * (s.middle[rows, :] + (branch + s.par[7:8, :]))
            s.enc_send[rows, :] = found.astype(BF16)
            return sums + jnp.sum(s.g_branch2[rows, :].astype(F32), axis=0, keepdims=True)

        s.sums[7:8, :] = by_rows(finish, jnp.zeros((1, D), F32))

    def feed_back_rows(frame):
        tokens = pl.ds(256 * frame, 256)
        s.other[...] = jnp.zeros((TOKENS, D), F32)

        def body(part, _):
            columns = lanes(D * part, D)
            s.other[...] += dot_nt(s.active[tokens, columns], s.w_fc1[:, :, :, columns].reshape(D, D))
            return 0

        lax.fori_loop(0, 2, body, 0)
        if frame:
            s.part_send[1] = s.other[...].astype(BF16)

    def norm_back(upstream, found, scale, gain):
        weighted = upstream * gain
        return scale * (
            weighted
            - jnp.mean(weighted, axis=-1, keepdims=True)
            - found * jnp.mean(weighted * found, axis=-1, keepdims=True)
        )

    def column_sum(values):
        return jnp.sum(values, axis=0, keepdims=True)

    def second_norm_back():
        def rows_back(rows, sums):
            upstream = s.other[rows, :] + s.part_recv[1, rows, :].astype(F32)
            found, scale = standardized(s.middle[rows, :])
            middle = s.g_branch2[rows, :].astype(F32) + norm_back(upstream, found, scale, s.par[1:2, :])
            s.g_middle[rows, :] = middle
            branch = middle.astype(BF16)
            s.g_branch[rows, :] = branch
            return (
                sums[0] + column_sum(upstream * found),
                sums[1] + column_sum(upstream),
                sums[2] + column_sum(branch.astype(F32)),
            )

        empty = jnp.zeros((1, D), F32)
        s.sums[1:2, :], s.sums[3:4, :], s.sums[6:7, :] = by_rows(rows_back, (empty, empty, empty))

    def attend_back():
        def body(two, _):
            spots = [lanes(128 * two + part, 128) for part in (0, D, 2 * D)]
            query, key, value = (s.mixed[:, spot] for spot in spots)
            upstream = s.g_attended[:, spots[0]]
            g_query, g_key, g_value = (jnp.zeros((TOKENS, 128), F32) for _ in range(3))
            for mask in head_masks():
                probs = softmax(dot_nt(query * mask, key))
                g_probs = dot_nt(upstream * mask, value)
                g_value = g_value + dot_tn(probs.astype(BF16), upstream * mask)
                inner = jnp.sum(probs * g_probs, axis=-1, keepdims=True)
                g_scores = (probs * (g_probs - inner)).astype(BF16)
                g_query = g_query + dot(g_scores, key * mask)
                g_key = g_key + dot_tn(g_scores, query * mask)
            g_query = 0.125 * g_query.astype(BF16).astype(F32)
            g_value = g_value.astype(BF16)
            s.g_mixed[:, spots[0]] = g_query.astype(BF16)
            s.g_mixed[:, spots[1]] = g_key.astype(BF16)
            s.g_mixed[:, spots[2]] = g_value
            s.sums[4:5, spots[0]] = column_sum(g_query)
            s.sums[5:6, spots[0]] = column_sum(g_value.astype(F32))
            return 0

        lax.fori_loop(0, HEADS // 2, body, 0)

    def first_norm_back():
        s.total[...] = jnp.zeros((TOKENS, D), F32)

        def body(level, _):
            columns = lanes(D * level, D)
            s.total[...] += dot_nt(s.g_mixed[:, columns], s.w_qkv[:, :, :, columns].reshape(D, D))
            return 0

        lax.fori_loop(0, 3, body, 0)

        def rows_back(rows, sums):
            upstream = s.total[rows, :]
            found, scale = standardized(s.rows_in[rows, :].astype(F32))
            result = s.g_middle[rows, :] + norm_back(upstream, found, scale, s.par[0:1, :])
            s.gx_send[rows, :] = result.astype(BF16)
            return (sums[0] + column_sum(upstream * found), sums[1] + column_sum(upstream))

        empty = jnp.zeros((1, D), F32)
        s.sums[0:1, :], s.sums[2:3, :] = by_rows(rows_back, (empty, empty))

    def pack_small():
        chips = lax.shift_right_logical(over((256, D), 0), 4)
        pieces = piece24(over((256, D), 1))
        spread = spread24()
        rows = jnp.broadcast_to(s.sums[...][None], (16, 16, D)).reshape(256, D)
        for side in (0, 1):
            placed = dot_nt(jnp.where(pieces == 2 * chips + side, rows, 0.0).astype(BF16), spread)
            s.g_small[:, :, :, 128 * side : 128 * side + 128] = placed.astype(BF16).reshape(4, 4, 16, 128)
        put = (over((256, 16), 0) == 16 * over((256, 16), 1) + 8).astype(F32).astype(BF16)
        spread = spread96()
        shape = (16, FF // 2)
        pieces = piece96(hidden_unit(over(shape, 1)))
        row = s.sums_fc1[0:1, :] + s.sums_fc1[1:2, :]
        for side in (0, 1):
            mine = pieces == 2 * over(shape, 0) + side
            placed = dot_nt(jnp.where(mine, row, 0.0).astype(BF16), spread).astype(BF16)
            here_ = s.g_small.at[:, :, :, pl.ds(128 * side, 128)]
            here_[...] = here_[...] + dot(put, placed).astype(BF16).reshape(4, 4, 16, 128)

    def to_patches(source, target):
        return [
            remote(
                source.at[pl.ds(pl.multiple_of(64 * (2 * py + pc), 64), 64), :],
                target.at[blk],
                (wide, 2 * py + pc),
            )
            for py, pc in blk_peers
        ]

    moved = {}

    def send_rows():
        moved["rows"] = to_frames(patches, s.rows_in)

    def send_cotangent():
        moved["cot"] = to_frames(cotangent, s.cot_in)

    def received(name):
        for copy in moved.pop(name):
            copy.wait_recv()

    def start_norm():
        received("rows")
        first_norm()

    def start_cotangent():
        received("cot")
        mask_cotangent()

    def send_encoded():
        moved["enc"] = to_patches(s.enc_send, encoded)
        encoded[blk] = s.enc_send[mine, :]

    def send_grad_rows():
        moved["grad"] = to_patches(s.gx_send, s.gx_recv)
        s.gx_recv[blk] = s.gx_send[mine, :]

    def project_attended():
        s.g_attended[...] = dot_nt(s.g_branch[...], s.w_out[...].reshape(D, D)).astype(BF16)

    def project_both(j):
        project_qkv(j)
        project_qkv(j + 3)

    def across(name, source, target):
        moved[name] = [remote(source, target, y_peer)]

    def send_normed():
        across("normed", s.normed2.at[0:256, :], s.normed2.at[256:512, :])

    def take_normed():
        received("normed")

    def transpose_other():
        s.normed2_t[:, 256:512] = s.normed2[256:512, :].T

    def send_masked():
        across("masked", s.g_branch2.at[0:256, :], s.g_branch2.at[256:512, :])

    def take_masked():
        received("masked")

    def send_part():
        across("part", s.part_send.at[0], s.part_recv.at[0])

    def start_output():
        received("part")
        output()

    def send_back():
        across("back", s.part_send.at[1], s.part_recv.at[1])

    def start_second():
        received("back")
        second_norm_back()

    def grad_fc1_weight(j):
        column_grad(s.normed2_t, s.active, 384 * j, s.g_fc1, 0, 768, 384)

    def grad_out_weight():
        column_grad(s.attended_t, s.g_branch, 0, s.g_out, 0, 384, 384)

    def grad_qkv_weight(j):
        column_grad(s.normed_t, s.g_mixed, 384 * j, s.g_qkv, 0, 1152, 384)

    g, r = types.SimpleNamespace(**gathers), types.SimpleNamespace(**scatters)
    g.h1.y()
    g.s0.z()
    g.o0.z()
    send_cotangent()
    g.h0.y()
    g.q0.z()
    g.q1.z()
    g.s0.p()
    g.s0.f()
    g.o0.p()
    g.q0.p()
    g.q2.z()
    g.q1.p()
    g.o0.f()
    g.h0.z()
    g.s0.g()
    g.q0.f()
    start_cotangent()
    g.q2.p()
    g.o0.g()
    g.q1.f()
    g.q1.g()
    g.q0.g()
    g.s0.l()
    g.h1.z()
    g.q2.f()
    g.q2.g()
    g.h0.x()
    send_rows()
    g.q1.l()
    g.q0.l()
    g.o0.l()
    g.s0.d()
    g.f0.z()
    g.f1.z()
    unpack_small()
    g.f2.z()
    g.q0.d()
    g.h1.x()
    send_masked()
    g.q2.l()
    start_norm()
    project_both(0)
    g.q1.d()
    g.q2.d()
    project_both(1)
    project_both(2)
    attend()
    g.o0.d()
    project_out()
    send_normed()
    g.f0.x()
    g.h1.l()
    g.f1.x()
    g.h0.l()
    g.h0.d()
    take_masked()
    g.f2.x()
    g.h1.d()
    g.f0.l()
    feed(1, 0)
    transpose_out()
    feed(0, 0)
    take_normed()
    feed(1, 1)
    feed(0, 1)
    weight_grad_fc2(2)
    r.f2.s()
    g.f1.l()
    weight_grad_fc2(1)
    r.f2.x()
    g.f2.l()
    weight_grad_fc2(0)
    g.f1.d()
    r.f1.s()
    g.f0.d()
    r.f0.s()
    g.f2.d()
    feed_back(1)
    feed_back_rows(1)
    send_back()
    transpose_other()
    r.f1.x()
    r.f0.x()
    feed_back(0)
    grad_fc1_weight(0)
    send_part()
    grad_fc1_weight(1)
    r.h1.s()
    r.h0.s()
    r.f2.z()
    r.f1.z()
    feed_back_rows(0)
    r.h1.x()
    r.h0.x()
    start_second()
    grad_out_weight()
    r.o0.s()
    r.f0.z()
    project_attended()
    r.o0.p()
    attend_back()
    grad_qkv_weight(2)
    r.q2.s()
    r.h1.z()
    start_output()
    send_encoded()
    r.q2.p()
    r.h0.z()
    grad_qkv_weight(1)
    r.q1.s()
    r.f1.l()
    r.o0.f()
    r.o0.g()
    r.q1.p()
    grad_qkv_weight(0)
    r.q2.f()
    r.q2.g()
    first_norm_back()
    r.o0.z()
    r.f2.l()
    r.q1.f()
    r.q0.s()
    r.q1.g()
    pack_small()
    r.s0.s()
    r.f0.l()
    r.q0.p()
    r.q2.z()
    r.s0.p()
    r.q0.f()
    r.q1.z()
    r.q0.g()
    r.h1.y()
    r.s0.f()
    r.h0.y()
    send_grad_rows()
    r.q2.l()
    r.s0.g()
    r.q0.z()
    r.s0.z()
    r.o0.l()
    r.q1.l()
    r.h1.l()
    r.h0.l()
    r.q0.l()
    r.s0.l()
    for name in list(moved):
        received(name)
    for copy in finals:
        copy.wait_recv()
    grad_patches[...] = s.gx_recv[...].astype(F32)
    sent(started)


def emit_kernel(*refs):
    count = len(refs) // 2
    for i in range(count):
        if i == FC1_OUTPUT:
            for side in (0, 1):
                for k in range(8):
                    source = refs[i][:, 1536 * side + 192 * k : 1536 * side + 192 * k + 192]
                    refs[count + i][:, 384 * k + 192 * side : 384 * k + 192 * side + 192] = source
        else:
            refs[count + i][...] = refs[i][...]


def emit(arrays):
    vmem = pl.BlockSpec(memory_space=pltpu.VMEM)
    return list(
        pl.pallas_call(
            emit_kernel,
            out_shape=[jax.ShapeDtypeStruct(a.shape, a.dtype) for a in arrays],
            in_specs=[vmem] * len(arrays),
            out_specs=[vmem] * len(arrays),
        )(*arrays)
    )


def fast(
    patches,
    norm_gain,
    norm_bias,
    qkv_weight,
    qv_bias,
    out_weight,
    fc1_weight,
    fc1_bias,
    fc2_weight,
    res_bias,
    cotangent,
    frame_valid,
):
    outputs = [
        ((4, 64, D), BF16),
        ((4, 64, D), F32),
        ((2, 24), F32),
        ((2, 24), F32),
        ((24, 3 * D), F32),
        ((2, 24), F32),
        ((24, D), F32),
        ((24, FF), F32),
        ((1, 96), F32),
        ((96, D), F32),
        ((2, 24), F32),
    ]
    vmem = pl.BlockSpec(memory_space=pltpu.VMEM)
    found = list(pl.pallas_call(
        layer_kernel,
        out_shape=[jax.ShapeDtypeStruct(shape, dtype) for shape, dtype in outputs],
        in_specs=[vmem] * 11 + [pl.BlockSpec(memory_space=pltpu.SMEM)],
        out_specs=[vmem] * len(outputs),
        scratch_shapes=list(scratch_shapes().values()),
        compiler_params=pltpu.CompilerParams(
            collective_id=0, has_side_effects=True, vmem_limit_bytes=63 * 2**20
        ),
    )(
        patches,
        norm_gain,
        norm_bias,
        qkv_weight,
        qv_bias,
        out_weight,
        fc1_weight,
        fc1_bias.reshape(1, 96),
        fc2_weight,
        res_bias,
        cotangent,
        frame_valid,
    ))
    found = emit(found)
    found[8] = found[8].reshape(96)
    return tuple(found)


def solution(mesh):
    in_specs = (
        P("wide", "blk", None),
        P(None, ("wide", "blk")),
        P(None, ("wide", "blk")),
        P(("wide", "blk"), None),
        P(None, ("wide", "blk")),
        P(("wide", "blk"), None),
        P(("wide", "blk"), None),
        P(("wide", "blk")),
        P(("wide", "blk"), None),
        P(None, ("wide", "blk")),
        P("wide", "blk", None),
        P("wide"),
    )
    out_specs = (
        P("wide", "blk", None),
        P("wide", "blk", None),
        P(None, ("wide", "blk")),
        P(None, ("wide", "blk")),
        P(("wide", "blk"), None),
        P(None, ("wide", "blk")),
        P(("wide", "blk"), None),
        P(("wide", "blk"), None),
        P(("wide", "blk")),
        P(("wide", "blk"), None),
        P(None, ("wide", "blk")),
    )
    body = fast if dict(mesh.shape) == {"wide": 8, "blk": 4} else local
    return jax.shard_map(body, mesh=mesh, in_specs=in_specs, out_specs=out_specs, check_vma=False)
```

```python
from functools import partial
import math
import types

import jax
import jax.numpy as jnp
from jax import lax
from jax.experimental import pallas as pl
from jax.experimental.pallas import tpu as pltpu
from jax.sharding import PartitionSpec as P

D = 768
HEADS = 12
HEAD = 64


EPSILON = 1e-06


def layer_normalize(token_rows, norm_gain_vector, norm_bias_vector):
    row_average = jnp.mean(token_rows, axis=-1, keepdims=True)
    centered_rows = token_rows - row_average
    inverse_deviation_scale = lax.rsqrt(
        jnp.mean(centered_rows * centered_rows, axis=-1, keepdims=True) + EPSILON
    )
    standardized_rows = centered_rows * inverse_deviation_scale
    return (
        standardized_rows * norm_gain_vector + norm_bias_vector,
        standardized_rows,
        inverse_deviation_scale,
    )


def layer_normalize_backward(
    incoming_gradient, standardized_rows, inverse_deviation_scale, norm_gain_vector
):
    gain_weighted_gradient = incoming_gradient * norm_gain_vector
    inner_product_sum = (
        gain_weighted_gradient
        - jnp.mean(gain_weighted_gradient, axis=-1, keepdims=True)
        - standardized_rows
        * jnp.mean(gain_weighted_gradient * standardized_rows, axis=-1, keepdims=True)
    )
    return (
        inverse_deviation_scale * inner_product_sum,
        jnp.sum(incoming_gradient * standardized_rows, axis=0),
        jnp.sum(incoming_gradient, axis=0),
    )


def frame_groups(array, count):
    return array.reshape((array.shape[0] // count, count) + array.shape[1:])


def attend_forward(query, keys, values):
    scores = jnp.einsum("gqhe,gkhe->ghqk", query, keys, preferred_element_type=jnp.float32)
    top = jnp.max(scores, axis=-1, keepdims=True)
    expo = jnp.exp(scores - top)
    total = jnp.sum(expo, axis=-1, keepdims=True)
    probs = (expo / total).astype(jnp.bfloat16)
    attended = jnp.einsum("ghqk,gkhe->gqhe", probs, values, preferred_element_type=jnp.float32)
    return (attended, top + jnp.log(total))


def attend_back(query, keys, values, logsum, grad_out):
    scores = jnp.einsum("gqhe,gkhe->ghqk", query, keys, preferred_element_type=jnp.float32)
    probs = jnp.exp(scores - logsum)
    grad_probs = jnp.einsum("gqhe,gkhe->ghqk", grad_out, values, preferred_element_type=jnp.float32)
    grad_values = jnp.einsum(
        "ghqk,gqhe->gkhe", probs.astype(jnp.bfloat16), grad_out, preferred_element_type=jnp.float32
    )
    grad_scores = (
        probs * (grad_probs - jnp.sum(probs * grad_probs, axis=-1, keepdims=True))
    ).astype(jnp.bfloat16)
    grad_query = jnp.einsum(
        "ghqk,gkhe->gqhe", grad_scores, keys, preferred_element_type=jnp.float32
    )
    grad_keys = jnp.einsum(
        "ghqk,gqhe->gkhe", grad_scores, query, preferred_element_type=jnp.float32
    )
    return (grad_query, grad_keys, grad_values)


def local(
    patches,
    norm_gain,
    norm_bias,
    qkv_weight,
    qv_bias,
    out_weight,
    fc1_weight,
    fc1_bias,
    fc2_weight,
    res_bias,
    cotangent,
    frame_valid,
):
    frames, frame_rows, width = patches.shape
    count = frames * frame_rows
    group = math.gcd(frames, 8)
    params = (
        lax.all_gather(norm_gain, ("wide", "blk"), axis=1, tiled=True),
        lax.all_gather(norm_bias, ("wide", "blk"), axis=1, tiled=True),
        lax.all_gather(qkv_weight, ("wide", "blk"), axis=0, tiled=True),
        lax.all_gather(qv_bias, ("wide", "blk"), axis=1, tiled=True),
        lax.all_gather(out_weight, ("wide", "blk"), axis=0, tiled=True),
        lax.all_gather(fc1_weight, ("wide", "blk"), axis=0, tiled=True),
        lax.all_gather(fc1_bias, ("wide", "blk"), axis=0, tiled=True),
        lax.all_gather(fc2_weight, ("wide", "blk"), axis=0, tiled=True),
        lax.all_gather(res_bias, ("wide", "blk"), axis=1, tiled=True),
    )
    norm_gain_pair = params[0].astype(jnp.float32)
    norm_bias_pair = params[1].astype(jnp.float32)
    biases_qv = params[3].astype(jnp.float32)
    bias_fc1 = params[6].astype(jnp.float32)
    biases_res = params[8].astype(jnp.float32)
    token_rows = patches.reshape(count, width).astype(jnp.float32)
    valid = jnp.repeat(frame_valid.astype(jnp.float32), frame_rows)[:, None]
    first_branch, first_standardized_rows, first_norm_scale = layer_normalize(
        token_rows, norm_gain_pair[0], norm_bias_pair[0]
    )
    normed = first_branch.astype(jnp.bfloat16)
    mixed = jnp.dot(normed, params[2], preferred_element_type=jnp.float32)
    query = ((mixed[:, :D] + biases_qv[0]) * 0.125).astype(jnp.bfloat16)
    keys = mixed[:, D : 2 * D].astype(jnp.bfloat16).reshape(frames, frame_rows, width)
    values = (
        (mixed[:, 2 * D :] + biases_qv[1]).astype(jnp.bfloat16).reshape(frames, frame_rows, width)
    )
    keys_all, values_all = (
        lax.all_gather(keys, "blk", axis=1, tiled=True),
        lax.all_gather(values, "blk", axis=1, tiled=True),
    )
    query_heads = frame_groups(query.reshape(frames, frame_rows, HEADS, HEAD), group)
    keys_heads = frame_groups(keys_all.reshape(frames, -1, HEADS, HEAD), group)
    values_heads = frame_groups(values_all.reshape(frames, -1, HEADS, HEAD), group)
    attended, logsum = lax.map(
        lambda item: attend_forward(item[0], item[1], item[2]),
        (query_heads, keys_heads, values_heads),
    )
    attended = attended.reshape(count, width).astype(jnp.bfloat16)
    middle_activation = (
        token_rows
        + jnp.dot(attended, params[4], preferred_element_type=jnp.float32)
        + biases_res[0]
    )
    second_branch, second_standardized_rows, second_norm_scale = layer_normalize(
        middle_activation, norm_gain_pair[1], norm_bias_pair[1]
    )
    normed2 = second_branch.astype(jnp.bfloat16)
    hidden = jnp.dot(normed2, params[5], preferred_element_type=jnp.float32) + bias_fc1
    active = jax.nn.gelu(hidden, approximate=False).astype(jnp.bfloat16)
    branch2 = jnp.dot(active, params[7], preferred_element_type=jnp.float32) + biases_res[1]
    encoded = (
        ((middle_activation + branch2) * valid)
        .astype(jnp.bfloat16)
        .reshape(frames, frame_rows, width)
    )
    params = (
        lax.all_gather(norm_gain, ("wide", "blk"), axis=1, tiled=True),
        lax.all_gather(norm_bias, ("wide", "blk"), axis=1, tiled=True),
        lax.all_gather(qkv_weight, ("wide", "blk"), axis=0, tiled=True),
        lax.all_gather(qv_bias, ("wide", "blk"), axis=1, tiled=True),
        lax.all_gather(out_weight, ("wide", "blk"), axis=0, tiled=True),
        lax.all_gather(fc1_weight, ("wide", "blk"), axis=0, tiled=True),
        lax.all_gather(fc1_bias, ("wide", "blk"), axis=0, tiled=True),
        lax.all_gather(fc2_weight, ("wide", "blk"), axis=0, tiled=True),
        lax.all_gather(res_bias, ("wide", "blk"), axis=1, tiled=True),
    )
    grad_out = cotangent.reshape(count, width).astype(jnp.float32) * valid
    grad_branch2 = grad_out.astype(jnp.bfloat16)
    grad_fc2 = jnp.dot(active.T, grad_branch2, preferred_element_type=jnp.float32)
    grad_res_two = jnp.sum(grad_branch2.astype(jnp.float32), axis=0)
    grad_active = jnp.dot(grad_branch2, params[7].T, preferred_element_type=jnp.float32)
    gelu_back = jax.vjp(partial(jax.nn.gelu, approximate=False), hidden)[1]
    grad_hidden = gelu_back(grad_active)[0].astype(jnp.bfloat16)
    grad_fc1 = jnp.dot(normed2.T, grad_hidden, preferred_element_type=jnp.float32)
    grad_bias_fc1 = jnp.sum(grad_hidden.astype(jnp.float32), axis=0)
    normed_input_gradient2 = jnp.dot(grad_hidden, params[5].T, preferred_element_type=jnp.float32)
    second_norm_gradient, second_norm_gain, second_norm_bias = layer_normalize_backward(
        normed_input_gradient2, second_standardized_rows, second_norm_scale, norm_gain_pair[1]
    )
    grad_middle = grad_out + second_norm_gradient
    grad_branch = grad_middle.astype(jnp.bfloat16)
    grad_out_proj = jnp.dot(attended.T, grad_branch, preferred_element_type=jnp.float32)
    grad_res_one = jnp.sum(grad_branch.astype(jnp.float32), axis=0)
    grad_attended = jnp.dot(grad_branch, params[4].T, preferred_element_type=jnp.float32).astype(
        jnp.bfloat16
    )
    grad_heads = frame_groups(grad_attended.reshape(frames, frame_rows, HEADS, HEAD), group)
    grad_query, grad_keys, grad_values = lax.map(
        lambda item: attend_back(item[0], item[1], item[2], item[3], item[4]),
        (query_heads, keys_heads, values_heads, logsum, grad_heads),
    )
    grad_keys, grad_values = (
        lax.psum_scatter(
            grad_keys.reshape(frames, -1, width).astype(jnp.bfloat16),
            "blk",
            scatter_dimension=1,
            tiled=True,
        ).astype(jnp.float32),
        lax.psum_scatter(
            grad_values.reshape(frames, -1, width).astype(jnp.bfloat16),
            "blk",
            scatter_dimension=1,
            tiled=True,
        ).astype(jnp.float32),
    )
    grad_query = grad_query.reshape(count, width).astype(jnp.bfloat16) * 0.125
    grad_keys = grad_keys.reshape(count, width).astype(jnp.bfloat16)
    grad_values = grad_values.reshape(count, width).astype(jnp.bfloat16)
    grad_mixed = jnp.concatenate([grad_query, grad_keys, grad_values], axis=1)
    grad_qkv = jnp.dot(normed.T, grad_mixed, preferred_element_type=jnp.float32)
    grad_qv = jnp.stack(
        [
            jnp.sum(grad_query.astype(jnp.float32), axis=0),
            jnp.sum(grad_values.astype(jnp.float32), axis=0),
        ]
    )
    normed_input_gradient = jnp.dot(grad_mixed, params[2].T, preferred_element_type=jnp.float32)
    first_norm_gradient, first_norm_gain, first_norm_bias = layer_normalize_backward(
        normed_input_gradient, first_standardized_rows, first_norm_scale, norm_gain_pair[0]
    )
    grad_rows = (grad_middle + first_norm_gradient).reshape(frames, frame_rows, width)
    grad_gain = jnp.stack([first_norm_gain, second_norm_gain])
    grad_shift = jnp.stack([first_norm_bias, second_norm_bias])
    grad_res = jnp.stack([grad_res_one, grad_res_two])
    summed = (
        lax.psum_scatter(grad_gain, ("wide", "blk"), scatter_dimension=1, tiled=True),
        lax.psum_scatter(grad_shift, ("wide", "blk"), scatter_dimension=1, tiled=True),
        lax.psum_scatter(grad_qkv, ("wide", "blk"), scatter_dimension=0, tiled=True),
        lax.psum_scatter(grad_qv, ("wide", "blk"), scatter_dimension=1, tiled=True),
        lax.psum_scatter(grad_out_proj, ("wide", "blk"), scatter_dimension=0, tiled=True),
        lax.psum_scatter(grad_fc1, ("wide", "blk"), scatter_dimension=0, tiled=True),
        lax.psum_scatter(grad_bias_fc1, ("wide", "blk"), scatter_dimension=0, tiled=True),
        lax.psum_scatter(grad_fc2, ("wide", "blk"), scatter_dimension=0, tiled=True),
        lax.psum_scatter(grad_res, ("wide", "blk"), scatter_dimension=1, tiled=True),
    )
    return (
        encoded,
        grad_rows,
        summed[0],
        summed[1],
        summed[2],
        summed[3],
        summed[4],
        summed[5],
        summed[6],
        summed[7],
        summed[8],
    )


MESH_ID = pl.DeviceIdType.MESH
BF16 = jnp.bfloat16
F32 = jnp.float32
FF = 3072
TOKENS = 256
ROWS = 64
ALL, THREE, BOTH = pl.ds(0, 4), pl.ds(0, 3), pl.ds(0, 2)
GATHER_WAYS = dict(q=(-2, -2, -2), o=(-2,), f=(1, 1, 0))
SCATTER_WAYS = dict(f=(0, 1, 1), o=(2,), q=(2, 2, 2))


TILES = ((0, 1536), (768, 384), (1920, 1152))


def tile(j, side):
    first, second = TILES[j]
    return first + side * (second - first)


def dot(left, right):
    return lax.dot_general(left, right, (((1,), (0,)), ((), ())), preferred_element_type=F32)


def dot_nt(left, right):
    return lax.dot_general(left, right, (((1,), (1,)), ((), ())), preferred_element_type=F32)


def dot_tn(left, right):
    return lax.dot_general(left, right, (((0,), (0,)), ((), ())), preferred_element_type=F32)


SENDS, ARRIVALS = 80, 130
FC1_OUTPUT = 7


def scratch_shapes():
    def vm(*shape, dtype=BF16):
        return pltpu.VMEM(shape, dtype)

    return dict(
        w_small=vm(4, 4, 16, 256),
        w_qkv=vm(4, 4, 48, 2304),
        w_out=vm(4, 4, 48, 768),
        w_fc1=vm(4, 4, 48, 1536),
        w_fc2=vm(4, 2, 2, 96, 768),
        fc1_other=vm(48, 768),
        own_small=vm(16, 128, dtype=F32),
        pair_rows=vm(48, 3072, dtype=F32),
        pair_send=vm(24, 3072, dtype=F32),
        par=vm(16, 768, dtype=F32),
        par_fc1=vm(8, 1536, dtype=F32),
        rows_in=vm(256, 768),
        cot_in=vm(512, 768),
        normed=vm(256, 768),
        normed_t=vm(768, 256),
        mixed=vm(256, 2304),
        attended=vm(256, 768),
        attended_t=vm(768, 256),
        middle=vm(256, 768, dtype=F32),
        normed2=vm(512, 768),
        normed2_t=vm(768, 512),
        slope=vm(512, 1536, dtype=F32),
        active=vm(512, 1536),
        g_hidden=vm(512, 1536),
        active_t=vm(16, 96, 512),
        g_branch2=vm(512, 768),
        part_across=vm(256, 768),
        part_recv=vm(128, 768),
        base_send=vm(128, 768),
        base_recv=vm(128, 768),
        back_send=vm(256, 768),
        back_recv=vm(256, 768),
        other=vm(256, 768, dtype=F32),
        total=vm(256, 768, dtype=F32),
        g_middle=vm(256, 768, dtype=F32),
        g_branch=vm(256, 768),
        g_attended=vm(256, 768),
        g_mixed=vm(256, 2304),
        enc_send=vm(2, 128, 768),
        gx_send=vm(256, 768),
        gx_recv=vm(4, 64, 768),
        sums=vm(16, 768, dtype=F32),
        sums_fc1=vm(8, 1536, dtype=F32),
        g_small=vm(4, 4, 16, 256),
        g_fc1=vm(4, 4, 48, 1536),
        g_fc2=vm(4, 2, 2, 96, 768),
        g_out=vm(4, 4, 48, 768),
        g_qkv=vm(4, 4, 48, 2304),
        pr_small=vm(4, 4, 16, 128),
        pr_a=vm(4, 4, 48, 1536),
        pr_fc1=vm(4, 4, 48, 768),
        pr_fc2=vm(4, 2, 2, 96, 384),
        dx_small=vm(4, 16, 128),
        dx_a=vm(4, 48, 1536),
        px_small=vm(4, 16, 128),
        px_a=vm(4, 48, 1536),
        px_fc1=vm(4, 2, 48, 768),
        px_fc2=vm(4, 2, 96, 384),
        py_small=vm(4, 16, 128),
        py_a=vm(4, 48, 1536),
        py_fc1=vm(48, 768),
        pz_small=vm(3, 16, 128),
        pz_a=vm(3, 48, 1536),
        pz_fc1=vm(3, 2, 48, 768),
        pz_fc2=vm(3, 2, 96, 384),
        bz_a=vm(3, 4, 48, 1536),
        bz_fc2=vm(3, 2, 2, 96, 384),
        last_a=vm(48, 1536, dtype=F32),
        last_fc1=vm(2, 48, 768, dtype=F32),
        send_fc1=vm(48, 768),
        last_fc2=vm(96, 384, dtype=F32),
        send_sem=pltpu.SemaphoreType.DMA((SENDS,)),
        recv_sem=pltpu.SemaphoreType.DMA((ARRIVALS,)),
    )


def layer_kernel(
    patches,
    norm_gain,
    norm_bias,
    qkv_weight,
    qv_bias,
    out_weight,
    fc1_weight,
    fc1_bias,
    fc2_weight,
    res_bias,
    cotangent,
    frame_valid,
    encoded,
    grad_patches,
    grad_gain,
    grad_shift,
    grad_qkv,
    grad_qv,
    grad_out,
    grad_fc1,
    grad_fc1_bias,
    grad_fc2,
    grad_res,
    *scratch,
):
    s = types.SimpleNamespace(**dict(zip(scratch_shapes(), scratch)))
    wide, blk = lax.axis_index("wide"), lax.axis_index("blk")
    z, x = lax.div(wide, 2), lax.rem(wide, 2)
    y, core = lax.div(blk, 2), lax.rem(blk, 2)
    here, at_x, at_y, at_d = 2 * x + y, 2 * (1 - x) + y, 2 * x + 1 - y, 2 * (1 - x) + 1 - y
    sibling = (wide, 2 * y + 1 - core)
    x_peer = (2 * z + 1 - x, blk)
    y_peer = (wide, 2 * (1 - y) + core)
    d_peer = (2 * z + 1 - x, 2 * (1 - y) + core)
    y_cross = (wide, 2 * (1 - y) + 1 - core)
    z_of = [lax.rem(z + step, 4) for step in range(4)]
    z_peers = [(2 * z_of[step] + x, blk) for step in range(4)]
    blk_peers = [(y, 1 - core), (1 - y, core), (1 - y, 1 - core)]

    barrier = pltpu.get_barrier_semaphore()
    peers = [sibling, x_peer, y_peer, d_peer, y_cross] + z_peers[1:]
    for peer in peers:
        pl.semaphore_signal(barrier, inc=1, device_id=peer, device_id_type=MESH_ID)

    started, groups = [], []

    class Group:
        def __init__(self):
            self.sem = s.recv_sem.at[len(groups)]
            groups.append(self)

        def wait(self, ref):
            pltpu.make_async_copy(ref, ref, self.sem).wait()

    def remote(source, target, peer, group=None):
        spot = len(started)
        if spot >= SENDS:
            started[spot - SENDS].wait_send()
        copy = pltpu.make_async_remote_copy(
            src_ref=source,
            dst_ref=target,
            send_sem=s.send_sem.at[spot % SENDS],
            recv_sem=(group or Group()).sem,
            device_id=peer,
            device_id_type=MESH_ID,
        )
        copy.start()
        started.append(copy)
        return copy

    def lanes(start, size):
        return pl.ds(pl.multiple_of(start, 128), size)

    s.own_small[...] = jnp.zeros((16, 128), F32)
    s.sums[...] = jnp.zeros((16, D), F32)
    s.own_small[0:2, 0:24] = norm_gain[...].astype(F32)
    s.own_small[2:4, 0:24] = norm_bias[...].astype(F32)
    s.own_small[4:6, 0:24] = qv_bias[...].astype(F32)
    s.own_small[6:8, 0:24] = res_bias[...].astype(F32)
    s.own_small[8:9, 0:96] = fc1_bias[...].astype(F32)
    s.w_small[z, here, :, lanes(128 * core, 128)] = s.own_small[...].astype(BF16)
    own_rows = pl.ds(pl.multiple_of(24 * core, 8), 24)
    for ref, start, columns in (
        (qkv_weight, 0, partial(tile, 0)),
        (qkv_weight, 384, partial(tile, 1)),
        (qkv_weight, 768, partial(tile, 2)),
        (out_weight, 1152, lambda side: 384 * side),
    ):
        s.pair_send[:, start : start + 384] = ref[:, lanes(columns(1 - core), 384)].astype(F32)
        s.pair_rows[own_rows, start : start + 384] = ref[:, lanes(columns(core), 384)].astype(F32)
    theirs = fc1_weight[:, lanes((1 - core) * 1536, 1536)].astype(F32)
    ours = fc1_weight[:, lanes(core * 1536, 1536)].astype(F32)
    for side in (0, 1):
        for k in range(4):
            at, found = 1536 + 768 * side + 192 * k, 384 * k + 192 * side
            s.pair_send[:, at : at + 192] = theirs[:, found : found + 192]
            s.pair_rows[own_rows, at : at + 192] = ours[:, found : found + 192]
    s.w_fc2[z, x, core] = fc2_weight[...]

    pl.semaphore_wait(barrier, len(peers))

    pair = remote(s.pair_send, s.pair_rows.at[own_rows, :], sibling)

    mine = pl.ds(pl.multiple_of(64 * blk, 64), 64)

    rows_moved = Group()
    for py, pc in blk_peers:
        remote(patches.at[2 * py + pc], s.rows_in.at[mine, :], (wide, 2 * py + pc), rows_moved)
    s.rows_in[mine, :] = patches[blk]

    class Gather:
        def __init__(self, part, low):
            self.part, self.low, self.high = part, pl.ds(0, low), pl.ds(low, 4 - low)
            self.by_z, self.by_x, self.by_y, self.far, self.pair = (Group() for _ in range(5))

        def z(self):
            own = self.part(z, here)
            for peer in z_peers[1:]:
                remote(own, own, peer, self.by_z)

        def p(self):
            self.by_z.wait(self.part(THREE, here))
            self.share(self.part(ALL, here))

        def share(self, block):
            remote(block, block, x_peer, self.by_x)
            remote(block, block, y_peer, self.by_y)
            remote(block, block, sibling, self.pair)

        def f(self):
            column = self.part(ALL, at_x)
            self.by_x.wait(column)
            some = self.part(self.low, at_x)
            remote(some, some, y_peer, self.far)
            remote(column, column, sibling, self.pair)

        def g(self):
            column = self.part(ALL, at_y)
            self.by_y.wait(column)
            some = self.part(self.high, at_y)
            remote(some, some, x_peer, self.far)
            remote(column, column, sibling, self.pair)

        def l(self):
            column = self.part(ALL, at_d)
            self.far.wait(column)
            remote(column, column, sibling, self.pair)

        def d(self):
            self.pair.wait(self.part(ALL, ALL))

    class FineGather(Gather):
        def z(self):
            own = self.part(z, here)
            self.z_copies = [remote(own, own, peer) for peer in z_peers[1:]]

        def o(self):
            self.share(self.part(z, here))

        def p(self):
            for step, copy in zip((1, 2, 3), self.z_copies):
                copy.wait_recv()
                self.share(self.part(z_of[4 - step], here))

    class SquareGather:
        def __init__(self, part):
            self.part, self.square, self.by_z, self.pair = part, Group(), Group(), Group()

        def p(self):
            own = self.part(z, here)
            for peer in (x_peer, y_peer, d_peer):
                remote(own, own, peer, self.square)

        def z(self):
            self.square.wait(self.part(z, THREE))
            level = self.part(z, ALL)
            for peer in z_peers[1:]:
                remote(level, level, peer, self.by_z)
            remote(level, level, sibling, self.pair)

        def l(self):
            self.by_z.wait(self.part(THREE, ALL))
            for step in (1, 2, 3):
                level = self.part(z_of[step], ALL)
                remote(level, level, sibling, self.pair)

        def d(self):
            self.pair.wait(self.part(ALL, ALL))

    class PlaneGather:
        def __init__(self, part, across=None):
            self.part, self.across, self.by_z, self.pair = part, across, Group(), Group()

        def y(self):
            source, target = self.across
            self.y_copy = remote(source, target, y_peer)

        def z(self):
            if self.across:
                self.y_copy.wait_recv()
            own = self.part(z, x)
            for peer in z_peers[1:]:
                remote(own, own, peer, self.by_z)

        def x(self):
            self.by_z.wait(self.part(THREE, x))
            column = self.part(ALL, x)
            self.x_copy = remote(column, column, x_peer)
            remote(column, column, sibling, self.pair)

        def l(self):
            self.x_copy.wait_recv()
            column = self.part(ALL, 1 - x)
            remote(column, column, sibling, self.pair)

        def d(self):
            self.pair.wait(self.part(ALL, BOTH))

    class AcrossGather:
        def __init__(self, part):
            self.part, self.by_z, self.pair = part, Group(), Group()

        def x(self):
            own = self.part(z, x)
            self.x_copy = remote(own, own, x_peer)

        def z(self):
            self.x_copy.wait_recv()
            level = self.part(z, BOTH)
            for peer in z_peers[1:]:
                remote(level, level, peer, self.by_z)
            remote(level, level, sibling, self.pair)

        def l(self):
            self.by_z.wait(self.part(THREE, BOTH))
            for step in (1, 2, 3):
                level = self.part(z_of[step], BOTH)
                remote(level, level, sibling, self.pair)

        def d(self):
            self.pair.wait(self.part(ALL, BOTH))

    def column_part(ref, start, size):
        return lambda levels, place: ref.at[levels, place, :, lanes(start, size)]

    def gather(part, way):
        return Gather(part, way) if way > 0 else FineGather(part, -way) if way else SquareGather(part)

    gathers = {
        "s0": gather(column_part(s.w_small, 128 * core, 128), 2),
        "o0": gather(column_part(s.w_out, 384 * core, 384), GATHER_WAYS["o"][0]),
    }
    for j in range(3):
        gathers["q" + str(j)] = gather(column_part(s.w_qkv, tile(j, core), 384), GATHER_WAYS["q"][j])

    def fc1_gather(j):
        columns = lanes(768 * core + 384 * j, 384)
        return PlaneGather(
            lambda levels, side: s.w_fc1.at[levels, ALL if side is BOTH else pl.ds(2 * side, 2), :, columns],
            (s.fc1_other.at[:, 384 * j : 384 * j + 384], s.w_fc1.at[z, here, :, columns]),
        )

    def fc2_gather(j, size, way):
        rows = pl.ds(size * j, size)
        part = lambda levels, side: s.w_fc2.at[levels, side, core, rows, :]
        return PlaneGather(part) if way else AcrossGather(part)

    for j in range(2):
        gathers["h" + str(j)] = fc1_gather(j)
    for j, way in enumerate(GATHER_WAYS["f"]):
        gathers["f" + str(j)] = fc2_gather(j, 96 // len(GATHER_WAYS["f"]), way)

    pair.wait_recv()
    for j in range(3):
        s.w_qkv[z, here, :, lanes(tile(j, core), 384)] = s.pair_rows[:, 384 * j : 384 * j + 384].astype(BF16)
    s.w_out[z, here, :, lanes(384 * core, 384)] = s.pair_rows[:, 1152:1536].astype(BF16)
    halves = lanes(1536 + 768 * y, 768), lanes(1536 + 768 * (1 - y), 768)
    s.w_fc1[z, here, :, lanes(768 * core, 768)] = s.pair_rows[:, halves[0]].astype(BF16)
    s.fc1_other[...] = s.pair_rows[:, halves[1]].astype(BF16)


    def by_rows(body, carry=None):
        def step(i, held):
            return body(pl.ds(pl.multiple_of(ROWS * i, ROWS), ROWS), held)

        return lax.fori_loop(0, TOKENS // ROWS, step, carry)

    def over(shape, axis):
        return lax.broadcasted_iota(jnp.int32, shape, axis)

    def piece24(columns):
        return lax.shift_right_logical(columns * 43691, 20)

    def piece96(columns):
        return lax.shift_right_logical(columns * 10923, 20)

    def spread24():
        columns = over((128, D), 1)
        return (columns - 24 * piece24(columns) == over((128, D), 0)).astype(F32).astype(BF16)

    def hidden_unit(columns):
        return columns + 192 * lax.shift_right_logical(columns * 21846, 22) + 192 * y

    def spread96():
        columns = hidden_unit(over((128, FF // 2), 1))
        return (columns - 96 * piece96(columns) == over((128, FF // 2), 0)).astype(F32).astype(BF16)

    def unpack_small():
        flat = s.w_small[...].reshape(256, 256)
        chips = lax.shift_right_logical(over((256, D), 0), 4)
        pieces = piece24(over((256, D), 1))
        spread = spread24()
        found = jnp.zeros((16, D), F32)
        for side in (0, 1):
            wide_rows = dot(flat[:, 128 * side : 128 * side + 128], spread)
            wide_rows = jnp.where(pieces == 2 * chips + side, wide_rows, 0.0)
            found = found + jnp.sum(wide_rows.reshape(16, 16, D), axis=0)
        s.par[...] = found
        pick = (over((16, 256), 1) == 16 * over((16, 256), 0) + 8).astype(F32).astype(BF16)
        spread = spread96()
        shape = (16, FF // 2)
        pieces = piece96(hidden_unit(over(shape, 1)))
        found = jnp.zeros(shape, F32)
        for side in (0, 1):
            rows = dot(pick, flat[:, 128 * side : 128 * side + 128]).astype(BF16)
            found = found + jnp.where(pieces == 2 * over(shape, 0) + side, dot(rows, spread), 0.0)
        s.par_fc1[0:1, :] = jnp.sum(found, axis=0, keepdims=True)

    def standardized(rows):
        centered = rows - jnp.mean(rows, axis=-1, keepdims=True)
        scale = lax.rsqrt(jnp.mean(centered * centered, axis=-1, keepdims=True) + EPSILON)
        return centered * scale, scale

    def first_norm():
        def body(rows, _):
            found, _ = standardized(s.rows_in[rows, :].astype(F32))
            s.normed[rows, :] = (found * s.par[0:1, :] + s.par[2:3, :]).astype(BF16)
            return 0

        by_rows(body, 0)
        s.normed_t[...] = s.normed[...].T

    def project_qkv(start):
        found = dot(s.normed[...], s.w_qkv[:, :, :, start : start + 384].reshape(D, 384))
        if start < D:
            found = (found + s.par[4:5, start : start + 384]) * 0.125
        if start >= 2 * D:
            found = found + s.par[5:6, start - 2 * D : start - 2 * D + 384]
        s.mixed[:, start : start + 384] = found.astype(BF16)

    def head_masks():
        first = (over((TOKENS, 128), 1) < 64).astype(F32)
        return first.astype(BF16), (1.0 - first).astype(BF16)

    def softmax(scores):
        expo = jnp.exp(scores - jnp.max(scores, axis=-1, keepdims=True))
        return expo * (1.0 / jnp.sum(expo, axis=-1, keepdims=True))

    def attend(part):
        def body(two, _):
            query, key, value = (s.mixed[:, lanes(128 * two + part, 128)] for part in (0, D, 2 * D))
            found = jnp.zeros((TOKENS, 128), F32)
            for mask in head_masks():
                probs = softmax(dot_nt(query * mask, key)).astype(BF16)
                found = found + dot(probs, value * mask)
            s.attended[:, lanes(128 * two, 128)] = found.astype(BF16)
            return 0

        lax.fori_loop(3 * part, 3 * part + 3, body, 0)

    def project_out():
        s.middle[...] = dot(s.attended[...], s.w_out[...].reshape(D, D))

        def body(rows, _):
            middle = s.rows_in[rows, :].astype(F32) + (s.middle[rows, :] + s.par[6:7, :])
            s.middle[rows, :] = middle
            found, _ = standardized(middle)
            s.normed2[rows, :] = (found * s.par[1:2, :] + s.par[3:4, :]).astype(BF16)
            return 0

        by_rows(body, 0)

    def transpose_out():
        s.attended_t[...] = s.attended[...].T
        s.normed2_t[:, 0:256] = s.normed2[0:256, :].T

    def feed(j, frame):
        def body(side, _):
            columns = lanes(768 * side + 384 * j, 384)
            tokens = pl.ds(256 * frame, 256)
            s.other[:, 0:384] = dot(s.normed2[tokens, :], s.w_fc1[:, :, :, columns].reshape(D, 384))

            def gelu(rows, _):
                there = pl.ds(pl.multiple_of(rows.start + 256 * frame, ROWS), ROWS)
                hidden = s.other[rows, 0:384] + s.par_fc1[0:1, columns]
                normal = 0.5 + 0.5 * lax.erf(hidden * (1.0 / math.sqrt(2.0)))
                bell = jnp.exp(-0.5 * hidden * hidden) * (1.0 / math.sqrt(2.0 * math.pi))
                s.slope[there, columns] = normal + hidden * bell
                s.active[there, columns] = (hidden * normal).astype(BF16)
                return 0

            by_rows(gelu, 0)
            found = s.active[tokens, columns].T.reshape(4, 96, 256)
            s.active_t[pl.ds(8 * side + 4 * j, 4), :, 256 * frame : 256 * frame + 256] = found
            return 0

        lax.fori_loop(0, 2, body, 0)

    ours_rows = pl.ds(pl.multiple_of(128 * y, 128), 128)
    theirs_rows = pl.ds(pl.multiple_of(128 * (1 - y), 128), 128)
    across_y = 2 * (1 - y) + core
    valid, valid_across = frame_valid[blk].astype(F32), frame_valid[across_y].astype(F32)

    def mask_cotangent():
        for frame, factor in enumerate((valid, valid_across)):

            def body(rows, _):
                there = pl.ds(pl.multiple_of(rows.start + 256 * frame, ROWS), ROWS)
                s.g_branch2[there, :] = (s.cot_in[there, :].astype(F32) * factor).astype(BF16)
                return 0

            by_rows(body, 0)


    class Scatter:
        every = ALL

        def __init__(self, own, other, pr, dx, dy, px, py, pz, finish, low=2):
            self.own, self.other, self.finish = own, other, finish
            self.pr, self.dx, self.dy, self.px, self.py, self.pz = pr, dx, dy, px, py, pz
            self.square, self.by_z = Group(), Group()
            self.low, self.high = pl.ds(0, low), pl.ds(low, 4 - low)

        def s(self):
            self.pair = remote(self.other(), self.pr(ALL, self.every), sibling)

        def add_pair(self):
            self.pair.wait_recv()

            def add(level, _):
                ref = self.own(level, self.every)
                ref[...] = ref[...] + self.pr(level, self.every)[...]
                return 0

            lax.fori_loop(0, 4, add, 0)

        def p(self):
            self.add_pair()
            low, high = self.low, self.high
            self.a = remote(self.own(low, at_d), self.dx(low), x_peer)
            self.b = remote(self.own(high, at_d), self.dy(high), y_peer)
            remote(self.own(low, at_x), self.px(low), x_peer, self.square)
            remote(self.own(high, at_y), self.py(high), y_peer, self.square)

        def f(self):
            self.a.wait_recv()
            ref = self.own(self.low, at_y)
            ref[...] = ref[...] + self.dx(self.low)[...]
            remote(ref, self.py(self.low), y_peer, self.square)

        def g(self):
            self.b.wait_recv()
            ref = self.own(self.high, at_x)
            ref[...] = ref[...] + self.dy(self.high)[...]
            remote(ref, self.px(self.high), x_peer, self.square)

        def z(self):
            self.square.wait(self.own(ALL, BOTH))

            def add(level, _):
                ref = self.own(level, here)
                ref[...] = (
                    ref[...].astype(F32)
                    + self.px(level)[...].astype(F32)
                    + self.py(level)[...].astype(F32)
                ).astype(BF16)
                return 0

            lax.fori_loop(0, 4, add, 0)
            for step in (1, 2, 3):
                remote(self.own(z_of[step], here), self.pz(step - 1), z_peers[step], self.by_z)

        def l(self):
            self.by_z.wait(self.pz(THREE))
            self.finish(self)

        def summed(self, view):
            found = view(self.own(z, here))[...].astype(F32)
            for i in range(3):
                found = found + view(self.pz(i))[...].astype(F32)
            return found

    class SquareScatter(Scatter):
        def __init__(self, own, other, pr, bz, pz, finish):
            self.own, self.other, self.finish = own, other, finish
            self.pr, self.bz, self.pz = pr, bz, pz
            self.square, self.by_z = Group(), Group()

        def z(self):
            self.add_pair()
            for step in (1, 2, 3):
                remote(self.own(z_of[step], ALL), self.bz(step - 1, ALL), z_peers[step], self.by_z)

        def p(self):
            self.by_z.wait(self.bz(THREE, ALL))

            def add(place, _):
                ref = self.own(z, place)
                found = ref[...].astype(F32)
                for i in range(3):
                    found = found + self.bz(i, place)[...].astype(F32)
                ref[...] = found.astype(BF16)
                return 0

            lax.fori_loop(0, 4, add, 0)
            targets = ((at_x, x_peer), (at_y, y_peer), (at_d, d_peer))
            for i, (place, peer) in enumerate(targets):
                remote(self.own(z, place), self.pz(i), peer, self.square)

        def l(self):
            self.square.wait(self.pz(THREE))
            self.finish(self)

    class PlaneScatter(Scatter):
        def __init__(self, own, other, pr, px, pz, finish, across=None):
            self.own, self.other, self.finish, self.across = own, other, finish, across
            self.pr, self.px, self.pz = pr, px, pz
            self.by_z = Group()

        def x(self):
            self.add_pair()
            self.x_copy = remote(self.own(ALL, 1 - x), self.px(ALL), x_peer)

        def z(self):
            self.x_copy.wait_recv()

            def add(level, _):
                ref = self.own(level, x)
                ref[...] = ref[...] + self.px(level)[...]
                return 0

            lax.fori_loop(0, 4, add, 0)
            for step in (1, 2, 3):
                remote(self.own(z_of[step], x), self.pz(step - 1), z_peers[step], self.by_z)

        def y(self):
            self.by_z.wait(self.pz(THREE))
            source, target = self.across(self)
            self.y_copy = remote(source, target, y_peer)

        def l(self):
            if self.across:
                self.y_copy.wait_recv()
            else:
                self.by_z.wait(self.pz(THREE))
            self.finish(self)

        def summed(self, view):
            found = view(self.own(z, x))[...].astype(F32)
            for i in range(3):
                found = found + view(self.pz(i))[...].astype(F32)
            return found

    class AcrossScatter(Scatter):
        def __init__(self, own, other, pr, bz, px, finish):
            self.own, self.other, self.finish = own, other, finish
            self.pr, self.bz, self.px = pr, bz, px
            self.by_z = Group()

        def z(self):
            self.add_pair()
            for step in (1, 2, 3):
                remote(self.own(z_of[step], ALL), self.bz(step - 1), z_peers[step], self.by_z)

        def x(self):
            self.by_z.wait(self.bz(THREE))
            ref = self.own(z, ALL)
            found = ref[...].astype(F32)
            for i in range(3):
                found = found + self.bz(i)[...].astype(F32)
            ref[...] = found.astype(BF16)
            self.x_copy = remote(self.own(z, 1 - x), self.px(), x_peer)

        def l(self):
            self.x_copy.wait_recv()
            self.finish(self)

        def summed(self, view):
            return view(self.own(z, x))[...].astype(F32) + view(self.px())[...].astype(F32)

    def columns_of(ref, columns, size):
        def own(levels, places):
            return ref.at[levels, places, :, lanes(columns(core), size)]

        def other():
            return ref.at[:, :, :, lanes(columns(1 - core), size)]

        return own, other

    def column_scatter(ref, columns, size, spot, output, way):
        at = pl.ds(spot, size)

        def finish(scatter):
            s.last_a[:, at] = scatter.summed(lambda ref: ref)
            target = lanes(columns(core), size)
            other_rows = pl.ds(pl.multiple_of(24 * (1 - core), 8), 24)
            finals.append(remote(s.last_a.at[other_rows, at], output.at[:, target], sibling))
            output[:, target] = s.last_a[own_rows, at]

        if not way:
            extra = pl.ds(spot, size)
            return SquareScatter(
                *columns_of(ref, columns, size),
                lambda levels, places: s.pr_a.at[levels, places, :, at],
                lambda i, places: s.bz_a.at[i, places, :, extra],
                lambda i: s.pz_a.at[i, :, at],
                finish,
            )
        return Scatter(
            *columns_of(ref, columns, size),
            lambda levels, places: s.pr_a.at[levels, places, :, at],
            lambda levels: s.dx_a.at[levels, :, at],
            lambda levels: s.dx_a.at[levels, :, at],
            lambda levels: s.px_a.at[levels, :, at],
            lambda levels: s.py_a.at[levels, :, at],
            lambda i: s.pz_a.at[i, :, at],
            finish,
            way,
        )

    def fc1_scatter(j):
        at = slice(384 * j, 384 * j + 384)

        def own_columns(side):
            return lanes(768 * side + 384 * j, 384)

        def own(levels, side):
            places = ALL if side is ALL else pl.ds(2 * side, 2)
            return s.g_fc1.at[levels, places, :, own_columns(core)]

        def across(scatter):
            s.last_fc1[0, :, at] = scatter.summed(lambda ref: ref.at[y])
            s.send_fc1[:, at] = scatter.summed(lambda ref: ref.at[1 - y]).astype(BF16)
            return s.send_fc1.at[:, at], s.py_fc1.at[:, at]

        def finish(scatter):
            s.last_fc1[1, :, at] = s.py_fc1[:, at].astype(F32)
            other_rows = pl.ds(pl.multiple_of(24 * (1 - core), 8), 24)
            for i, half in enumerate((y, 1 - y)):
                target = lanes(1536 * half + 768 * core + 384 * j, 384)
                finals.append(remote(s.last_fc1.at[i, other_rows, at], grad_fc1.at[:, target], sibling))
                grad_fc1[:, target] = s.last_fc1[i, own_rows, at]

        return PlaneScatter(
            own,
            lambda: s.g_fc1.at[:, :, :, own_columns(1 - core)],
            lambda levels, places: s.pr_fc1.at[levels, places, :, at],
            lambda levels: s.px_fc1.at[levels, :, :, at],
            lambda i: s.pz_fc1.at[i, :, :, at],
            finish,
            across,
        )

    def fc2_scatter(j, size, way):
        rows = pl.ds(size * j, size)
        half = lanes(384 * core, 384)

        def finish(scatter):
            s.last_fc2[rows, :] = scatter.summed(lambda ref: ref.at[1 - core])
            finals.append(remote(s.last_fc2.at[rows, :], grad_fc2.at[rows, half], sibling))
            grad_fc2[rows, half] = scatter.summed(lambda ref: ref.at[core])

        def sides(side):
            return BOTH if side is ALL else side

        own = lambda levels, side: s.g_fc2.at[levels, sides(side), :, rows, half]
        other = lambda: s.g_fc2.at[:, :, :, rows, lanes(384 * (1 - core), 384)]
        pr = lambda levels, side: s.pr_fc2.at[levels, sides(side), :, rows, :]
        if not way:
            bz = lambda i: s.bz_fc2.at[i, :, :, rows, :]
            return AcrossScatter(own, other, pr, bz, lambda: s.pz_fc2.at[0, :, rows, :], finish)
        return PlaneScatter(
            own,
            other,
            pr,
            lambda levels: s.px_fc2.at[levels, :, rows, :],
            lambda i: s.pz_fc2.at[i, :, rows, :],
            finish,
        )

    def small_finish(scatter):
        found = scatter.summed(lambda ref: ref)
        grad_gain[...] = found[0:2, 0:24]
        grad_shift[...] = found[2:4, 0:24]
        grad_qv[...] = found[4:6, 0:24]
        grad_res[...] = found[6:8, 0:24]
        grad_fc1_bias[...] = found[8:9, 0:96]

    finals = []
    scatters = {}
    for j, way in enumerate(SCATTER_WAYS["f"]):
        scatters["f" + str(j)] = fc2_scatter(j, 96 // len(SCATTER_WAYS["f"]), way)
    for j in range(2):
        scatters["h" + str(j)] = fc1_scatter(j)
    scatters["o0"] = column_scatter(s.g_out, lambda side: 384 * side, 384, 0, grad_out, SCATTER_WAYS["o"][0])
    for j in range(3):
        scatters["q" + str(j)] = column_scatter(
            s.g_qkv, partial(tile, j), 384, 384 + 384 * j, grad_qkv, SCATTER_WAYS["q"][j]
        )
    scatters["s0"] = Scatter(
        *columns_of(s.g_small, lambda side: 128 * side, 128),
        lambda levels, places: s.pr_small.at[levels, places],
        lambda levels: s.dx_small.at[levels],
        lambda levels: s.dx_small.at[levels],
        lambda levels: s.px_small.at[levels],
        lambda levels: s.py_small.at[levels],
        lambda i: s.pz_small.at[i],
        small_finish,
    )

    def weight_grad_fc2(j):
        size = 96 // len(SCATTER_WAYS["f"])
        rows = pl.ds(size * j, size)

        def body(turn, _):
            columns = lanes(384 * (turn * core + (1 - turn) * (1 - core)), 384)
            found = dot(s.active_t[:, rows, :].reshape(16 * size, 512), s.g_branch2[:, columns])
            s.g_fc2[:, :, :, rows, columns] = found.astype(BF16).reshape(4, 2, 2, size, 384)
            return 0

        lax.fori_loop(0, 2, body, 0)

    def column_grad(left, right, ref, columns):
        def body(turn, _):
            at = lanes(columns(turn * core + (1 - turn) * (1 - core)), 384)
            ref[:, :, :, at] = dot(left[...], right[:, at]).astype(BF16).reshape(4, 4, 48, 384)
            return 0

        lax.fori_loop(0, 2, body, 0)

    def feed_back(frame):
        tokens = pl.ds(256 * frame, 256)

        def body(part, _):
            columns = lanes(D * part, D)
            s.other[...] = dot_nt(s.g_branch2[tokens, :], s.w_fc2[pl.ds(2 * part, 2)].reshape(D, D))

            def slope(rows, sums):
                there = pl.ds(pl.multiple_of(rows.start + 256 * frame, ROWS), ROWS)
                found = (s.other[rows, :] * s.slope[there, columns]).astype(BF16)
                s.g_hidden[there, columns] = found
                return sums + jnp.sum(found.astype(F32), axis=0, keepdims=True)

            s.sums_fc1[frame : frame + 1, columns] = by_rows(slope, jnp.zeros((1, D), F32))
            return 0

        lax.fori_loop(0, 2, body, 0)

    def feed_out(frame):
        tokens = pl.ds(256 * frame, 256)
        s.total[...] = jnp.zeros((TOKENS, D), F32)

        def body(part, _):
            weight = s.w_fc2[pl.ds(2 * part, 2)].reshape(D, D)
            s.total[...] += dot(s.active[tokens, lanes(D * part, D)], weight)
            return 0

        lax.fori_loop(0, 2, body, 0)
        if frame:
            s.part_across[...] = s.total[...].astype(BF16)
        else:

            def add(rows, _):
                s.total[rows, :] = s.middle[rows, :] + (s.total[rows, :] + s.par[7:8, :])
                return 0

            by_rows(add, 0)
            s.base_send[...] = (valid * s.total[theirs_rows, :]).astype(BF16)

    def output():
        s.enc_send[0] = (valid * (s.total[ours_rows, :] + s.part_recv[...].astype(F32))).astype(BF16)
        part = valid_across * s.part_across[ours_rows, :].astype(F32)
        s.enc_send[1] = (s.base_recv[...].astype(F32) + part).astype(BF16)

        def body(rows, sums):
            return sums + jnp.sum(s.g_branch2[rows, :].astype(F32), axis=0, keepdims=True)

        s.sums[7:8, :] = by_rows(body, jnp.zeros((1, D), F32))

    def feed_back_rows(frame):
        tokens = pl.ds(256 * frame, 256)
        s.other[...] = jnp.zeros((TOKENS, D), F32)

        def body(part, _):
            columns = lanes(D * part, D)
            s.other[...] += dot_nt(s.g_hidden[tokens, columns], s.w_fc1[:, :, :, columns].reshape(D, D))
            return 0

        lax.fori_loop(0, 2, body, 0)
        if frame:
            s.back_send[...] = s.other[...].astype(BF16)

    def norm_back(upstream, found, scale, gain):
        weighted = upstream * gain
        return scale * (
            weighted
            - jnp.mean(weighted, axis=-1, keepdims=True)
            - found * jnp.mean(weighted * found, axis=-1, keepdims=True)
        )

    def column_sum(values):
        return jnp.sum(values, axis=0, keepdims=True)

    def second_norm_back():
        def rows_back(rows, sums):
            upstream = s.other[rows, :] + s.back_recv[rows, :].astype(F32)
            found, scale = standardized(s.middle[rows, :])
            middle = s.g_branch2[rows, :].astype(F32) + norm_back(upstream, found, scale, s.par[1:2, :])
            s.g_middle[rows, :] = middle
            branch = middle.astype(BF16)
            s.g_branch[rows, :] = branch
            return (
                sums[0] + column_sum(upstream * found),
                sums[1] + column_sum(upstream),
                sums[2] + column_sum(branch.astype(F32)),
            )

        empty = jnp.zeros((1, D), F32)
        s.sums[1:2, :], s.sums[3:4, :], s.sums[6:7, :] = by_rows(rows_back, (empty, empty, empty))

    def attend_back(part):
        def body(two, _):
            spots = [lanes(128 * two + part, 128) for part in (0, D, 2 * D)]
            query, key, value = (s.mixed[:, spot] for spot in spots)
            upstream = s.g_attended[:, spots[0]]
            g_query, g_key, g_value = (jnp.zeros((TOKENS, 128), F32) for _ in range(3))
            for mask in head_masks():
                probs = softmax(dot_nt(query * mask, key))
                g_probs = dot_nt(upstream * mask, value)
                g_value = g_value + dot_tn(probs.astype(BF16), upstream * mask)
                inner = jnp.sum(probs * g_probs, axis=-1, keepdims=True)
                g_scores = (probs * (g_probs - inner)).astype(BF16)
                g_query = g_query + dot(g_scores, key * mask)
                g_key = g_key + dot_tn(g_scores, query * mask)
            g_query = 0.125 * g_query.astype(BF16).astype(F32)
            g_value = g_value.astype(BF16)
            s.g_mixed[:, spots[0]] = g_query.astype(BF16)
            s.g_mixed[:, spots[1]] = g_key.astype(BF16)
            s.g_mixed[:, spots[2]] = g_value
            s.sums[4:5, spots[0]] = column_sum(g_query)
            s.sums[5:6, spots[0]] = column_sum(g_value.astype(F32))
            return 0

        lax.fori_loop(3 * part, 3 * part + 3, body, 0)

    def first_norm_back():
        s.total[...] = jnp.zeros((TOKENS, D), F32)

        def body(level, _):
            columns = lanes(D * level, D)
            s.total[...] += dot_nt(s.g_mixed[:, columns], s.w_qkv[:, :, :, columns].reshape(D, D))
            return 0

        lax.fori_loop(0, 3, body, 0)

        def rows_back(rows, sums):
            upstream = s.total[rows, :]
            found, scale = standardized(s.rows_in[rows, :].astype(F32))
            result = s.g_middle[rows, :] + norm_back(upstream, found, scale, s.par[0:1, :])
            s.gx_send[rows, :] = result.astype(BF16)
            return (sums[0] + column_sum(upstream * found), sums[1] + column_sum(upstream))

        empty = jnp.zeros((1, D), F32)
        s.sums[0:1, :], s.sums[2:3, :] = by_rows(rows_back, (empty, empty))

    def pack_small():
        chips = lax.shift_right_logical(over((256, D), 0), 4)
        pieces = piece24(over((256, D), 1))
        spread = spread24()
        rows = jnp.broadcast_to(s.sums[...][None], (16, 16, D)).reshape(256, D)
        for side in (0, 1):
            placed = dot_nt(jnp.where(pieces == 2 * chips + side, rows, 0.0).astype(BF16), spread)
            s.g_small[:, :, :, 128 * side : 128 * side + 128] = placed.astype(BF16).reshape(4, 4, 16, 128)
        put = (over((256, 16), 0) == 16 * over((256, 16), 1) + 8).astype(F32).astype(BF16)
        spread = spread96()
        shape = (16, FF // 2)
        pieces = piece96(hidden_unit(over(shape, 1)))
        row = s.sums_fc1[0:1, :] + s.sums_fc1[1:2, :]
        for side in (0, 1):
            mine = pieces == 2 * over(shape, 0) + side
            placed = dot_nt(jnp.where(mine, row, 0.0).astype(BF16), spread).astype(BF16)
            here_ = s.g_small.at[:, :, :, pl.ds(128 * side, 128)]
            here_[...] = here_[...] + dot(put, placed).astype(BF16).reshape(4, 4, 16, 128)

    moved = {"rows": (rows_moved, s.rows_in.at[0:192, :])}

    def send_cotangent():
        group = Group()
        after = pl.ds(pl.multiple_of(64 * blk + 256, 64), 64)
        for py, pc in blk_peers:
            for there, frame in ((mine, 2 * py + pc), (after, 2 * (1 - py) + pc)):
                remote(cotangent.at[frame], s.cot_in.at[there, :], (wide, 2 * py + pc), group)
        moved["cot"] = group, s.cot_in.at[0:384, :]
        s.cot_in[mine, :] = cotangent[blk]
        s.cot_in[after, :] = cotangent[across_y]

    def received(name):
        group, ref = moved.pop(name)
        group.wait(ref)

    def start_norm():
        received("rows")
        first_norm()

    def start_cotangent():
        received("cot")
        mask_cotangent()

    def send_encoded():
        ours = pl.ds(pl.multiple_of(64 * core, 64), 64)
        theirs = pl.ds(pl.multiple_of(64 * (1 - core), 64), 64)
        group = Group()
        for i, frame in enumerate((blk, across_y)):
            remote(s.enc_send.at[i, theirs, :], encoded.at[frame], sibling, group)
        moved["enc"] = group, encoded.at[BOTH]
        encoded[blk] = s.enc_send[0, ours, :]
        encoded[across_y] = s.enc_send[1, ours, :]

    def send_grad_rows():
        group = Group()
        for py, pc in blk_peers:
            rows = pl.ds(pl.multiple_of(64 * (2 * py + pc), 64), 64)
            remote(s.gx_send.at[rows, :], s.gx_recv.at[blk], (wide, 2 * py + pc), group)
        moved["grad"] = group, s.gx_recv.at[THREE]
        s.gx_recv[blk] = s.gx_send[mine, :]

    def project_attended():
        s.g_attended[...] = dot_nt(s.g_branch[...], s.w_out[...].reshape(D, D)).astype(BF16)

    def project_both(j):
        project_qkv(tile(j, 0))
        project_qkv(tile(j, 1))

    def across(name, source, target):
        moved[name] = Group(), target
        remote(source, target, y_peer, moved[name][0])

    def send_normed():
        across("normed", s.normed2.at[0:256, :], s.normed2.at[256:512, :])

    def take_normed():
        received("normed")

    def transpose_other():
        s.normed2_t[:, 256:512] = s.normed2[256:512, :].T

    def send_part():
        across("part", s.part_across.at[theirs_rows, :], s.part_recv)

    def send_base():
        across("base", s.base_send, s.base_recv)

    def start_output():
        received("part")
        received("base")
        output()

    def send_back():
        across("back", s.back_send, s.back_recv)

    def start_second():
        received("back")
        second_norm_back()

    def grad_fc1_weight(j):
        column_grad(s.normed2_t, s.g_hidden, s.g_fc1, lambda side: 768 * side + 384 * j)

    def grad_out_weight():
        column_grad(s.attended_t, s.g_branch, s.g_out, lambda side: 384 * side)

    def grad_qkv_weight(j):
        column_grad(s.normed_t, s.g_mixed, s.g_qkv, partial(tile, j))

    g, r = types.SimpleNamespace(**gathers), types.SimpleNamespace(**scatters)
    g.s0.z()
    g.q0.z()
    g.q1.z()
    g.q2.z()
    g.q1.o()
    g.f2.x()
    g.o0.z()
    g.s0.p()
    g.q2.o()
    g.q0.o()
    g.h0.y()
    g.s0.f()
    g.o0.o()
    g.q0.p()
    g.s0.g()
    g.h1.y()
    g.h0.z()
    g.q1.p()
    g.s0.l()
    g.q0.f()
    g.q0.g()
    g.h1.z()
    g.q2.p()
    g.o0.p()
    g.q1.f()
    g.q1.g()
    g.f0.z()
    g.q0.l()
    g.s0.d()
    unpack_small()
    g.q2.f()
    g.q2.g()
    g.o0.f()
    g.q0.d()
    start_norm()
    g.o0.g()
    g.f1.z()
    g.h0.x()
    project_both(0)
    g.q1.l()
    send_cotangent()
    g.q2.l()
    g.q1.d()
    project_both(1)
    attend(0)
    g.q2.d()
    project_both(2)
    g.o0.l()
    g.f2.z()
    g.h1.x()
    attend(1)
    g.o0.d()
    project_out()
    send_normed()
    g.h0.l()
    transpose_out()
    g.h0.d()
    g.f0.x()
    feed(0, 0)
    start_cotangent()
    g.f1.x()
    g.h1.l()
    g.h1.d()
    feed(1, 0)
    g.f0.l()
    take_normed()
    feed(1, 1)
    feed(0, 1)
    weight_grad_fc2(1)
    r.f1.s()
    g.f1.l()
    g.f2.l()
    weight_grad_fc2(2)
    r.f2.s()
    r.f1.x()
    weight_grad_fc2(0)
    r.f0.s()
    g.f2.d()
    g.f1.d()
    g.f0.d()
    feed_back(1)
    feed_back_rows(1)
    send_back()
    transpose_other()
    r.f0.z()
    r.f2.x()
    feed_back(0)
    grad_fc1_weight(1)
    r.h1.s()
    grad_fc1_weight(0)
    r.h1.x()
    feed_out(1)
    feed_out(0)
    r.h0.s()
    r.f2.z()
    send_part()
    r.f1.z()
    feed_back_rows(0)
    r.h0.x()
    send_base()
    start_second()
    project_attended()
    grad_out_weight()
    r.o0.s()
    attend_back(0)
    grad_qkv_weight(0)
    r.q0.s()
    r.h1.z()
    r.o0.p()
    r.q0.p()
    attend_back(1)
    grad_qkv_weight(2)
    r.q2.s()
    r.h0.z()
    r.o0.f()
    r.o0.g()
    grad_qkv_weight(1)
    r.q2.p()
    r.q0.f()
    r.q0.g()
    r.q1.s()
    start_output()
    first_norm_back()
    r.q2.f()
    r.q2.g()
    r.o0.z()
    r.q1.p()
    r.q0.z()
    pack_small()
    r.s0.s()
    r.s0.p()
    r.q1.f()
    r.q1.g()
    r.f0.x()
    r.q2.z()
    r.h1.y()
    r.o0.l()
    r.h0.y()
    r.q0.l()
    r.s0.f()
    r.s0.g()
    send_grad_rows()
    r.f1.l()
    r.f2.l()
    r.q1.z()
    r.q2.l()
    send_encoded()
    r.h1.l()
    r.f0.l()
    r.s0.z()
    r.h0.l()
    r.q1.l()
    r.s0.l()
    for name in list(moved):
        received(name)
    for copy in finals:
        copy.wait_recv()
    grad_patches[...] = s.gx_recv[...].astype(F32)
    for copy in started[-SENDS:]:
        copy.wait_send()


def emit_kernel(*refs):
    count = (len(refs) - 3) // 3
    given, made, held = refs[:count], refs[count : 2 * count], refs[2 * count : 3 * count]
    ordered, in_sem, out_sem = refs[3 * count :]
    arrive = [pltpu.make_async_copy(given[i], held[i], in_sem.at[i]) for i in range(count)]
    leave = [
        pltpu.make_async_copy(ordered if i == FC1_OUTPUT else held[i], made[i], out_sem.at[i]) for i in range(count)
    ]
    for copy in arrive:
        copy.start()
    for i in range(count):
        arrive[i].wait()
        if i == FC1_OUTPUT:
            for side in (0, 1):
                for k in range(8):
                    source = held[i][:, 1536 * side + 192 * k : 1536 * side + 192 * k + 192]
                    ordered[:, 384 * k + 192 * side : 384 * k + 192 * side + 192] = source
        leave[i].start()
    for copy in leave:
        copy.wait()


def emit(arrays):
    anywhere = pl.BlockSpec(memory_space=pl.ANY)
    count = len(arrays)
    return list(
        pl.pallas_call(
            emit_kernel,
            out_shape=[jax.ShapeDtypeStruct(a.shape, a.dtype) for a in arrays],
            in_specs=[anywhere] * count,
            out_specs=[anywhere] * count,
            scratch_shapes=[pltpu.VMEM(a.shape, a.dtype) for a in arrays]
            + [pltpu.VMEM(arrays[FC1_OUTPUT].shape, F32)]
            + [pltpu.SemaphoreType.DMA((count,))] * 2,
        )(*arrays)
    )


def fast(
    patches,
    norm_gain,
    norm_bias,
    qkv_weight,
    qv_bias,
    out_weight,
    fc1_weight,
    fc1_bias,
    fc2_weight,
    res_bias,
    cotangent,
    frame_valid,
):
    outputs = [
        ((4, 64, D), BF16),
        ((4, 64, D), F32),
        ((2, 24), F32),
        ((2, 24), F32),
        ((24, 3 * D), F32),
        ((2, 24), F32),
        ((24, D), F32),
        ((24, FF), F32),
        ((1, 96), F32),
        ((96, D), F32),
        ((2, 24), F32),
    ]
    vmem = pl.BlockSpec(memory_space=pltpu.VMEM)
    found = list(pl.pallas_call(
        layer_kernel,
        out_shape=[jax.ShapeDtypeStruct(shape, dtype) for shape, dtype in outputs],
        in_specs=[vmem] * 11 + [pl.BlockSpec(memory_space=pltpu.SMEM)],
        out_specs=[vmem] * len(outputs),
        scratch_shapes=list(scratch_shapes().values()),
        compiler_params=pltpu.CompilerParams(
            collective_id=0, has_side_effects=True, vmem_limit_bytes=63 * 2**20
        ),
    )(
        patches,
        norm_gain,
        norm_bias,
        qkv_weight,
        qv_bias,
        out_weight,
        fc1_weight,
        fc1_bias.reshape(1, 96),
        fc2_weight,
        res_bias,
        cotangent,
        frame_valid,
    ))
    found = emit(found)
    found[8] = found[8].reshape(96)
    return tuple(found)


def solution(mesh):
    in_specs = (
        P("wide", "blk", None),
        P(None, ("wide", "blk")),
        P(None, ("wide", "blk")),
        P(("wide", "blk"), None),
        P(None, ("wide", "blk")),
        P(("wide", "blk"), None),
        P(("wide", "blk"), None),
        P(("wide", "blk")),
        P(("wide", "blk"), None),
        P(None, ("wide", "blk")),
        P("wide", "blk", None),
        P("wide"),
    )
    out_specs = (
        P("wide", "blk", None),
        P("wide", "blk", None),
        P(None, ("wide", "blk")),
        P(None, ("wide", "blk")),
        P(("wide", "blk"), None),
        P(None, ("wide", "blk")),
        P(("wide", "blk"), None),
        P(("wide", "blk"), None),
        P(("wide", "blk")),
        P(("wide", "blk"), None),
        P(None, ("wide", "blk")),
    )
    body = fast if dict(mesh.shape) == {"wide": 8, "blk": 4} else local
    return jax.shard_map(body, mesh=mesh, in_specs=in_specs, out_specs=out_specs, check_vma=False)
```

```python
from functools import partial
import math
import types

import jax
import jax.numpy as jnp
from jax import lax
from jax.experimental import pallas as pl
from jax.experimental.pallas import tpu as pltpu
from jax.sharding import PartitionSpec as P

D = 768
HEADS = 12
HEAD = 64


EPSILON = 1e-06


def layer_normalize(token_rows, norm_gain_vector, norm_bias_vector):
    row_average = jnp.mean(token_rows, axis=-1, keepdims=True)
    centered_rows = token_rows - row_average
    inverse_deviation_scale = lax.rsqrt(
        jnp.mean(centered_rows * centered_rows, axis=-1, keepdims=True) + EPSILON
    )
    standardized_rows = centered_rows * inverse_deviation_scale
    return (
        standardized_rows * norm_gain_vector + norm_bias_vector,
        standardized_rows,
        inverse_deviation_scale,
    )


def layer_normalize_backward(
    incoming_gradient, standardized_rows, inverse_deviation_scale, norm_gain_vector
):
    gain_weighted_gradient = incoming_gradient * norm_gain_vector
    inner_product_sum = (
        gain_weighted_gradient
        - jnp.mean(gain_weighted_gradient, axis=-1, keepdims=True)
        - standardized_rows
        * jnp.mean(gain_weighted_gradient * standardized_rows, axis=-1, keepdims=True)
    )
    return (
        inverse_deviation_scale * inner_product_sum,
        jnp.sum(incoming_gradient * standardized_rows, axis=0),
        jnp.sum(incoming_gradient, axis=0),
    )


def frame_groups(array, count):
    return array.reshape((array.shape[0] // count, count) + array.shape[1:])


def attend_forward(query, keys, values):
    scores = jnp.einsum("gqhe,gkhe->ghqk", query, keys, preferred_element_type=jnp.float32)
    top = jnp.max(scores, axis=-1, keepdims=True)
    expo = jnp.exp(scores - top)
    total = jnp.sum(expo, axis=-1, keepdims=True)
    probs = (expo / total).astype(jnp.bfloat16)
    attended = jnp.einsum("ghqk,gkhe->gqhe", probs, values, preferred_element_type=jnp.float32)
    return (attended, top + jnp.log(total))


def attend_back(query, keys, values, logsum, grad_out):
    scores = jnp.einsum("gqhe,gkhe->ghqk", query, keys, preferred_element_type=jnp.float32)
    probs = jnp.exp(scores - logsum)
    grad_probs = jnp.einsum("gqhe,gkhe->ghqk", grad_out, values, preferred_element_type=jnp.float32)
    grad_values = jnp.einsum(
        "ghqk,gqhe->gkhe", probs.astype(jnp.bfloat16), grad_out, preferred_element_type=jnp.float32
    )
    grad_scores = (
        probs * (grad_probs - jnp.sum(probs * grad_probs, axis=-1, keepdims=True))
    ).astype(jnp.bfloat16)
    grad_query = jnp.einsum(
        "ghqk,gkhe->gqhe", grad_scores, keys, preferred_element_type=jnp.float32
    )
    grad_keys = jnp.einsum(
        "ghqk,gqhe->gkhe", grad_scores, query, preferred_element_type=jnp.float32
    )
    return (grad_query, grad_keys, grad_values)


def local(
    patches,
    norm_gain,
    norm_bias,
    qkv_weight,
    qv_bias,
    out_weight,
    fc1_weight,
    fc1_bias,
    fc2_weight,
    res_bias,
    cotangent,
    frame_valid,
):
    frames, frame_rows, width = patches.shape
    count = frames * frame_rows
    group = math.gcd(frames, 8)
    params = (
        lax.all_gather(norm_gain, ("wide", "blk"), axis=1, tiled=True),
        lax.all_gather(norm_bias, ("wide", "blk"), axis=1, tiled=True),
        lax.all_gather(qkv_weight, ("wide", "blk"), axis=0, tiled=True),
        lax.all_gather(qv_bias, ("wide", "blk"), axis=1, tiled=True),
        lax.all_gather(out_weight, ("wide", "blk"), axis=0, tiled=True),
        lax.all_gather(fc1_weight, ("wide", "blk"), axis=0, tiled=True),
        lax.all_gather(fc1_bias, ("wide", "blk"), axis=0, tiled=True),
        lax.all_gather(fc2_weight, ("wide", "blk"), axis=0, tiled=True),
        lax.all_gather(res_bias, ("wide", "blk"), axis=1, tiled=True),
    )
    norm_gain_pair = params[0].astype(jnp.float32)
    norm_bias_pair = params[1].astype(jnp.float32)
    biases_qv = params[3].astype(jnp.float32)
    bias_fc1 = params[6].astype(jnp.float32)
    biases_res = params[8].astype(jnp.float32)
    token_rows = patches.reshape(count, width).astype(jnp.float32)
    valid = jnp.repeat(frame_valid.astype(jnp.float32), frame_rows)[:, None]
    first_branch, first_standardized_rows, first_norm_scale = layer_normalize(
        token_rows, norm_gain_pair[0], norm_bias_pair[0]
    )
    normed = first_branch.astype(jnp.bfloat16)
    mixed = jnp.dot(normed, params[2], preferred_element_type=jnp.float32)
    query = ((mixed[:, :D] + biases_qv[0]) * 0.125).astype(jnp.bfloat16)
    keys = mixed[:, D : 2 * D].astype(jnp.bfloat16).reshape(frames, frame_rows, width)
    values = (
        (mixed[:, 2 * D :] + biases_qv[1]).astype(jnp.bfloat16).reshape(frames, frame_rows, width)
    )
    keys_all, values_all = (
        lax.all_gather(keys, "blk", axis=1, tiled=True),
        lax.all_gather(values, "blk", axis=1, tiled=True),
    )
    query_heads = frame_groups(query.reshape(frames, frame_rows, HEADS, HEAD), group)
    keys_heads = frame_groups(keys_all.reshape(frames, -1, HEADS, HEAD), group)
    values_heads = frame_groups(values_all.reshape(frames, -1, HEADS, HEAD), group)
    attended, logsum = lax.map(
        lambda item: attend_forward(item[0], item[1], item[2]),
        (query_heads, keys_heads, values_heads),
    )
    attended = attended.reshape(count, width).astype(jnp.bfloat16)
    middle_activation = (
        token_rows
        + jnp.dot(attended, params[4], preferred_element_type=jnp.float32)
        + biases_res[0]
    )
    second_branch, second_standardized_rows, second_norm_scale = layer_normalize(
        middle_activation, norm_gain_pair[1], norm_bias_pair[1]
    )
    normed2 = second_branch.astype(jnp.bfloat16)
    hidden = jnp.dot(normed2, params[5], preferred_element_type=jnp.float32) + bias_fc1
    active = jax.nn.gelu(hidden, approximate=False).astype(jnp.bfloat16)
    branch2 = jnp.dot(active, params[7], preferred_element_type=jnp.float32) + biases_res[1]
    encoded = (
        ((middle_activation + branch2) * valid)
        .astype(jnp.bfloat16)
        .reshape(frames, frame_rows, width)
    )
    params = (
        lax.all_gather(norm_gain, ("wide", "blk"), axis=1, tiled=True),
        lax.all_gather(norm_bias, ("wide", "blk"), axis=1, tiled=True),
        lax.all_gather(qkv_weight, ("wide", "blk"), axis=0, tiled=True),
        lax.all_gather(qv_bias, ("wide", "blk"), axis=1, tiled=True),
        lax.all_gather(out_weight, ("wide", "blk"), axis=0, tiled=True),
        lax.all_gather(fc1_weight, ("wide", "blk"), axis=0, tiled=True),
        lax.all_gather(fc1_bias, ("wide", "blk"), axis=0, tiled=True),
        lax.all_gather(fc2_weight, ("wide", "blk"), axis=0, tiled=True),
        lax.all_gather(res_bias, ("wide", "blk"), axis=1, tiled=True),
    )
    grad_out = cotangent.reshape(count, width).astype(jnp.float32) * valid
    grad_branch2 = grad_out.astype(jnp.bfloat16)
    grad_fc2 = jnp.dot(active.T, grad_branch2, preferred_element_type=jnp.float32)
    grad_res_two = jnp.sum(grad_branch2.astype(jnp.float32), axis=0)
    grad_active = jnp.dot(grad_branch2, params[7].T, preferred_element_type=jnp.float32)
    gelu_back = jax.vjp(partial(jax.nn.gelu, approximate=False), hidden)[1]
    grad_hidden = gelu_back(grad_active)[0].astype(jnp.bfloat16)
    grad_fc1 = jnp.dot(normed2.T, grad_hidden, preferred_element_type=jnp.float32)
    grad_bias_fc1 = jnp.sum(grad_hidden.astype(jnp.float32), axis=0)
    normed_input_gradient2 = jnp.dot(grad_hidden, params[5].T, preferred_element_type=jnp.float32)
    second_norm_gradient, second_norm_gain, second_norm_bias = layer_normalize_backward(
        normed_input_gradient2, second_standardized_rows, second_norm_scale, norm_gain_pair[1]
    )
    grad_middle = grad_out + second_norm_gradient
    grad_branch = grad_middle.astype(jnp.bfloat16)
    grad_out_proj = jnp.dot(attended.T, grad_branch, preferred_element_type=jnp.float32)
    grad_res_one = jnp.sum(grad_branch.astype(jnp.float32), axis=0)
    grad_attended = jnp.dot(grad_branch, params[4].T, preferred_element_type=jnp.float32).astype(
        jnp.bfloat16
    )
    grad_heads = frame_groups(grad_attended.reshape(frames, frame_rows, HEADS, HEAD), group)
    grad_query, grad_keys, grad_values = lax.map(
        lambda item: attend_back(item[0], item[1], item[2], item[3], item[4]),
        (query_heads, keys_heads, values_heads, logsum, grad_heads),
    )
    grad_keys, grad_values = (
        lax.psum_scatter(
            grad_keys.reshape(frames, -1, width).astype(jnp.bfloat16),
            "blk",
            scatter_dimension=1,
            tiled=True,
        ).astype(jnp.float32),
        lax.psum_scatter(
            grad_values.reshape(frames, -1, width).astype(jnp.bfloat16),
            "blk",
            scatter_dimension=1,
            tiled=True,
        ).astype(jnp.float32),
    )
    grad_query = grad_query.reshape(count, width).astype(jnp.bfloat16) * 0.125
    grad_keys = grad_keys.reshape(count, width).astype(jnp.bfloat16)
    grad_values = grad_values.reshape(count, width).astype(jnp.bfloat16)
    grad_mixed = jnp.concatenate([grad_query, grad_keys, grad_values], axis=1)
    grad_qkv = jnp.dot(normed.T, grad_mixed, preferred_element_type=jnp.float32)
    grad_qv = jnp.stack(
        [
            jnp.sum(grad_query.astype(jnp.float32), axis=0),
            jnp.sum(grad_values.astype(jnp.float32), axis=0),
        ]
    )
    normed_input_gradient = jnp.dot(grad_mixed, params[2].T, preferred_element_type=jnp.float32)
    first_norm_gradient, first_norm_gain, first_norm_bias = layer_normalize_backward(
        normed_input_gradient, first_standardized_rows, first_norm_scale, norm_gain_pair[0]
    )
    grad_rows = (grad_middle + first_norm_gradient).reshape(frames, frame_rows, width)
    grad_gain = jnp.stack([first_norm_gain, second_norm_gain])
    grad_shift = jnp.stack([first_norm_bias, second_norm_bias])
    grad_res = jnp.stack([grad_res_one, grad_res_two])
    summed = (
        lax.psum_scatter(grad_gain, ("wide", "blk"), scatter_dimension=1, tiled=True),
        lax.psum_scatter(grad_shift, ("wide", "blk"), scatter_dimension=1, tiled=True),
        lax.psum_scatter(grad_qkv, ("wide", "blk"), scatter_dimension=0, tiled=True),
        lax.psum_scatter(grad_qv, ("wide", "blk"), scatter_dimension=1, tiled=True),
        lax.psum_scatter(grad_out_proj, ("wide", "blk"), scatter_dimension=0, tiled=True),
        lax.psum_scatter(grad_fc1, ("wide", "blk"), scatter_dimension=0, tiled=True),
        lax.psum_scatter(grad_bias_fc1, ("wide", "blk"), scatter_dimension=0, tiled=True),
        lax.psum_scatter(grad_fc2, ("wide", "blk"), scatter_dimension=0, tiled=True),
        lax.psum_scatter(grad_res, ("wide", "blk"), scatter_dimension=1, tiled=True),
    )
    return (
        encoded,
        grad_rows,
        summed[0],
        summed[1],
        summed[2],
        summed[3],
        summed[4],
        summed[5],
        summed[6],
        summed[7],
        summed[8],
    )


MESH_ID = pl.DeviceIdType.MESH
BF16 = jnp.bfloat16
F32 = jnp.float32
FF = 3072
TOKENS = 256
ROWS = 64
ALL, THREE, BOTH = pl.ds(0, 4), pl.ds(0, 3), pl.ds(0, 2)
GATHER_WAYS = dict(q=(-1, -2, -2), o=(-1,), f=(1, 0, 0))
SCATTER_WAYS = dict(f=(0, 0, 1), o=(2,), q=(2, 2, 2))
GATHER_LINES = dict(q=(0, 0, 0), o=(0,), h=(1, 1), f=(1, 1, 1))
SCATTER_LINES = dict(q=(0, 0, 0), o=(0,), h=(1, 1), f=(1, 1, 1))


TILES = ((0, 1536), (768, 384), (1920, 1152))


def tile(j, side):
    first, second = TILES[j]
    return first + side * (second - first)


def dot(left, right):
    return lax.dot_general(left, right, (((1,), (0,)), ((), ())), preferred_element_type=F32)


def dot_nt(left, right):
    return lax.dot_general(left, right, (((1,), (1,)), ((), ())), preferred_element_type=F32)


def dot_tn(left, right):
    return lax.dot_general(left, right, (((0,), (0,)), ((), ())), preferred_element_type=F32)


SENDS, ARRIVALS = 80, 150
FC1_OUTPUT = 7


def scratch_shapes():
    def vm(*shape, dtype=BF16):
        return pltpu.VMEM(shape, dtype)

    return dict(
        w_small=vm(4, 4, 16, 256),
        w_qkv=vm(4, 4, 48, 2304),
        w_out=vm(4, 4, 48, 768),
        w_fc1=vm(4, 4, 48, 1536),
        w_fc2=vm(4, 2, 2, 96, 768),
        fc1_other=vm(48, 768),
        own_small=vm(16, 128, dtype=F32),
        pair_rows=vm(48, 3072, dtype=F32),
        pair_send=vm(24, 3072, dtype=F32),
        par=vm(16, 768, dtype=F32),
        par_fc1=vm(8, 1536, dtype=F32),
        rows_in=vm(256, 768),
        cot_in=vm(512, 768),
        normed=vm(256, 768),
        normed_t=vm(768, 256),
        mixed=vm(256, 2304),
        attended=vm(256, 768),
        attended_t=vm(768, 256),
        middle=vm(256, 768, dtype=F32),
        normed2=vm(512, 768),
        normed2_t=vm(768, 512),
        slope=vm(512, 1536, dtype=F32),
        active=vm(512, 1536),
        g_hidden=vm(512, 1536),
        active_t=vm(16, 96, 512),
        g_branch2=vm(512, 768),
        part_across=vm(256, 768),
        part_recv=vm(128, 768),
        base_send=vm(128, 768),
        base_recv=vm(128, 768),
        back_send=vm(256, 768),
        back_recv=vm(256, 768),
        other=vm(256, 768, dtype=F32),
        total=vm(256, 768, dtype=F32),
        g_middle=vm(256, 768, dtype=F32),
        g_branch=vm(256, 768),
        g_attended=vm(256, 768),
        g_mixed=vm(256, 2304),
        enc_send=vm(2, 128, 768),
        gx_send=vm(256, 768),
        gx_recv=vm(4, 64, 768),
        sums=vm(16, 768, dtype=F32),
        sums_fc1=vm(8, 1536, dtype=F32),
        g_small=vm(4, 4, 16, 256),
        g_fc1=vm(4, 4, 48, 1536),
        g_fc2=vm(4, 2, 2, 96, 768),
        g_out=vm(4, 4, 48, 768),
        g_qkv=vm(4, 4, 48, 2304),
        pr_small=vm(4, 4, 16, 128),
        pr_a=vm(4, 4, 48, 1536),
        pr_fc1=vm(4, 4, 48, 768),
        pr_fc2=vm(4, 2, 2, 96, 384),
        dx_small=vm(4, 16, 128),
        dx_a=vm(4, 48, 1536),
        px_small=vm(4, 16, 128),
        px_a=vm(4, 48, 1536),
        px_fc1=vm(4, 2, 48, 768),
        px_fc2=vm(4, 2, 96, 384),
        py_small=vm(4, 16, 128),
        py_a=vm(4, 48, 1536),
        py_fc1=vm(48, 768),
        pz_small=vm(3, 16, 128),
        pz_a=vm(3, 48, 1536),
        pz_fc1=vm(3, 2, 48, 768),
        pz_fc2=vm(3, 2, 96, 384),
        bz_a=vm(3, 4, 48, 1536),
        cz_a=vm(3, 4, 48, 1536),
        qz_a=vm(3, 48, 1536),
        qz_fc1=vm(3, 2, 48, 768),
        qz_fc2=vm(3, 2, 96, 384),
        bz_fc2=vm(3, 2, 2, 96, 384),
        cz_fc2=vm(3, 2, 2, 96, 384),
        last_a=vm(48, 1536, dtype=F32),
        last_fc1=vm(2, 48, 768, dtype=F32),
        send_fc1=vm(48, 768),
        last_fc2=vm(96, 384, dtype=F32),
        send_sem=pltpu.SemaphoreType.DMA((SENDS,)),
        recv_sem=pltpu.SemaphoreType.DMA((ARRIVALS,)),
    )


def layer_kernel(
    patches,
    norm_gain,
    norm_bias,
    qkv_weight,
    qv_bias,
    out_weight,
    fc1_weight,
    fc1_bias,
    fc2_weight,
    res_bias,
    cotangent,
    frame_valid,
    encoded,
    grad_patches,
    grad_gain,
    grad_shift,
    grad_qkv,
    grad_qv,
    grad_out,
    grad_fc1,
    grad_fc1_bias,
    grad_fc2,
    grad_res,
    *scratch,
):
    s = types.SimpleNamespace(**dict(zip(scratch_shapes(), scratch)))
    wide, blk = lax.axis_index("wide"), lax.axis_index("blk")
    z, x = lax.div(wide, 2), lax.rem(wide, 2)
    y, core = lax.div(blk, 2), lax.rem(blk, 2)
    here, at_x, at_y, at_d = 2 * x + y, 2 * (1 - x) + y, 2 * x + 1 - y, 2 * (1 - x) + 1 - y
    sibling = (wide, 2 * y + 1 - core)
    x_peer = (2 * z + 1 - x, blk)
    y_peer = (wide, 2 * (1 - y) + core)
    d_peer = (2 * z + 1 - x, 2 * (1 - y) + core)
    y_cross = (wide, 2 * (1 - y) + 1 - core)
    z_of = [lax.rem(z + step, 4) for step in range(4)]
    z_peers = [(2 * z_of[step] + x, blk) for step in range(4)]
    z_order = (z_peers[1], z_peers[3], z_peers[2])
    inner, end = lax.rem(z + 1, 4) >= 2, lax.rem(z + 1, 4) < 2
    z_in, z_out = 1 + lax.rem(z, 2), 3 * lax.div(z, 2)
    in_peer, out_peer = (2 * z_in + x, blk), (2 * z_out + x, blk)
    blk_peers = [(y, 1 - core), (1 - y, core), (1 - y, 1 - core)]

    barrier = pltpu.get_barrier_semaphore()
    peers = [sibling, x_peer, y_peer, d_peer, y_cross] + z_peers[1:]
    for peer in peers:
        pl.semaphore_signal(barrier, inc=1, device_id=peer, device_id_type=MESH_ID)

    started, groups = [], []

    class Group:
        def __init__(self):
            self.sem = s.recv_sem.at[len(groups)]
            groups.append(self)

        def wait(self, ref):
            pltpu.make_async_copy(ref, ref, self.sem).wait()

    def leave(spot):
        copy, only = started[spot]
        if only is None:
            copy.wait_send()
        else:
            pl.when(only)(copy.wait_send)

    def prepare(source, target, peer, group=None, only=None):
        spot = len(started)
        if spot >= SENDS:
            leave(spot - SENDS)
        copy = pltpu.make_async_remote_copy(
            src_ref=source,
            dst_ref=target,
            send_sem=s.send_sem.at[spot % SENDS],
            recv_sem=(group or Group()).sem,
            device_id=peer,
            device_id_type=MESH_ID,
        )
        started.append((copy, only))
        return copy

    def remote(source, target, peer, group=None, only=None):
        copy = prepare(source, target, peer, group, only)
        if only is None:
            copy.start()
        else:
            pl.when(only)(copy.start)
        return copy

    def lanes(start, size):
        return pl.ds(pl.multiple_of(start, 128), size)

    s.own_small[...] = jnp.zeros((16, 128), F32)
    s.sums[...] = jnp.zeros((16, D), F32)
    s.own_small[0:2, 0:24] = norm_gain[...].astype(F32)
    s.own_small[2:4, 0:24] = norm_bias[...].astype(F32)
    s.own_small[4:6, 0:24] = qv_bias[...].astype(F32)
    s.own_small[6:8, 0:24] = res_bias[...].astype(F32)
    s.own_small[8:9, 0:96] = fc1_bias[...].astype(F32)
    s.w_small[z, here, :, lanes(128 * core, 128)] = s.own_small[...].astype(BF16)
    own_rows = pl.ds(pl.multiple_of(24 * core, 8), 24)
    for ref, start, columns in (
        (qkv_weight, 0, partial(tile, 0)),
        (qkv_weight, 384, partial(tile, 1)),
        (qkv_weight, 768, partial(tile, 2)),
        (out_weight, 1152, lambda side: 384 * side),
    ):
        s.pair_send[:, start : start + 384] = ref[:, lanes(columns(1 - core), 384)].astype(F32)
        s.pair_rows[own_rows, start : start + 384] = ref[:, lanes(columns(core), 384)].astype(F32)
    theirs = fc1_weight[:, lanes((1 - core) * 1536, 1536)].astype(F32)
    ours = fc1_weight[:, lanes(core * 1536, 1536)].astype(F32)
    for side in (0, 1):
        for k in range(4):
            at, found = 1536 + 768 * side + 192 * k, 384 * k + 192 * side
            s.pair_send[:, at : at + 192] = theirs[:, found : found + 192]
            s.pair_rows[own_rows, at : at + 192] = ours[:, found : found + 192]
    s.w_fc2[z, x, core] = fc2_weight[...]

    pl.semaphore_wait(barrier, len(peers))

    pair = remote(s.pair_send, s.pair_rows.at[own_rows, :], sibling)

    mine = pl.ds(pl.multiple_of(64 * blk, 64), 64)

    rows_moved = Group()
    for py, pc in blk_peers:
        remote(patches.at[2 * py + pc], s.rows_in.at[mine, :], (wide, 2 * py + pc), rows_moved)
    s.rows_in[mine, :] = patches[blk]

    class Direct:
        def __init__(self, block):
            self.block, self.arrived = block, Group()

        def start(self):
            own = self.block(z)
            for peer in z_order:
                remote(own, own, peer, self.arrived)

        def wait(self):
            self.arrived.wait(self.block(THREE))

    class Line:
        def __init__(self, block):
            self.block, self.first = block, len(groups)
            self.arrived = [Group() for _ in range(3)]

        def start(self):
            own = self.block(z)
            to_in = types.SimpleNamespace(sem=s.recv_sem.at[self.first + lax.div(lax.rem(z + 1, 4), 2)])
            remote(own, own, in_peer, to_in)
            remote(own, own, out_peer, self.arrived[0], inner)

        def pass_on(self):
            outer, other = self.block(z_out), self.block(z_in)
            inward = prepare(outer, outer, in_peer, self.arrived[2], inner)
            outward = prepare(other, other, out_peer, self.arrived[1], inner)

            @pl.when(inner)
            def _():
                self.arrived[0].wait(outer)
                inward.start()
                self.arrived[1].wait(other)
                outward.start()

        def pass_last(self):
            far = self.block(3 - z_out)
            outward = prepare(far, far, out_peer, self.arrived[2], inner)

            @pl.when(inner)
            def _():
                self.arrived[2].wait(far)
                outward.start()

        def wait(self):
            @pl.when(end)
            def _():
                for arrived, level in zip(self.arrived, (z_in, 3 - z_in, 3 - z)):
                    arrived.wait(self.block(level))

    class DirectSum:
        def __init__(self, own, parts, _):
            self.own, self.parts, self.arrived = own, parts, Group()

        def start(self):
            for step in (1, 3, 2):
                remote(self.own(z_of[step]), self.parts(step - 1), z_peers[step], self.arrived)

        def wait(self):
            self.arrived.wait(self.parts(THREE))

        def summed(self, view):
            found = view(self.own(z))[...].astype(F32)
            for i in range(3):
                found = found + view(self.parts(i))[...].astype(F32)
            return found

    class LineSum:
        def __init__(self, own, parts, more):
            self.own, self.parts, self.more = own, parts, more
            self.arrived = [Group() for _ in range(3)]

        def start(self):
            remote(self.own(pl.ds(1 - lax.div(z, 2), 3)), self.parts(THREE), in_peer, self.arrived[0], end)

        def pass_on(self):
            source = self.own(pl.ds(2 - 2 * lax.div(z, 2), 2))
            inward = prepare(source, self.more(BOTH), in_peer, self.arrived[1], inner)

            @pl.when(inner)
            def _():
                self.arrived[0].wait(self.parts(THREE))
                for level in (z_in, 3 - z_out):
                    ref = self.own(level)
                    ref[...] = ref[...] + self.parts(level - 1 + lax.div(z, 2))[...]
                inward.start()

        def pass_last(self):
            outward = prepare(self.own(z_out), self.more(2), out_peer, self.arrived[2], inner)

            @pl.when(inner)
            def _():
                self.arrived[1].wait(self.more(BOTH))
                base = 2 * lax.div(z, 2)
                ref = self.own(z_out)
                ref[...] = ref[...] + self.more(z_out - base)[...]
                outward.start()
                ref = self.own(z)
                found = ref[...].astype(F32) + self.parts(z - 1 + lax.div(z, 2))[...].astype(F32)
                ref[...] = (found + self.more(z - base)[...].astype(F32)).astype(BF16)

        def wait(self):
            @pl.when(end)
            def _():
                self.arrived[2].wait(self.more(2))
                ref = self.own(z)
                ref[...] = ref[...] + self.more(2)[...]

        def summed(self, view):
            return view(self.own(z))[...].astype(F32)

    class Steps:
        def w(self):
            self.line.pass_on()

        def v(self):
            self.line.pass_last()

    class Gather(Steps):
        def __init__(self, part, low, line):
            self.part, self.low, self.high = part, pl.ds(0, low), pl.ds(low, 4 - low)
            self.by_x, self.by_y, self.far, self.pair = (Group() for _ in range(4))
            self.line = line(lambda levels: part(levels, here))

        def z(self):
            self.line.start()

        def p(self):
            self.line.wait()
            self.share(self.part(ALL, here))

        def share(self, block):
            remote(block, block, x_peer, self.by_x)
            remote(block, block, y_peer, self.by_y)
            remote(block, block, sibling, self.pair)

        def f(self):
            column = self.part(ALL, at_x)
            self.by_x.wait(column)
            some = self.part(self.low, at_x)
            remote(some, some, y_peer, self.far)
            remote(column, column, sibling, self.pair)

        def g(self):
            column = self.part(ALL, at_y)
            self.by_y.wait(column)
            some = self.part(self.high, at_y)
            remote(some, some, x_peer, self.far)
            remote(column, column, sibling, self.pair)

        def l(self):
            column = self.part(ALL, at_d)
            self.far.wait(column)
            remote(column, column, sibling, self.pair)

        def d(self):
            self.pair.wait(self.part(ALL, ALL))

    class FineGather(Gather):
        def z(self):
            own = self.part(z, here)
            self.z_copies = [remote(own, own, peer) for peer in z_order]

        def o(self):
            self.share(self.part(z, here))

        def p(self):
            for step, copy in zip((1, 3, 2), self.z_copies):
                copy.wait_recv()
                self.share(self.part(z_of[4 - step], here))

    class SquareGather(Steps):
        def __init__(self, part, line):
            self.part, self.square, self.pair = part, Group(), Group()
            self.line = line(lambda levels: part(levels, ALL))

        def p(self):
            own = self.part(z, here)
            for peer in (x_peer, y_peer, d_peer):
                remote(own, own, peer, self.square)

        def z(self):
            self.square.wait(self.part(z, THREE))
            self.line.start()
            level = self.part(z, ALL)
            remote(level, level, sibling, self.pair)

        def l(self):
            self.line.wait()
            for step in (1, 2, 3):
                level = self.part(z_of[step], ALL)
                remote(level, level, sibling, self.pair)

        def d(self):
            self.pair.wait(self.part(ALL, ALL))

    class PlaneGather(Steps):
        def __init__(self, part, line, across=None):
            self.part, self.across, self.pair = part, across, Group()
            self.line = line(lambda levels: part(levels, x))

        def y(self):
            source, target = self.across
            self.y_copy = remote(source, target, y_peer)

        def z(self):
            if self.across:
                self.y_copy.wait_recv()
            self.line.start()

        def x(self):
            self.line.wait()
            column = self.part(ALL, x)
            self.x_copy = remote(column, column, x_peer)
            remote(column, column, sibling, self.pair)

        def l(self):
            self.x_copy.wait_recv()
            column = self.part(ALL, 1 - x)
            remote(column, column, sibling, self.pair)

        def d(self):
            self.pair.wait(self.part(ALL, BOTH))

    class AcrossGather(Steps):
        def __init__(self, part, line):
            self.part, self.pair = part, Group()
            self.line = line(lambda levels: part(levels, BOTH))

        def x(self):
            own = self.part(z, x)
            self.x_copy = remote(own, own, x_peer)

        def z(self):
            self.x_copy.wait_recv()
            self.line.start()
            level = self.part(z, BOTH)
            remote(level, level, sibling, self.pair)

        def l(self):
            self.line.wait()
            for step in (1, 2, 3):
                level = self.part(z_of[step], BOTH)
                remote(level, level, sibling, self.pair)

        def d(self):
            self.pair.wait(self.part(ALL, BOTH))

    def column_part(ref, start, size):
        return lambda levels, place: ref.at[levels, place, :, lanes(start, size)]

    def gather(part, way, chained=0):
        kind = Gather if way > 0 else FineGather
        line = Line if chained else Direct
        return kind(part, abs(way), line) if way else SquareGather(part, line)

    gathers = {
        "s0": gather(column_part(s.w_small, 128 * core, 128), 2),
        "o0": gather(column_part(s.w_out, 384 * core, 384), GATHER_WAYS["o"][0], GATHER_LINES["o"][0]),
    }
    for j in range(3):
        gathers["q" + str(j)] = gather(column_part(s.w_qkv, tile(j, core), 384), GATHER_WAYS["q"][j], GATHER_LINES["q"][j])

    def fc1_gather(j):
        columns = lanes(768 * core + 384 * j, 384)
        return PlaneGather(
            lambda levels, side: s.w_fc1.at[levels, ALL if side is BOTH else pl.ds(2 * side, 2), :, columns],
            Line if GATHER_LINES["h"][j] else Direct,
            (s.fc1_other.at[:, 384 * j : 384 * j + 384], s.w_fc1.at[z, here, :, columns]),
        )

    def fc2_gather(j, size, way):
        rows = pl.ds(size * j, size)
        part = lambda levels, side: s.w_fc2.at[levels, side, core, rows, :]
        return (PlaneGather if way else AcrossGather)(part, Line if GATHER_LINES["f"][j] else Direct)

    for j in range(2):
        gathers["h" + str(j)] = fc1_gather(j)
    for j, way in enumerate(GATHER_WAYS["f"]):
        gathers["f" + str(j)] = fc2_gather(j, 96 // len(GATHER_WAYS["f"]), way)

    pair.wait_recv()
    for j in range(3):
        s.w_qkv[z, here, :, lanes(tile(j, core), 384)] = s.pair_rows[:, 384 * j : 384 * j + 384].astype(BF16)
    s.w_out[z, here, :, lanes(384 * core, 384)] = s.pair_rows[:, 1152:1536].astype(BF16)
    halves = lanes(1536 + 768 * y, 768), lanes(1536 + 768 * (1 - y), 768)
    s.w_fc1[z, here, :, lanes(768 * core, 768)] = s.pair_rows[:, halves[0]].astype(BF16)
    s.fc1_other[...] = s.pair_rows[:, halves[1]].astype(BF16)


    def by_rows(body, carry=None):
        def step(i, held):
            return body(pl.ds(pl.multiple_of(ROWS * i, ROWS), ROWS), held)

        return lax.fori_loop(0, TOKENS // ROWS, step, carry)

    def over(shape, axis):
        return lax.broadcasted_iota(jnp.int32, shape, axis)

    def piece24(columns):
        return lax.shift_right_logical(columns * 43691, 20)

    def piece96(columns):
        return lax.shift_right_logical(columns * 10923, 20)

    def spread24():
        columns = over((128, D), 1)
        return (columns - 24 * piece24(columns) == over((128, D), 0)).astype(F32).astype(BF16)

    def hidden_unit(columns):
        return columns + 192 * lax.shift_right_logical(columns * 21846, 22) + 192 * y

    def spread96():
        columns = hidden_unit(over((128, FF // 2), 1))
        return (columns - 96 * piece96(columns) == over((128, FF // 2), 0)).astype(F32).astype(BF16)

    def unpack_small():
        flat = s.w_small[...].reshape(256, 256)
        chips = lax.shift_right_logical(over((256, D), 0), 4)
        pieces = piece24(over((256, D), 1))
        spread = spread24()
        found = jnp.zeros((16, D), F32)
        for side in (0, 1):
            wide_rows = dot(flat[:, 128 * side : 128 * side + 128], spread)
            wide_rows = jnp.where(pieces == 2 * chips + side, wide_rows, 0.0)
            found = found + jnp.sum(wide_rows.reshape(16, 16, D), axis=0)
        s.par[...] = found
        pick = (over((16, 256), 1) == 16 * over((16, 256), 0) + 8).astype(F32).astype(BF16)
        spread = spread96()
        shape = (16, FF // 2)
        pieces = piece96(hidden_unit(over(shape, 1)))
        found = jnp.zeros(shape, F32)
        for side in (0, 1):
            rows = dot(pick, flat[:, 128 * side : 128 * side + 128]).astype(BF16)
            found = found + jnp.where(pieces == 2 * over(shape, 0) + side, dot(rows, spread), 0.0)
        s.par_fc1[0:1, :] = jnp.sum(found, axis=0, keepdims=True)

    def standardized(rows):
        centered = rows - jnp.mean(rows, axis=-1, keepdims=True)
        scale = lax.rsqrt(jnp.mean(centered * centered, axis=-1, keepdims=True) + EPSILON)
        return centered * scale, scale

    def first_norm():
        def body(rows, _):
            found, _ = standardized(s.rows_in[rows, :].astype(F32))
            s.normed[rows, :] = (found * s.par[0:1, :] + s.par[2:3, :]).astype(BF16)
            return 0

        by_rows(body, 0)
        s.normed_t[...] = s.normed[...].T

    def project_qkv(start):
        found = dot(s.normed[...], s.w_qkv[:, :, :, start : start + 384].reshape(D, 384))
        if start < D:
            found = (found + s.par[4:5, start : start + 384]) * 0.125
        if start >= 2 * D:
            found = found + s.par[5:6, start - 2 * D : start - 2 * D + 384]
        s.mixed[:, start : start + 384] = found.astype(BF16)

    def head_masks():
        first = (over((TOKENS, 128), 1) < 64).astype(F32)
        return first.astype(BF16), (1.0 - first).astype(BF16)

    def softmax(scores):
        expo = jnp.exp(scores - jnp.max(scores, axis=-1, keepdims=True))
        return expo * (1.0 / jnp.sum(expo, axis=-1, keepdims=True))

    def attend(part):
        def body(two, _):
            query, key, value = (s.mixed[:, lanes(128 * two + part, 128)] for part in (0, D, 2 * D))
            found = jnp.zeros((TOKENS, 128), F32)
            for mask in head_masks():
                probs = softmax(dot_nt(query * mask, key)).astype(BF16)
                found = found + dot(probs, value * mask)
            s.attended[:, lanes(128 * two, 128)] = found.astype(BF16)
            return 0

        lax.fori_loop(3 * part, 3 * part + 3, body, 0)

    def project_out():
        s.middle[...] = dot(s.attended[...], s.w_out[...].reshape(D, D))

        def body(rows, _):
            middle = s.rows_in[rows, :].astype(F32) + (s.middle[rows, :] + s.par[6:7, :])
            s.middle[rows, :] = middle
            found, _ = standardized(middle)
            s.normed2[rows, :] = (found * s.par[1:2, :] + s.par[3:4, :]).astype(BF16)
            return 0

        by_rows(body, 0)

    def transpose_out():
        s.attended_t[...] = s.attended[...].T
        s.normed2_t[:, 0:256] = s.normed2[0:256, :].T

    def feed(j, frame):
        def body(side, _):
            columns = lanes(768 * side + 384 * j, 384)
            tokens = pl.ds(256 * frame, 256)
            s.other[:, 0:384] = dot(s.normed2[tokens, :], s.w_fc1[:, :, :, columns].reshape(D, 384))

            def gelu(rows, _):
                there = pl.ds(pl.multiple_of(rows.start + 256 * frame, ROWS), ROWS)
                hidden = s.other[rows, 0:384] + s.par_fc1[0:1, columns]
                normal = 0.5 + 0.5 * lax.erf(hidden * (1.0 / math.sqrt(2.0)))
                bell = jnp.exp(-0.5 * hidden * hidden) * (1.0 / math.sqrt(2.0 * math.pi))
                s.slope[there, columns] = normal + hidden * bell
                s.active[there, columns] = (hidden * normal).astype(BF16)
                return 0

            by_rows(gelu, 0)
            found = s.active[tokens, columns].T.reshape(4, 96, 256)
            s.active_t[pl.ds(8 * side + 4 * j, 4), :, 256 * frame : 256 * frame + 256] = found
            return 0

        lax.fori_loop(0, 2, body, 0)

    ours_rows = pl.ds(pl.multiple_of(128 * y, 128), 128)
    theirs_rows = pl.ds(pl.multiple_of(128 * (1 - y), 128), 128)
    across_y = 2 * (1 - y) + core
    valid, valid_across = frame_valid[blk].astype(F32), frame_valid[across_y].astype(F32)

    def mask_cotangent(frame):
        def body(rows, _):
            there = pl.ds(pl.multiple_of(rows.start + 256 * frame, ROWS), ROWS)
            masked = s.cot_in[there, :].astype(F32) * (valid_across if frame else valid)
            s.g_branch2[there, :] = masked.astype(BF16)
            return 0

        by_rows(body, 0)


    class Scatter(Steps):
        every = ALL

        def __init__(self, own, other, pr, dx, dy, px, py, pz, finish, low=2, line=DirectSum, more=None):
            self.own, self.other, self.finish = own, other, finish
            self.pr, self.dx, self.dy, self.px, self.py = pr, dx, dy, px, py
            self.line = line(lambda levels: own(levels, here), pz, more)
            self.square = Group()
            self.low, self.high = pl.ds(0, low), pl.ds(low, 4 - low)

        def s(self):
            self.pair = remote(self.other(), self.pr(ALL, self.every), sibling)

        def add_pair(self):
            self.pair.wait_recv()

            def add(level, _):
                ref = self.own(level, self.every)
                ref[...] = ref[...] + self.pr(level, self.every)[...]
                return 0

            lax.fori_loop(0, 4, add, 0)

        def p(self):
            self.add_pair()
            low, high = self.low, self.high
            self.a = remote(self.own(low, at_d), self.dx(low), x_peer)
            self.b = remote(self.own(high, at_d), self.dy(high), y_peer)
            remote(self.own(low, at_x), self.px(low), x_peer, self.square)
            remote(self.own(high, at_y), self.py(high), y_peer, self.square)

        def f(self):
            self.a.wait_recv()
            ref = self.own(self.low, at_y)
            ref[...] = ref[...] + self.dx(self.low)[...]
            remote(ref, self.py(self.low), y_peer, self.square)

        def g(self):
            self.b.wait_recv()
            ref = self.own(self.high, at_x)
            ref[...] = ref[...] + self.dy(self.high)[...]
            remote(ref, self.px(self.high), x_peer, self.square)

        def z(self):
            self.square.wait(self.own(ALL, BOTH))

            def add(level, _):
                ref = self.own(level, here)
                ref[...] = (
                    ref[...].astype(F32)
                    + self.px(level)[...].astype(F32)
                    + self.py(level)[...].astype(F32)
                ).astype(BF16)
                return 0

            lax.fori_loop(0, 4, add, 0)
            self.line.start()

        def l(self):
            self.line.wait()
            self.finish(self)

        def summed(self, view):
            return self.line.summed(view)

    class SquareScatter(Scatter):
        def __init__(self, own, other, pr, bz, pz, finish, line, more):
            self.own, self.other, self.finish = own, other, finish
            self.pr, self.pz, self.square = pr, pz, Group()
            self.line = line(lambda levels: own(levels, ALL), bz, more)

        def z(self):
            self.add_pair()
            self.line.start()

        def p(self):
            self.line.wait()
            if isinstance(self.line, DirectSum):
                self.own(z, ALL)[...] = self.line.summed(lambda ref: ref).astype(BF16)
            targets = ((at_x, x_peer), (at_y, y_peer), (at_d, d_peer))
            for i, (place, peer) in enumerate(targets):
                remote(self.own(z, place), self.pz(i), peer, self.square)

        def l(self):
            self.square.wait(self.pz(THREE))
            self.finish(self)

        def summed(self, view):
            found = view(self.own(z, here))[...].astype(F32)
            for i in range(3):
                found = found + view(self.pz(i))[...].astype(F32)
            return found

    class PlaneScatter(Scatter):
        def __init__(self, own, other, pr, px, pz, finish, line, more, across=None):
            self.own, self.other, self.finish, self.across = own, other, finish, across
            self.pr, self.px = pr, px
            self.line = line(lambda levels: own(levels, x), pz, more)

        def x(self):
            self.add_pair()
            self.x_copy = remote(self.own(ALL, 1 - x), self.px(ALL), x_peer)

        def z(self):
            self.x_copy.wait_recv()

            def add(level, _):
                ref = self.own(level, x)
                ref[...] = ref[...] + self.px(level)[...]
                return 0

            lax.fori_loop(0, 4, add, 0)
            self.line.start()

        def y(self):
            self.line.wait()
            source, target = self.across(self)
            self.y_copy = remote(source, target, y_peer)

        def l(self):
            if self.across:
                self.y_copy.wait_recv()
            else:
                self.line.wait()
            self.finish(self)

    class AcrossScatter(Scatter):
        def __init__(self, own, other, pr, bz, px, finish, line, more):
            self.own, self.other, self.finish = own, other, finish
            self.pr, self.px = pr, px
            self.line = line(lambda levels: own(levels, ALL), bz, more)

        def z(self):
            self.add_pair()
            self.line.start()

        def x(self):
            self.line.wait()
            if isinstance(self.line, DirectSum):
                self.own(z, ALL)[...] = self.line.summed(lambda ref: ref).astype(BF16)
            self.x_copy = remote(self.own(z, 1 - x), self.px(), x_peer)

        def l(self):
            self.x_copy.wait_recv()
            self.finish(self)

        def summed(self, view):
            return view(self.own(z, x))[...].astype(F32) + view(self.px())[...].astype(F32)

    def columns_of(ref, columns, size):
        def own(levels, places):
            return ref.at[levels, places, :, lanes(columns(core), size)]

        def other():
            return ref.at[:, :, :, lanes(columns(1 - core), size)]

        return own, other

    def column_scatter(ref, columns, size, spot, output, way, chained):
        at = pl.ds(spot, size)

        def finish(scatter):
            s.last_a[:, at] = scatter.summed(lambda ref: ref)
            target = lanes(columns(core), size)
            other_rows = pl.ds(pl.multiple_of(24 * (1 - core), 8), 24)
            finals.append(remote(s.last_a.at[other_rows, at], output.at[:, target], sibling))
            output[:, target] = s.last_a[own_rows, at]

        if not way:
            return SquareScatter(
                *columns_of(ref, columns, size),
                lambda levels, places: s.pr_a.at[levels, places, :, at],
                lambda i: s.bz_a.at[i, :, :, at],
                lambda i: s.pz_a.at[i, :, at],
                finish,
                LineSum if chained else DirectSum,
                lambda i: s.cz_a.at[i, :, :, at],
            )
        return Scatter(
            *columns_of(ref, columns, size),
            lambda levels, places: s.pr_a.at[levels, places, :, at],
            lambda levels: s.dx_a.at[levels, :, at],
            lambda levels: s.dx_a.at[levels, :, at],
            lambda levels: s.px_a.at[levels, :, at],
            lambda levels: s.py_a.at[levels, :, at],
            lambda i: s.pz_a.at[i, :, at],
            finish,
            way,
            LineSum if chained else DirectSum,
            lambda i: s.qz_a.at[i, :, at],
        )

    def fc1_scatter(j):
        at = slice(384 * j, 384 * j + 384)

        def own_columns(side):
            return lanes(768 * side + 384 * j, 384)

        def own(levels, side):
            places = ALL if side is ALL else pl.ds(2 * side, 2)
            return s.g_fc1.at[levels, places, :, own_columns(core)]

        def across(scatter):
            s.last_fc1[0, :, at] = scatter.summed(lambda ref: ref.at[y])
            s.send_fc1[:, at] = scatter.summed(lambda ref: ref.at[1 - y]).astype(BF16)
            return s.send_fc1.at[:, at], s.py_fc1.at[:, at]

        def finish(scatter):
            s.last_fc1[1, :, at] = s.py_fc1[:, at].astype(F32)
            other_rows = pl.ds(pl.multiple_of(24 * (1 - core), 8), 24)
            for i, half in enumerate((y, 1 - y)):
                target = lanes(1536 * half + 768 * core + 384 * j, 384)
                finals.append(remote(s.last_fc1.at[i, other_rows, at], grad_fc1.at[:, target], sibling))
                grad_fc1[:, target] = s.last_fc1[i, own_rows, at]

        return PlaneScatter(
            own,
            lambda: s.g_fc1.at[:, :, :, own_columns(1 - core)],
            lambda levels, places: s.pr_fc1.at[levels, places, :, at],
            lambda levels: s.px_fc1.at[levels, :, :, at],
            lambda i: s.pz_fc1.at[i, :, :, at],
            finish,
            LineSum if SCATTER_LINES["h"][j] else DirectSum,
            lambda i: s.qz_fc1.at[i, :, :, at],
            across,
        )

    def fc2_scatter(j, size, way):
        rows = pl.ds(size * j, size)
        half = lanes(384 * core, 384)

        def finish(scatter):
            s.last_fc2[rows, :] = scatter.summed(lambda ref: ref.at[1 - core])
            finals.append(remote(s.last_fc2.at[rows, :], grad_fc2.at[rows, half], sibling))
            grad_fc2[rows, half] = scatter.summed(lambda ref: ref.at[core])

        def sides(side):
            return BOTH if side is ALL else side

        own = lambda levels, side: s.g_fc2.at[levels, sides(side), :, rows, half]
        other = lambda: s.g_fc2.at[:, :, :, rows, lanes(384 * (1 - core), 384)]
        pr = lambda levels, side: s.pr_fc2.at[levels, sides(side), :, rows, :]
        if not way:
            bz = lambda i: s.bz_fc2.at[i, :, :, rows, :]
            line = LineSum if SCATTER_LINES["f"][j] else DirectSum
            more = lambda i: s.cz_fc2.at[i, :, :, rows, :]
            return AcrossScatter(own, other, pr, bz, lambda: s.pz_fc2.at[0, :, rows, :], finish, line, more)
        return PlaneScatter(
            own,
            other,
            pr,
            lambda levels: s.px_fc2.at[levels, :, rows, :],
            lambda i: s.pz_fc2.at[i, :, rows, :],
            finish,
            LineSum if SCATTER_LINES["f"][j] else DirectSum,
            lambda i: s.qz_fc2.at[i, :, rows, :],
        )

    def small_finish(scatter):
        found = scatter.summed(lambda ref: ref)
        grad_gain[...] = found[0:2, 0:24]
        grad_shift[...] = found[2:4, 0:24]
        grad_qv[...] = found[4:6, 0:24]
        grad_res[...] = found[6:8, 0:24]
        grad_fc1_bias[...] = found[8:9, 0:96]

    finals = []
    scatters = {}
    for j, way in enumerate(SCATTER_WAYS["f"]):
        scatters["f" + str(j)] = fc2_scatter(j, 96 // len(SCATTER_WAYS["f"]), way)
    for j in range(2):
        scatters["h" + str(j)] = fc1_scatter(j)
    scatters["o0"] = column_scatter(s.g_out, lambda side: 384 * side, 384, 0, grad_out, SCATTER_WAYS["o"][0], SCATTER_LINES["o"][0])
    for j in range(3):
        scatters["q" + str(j)] = column_scatter(
            s.g_qkv, partial(tile, j), 384, 384 + 384 * j, grad_qkv, SCATTER_WAYS["q"][j], SCATTER_LINES["q"][j]
        )
    scatters["s0"] = Scatter(
        *columns_of(s.g_small, lambda side: 128 * side, 128),
        lambda levels, places: s.pr_small.at[levels, places],
        lambda levels: s.dx_small.at[levels],
        lambda levels: s.dx_small.at[levels],
        lambda levels: s.px_small.at[levels],
        lambda levels: s.py_small.at[levels],
        lambda i: s.pz_small.at[i],
        small_finish,
    )

    def weight_grad_fc2(j):
        size = 96 // len(SCATTER_WAYS["f"])
        rows = pl.ds(size * j, size)

        def body(turn, _):
            columns = lanes(384 * (turn * core + (1 - turn) * (1 - core)), 384)
            found = dot(s.active_t[:, rows, :].reshape(16 * size, 512), s.g_branch2[:, columns])
            s.g_fc2[:, :, :, rows, columns] = found.astype(BF16).reshape(4, 2, 2, size, 384)
            return 0

        lax.fori_loop(0, 2, body, 0)

    def column_grad(left, right, ref, columns):
        def body(turn, _):
            at = lanes(columns(turn * core + (1 - turn) * (1 - core)), 384)
            ref[:, :, :, at] = dot(left[...], right[:, at]).astype(BF16).reshape(4, 4, 48, 384)
            return 0

        lax.fori_loop(0, 2, body, 0)

    def feed_back(frame):
        tokens = pl.ds(256 * frame, 256)

        def body(part, _):
            columns = lanes(D * part, D)
            s.other[...] = dot_nt(s.g_branch2[tokens, :], s.w_fc2[pl.ds(2 * part, 2)].reshape(D, D))

            def slope(rows, sums):
                there = pl.ds(pl.multiple_of(rows.start + 256 * frame, ROWS), ROWS)
                found = (s.other[rows, :] * s.slope[there, columns]).astype(BF16)
                s.g_hidden[there, columns] = found
                return sums + jnp.sum(found.astype(F32), axis=0, keepdims=True)

            s.sums_fc1[frame : frame + 1, columns] = by_rows(slope, jnp.zeros((1, D), F32))
            return 0

        lax.fori_loop(0, 2, body, 0)

    def feed_out(frame):
        tokens = pl.ds(256 * frame, 256)
        s.total[...] = jnp.zeros((TOKENS, D), F32)

        def body(part, _):
            weight = s.w_fc2[pl.ds(2 * part, 2)].reshape(D, D)
            s.total[...] += dot(s.active[tokens, lanes(D * part, D)], weight)
            return 0

        lax.fori_loop(0, 2, body, 0)
        if frame:
            s.part_across[...] = s.total[...].astype(BF16)
        else:

            def add(rows, _):
                s.total[rows, :] = s.middle[rows, :] + (s.total[rows, :] + s.par[7:8, :])
                return 0

            by_rows(add, 0)
            s.base_send[...] = (valid * s.total[theirs_rows, :]).astype(BF16)

    def output():
        s.enc_send[0] = (valid * (s.total[ours_rows, :] + s.part_recv[...].astype(F32))).astype(BF16)
        part = valid_across * s.part_across[ours_rows, :].astype(F32)
        s.enc_send[1] = (s.base_recv[...].astype(F32) + part).astype(BF16)

        def body(rows, sums):
            return sums + jnp.sum(s.g_branch2[rows, :].astype(F32), axis=0, keepdims=True)

        s.sums[7:8, :] = by_rows(body, jnp.zeros((1, D), F32))

    def feed_back_rows(frame):
        tokens = pl.ds(256 * frame, 256)
        s.other[...] = jnp.zeros((TOKENS, D), F32)

        def body(part, _):
            columns = lanes(D * part, D)
            s.other[...] += dot_nt(s.g_hidden[tokens, columns], s.w_fc1[:, :, :, columns].reshape(D, D))
            return 0

        lax.fori_loop(0, 2, body, 0)
        if frame:
            s.back_send[...] = s.other[...].astype(BF16)

    def norm_back(upstream, found, scale, gain):
        weighted = upstream * gain
        return scale * (
            weighted
            - jnp.mean(weighted, axis=-1, keepdims=True)
            - found * jnp.mean(weighted * found, axis=-1, keepdims=True)
        )

    def column_sum(values):
        return jnp.sum(values, axis=0, keepdims=True)

    def second_norm_back():
        def rows_back(rows, sums):
            upstream = s.other[rows, :] + s.back_recv[rows, :].astype(F32)
            found, scale = standardized(s.middle[rows, :])
            middle = s.g_branch2[rows, :].astype(F32) + norm_back(upstream, found, scale, s.par[1:2, :])
            s.g_middle[rows, :] = middle
            branch = middle.astype(BF16)
            s.g_branch[rows, :] = branch
            return (
                sums[0] + column_sum(upstream * found),
                sums[1] + column_sum(upstream),
                sums[2] + column_sum(branch.astype(F32)),
            )

        empty = jnp.zeros((1, D), F32)
        s.sums[1:2, :], s.sums[3:4, :], s.sums[6:7, :] = by_rows(rows_back, (empty, empty, empty))

    def attend_back(part):
        def body(two, _):
            spots = [lanes(128 * two + part, 128) for part in (0, D, 2 * D)]
            query, key, value = (s.mixed[:, spot] for spot in spots)
            upstream = s.g_attended[:, spots[0]]
            g_query, g_key, g_value = (jnp.zeros((TOKENS, 128), F32) for _ in range(3))
            for mask in head_masks():
                probs = softmax(dot_nt(query * mask, key))
                g_probs = dot_nt(upstream * mask, value)
                g_value = g_value + dot_tn(probs.astype(BF16), upstream * mask)
                inner = jnp.sum(probs * g_probs, axis=-1, keepdims=True)
                g_scores = (probs * (g_probs - inner)).astype(BF16)
                g_query = g_query + dot(g_scores, key * mask)
                g_key = g_key + dot_tn(g_scores, query * mask)
            g_query = 0.125 * g_query.astype(BF16).astype(F32)
            g_value = g_value.astype(BF16)
            s.g_mixed[:, spots[0]] = g_query.astype(BF16)
            s.g_mixed[:, spots[1]] = g_key.astype(BF16)
            s.g_mixed[:, spots[2]] = g_value
            s.sums[4:5, spots[0]] = column_sum(g_query)
            s.sums[5:6, spots[0]] = column_sum(g_value.astype(F32))
            return 0

        lax.fori_loop(3 * part, 3 * part + 3, body, 0)

    def first_norm_back():
        s.total[...] = jnp.zeros((TOKENS, D), F32)

        def body(level, _):
            columns = lanes(D * level, D)
            s.total[...] += dot_nt(s.g_mixed[:, columns], s.w_qkv[:, :, :, columns].reshape(D, D))
            return 0

        lax.fori_loop(0, 3, body, 0)

        def rows_back(rows, sums):
            upstream = s.total[rows, :]
            found, scale = standardized(s.rows_in[rows, :].astype(F32))
            result = s.g_middle[rows, :] + norm_back(upstream, found, scale, s.par[0:1, :])
            s.gx_send[rows, :] = result.astype(BF16)
            return (sums[0] + column_sum(upstream * found), sums[1] + column_sum(upstream))

        empty = jnp.zeros((1, D), F32)
        s.sums[0:1, :], s.sums[2:3, :] = by_rows(rows_back, (empty, empty))

    def pack_small():
        chips = lax.shift_right_logical(over((256, D), 0), 4)
        pieces = piece24(over((256, D), 1))
        spread = spread24()
        rows = jnp.broadcast_to(s.sums[...][None], (16, 16, D)).reshape(256, D)
        for side in (0, 1):
            placed = dot_nt(jnp.where(pieces == 2 * chips + side, rows, 0.0).astype(BF16), spread)
            s.g_small[:, :, :, 128 * side : 128 * side + 128] = placed.astype(BF16).reshape(4, 4, 16, 128)
        put = (over((256, 16), 0) == 16 * over((256, 16), 1) + 8).astype(F32).astype(BF16)
        spread = spread96()
        shape = (16, FF // 2)
        pieces = piece96(hidden_unit(over(shape, 1)))
        row = s.sums_fc1[0:1, :] + s.sums_fc1[1:2, :]
        for side in (0, 1):
            mine = pieces == 2 * over(shape, 0) + side
            placed = dot_nt(jnp.where(mine, row, 0.0).astype(BF16), spread).astype(BF16)
            here_ = s.g_small.at[:, :, :, pl.ds(128 * side, 128)]
            here_[...] = here_[...] + dot(put, placed).astype(BF16).reshape(4, 4, 16, 128)

    moved = {"rows": (rows_moved, s.rows_in.at[0:192, :])}

    def send_cotangent(frame):
        group, there = Group(), pl.ds(pl.multiple_of(64 * blk + 256 * frame, 64), 64)
        for py, pc in blk_peers:
            source = cotangent.at[2 * (1 - py if frame else py) + pc]
            remote(source, s.cot_in.at[there, :], (wide, 2 * py + pc), group)
        moved["cot" + str(frame)] = group, s.cot_in.at[256 * frame : 256 * frame + 192, :]
        s.cot_in[there, :] = cotangent[across_y if frame else blk]

    def received(name):
        group, ref = moved.pop(name)
        group.wait(ref)

    def start_norm():
        received("rows")
        first_norm()

    def start_cotangent(frame):
        received("cot" + str(frame))
        mask_cotangent(frame)

    def send_encoded():
        ours = pl.ds(pl.multiple_of(64 * core, 64), 64)
        theirs = pl.ds(pl.multiple_of(64 * (1 - core), 64), 64)
        group = Group()
        for i, frame in enumerate((blk, across_y)):
            remote(s.enc_send.at[i, theirs, :], encoded.at[frame], sibling, group)
        moved["enc"] = group, encoded.at[BOTH]
        encoded[blk] = s.enc_send[0, ours, :]
        encoded[across_y] = s.enc_send[1, ours, :]

    def send_grad_rows():
        group = Group()
        for py, pc in blk_peers:
            rows = pl.ds(pl.multiple_of(64 * (2 * py + pc), 64), 64)
            remote(s.gx_send.at[rows, :], s.gx_recv.at[blk], (wide, 2 * py + pc), group)
        moved["grad"] = group, s.gx_recv.at[THREE]
        s.gx_recv[blk] = s.gx_send[mine, :]

    def project_attended():
        s.g_attended[...] = dot_nt(s.g_branch[...], s.w_out[...].reshape(D, D)).astype(BF16)

    def project_both(j):
        project_qkv(tile(j, 0))
        project_qkv(tile(j, 1))

    def across(name, source, target):
        moved[name] = Group(), target
        remote(source, target, y_peer, moved[name][0])

    def send_normed():
        across("normed", s.normed2.at[0:256, :], s.normed2.at[256:512, :])

    def take_normed():
        received("normed")

    def transpose_other():
        s.normed2_t[:, 256:512] = s.normed2[256:512, :].T

    def send_part():
        across("part", s.part_across.at[theirs_rows, :], s.part_recv)

    def send_base():
        across("base", s.base_send, s.base_recv)

    def start_output():
        received("part")
        received("base")
        output()

    def send_back():
        across("back", s.back_send, s.back_recv)

    def start_second():
        received("back")
        second_norm_back()

    def grad_fc1_weight(j):
        column_grad(s.normed2_t, s.g_hidden, s.g_fc1, lambda side: 768 * side + 384 * j)

    def grad_out_weight():
        column_grad(s.attended_t, s.g_branch, s.g_out, lambda side: 384 * side)

    def grad_qkv_weight(j):
        column_grad(s.normed_t, s.g_mixed, s.g_qkv, partial(tile, j))

    g, r = types.SimpleNamespace(**gathers), types.SimpleNamespace(**scatters)
    g.s0.z()
    g.q2.z()
    g.q1.z()
    g.q2.o()
    g.q0.z()
    g.o0.z()
    g.h0.y()
    g.q0.o()
    g.f2.x()
    g.f1.x()
    g.s0.p()
    g.q1.o()
    g.o0.o()
    g.q2.p()
    g.h0.z()
    g.s0.f()
    g.h1.y()
    g.s0.g()
    g.q1.p()
    g.q2.f()
    g.q2.g()
    g.h1.z()
    g.q0.p()
    g.o0.p()
    g.s0.l()
    g.q1.f()
    g.h0.w()
    g.q2.l()
    g.s0.d()
    g.q1.g()
    unpack_small()
    g.h1.w()
    g.q0.f()
    g.q0.g()
    g.h0.v()
    g.o0.f()
    start_norm()
    g.f0.z()
    g.o0.g()
    send_cotangent(1)
    g.h1.v()
    g.f1.z()
    g.q1.l()
    send_cotangent(0)
    g.q2.d()
    project_both(2)
    g.f2.z()
    g.q1.d()
    g.q0.l()
    g.h0.x()
    project_both(1)
    g.f0.w()
    g.q0.d()
    project_both(0)
    attend(0)
    g.o0.l()
    attend(1)
    g.o0.d()
    g.f2.w()
    g.h1.x()
    project_out()
    send_normed()
    g.f0.v()
    g.f1.w()
    start_cotangent(0)
    g.h0.l()
    g.f2.v()
    start_cotangent(1)
    g.h0.d()
    transpose_out()
    g.f1.v()
    g.f0.x()
    feed(0, 0)
    g.h1.l()
    g.f2.l()
    g.h1.d()
    feed(1, 0)
    g.f1.l()
    take_normed()
    feed(0, 1)
    feed(1, 1)
    g.f0.l()
    weight_grad_fc2(2)
    g.f2.d()
    weight_grad_fc2(0)
    g.f0.d()
    r.f0.s()
    r.f2.s()
    g.f1.d()
    feed_back(1)
    feed_back_rows(1)
    send_back()
    r.f0.z()
    transpose_other()
    r.f2.x()
    feed_back(0)
    grad_fc1_weight(0)
    r.h0.s()
    grad_fc1_weight(1)
    r.h0.x()
    feed_out(1)
    r.h1.s()
    weight_grad_fc2(1)
    send_part()
    r.f2.z()
    r.f1.s()
    feed_out(0)
    r.h1.x()
    feed_back_rows(0)
    r.f1.z()
    send_base()
    r.f0.w()
    start_second()
    grad_out_weight()
    project_attended()
    r.o0.s()
    attend_back(0)
    r.h0.z()
    r.o0.p()
    grad_qkv_weight(0)
    r.q0.s()
    r.f2.w()
    r.f1.w()
    r.h1.z()
    r.q0.p()
    attend_back(1)
    r.o0.f()
    r.o0.g()
    grad_qkv_weight(2)
    r.q2.s()
    r.h0.w()
    r.q0.f()
    r.q0.g()
    r.f0.v()
    grad_qkv_weight(1)
    r.f2.v()
    r.q1.s()
    r.q2.p()
    start_output()
    r.f1.v()
    r.o0.z()
    r.q1.p()
    r.h1.w()
    first_norm_back()
    r.h0.v()
    pack_small()
    r.q2.f()
    r.s0.s()
    r.q2.g()
    r.q0.z()
    r.q1.f()
    r.f2.l()
    r.s0.p()
    r.f1.x()
    r.q1.g()
    send_encoded()
    r.f0.x()
    r.h0.y()
    r.h1.v()
    r.q2.z()
    r.s0.f()
    send_grad_rows()
    r.h0.l()
    r.q1.z()
    r.s0.g()
    r.h1.y()
    r.q0.l()
    r.o0.l()
    r.q2.l()
    r.s0.z()
    r.f0.l()
    r.h1.l()
    r.f1.l()
    r.q1.l()
    r.s0.l()
    for name in list(moved):
        received(name)
    for copy in finals:
        copy.wait_recv()
    grad_patches[...] = s.gx_recv[...].astype(F32)
    for spot in range(max(0, len(started) - SENDS), len(started)):
        leave(spot)


def emit_kernel(*refs):
    count = (len(refs) - 3) // 3
    given, made, held = refs[:count], refs[count : 2 * count], refs[2 * count : 3 * count]
    ordered, in_sem, out_sem = refs[3 * count :]
    arrive = [pltpu.make_async_copy(given[i], held[i], in_sem.at[i]) for i in range(count)]
    leave = [
        pltpu.make_async_copy(ordered if i == FC1_OUTPUT else held[i], made[i], out_sem.at[i]) for i in range(count)
    ]
    for copy in arrive:
        copy.start()
    for i in range(count):
        arrive[i].wait()
        if i == FC1_OUTPUT:
            for side in (0, 1):
                for k in range(8):
                    source = held[i][:, 1536 * side + 192 * k : 1536 * side + 192 * k + 192]
                    ordered[:, 384 * k + 192 * side : 384 * k + 192 * side + 192] = source
        leave[i].start()
    for copy in leave:
        copy.wait()


def emit(arrays):
    anywhere = pl.BlockSpec(memory_space=pl.ANY)
    count = len(arrays)
    return list(
        pl.pallas_call(
            emit_kernel,
            out_shape=[jax.ShapeDtypeStruct(a.shape, a.dtype) for a in arrays],
            in_specs=[anywhere] * count,
            out_specs=[anywhere] * count,
            scratch_shapes=[pltpu.VMEM(a.shape, a.dtype) for a in arrays]
            + [pltpu.VMEM(arrays[FC1_OUTPUT].shape, F32)]
            + [pltpu.SemaphoreType.DMA((count,))] * 2,
        )(*arrays)
    )


def fast(
    patches,
    norm_gain,
    norm_bias,
    qkv_weight,
    qv_bias,
    out_weight,
    fc1_weight,
    fc1_bias,
    fc2_weight,
    res_bias,
    cotangent,
    frame_valid,
):
    outputs = [
        ((4, 64, D), BF16),
        ((4, 64, D), F32),
        ((2, 24), F32),
        ((2, 24), F32),
        ((24, 3 * D), F32),
        ((2, 24), F32),
        ((24, D), F32),
        ((24, FF), F32),
        ((1, 96), F32),
        ((96, D), F32),
        ((2, 24), F32),
    ]
    vmem = pl.BlockSpec(memory_space=pltpu.VMEM)
    found = list(pl.pallas_call(
        layer_kernel,
        out_shape=[jax.ShapeDtypeStruct(shape, dtype) for shape, dtype in outputs],
        in_specs=[vmem] * 11 + [pl.BlockSpec(memory_space=pltpu.SMEM)],
        out_specs=[vmem] * len(outputs),
        scratch_shapes=list(scratch_shapes().values()),
        compiler_params=pltpu.CompilerParams(
            collective_id=0, has_side_effects=True, vmem_limit_bytes=63 * 2**20
        ),
    )(
        patches,
        norm_gain,
        norm_bias,
        qkv_weight,
        qv_bias,
        out_weight,
        fc1_weight,
        fc1_bias.reshape(1, 96),
        fc2_weight,
        res_bias,
        cotangent,
        frame_valid,
    ))
    found = emit(found)
    found[8] = found[8].reshape(96)
    return tuple(found)


def solution(mesh):
    in_specs = (
        P("wide", "blk", None),
        P(None, ("wide", "blk")),
        P(None, ("wide", "blk")),
        P(("wide", "blk"), None),
        P(None, ("wide", "blk")),
        P(("wide", "blk"), None),
        P(("wide", "blk"), None),
        P(("wide", "blk")),
        P(("wide", "blk"), None),
        P(None, ("wide", "blk")),
        P("wide", "blk", None),
        P("wide"),
    )
    out_specs = (
        P("wide", "blk", None),
        P("wide", "blk", None),
        P(None, ("wide", "blk")),
        P(None, ("wide", "blk")),
        P(("wide", "blk"), None),
        P(None, ("wide", "blk")),
        P(("wide", "blk"), None),
        P(("wide", "blk"), None),
        P(("wide", "blk")),
        P(("wide", "blk"), None),
        P(None, ("wide", "blk")),
    )
    body = fast if dict(mesh.shape) == {"wide": 8, "blk": 4} else local
    return jax.shard_map(body, mesh=mesh, in_specs=in_specs, out_specs=out_specs, check_vma=False)
```

```python
from functools import partial
import math
import types

import jax
import jax.numpy as jnp
from jax import lax
from jax.experimental import pallas as pl
from jax.experimental.pallas import tpu as pltpu
from jax.sharding import PartitionSpec as P

D = 768
HEADS = 12
HEAD = 64


EPSILON = 1e-06


def layer_normalize(token_rows, norm_gain_vector, norm_bias_vector):
    row_average = jnp.mean(token_rows, axis=-1, keepdims=True)
    centered_rows = token_rows - row_average
    inverse_deviation_scale = lax.rsqrt(
        jnp.mean(centered_rows * centered_rows, axis=-1, keepdims=True) + EPSILON
    )
    standardized_rows = centered_rows * inverse_deviation_scale
    return (
        standardized_rows * norm_gain_vector + norm_bias_vector,
        standardized_rows,
        inverse_deviation_scale,
    )


def layer_normalize_backward(
    incoming_gradient, standardized_rows, inverse_deviation_scale, norm_gain_vector
):
    gain_weighted_gradient = incoming_gradient * norm_gain_vector
    inner_product_sum = (
        gain_weighted_gradient
        - jnp.mean(gain_weighted_gradient, axis=-1, keepdims=True)
        - standardized_rows
        * jnp.mean(gain_weighted_gradient * standardized_rows, axis=-1, keepdims=True)
    )
    return (
        inverse_deviation_scale * inner_product_sum,
        jnp.sum(incoming_gradient * standardized_rows, axis=0),
        jnp.sum(incoming_gradient, axis=0),
    )


def frame_groups(array, count):
    return array.reshape((array.shape[0] // count, count) + array.shape[1:])


def attend_forward(query, keys, values):
    scores = jnp.einsum("gqhe,gkhe->ghqk", query, keys, preferred_element_type=jnp.float32)
    top = jnp.max(scores, axis=-1, keepdims=True)
    expo = jnp.exp(scores - top)
    total = jnp.sum(expo, axis=-1, keepdims=True)
    probs = (expo / total).astype(jnp.bfloat16)
    attended = jnp.einsum("ghqk,gkhe->gqhe", probs, values, preferred_element_type=jnp.float32)
    return (attended, top + jnp.log(total))


def attend_back(query, keys, values, logsum, grad_out):
    scores = jnp.einsum("gqhe,gkhe->ghqk", query, keys, preferred_element_type=jnp.float32)
    probs = jnp.exp(scores - logsum)
    grad_probs = jnp.einsum("gqhe,gkhe->ghqk", grad_out, values, preferred_element_type=jnp.float32)
    grad_values = jnp.einsum(
        "ghqk,gqhe->gkhe", probs.astype(jnp.bfloat16), grad_out, preferred_element_type=jnp.float32
    )
    grad_scores = (
        probs * (grad_probs - jnp.sum(probs * grad_probs, axis=-1, keepdims=True))
    ).astype(jnp.bfloat16)
    grad_query = jnp.einsum(
        "ghqk,gkhe->gqhe", grad_scores, keys, preferred_element_type=jnp.float32
    )
    grad_keys = jnp.einsum(
        "ghqk,gqhe->gkhe", grad_scores, query, preferred_element_type=jnp.float32
    )
    return (grad_query, grad_keys, grad_values)


def local(
    patches,
    norm_gain,
    norm_bias,
    qkv_weight,
    qv_bias,
    out_weight,
    fc1_weight,
    fc1_bias,
    fc2_weight,
    res_bias,
    cotangent,
    frame_valid,
):
    frames, frame_rows, width = patches.shape
    count = frames * frame_rows
    group = math.gcd(frames, 8)
    params = (
        lax.all_gather(norm_gain, ("wide", "blk"), axis=1, tiled=True),
        lax.all_gather(norm_bias, ("wide", "blk"), axis=1, tiled=True),
        lax.all_gather(qkv_weight, ("wide", "blk"), axis=0, tiled=True),
        lax.all_gather(qv_bias, ("wide", "blk"), axis=1, tiled=True),
        lax.all_gather(out_weight, ("wide", "blk"), axis=0, tiled=True),
        lax.all_gather(fc1_weight, ("wide", "blk"), axis=0, tiled=True),
        lax.all_gather(fc1_bias, ("wide", "blk"), axis=0, tiled=True),
        lax.all_gather(fc2_weight, ("wide", "blk"), axis=0, tiled=True),
        lax.all_gather(res_bias, ("wide", "blk"), axis=1, tiled=True),
    )
    norm_gain_pair = params[0].astype(jnp.float32)
    norm_bias_pair = params[1].astype(jnp.float32)
    biases_qv = params[3].astype(jnp.float32)
    bias_fc1 = params[6].astype(jnp.float32)
    biases_res = params[8].astype(jnp.float32)
    token_rows = patches.reshape(count, width).astype(jnp.float32)
    valid = jnp.repeat(frame_valid.astype(jnp.float32), frame_rows)[:, None]
    first_branch, first_standardized_rows, first_norm_scale = layer_normalize(
        token_rows, norm_gain_pair[0], norm_bias_pair[0]
    )
    normed = first_branch.astype(jnp.bfloat16)
    mixed = jnp.dot(normed, params[2], preferred_element_type=jnp.float32)
    query = ((mixed[:, :D] + biases_qv[0]) * 0.125).astype(jnp.bfloat16)
    keys = mixed[:, D : 2 * D].astype(jnp.bfloat16).reshape(frames, frame_rows, width)
    values = (
        (mixed[:, 2 * D :] + biases_qv[1]).astype(jnp.bfloat16).reshape(frames, frame_rows, width)
    )
    keys_all, values_all = (
        lax.all_gather(keys, "blk", axis=1, tiled=True),
        lax.all_gather(values, "blk", axis=1, tiled=True),
    )
    query_heads = frame_groups(query.reshape(frames, frame_rows, HEADS, HEAD), group)
    keys_heads = frame_groups(keys_all.reshape(frames, -1, HEADS, HEAD), group)
    values_heads = frame_groups(values_all.reshape(frames, -1, HEADS, HEAD), group)
    attended, logsum = lax.map(
        lambda item: attend_forward(item[0], item[1], item[2]),
        (query_heads, keys_heads, values_heads),
    )
    attended = attended.reshape(count, width).astype(jnp.bfloat16)
    middle_activation = (
        token_rows
        + jnp.dot(attended, params[4], preferred_element_type=jnp.float32)
        + biases_res[0]
    )
    second_branch, second_standardized_rows, second_norm_scale = layer_normalize(
        middle_activation, norm_gain_pair[1], norm_bias_pair[1]
    )
    normed2 = second_branch.astype(jnp.bfloat16)
    hidden = jnp.dot(normed2, params[5], preferred_element_type=jnp.float32) + bias_fc1
    active = jax.nn.gelu(hidden, approximate=False).astype(jnp.bfloat16)
    branch2 = jnp.dot(active, params[7], preferred_element_type=jnp.float32) + biases_res[1]
    encoded = (
        ((middle_activation + branch2) * valid)
        .astype(jnp.bfloat16)
        .reshape(frames, frame_rows, width)
    )
    params = (
        lax.all_gather(norm_gain, ("wide", "blk"), axis=1, tiled=True),
        lax.all_gather(norm_bias, ("wide", "blk"), axis=1, tiled=True),
        lax.all_gather(qkv_weight, ("wide", "blk"), axis=0, tiled=True),
        lax.all_gather(qv_bias, ("wide", "blk"), axis=1, tiled=True),
        lax.all_gather(out_weight, ("wide", "blk"), axis=0, tiled=True),
        lax.all_gather(fc1_weight, ("wide", "blk"), axis=0, tiled=True),
        lax.all_gather(fc1_bias, ("wide", "blk"), axis=0, tiled=True),
        lax.all_gather(fc2_weight, ("wide", "blk"), axis=0, tiled=True),
        lax.all_gather(res_bias, ("wide", "blk"), axis=1, tiled=True),
    )
    grad_out = cotangent.reshape(count, width).astype(jnp.float32) * valid
    grad_branch2 = grad_out.astype(jnp.bfloat16)
    grad_fc2 = jnp.dot(active.T, grad_branch2, preferred_element_type=jnp.float32)
    grad_res_two = jnp.sum(grad_branch2.astype(jnp.float32), axis=0)
    grad_active = jnp.dot(grad_branch2, params[7].T, preferred_element_type=jnp.float32)
    gelu_back = jax.vjp(partial(jax.nn.gelu, approximate=False), hidden)[1]
    grad_hidden = gelu_back(grad_active)[0].astype(jnp.bfloat16)
    grad_fc1 = jnp.dot(normed2.T, grad_hidden, preferred_element_type=jnp.float32)
    grad_bias_fc1 = jnp.sum(grad_hidden.astype(jnp.float32), axis=0)
    normed_input_gradient2 = jnp.dot(grad_hidden, params[5].T, preferred_element_type=jnp.float32)
    second_norm_gradient, second_norm_gain, second_norm_bias = layer_normalize_backward(
        normed_input_gradient2, second_standardized_rows, second_norm_scale, norm_gain_pair[1]
    )
    grad_middle = grad_out + second_norm_gradient
    grad_branch = grad_middle.astype(jnp.bfloat16)
    grad_out_proj = jnp.dot(attended.T, grad_branch, preferred_element_type=jnp.float32)
    grad_res_one = jnp.sum(grad_branch.astype(jnp.float32), axis=0)
    grad_attended = jnp.dot(grad_branch, params[4].T, preferred_element_type=jnp.float32).astype(
        jnp.bfloat16
    )
    grad_heads = frame_groups(grad_attended.reshape(frames, frame_rows, HEADS, HEAD), group)
    grad_query, grad_keys, grad_values = lax.map(
        lambda item: attend_back(item[0], item[1], item[2], item[3], item[4]),
        (query_heads, keys_heads, values_heads, logsum, grad_heads),
    )
    grad_keys, grad_values = (
        lax.psum_scatter(
            grad_keys.reshape(frames, -1, width).astype(jnp.bfloat16),
            "blk",
            scatter_dimension=1,
            tiled=True,
        ).astype(jnp.float32),
        lax.psum_scatter(
            grad_values.reshape(frames, -1, width).astype(jnp.bfloat16),
            "blk",
            scatter_dimension=1,
            tiled=True,
        ).astype(jnp.float32),
    )
    grad_query = grad_query.reshape(count, width).astype(jnp.bfloat16) * 0.125
    grad_keys = grad_keys.reshape(count, width).astype(jnp.bfloat16)
    grad_values = grad_values.reshape(count, width).astype(jnp.bfloat16)
    grad_mixed = jnp.concatenate([grad_query, grad_keys, grad_values], axis=1)
    grad_qkv = jnp.dot(normed.T, grad_mixed, preferred_element_type=jnp.float32)
    grad_qv = jnp.stack(
        [
            jnp.sum(grad_query.astype(jnp.float32), axis=0),
            jnp.sum(grad_values.astype(jnp.float32), axis=0),
        ]
    )
    normed_input_gradient = jnp.dot(grad_mixed, params[2].T, preferred_element_type=jnp.float32)
    first_norm_gradient, first_norm_gain, first_norm_bias = layer_normalize_backward(
        normed_input_gradient, first_standardized_rows, first_norm_scale, norm_gain_pair[0]
    )
    grad_rows = (grad_middle + first_norm_gradient).reshape(frames, frame_rows, width)
    grad_gain = jnp.stack([first_norm_gain, second_norm_gain])
    grad_shift = jnp.stack([first_norm_bias, second_norm_bias])
    grad_res = jnp.stack([grad_res_one, grad_res_two])
    summed = (
        lax.psum_scatter(grad_gain, ("wide", "blk"), scatter_dimension=1, tiled=True),
        lax.psum_scatter(grad_shift, ("wide", "blk"), scatter_dimension=1, tiled=True),
        lax.psum_scatter(grad_qkv, ("wide", "blk"), scatter_dimension=0, tiled=True),
        lax.psum_scatter(grad_qv, ("wide", "blk"), scatter_dimension=1, tiled=True),
        lax.psum_scatter(grad_out_proj, ("wide", "blk"), scatter_dimension=0, tiled=True),
        lax.psum_scatter(grad_fc1, ("wide", "blk"), scatter_dimension=0, tiled=True),
        lax.psum_scatter(grad_bias_fc1, ("wide", "blk"), scatter_dimension=0, tiled=True),
        lax.psum_scatter(grad_fc2, ("wide", "blk"), scatter_dimension=0, tiled=True),
        lax.psum_scatter(grad_res, ("wide", "blk"), scatter_dimension=1, tiled=True),
    )
    return (
        encoded,
        grad_rows,
        summed[0],
        summed[1],
        summed[2],
        summed[3],
        summed[4],
        summed[5],
        summed[6],
        summed[7],
        summed[8],
    )


MESH_ID = pl.DeviceIdType.MESH
BF16 = jnp.bfloat16
F32 = jnp.float32
FF = 3072
TOKENS = 256
ROWS = 64
ALL, THREE, BOTH = pl.ds(0, 4), pl.ds(0, 3), pl.ds(0, 2)
GATHER_UNITS = (
    ("q0", 0, 0, 3, -1, 0),
    ("q1", 1, 0, 3, -2, 0),
    ("q2", 2, 0, 3, -2, 0),
    ("o0", 3, 0, 3, -1, 0),
)
SCATTER_UNITS = (
    ("o0", 3, 0, 3, 2, 0),
    ("q0", 0, 0, 3, 2, 0),
    ("q1", 1, 0, 3, 2, 0),
    ("q2", 2, 0, 3, 2, 0),
)
GATHER_FC2, SCATTER_FC2 = (1, 0, 0), (0, 0, 1)
GATHER_LINES = dict(h=(1, 1), f=(1, 1, 1))
SCATTER_LINES = dict(h=(1, 1), f=(1, 1, 1))


PIECES = (((0, 12, 7), (6, 1, 13)), ((2, 14, 9), (8, 3, 15)), ((4, 16, 11), (10, 5, 17)))


def piece(j, side, t):
    first, second = PIECES[j][0][t], PIECES[j][1][t]
    return 128 * (first + side * (second - first))


def pair_places(j, i):
    return 768 * j + 512 * i, 768 * j + 384 - 128 * i, 768 * j + 128 + 512 * i


def dot(left, right):
    return lax.dot_general(left, right, (((1,), (0,)), ((), ())), preferred_element_type=F32)


def dot_nt(left, right):
    return lax.dot_general(left, right, (((1,), (1,)), ((), ())), preferred_element_type=F32)


def dot_tn(left, right):
    return lax.dot_general(left, right, (((0,), (0,)), ((), ())), preferred_element_type=F32)


SENDS, ARRIVALS, KEPT = 48, 143, 28
FC1_OUTPUT = 7


def scratch_shapes():
    def vm(*shape, dtype=BF16):
        return pltpu.VMEM(shape, dtype)

    return dict(
        w_small=vm(4, 4, 16, 256),
        w_qkv=vm(4, 4, 48, 2304),
        w_out=vm(4, 4, 48, 768),
        w_fc1=vm(4, 4, 48, 1536),
        w_fc2=vm(4, 2, 2, 96, 768),
        fc1_other=vm(48, 768),
        own_small=vm(16, 128, dtype=F32),
        pair_rows=vm(48, 1536, dtype=F32),
        pair_send=vm(24, 1536, dtype=F32),
        pair_rows_h=vm(48, 1536, dtype=F32),
        pair_send_h=vm(24, 1536, dtype=F32),
        par=vm(16, 768, dtype=F32),
        par_fc1=vm(8, 1536, dtype=F32),
        rows_in=vm(256, 768),
        cot_in=vm(512, 768),
        normed=vm(256, 768),
        normed_t=vm(768, 256),
        mixed=vm(256, 2304),
        attended=vm(256, 768),
        attended_t=vm(768, 256),
        middle=vm(256, 768, dtype=F32),
        normed2=vm(512, 768),
        normed2_t=vm(768, 512),
        slope=vm(512, 1536, dtype=F32),
        active=vm(512, 1536),
        g_hidden=vm(512, 1536),
        active_t=vm(16, 96, 512),
        g_branch2=vm(512, 768),
        part_across=vm(256, 768),
        part_recv=vm(128, 768),
        base_send=vm(128, 768),
        base_recv=vm(128, 768),
        back_send=vm(256, 768),
        back_recv=vm(256, 768),
        other=vm(256, 768, dtype=F32),
        total=vm(256, 768, dtype=F32),
        g_middle=vm(256, 768, dtype=F32),
        g_branch=vm(256, 768),
        g_attended=vm(256, 768),
        g_mixed=vm(256, 2304),
        enc_send=vm(2, 128, 768),
        gx_send=vm(256, 768),
        gx_recv=vm(4, 64, 768),
        sums=vm(16, 768, dtype=F32),
        sums_fc1=vm(8, 1536, dtype=F32),
        g_small=vm(4, 4, 16, 256),
        g_fc1=vm(4, 4, 48, 1536),
        g_fc2=vm(4, 2, 2, 96, 768),
        g_out=vm(4, 4, 48, 768),
        g_qkv=vm(4, 4, 48, 2304),
        pr_small=vm(4, 4, 16, 128),
        pr_a=vm(4, 4, 48, 1536),
        pr_fc1=vm(4, 4, 48, 768),
        pr_fc2=vm(4, 2, 2, 96, 384),
        dx_small=vm(4, 16, 128),
        dx_a=vm(4, 48, 1536),
        px_small=vm(4, 16, 128),
        px_a=vm(4, 48, 1536),
        px2_a=vm(4, 2, 48, 1536),
        send_a=vm(48, 1536),
        px_fc1=vm(4, 2, 48, 768),
        px_fc2=vm(4, 2, 96, 384),
        py_small=vm(4, 16, 128),
        py_a=vm(4, 48, 1536),
        py_fc1=vm(48, 768),
        pz_small=vm(3, 16, 128),
        pz_a=vm(3, 48, 1536),
        pz_fc1=vm(3, 2, 48, 768),
        pz_fc2=vm(3, 2, 96, 384),
        bz_a=vm(3, 4, 48, 1536),
        cz_a=vm(3, 4, 48, 1536),
        qz_a=vm(3, 48, 1536),
        qz_fc1=vm(3, 2, 48, 768),
        qz_fc2=vm(3, 2, 96, 384),
        bz_fc2=vm(3, 2, 2, 96, 384),
        cz_fc2=vm(3, 2, 2, 96, 384),
        last_a=vm(48, 1536, dtype=F32),
        last_fc1=vm(2, 48, 768, dtype=F32),
        send_fc1=vm(48, 768),
        last_fc2=vm(96, 384, dtype=F32),
        kept_fc2=vm(96, 384, dtype=F32),
        gx_out=vm(4, 64, 768, dtype=F32),
        local_sem=pltpu.SemaphoreType.DMA((KEPT,)),
        send_sem=pltpu.SemaphoreType.DMA((SENDS,)),
        recv_sem=pltpu.SemaphoreType.DMA((ARRIVALS,)),
    )


def layer_kernel(
    patches,
    norm_gain,
    norm_bias,
    qkv_weight,
    qv_bias,
    out_weight,
    fc1_weight,
    fc1_bias,
    fc2_weight,
    res_bias,
    cotangent,
    frame_valid,
    encoded,
    grad_patches,
    grad_gain,
    grad_shift,
    grad_qkv,
    grad_qv,
    grad_out,
    grad_fc1,
    grad_fc1_bias,
    grad_fc2,
    grad_res,
    *scratch,
):
    s = types.SimpleNamespace(**dict(zip(scratch_shapes(), scratch)))
    wide, blk = lax.axis_index("wide"), lax.axis_index("blk")
    z, x = lax.div(wide, 2), lax.rem(wide, 2)
    y, core = lax.div(blk, 2), lax.rem(blk, 2)
    here, at_x, at_y, at_d = 2 * x + y, 2 * (1 - x) + y, 2 * x + 1 - y, 2 * (1 - x) + 1 - y
    sibling = (wide, 2 * y + 1 - core)
    x_peer = (2 * z + 1 - x, blk)
    y_peer = (wide, 2 * (1 - y) + core)
    d_peer = (2 * z + 1 - x, 2 * (1 - y) + core)
    y_cross = (wide, 2 * (1 - y) + 1 - core)
    z_of = [lax.rem(z + step, 4) for step in range(4)]
    z_peers = [(2 * z_of[step] + x, blk) for step in range(4)]
    z_order = (z_peers[1], z_peers[3], z_peers[2])
    inner, end = lax.rem(z + 1, 4) >= 2, lax.rem(z + 1, 4) < 2
    z_in, z_out = 1 + lax.rem(z, 2), 3 * lax.div(z, 2)
    in_peer, out_peer = (2 * z_in + x, blk), (2 * z_out + x, blk)
    blk_peers = [(y, 1 - core), (1 - y, core), (1 - y, 1 - core)]

    barrier = pltpu.get_barrier_semaphore()
    peers = [sibling, x_peer, y_peer, d_peer, y_cross] + z_peers[1:]
    for peer in peers:
        pl.semaphore_signal(barrier, inc=1, device_id=peer, device_id_type=MESH_ID)

    started, groups = [], []

    class Group:
        def __init__(self):
            self.sem = s.recv_sem.at[len(groups)]
            groups.append(self)

        def wait(self, ref):
            pltpu.make_async_copy(ref, ref, self.sem).wait()

    def leave(spot):
        copy, only = started[spot]
        if only is None:
            copy.wait_send()
        else:
            pl.when(only)(copy.wait_send)

    def prepare(source, target, peer, group=None, only=None):
        spot = len(started)
        if spot >= SENDS:
            leave(spot - SENDS)
        copy = pltpu.make_async_remote_copy(
            src_ref=source,
            dst_ref=target,
            send_sem=s.send_sem.at[spot % SENDS],
            recv_sem=(group or Group()).sem,
            device_id=peer,
            device_id_type=MESH_ID,
        )
        started.append((copy, only))
        return copy

    def remote(source, target, peer, group=None, only=None):
        copy = prepare(source, target, peer, group, only)
        if only is None:
            copy.start()
        else:
            pl.when(only)(copy.start)
        return copy

    kept = []

    class Local:
        def __init__(self, source, target):
            self.copy, self.waited = pltpu.make_async_copy(source, target, s.local_sem.at[len(kept)]), False
            self.copy.start()
            kept.append(self)

        def wait(self):
            if not self.waited:
                self.waited = True
                self.copy.wait()

    def lanes(start, size):
        return pl.ds(pl.multiple_of(start, 128), size)

    mine = pl.ds(pl.multiple_of(64 * blk, 64), 64)
    taken = [Local(fc2_weight, s.w_fc2.at[z, x, core]), Local(patches.at[blk], s.rows_in.at[mine, :])]
    s.own_small[...] = jnp.zeros((16, 128), F32)
    s.sums[...] = jnp.zeros((16, D), F32)
    s.own_small[0:2, 0:24] = norm_gain[...].astype(F32)
    s.own_small[2:4, 0:24] = norm_bias[...].astype(F32)
    s.own_small[4:6, 0:24] = qv_bias[...].astype(F32)
    s.own_small[6:8, 0:24] = res_bias[...].astype(F32)
    s.own_small[8:9, 0:96] = fc1_bias[...].astype(F32)
    s.w_small[z, here, :, lanes(128 * core, 128)] = s.own_small[...].astype(BF16)
    own_rows = pl.ds(pl.multiple_of(24 * core, 8), 24)
    pieces = [(qkv_weight, 384 * j + 128 * t, partial(piece, j, t=t)) for j in range(3) for t in range(3)]
    pieces += [(out_weight, 1152 + 128 * t, lambda side, t=t: 384 * side + 128 * t) for t in range(3)]
    for ref, start, columns in pieces:
        s.pair_send[:, start : start + 128] = ref[:, lanes(columns(1 - core), 128)].astype(F32)
        s.pair_rows[own_rows, start : start + 128] = ref[:, lanes(columns(core), 128)].astype(F32)
    theirs = fc1_weight[:, lanes((1 - core) * 1536, 1536)].astype(F32)
    ours = fc1_weight[:, lanes(core * 1536, 1536)].astype(F32)
    for side in (0, 1):
        for k in range(4):
            at, found = 768 * side + 192 * k, 384 * k + 192 * side
            s.pair_send_h[:, at : at + 192] = theirs[:, found : found + 192]
            s.pair_rows_h[own_rows, at : at + 192] = ours[:, found : found + 192]

    pl.semaphore_wait(barrier, len(peers))

    pairs = {}
    for name, start in (("q0", 0), ("q1", 384), ("q2", 768), ("o", 1152)):
        columns = slice(start, start + 384)
        pairs[name] = remote(s.pair_send.at[:, columns], s.pair_rows.at[own_rows, columns], sibling)
    pairs["h"] = remote(s.pair_send_h, s.pair_rows_h.at[own_rows, :], sibling)


    rows_moved = Group()
    for py, pc in blk_peers:
        remote(patches.at[2 * py + pc], s.rows_in.at[mine, :], (wide, 2 * py + pc), rows_moved)

    class Direct:
        def __init__(self, block):
            self.block, self.arrived = block, Group()

        def start(self):
            own = self.block(z)
            for peer in z_order:
                remote(own, own, peer, self.arrived)

        def wait(self):
            self.arrived.wait(self.block(THREE))

    class Line:
        def __init__(self, block):
            self.block, self.first = block, len(groups)
            self.arrived = [Group() for _ in range(3)]

        def start(self):
            own = self.block(z)
            to_in = types.SimpleNamespace(sem=s.recv_sem.at[self.first + lax.div(lax.rem(z + 1, 4), 2)])
            remote(own, own, in_peer, to_in)
            remote(own, own, out_peer, self.arrived[0], inner)

        def pass_on(self):
            outer, other = self.block(z_out), self.block(z_in)
            inward = prepare(outer, outer, in_peer, self.arrived[2], inner)
            outward = prepare(other, other, out_peer, self.arrived[1], inner)

            @pl.when(inner)
            def _():
                self.arrived[0].wait(outer)
                inward.start()
                self.arrived[1].wait(other)
                outward.start()

        def pass_last(self):
            far = self.block(3 - z_out)
            outward = prepare(far, far, out_peer, self.arrived[2], inner)

            @pl.when(inner)
            def _():
                self.arrived[2].wait(far)
                outward.start()

        def wait(self):
            @pl.when(end)
            def _():
                for arrived, level in zip(self.arrived, (z_in, 3 - z_in, 3 - z)):
                    arrived.wait(self.block(level))

    class DirectSum:
        def __init__(self, own, parts, _):
            self.own, self.parts, self.arrived = own, parts, Group()

        def start(self):
            for step in (1, 3, 2):
                remote(self.own(z_of[step]), self.parts(step - 1), z_peers[step], self.arrived)

        def wait(self):
            self.arrived.wait(self.parts(THREE))

        def summed(self, view):
            found = view(self.own(z))[...].astype(F32)
            for i in range(3):
                found = found + view(self.parts(i))[...].astype(F32)
            return found

    class LineSum:
        def __init__(self, own, parts, more):
            self.own, self.parts, self.more = own, parts, more
            self.arrived = [Group() for _ in range(3)]

        def start(self):
            remote(self.own(pl.ds(1 - lax.div(z, 2), 3)), self.parts(THREE), in_peer, self.arrived[0], end)

        def pass_on(self):
            source = self.own(pl.ds(2 - 2 * lax.div(z, 2), 2))
            inward = prepare(source, self.more(BOTH), in_peer, self.arrived[1], inner)

            @pl.when(inner)
            def _():
                self.arrived[0].wait(self.parts(THREE))
                for level in (z_in, 3 - z_out):
                    ref = self.own(level)
                    ref[...] = ref[...] + self.parts(level - 1 + lax.div(z, 2))[...]
                inward.start()

        def pass_last(self):
            outward = prepare(self.own(z_out), self.more(2), out_peer, self.arrived[2], inner)

            @pl.when(inner)
            def _():
                self.arrived[1].wait(self.more(BOTH))
                base = 2 * lax.div(z, 2)
                ref = self.own(z_out)
                ref[...] = ref[...] + self.more(z_out - base)[...]
                outward.start()
                ref = self.own(z)
                found = ref[...].astype(F32) + self.parts(z - 1 + lax.div(z, 2))[...].astype(F32)
                ref[...] = (found + self.more(z - base)[...].astype(F32)).astype(BF16)

        def wait(self):
            @pl.when(end)
            def _():
                self.arrived[2].wait(self.more(2))
                ref = self.own(z)
                ref[...] = ref[...] + self.more(2)[...]

        def summed(self, view):
            return view(self.own(z))[...].astype(F32)

    def wait_fc2():
        taken[0].wait()

    class Steps:
        def w(self):
            self.line.pass_on()

        def v(self):
            self.line.pass_last()

    class Gather(Steps):
        def __init__(self, part, low, line):
            self.part, self.low, self.high = part, pl.ds(0, low), pl.ds(low, 4 - low)
            self.by_x, self.by_y, self.far, self.pair = (Group() for _ in range(4))
            self.line = line(lambda levels: part(levels, here))

        def z(self):
            self.line.start()

        def p(self):
            self.line.wait()
            self.share(self.part(ALL, here))

        def share(self, block):
            remote(block, block, x_peer, self.by_x)
            remote(block, block, y_peer, self.by_y)
            remote(block, block, sibling, self.pair)

        def f(self):
            column = self.part(ALL, at_x)
            self.by_x.wait(column)
            some = self.part(self.low, at_x)
            remote(some, some, y_peer, self.far)
            remote(column, column, sibling, self.pair)

        def g(self):
            column = self.part(ALL, at_y)
            self.by_y.wait(column)
            some = self.part(self.high, at_y)
            remote(some, some, x_peer, self.far)
            remote(column, column, sibling, self.pair)

        def l(self):
            column = self.part(ALL, at_d)
            self.far.wait(column)
            remote(column, column, sibling, self.pair)

        def d(self):
            self.pair.wait(self.part(ALL, ALL))

    class FineGather(Gather):
        def z(self):
            own = self.part(z, here)
            self.z_copies = [remote(own, own, peer) for peer in z_order]

        def o(self):
            self.share(self.part(z, here))

        def p(self):
            for step, copy in zip((1, 3, 2), self.z_copies):
                copy.wait_recv()
                self.share(self.part(z_of[4 - step], here))

    class SquareGather(Steps):
        def __init__(self, part, line):
            self.part, self.square, self.pair = part, Group(), Group()
            self.line = line(lambda levels: part(levels, ALL))

        def p(self):
            own = self.part(z, here)
            for peer in (x_peer, y_peer, d_peer):
                remote(own, own, peer, self.square)

        def z(self):
            self.square.wait(self.part(z, THREE))
            self.line.start()
            level = self.part(z, ALL)
            remote(level, level, sibling, self.pair)

        def l(self):
            self.line.wait()
            for step in (1, 2, 3):
                level = self.part(z_of[step], ALL)
                remote(level, level, sibling, self.pair)

        def d(self):
            self.pair.wait(self.part(ALL, ALL))

    class PlaneGather(Steps):
        def __init__(self, part, line, across=None):
            self.part, self.across, self.pair = part, across, Group()
            self.line = line(lambda levels: part(levels, x))

        def y(self):
            source, target = self.across
            self.y_copy = remote(source, target, y_peer)

        def z(self):
            if self.across:
                self.y_copy.wait_recv()
            else:
                wait_fc2()
            self.line.start()

        def x(self):
            self.line.wait()
            column = self.part(ALL, x)
            self.x_copy = remote(column, column, x_peer)
            remote(column, column, sibling, self.pair)

        def l(self):
            self.x_copy.wait_recv()
            column = self.part(ALL, 1 - x)
            remote(column, column, sibling, self.pair)

        def d(self):
            self.pair.wait(self.part(ALL, BOTH))

    class AcrossGather(Steps):
        def __init__(self, part, line):
            self.part, self.pair = part, Group()
            self.line = line(lambda levels: part(levels, BOTH))

        def x(self):
            wait_fc2()
            own = self.part(z, x)
            self.x_copy = remote(own, own, x_peer)

        def z(self):
            self.x_copy.wait_recv()
            self.line.start()
            level = self.part(z, BOTH)
            remote(level, level, sibling, self.pair)

        def l(self):
            self.line.wait()
            for step in (1, 2, 3):
                level = self.part(z_of[step], BOTH)
                remote(level, level, sibling, self.pair)

        def d(self):
            self.pair.wait(self.part(ALL, BOTH))

    def column_part(ref, start, size):
        return lambda levels, place: ref.at[levels, place, :, lanes(start, size)]

    def column_gather(ref, start, size, way, chained):
        part, line = column_part(ref, start, size), Line if chained else Direct
        if way == 9:
            own = part(z, here)
            sides = lambda levels, side: part(levels, ALL if side is BOTH else pl.ds(2 * side, 2))
            return PlaneGather(sides, line, (own, own))
        if way == 0:
            return SquareGather(part, line)
        return (Gather if way > 0 else FineGather)(part, abs(way), line)

    gathers = {"s0": column_gather(s.w_small, 128 * core, 128, 2, 0)}
    for name, j, start, size, way, chained in GATHER_UNITS:
        if j < 3:
            ref, first = s.w_qkv, 768 * j + 384 * core
        else:
            ref, first = s.w_out, 384 * core
        gathers[name] = column_gather(ref, first + 128 * start, 128 * size, way, chained)

    def fc1_gather(j):
        columns = lanes(768 * core + 384 * j, 384)
        return PlaneGather(
            lambda levels, side: s.w_fc1.at[levels, ALL if side is BOTH else pl.ds(2 * side, 2), :, columns],
            Line if GATHER_LINES["h"][j] else Direct,
            (s.fc1_other.at[:, 384 * j : 384 * j + 384], s.w_fc1.at[z, here, :, columns]),
        )

    def fc2_gather(j, size, way):
        rows = pl.ds(size * j, size)
        part = lambda levels, side: s.w_fc2.at[levels, side, core, rows, :]
        return (PlaneGather if way else AcrossGather)(part, Line if GATHER_LINES["f"][j] else Direct)

    for j in range(2):
        gathers["h" + str(j)] = fc1_gather(j)
    for j, way in enumerate(GATHER_FC2):
        gathers["f" + str(j)] = fc2_gather(j, 96 // len(GATHER_FC2), way)

    def assemble(name):
        pairs[name].wait_recv()
        if name == "h":
            halves = lanes(768 * y, 768), lanes(768 * (1 - y), 768)
            s.w_fc1[z, here, :, lanes(768 * core, 768)] = s.pair_rows_h[:, halves[0]].astype(BF16)
            s.fc1_other[...] = s.pair_rows_h[:, halves[1]].astype(BF16)
        elif name == "o":
            s.w_out[z, here, :, lanes(384 * core, 384)] = s.pair_rows[:, 1152:1536].astype(BF16)
        else:
            j = int(name[1])
            found = s.pair_rows[:, 384 * j : 384 * j + 384].astype(BF16)
            s.w_qkv[z, here, :, lanes(768 * j + 384 * core, 384)] = found


    def by_rows(body, carry=None):
        def step(i, held):
            return body(pl.ds(pl.multiple_of(ROWS * i, ROWS), ROWS), held)

        return lax.fori_loop(0, TOKENS // ROWS, step, carry)

    def over(shape, axis):
        return lax.broadcasted_iota(jnp.int32, shape, axis)

    def piece24(columns):
        return lax.shift_right_logical(columns * 43691, 20)

    def piece96(columns):
        return lax.shift_right_logical(columns * 10923, 20)

    def spread24():
        columns = over((128, D), 1)
        return (columns - 24 * piece24(columns) == over((128, D), 0)).astype(F32).astype(BF16)

    def hidden_unit(columns):
        return columns + 192 * lax.shift_right_logical(columns * 21846, 22) + 192 * y

    def spread96():
        columns = hidden_unit(over((128, FF // 2), 1))
        return (columns - 96 * piece96(columns) == over((128, FF // 2), 0)).astype(F32).astype(BF16)

    def unpack_small():
        flat = s.w_small[...].reshape(256, 256)
        chips = lax.shift_right_logical(over((256, D), 0), 4)
        pieces = piece24(over((256, D), 1))
        spread = spread24()
        found = jnp.zeros((16, D), F32)
        for side in (0, 1):
            wide_rows = dot(flat[:, 128 * side : 128 * side + 128], spread)
            wide_rows = jnp.where(pieces == 2 * chips + side, wide_rows, 0.0)
            found = found + jnp.sum(wide_rows.reshape(16, 16, D), axis=0)
        s.par[...] = found
        pick = (over((16, 256), 1) == 16 * over((16, 256), 0) + 8).astype(F32).astype(BF16)
        spread = spread96()
        shape = (16, FF // 2)
        pieces = piece96(hidden_unit(over(shape, 1)))
        found = jnp.zeros(shape, F32)
        for side in (0, 1):
            rows = dot(pick, flat[:, 128 * side : 128 * side + 128]).astype(BF16)
            found = found + jnp.where(pieces == 2 * over(shape, 0) + side, dot(rows, spread), 0.0)
        s.par_fc1[0:1, :] = jnp.sum(found, axis=0, keepdims=True)

    def standardized(rows):
        centered = rows - jnp.mean(rows, axis=-1, keepdims=True)
        scale = lax.rsqrt(jnp.mean(centered * centered, axis=-1, keepdims=True) + EPSILON)
        return centered * scale, scale

    def first_norm():
        def body(rows, _):
            found, _ = standardized(s.rows_in[rows, :].astype(F32))
            s.normed[rows, :] = (found * s.par[0:1, :] + s.par[2:3, :]).astype(BF16)
            return 0

        by_rows(body, 0)
        s.normed_t[...] = s.normed[...].T

    def project_qkv(j):
        found = dot(s.normed[...], s.w_qkv[:, :, :, 768 * j : 768 * j + 768].reshape(D, D))
        for i in (0, 1):
            query, key, value = (slice(at, at + 128) for at in pair_places(0, i))
            natural = slice(128 * (2 * j + i), 128 * (2 * j + i) + 128)
            parts = (
                (query, (found[:, query] + s.par[4:5, natural]) * 0.125),
                (key, found[:, key]),
                (value, found[:, value] + s.par[5:6, natural]),
            )
            for at, part in parts:
                s.mixed[:, 768 * j + at.start : 768 * j + at.stop] = part.astype(BF16)

    def head_masks():
        first = (over((TOKENS, 128), 1) < 64).astype(F32)
        return first.astype(BF16), (1.0 - first).astype(BF16)

    def softmax(scores):
        expo = jnp.exp(scores - jnp.max(scores, axis=-1, keepdims=True))
        return expo * (1.0 / jnp.sum(expo, axis=-1, keepdims=True))

    def attend(j):
        def body(i, _):
            query, key, value = (s.mixed[:, lanes(at, 128)] for at in pair_places(j, i))
            found = jnp.zeros((TOKENS, 128), F32)
            for mask in head_masks():
                probs = softmax(dot_nt(query * mask, key)).astype(BF16)
                found = found + dot(probs, value * mask)
            s.attended[:, lanes(128 * (2 * j + i), 128)] = found.astype(BF16)
            return 0

        lax.fori_loop(0, 2, body, 0)

    def some_rows(body, carry, start, count):
        def step(i, held):
            return body(pl.ds(pl.multiple_of(ROWS * i + start, ROWS), ROWS), held)

        return lax.fori_loop(0, count // ROWS, step, carry)

    def project_out(part):
        half = pl.ds(128 * part, 128)
        s.middle[half, :] = dot(s.attended[half, :], s.w_out[...].reshape(D, D))

        def body(rows, _):
            middle = s.rows_in[rows, :].astype(F32) + (s.middle[rows, :] + s.par[6:7, :])
            s.middle[rows, :] = middle
            found, _ = standardized(middle)
            s.normed2[rows, :] = (found * s.par[1:2, :] + s.par[3:4, :]).astype(BF16)
            return 0

        some_rows(body, 0, 128 * part, 128)

    def transpose_out():
        s.attended_t[...] = s.attended[...].T
        s.normed2_t[:, 0:256] = s.normed2[0:256, :].T

    def feed(j, start, count):
        def body(side, _):
            columns = lanes(768 * side + 384 * j, 384)
            tokens = pl.ds(start, count)
            s.other[0:count, 0:384] = dot(s.normed2[tokens, :], s.w_fc1[:, :, :, columns].reshape(D, 384))

            def gelu(rows, _):
                there = pl.ds(pl.multiple_of(rows.start + start, ROWS), ROWS)
                hidden = s.other[rows, 0:384] + s.par_fc1[0:1, columns]
                bell = jnp.exp(-0.5 * hidden * hidden)
                normal = 0.5 + 0.5 * lax.erf(hidden * (1.0 / math.sqrt(2.0)))
                s.slope[there, columns] = normal + hidden * (bell * (1.0 / math.sqrt(2.0 * math.pi)))
                s.active[there, columns] = (hidden * normal).astype(BF16)
                return 0

            some_rows(gelu, 0, 0, count)
            found = s.active[tokens, columns].T.reshape(4, 96, count)
            s.active_t[pl.ds(8 * side + 4 * j, 4), :, start : start + count] = found
            return 0

        lax.fori_loop(0, 2, body, 0)

    def feed_own(j):
        feed(j, 0, 256)

    def feed_other(j, part):
        feed(j, 256 + 128 * part, 128)

    ours_rows = pl.ds(pl.multiple_of(128 * y, 128), 128)
    theirs_rows = pl.ds(pl.multiple_of(128 * (1 - y), 128), 128)
    across_y = 2 * (1 - y) + core
    valid, valid_across = frame_valid[blk].astype(F32), frame_valid[across_y].astype(F32)

    def mask_cotangent(frame):
        def body(rows, _):
            there = pl.ds(pl.multiple_of(rows.start + 256 * frame, ROWS), ROWS)
            masked = s.cot_in[there, :].astype(F32) * (valid_across if frame else valid)
            s.g_branch2[there, :] = masked.astype(BF16)
            return 0

        by_rows(body, 0)


    class Scatter(Steps):
        every = ALL

        def view(self, ref):
            return ref

        def __init__(self, own, other, pr, dx, dy, px, py, pz, finish, low=2, line=DirectSum, more=None):
            self.own, self.other, self.finish = own, other, finish
            self.pr, self.dx, self.dy, self.px, self.py = pr, dx, dy, px, py
            self.line = line(lambda levels: own(levels, here), pz, more)
            self.square = Group()
            self.low, self.high = pl.ds(0, low), pl.ds(low, 4 - low)

        def s(self):
            self.pair = remote(self.other(), self.pr(ALL, self.every), sibling)

        def add_pair(self):
            self.pair.wait_recv()

            def add(level, _):
                ref = self.own(level, self.every)
                ref[...] = ref[...] + self.pr(level, self.every)[...]
                return 0

            lax.fori_loop(0, 4, add, 0)

        def p(self):
            self.add_pair()
            low, high = self.low, self.high
            self.a = remote(self.own(low, at_d), self.dx(low), x_peer)
            self.b = remote(self.own(high, at_d), self.dy(high), y_peer)
            remote(self.own(low, at_x), self.px(low), x_peer, self.square)
            remote(self.own(high, at_y), self.py(high), y_peer, self.square)

        def f(self):
            self.a.wait_recv()
            ref = self.own(self.low, at_y)
            ref[...] = ref[...] + self.dx(self.low)[...]
            remote(ref, self.py(self.low), y_peer, self.square)

        def g(self):
            self.b.wait_recv()
            ref = self.own(self.high, at_x)
            ref[...] = ref[...] + self.dy(self.high)[...]
            remote(ref, self.px(self.high), x_peer, self.square)

        def z(self):
            self.square.wait(self.own(ALL, BOTH))

            def add(level, _):
                ref = self.own(level, here)
                ref[...] = (
                    ref[...].astype(F32)
                    + self.px(level)[...].astype(F32)
                    + self.py(level)[...].astype(F32)
                ).astype(BF16)
                return 0

            lax.fori_loop(0, 4, add, 0)
            self.line.start()

        def l(self):
            self.line.wait()
            self.finish(self)

        def summed(self, view):
            return self.line.summed(view)

    class SquareScatter(Scatter):
        def __init__(self, own, other, pr, bz, pz, finish, line, more):
            self.own, self.other, self.finish = own, other, finish
            self.pr, self.pz, self.square = pr, pz, Group()
            self.line = line(lambda levels: own(levels, ALL), bz, more)

        def z(self):
            self.add_pair()
            self.line.start()

        def p(self):
            self.line.wait()
            if isinstance(self.line, DirectSum):
                self.own(z, ALL)[...] = self.line.summed(lambda ref: ref).astype(BF16)
            targets = ((at_x, x_peer), (at_y, y_peer), (at_d, d_peer))
            for i, (place, peer) in enumerate(targets):
                remote(self.own(z, place), self.pz(i), peer, self.square)

        def l(self):
            self.square.wait(self.pz(THREE))
            self.finish(self)

        def summed(self, view):
            found = view(self.own(z, here))[...].astype(F32)
            for i in range(3):
                found = found + view(self.pz(i))[...].astype(F32)
            return found

    class PlaneScatter(Scatter):
        def __init__(self, own, other, pr, px, pz, finish, line, more, across=None, view=None):
            self.own, self.other, self.finish, self.across, self.view = own, other, finish, across, view
            self.pr, self.px = pr, px
            self.line = line(lambda levels: own(levels, x), pz, more)

        def x(self):
            self.add_pair()
            self.x_copy = remote(self.own(ALL, 1 - x), self.px(ALL), x_peer)

        def z(self):
            self.x_copy.wait_recv()

            def add(level, _):
                ref = self.own(level, x)
                ref[...] = ref[...] + self.px(level)[...]
                return 0

            lax.fori_loop(0, 4, add, 0)
            self.line.start()

        def y(self):
            self.line.wait()
            source, target = self.across(self)
            self.y_copy = remote(source, target, y_peer)

        def l(self):
            if self.across:
                self.y_copy.wait_recv()
            else:
                self.line.wait()
            self.finish(self)

    class AcrossScatter(Scatter):
        def __init__(self, own, other, pr, bz, px, finish, line, more):
            self.own, self.other, self.finish = own, other, finish
            self.pr, self.px = pr, px
            self.line = line(lambda levels: own(levels, ALL), bz, more)

        def z(self):
            self.add_pair()
            self.line.start()

        def x(self):
            self.line.wait()
            if isinstance(self.line, DirectSum):
                self.own(z, ALL)[...] = self.line.summed(lambda ref: ref).astype(BF16)
            self.x_copy = remote(self.own(z, 1 - x), self.px(), x_peer)

        def l(self):
            self.x_copy.wait_recv()
            self.finish(self)

        def summed(self, view):
            return view(self.own(z, x))[...].astype(F32) + view(self.px())[...].astype(F32)

    def columns_of(ref, columns, size):
        def own(levels, places):
            return ref.at[levels, places, :, lanes(columns(core), size)]

        def other():
            return ref.at[:, :, :, lanes(columns(1 - core), size)]

        return own, other

    def column_scatter(ref, columns, natural, size, spot, output, way, chained):
        at = pl.ds(spot, size)

        def finish(scatter):
            total = scatter.summed(scatter.view)
            if way == 9:
                total = total + s.py_a[0, :, at].astype(F32)
            s.last_a[:, at] = total
            other_rows = pl.ds(pl.multiple_of(24 * (1 - core), 8), 24)
            group = Group()
            finals.append((group, s.last_a.at[own_rows, at]))
            for t in range(size // 128):
                some = slice(spot + 128 * t, spot + 128 * t + 128)
                target = lanes(natural(core, t), 128)
                remote(s.last_a.at[other_rows, some], output.at[:, target], sibling, group)
                Local(s.last_a.at[own_rows, some], output.at[:, target])

        if way == 9:

            def across(scatter):
                s.send_a[:, at] = scatter.summed(lambda ref: ref.at[1 - y]).astype(BF16)
                return s.send_a.at[:, at], s.py_a.at[0, :, at]

            def sides(ref):
                return lambda levels, side: ref(levels, ALL if side is ALL else pl.ds(2 * side, 2))

            own, other = columns_of(ref, columns, size)
            return PlaneScatter(
                sides(own),
                other,
                lambda levels, places: s.pr_a.at[levels, places, :, at],
                lambda levels: s.px2_a.at[levels, :, :, at],
                lambda i: s.bz_a.at[i, BOTH, :, at],
                finish,
                LineSum if chained else DirectSum,
                lambda i: s.cz_a.at[i, BOTH, :, at],
                across,
                lambda ref: ref.at[y],
            )

        if not way:
            return SquareScatter(
                *columns_of(ref, columns, size),
                lambda levels, places: s.pr_a.at[levels, places, :, at],
                lambda i: s.bz_a.at[i, :, :, at],
                lambda i: s.pz_a.at[i, :, at],
                finish,
                LineSum if chained else DirectSum,
                lambda i: s.cz_a.at[i, :, :, at],
            )
        return Scatter(
            *columns_of(ref, columns, size),
            lambda levels, places: s.pr_a.at[levels, places, :, at],
            lambda levels: s.dx_a.at[levels, :, at],
            lambda levels: s.dx_a.at[levels, :, at],
            lambda levels: s.px_a.at[levels, :, at],
            lambda levels: s.py_a.at[levels, :, at],
            lambda i: s.pz_a.at[i, :, at],
            finish,
            way,
            LineSum if chained else DirectSum,
            lambda i: s.qz_a.at[i, :, at],
        )

    def fc1_scatter(j):
        at = slice(384 * j, 384 * j + 384)

        def own_columns(side):
            return lanes(768 * side + 384 * j, 384)

        def own(levels, side):
            places = ALL if side is ALL else pl.ds(2 * side, 2)
            return s.g_fc1.at[levels, places, :, own_columns(core)]

        def across(scatter):
            s.last_fc1[0, :, at] = scatter.summed(lambda ref: ref.at[y])
            s.send_fc1[:, at] = scatter.summed(lambda ref: ref.at[1 - y]).astype(BF16)
            return s.send_fc1.at[:, at], s.py_fc1.at[:, at]

        def finish(scatter):
            s.last_fc1[1, :, at] = s.py_fc1[:, at].astype(F32)
            other_rows = pl.ds(pl.multiple_of(24 * (1 - core), 8), 24)
            for i, half in enumerate((y, 1 - y)):
                target = lanes(1536 * half + 768 * core + 384 * j, 384)
                copy = remote(s.last_fc1.at[i, other_rows, at], grad_fc1.at[:, target], sibling)
                finals.append((copy, None))
                Local(s.last_fc1.at[i, own_rows, at], grad_fc1.at[:, target])

        return PlaneScatter(
            own,
            lambda: s.g_fc1.at[:, :, :, own_columns(1 - core)],
            lambda levels, places: s.pr_fc1.at[levels, places, :, at],
            lambda levels: s.px_fc1.at[levels, :, :, at],
            lambda i: s.pz_fc1.at[i, :, :, at],
            finish,
            LineSum if SCATTER_LINES["h"][j] else DirectSum,
            lambda i: s.qz_fc1.at[i, :, :, at],
            across,
        )

    def fc2_scatter(j, size, way):
        rows = pl.ds(size * j, size)
        half = lanes(384 * core, 384)

        def finish(scatter):
            s.last_fc2[rows, :] = scatter.summed(lambda ref: ref.at[1 - core])
            finals.append((remote(s.last_fc2.at[rows, :], grad_fc2.at[rows, half], sibling), None))
            s.kept_fc2[rows, :] = scatter.summed(lambda ref: ref.at[core])
            Local(s.kept_fc2.at[rows, :], grad_fc2.at[rows, half])

        def sides(side):
            return BOTH if side is ALL else side

        own = lambda levels, side: s.g_fc2.at[levels, sides(side), :, rows, half]
        other = lambda: s.g_fc2.at[:, :, :, rows, lanes(384 * (1 - core), 384)]
        pr = lambda levels, side: s.pr_fc2.at[levels, sides(side), :, rows, :]
        if not way:
            bz = lambda i: s.bz_fc2.at[i, :, :, rows, :]
            line = LineSum if SCATTER_LINES["f"][j] else DirectSum
            more = lambda i: s.cz_fc2.at[i, :, :, rows, :]
            return AcrossScatter(own, other, pr, bz, lambda: s.pz_fc2.at[0, :, rows, :], finish, line, more)
        return PlaneScatter(
            own,
            other,
            pr,
            lambda levels: s.px_fc2.at[levels, :, rows, :],
            lambda i: s.pz_fc2.at[i, :, rows, :],
            finish,
            LineSum if SCATTER_LINES["f"][j] else DirectSum,
            lambda i: s.qz_fc2.at[i, :, rows, :],
        )

    def small_finish(scatter):
        found = scatter.summed(lambda ref: ref)
        grad_gain[...] = found[0:2, 0:24]
        grad_shift[...] = found[2:4, 0:24]
        grad_qv[...] = found[4:6, 0:24]
        grad_res[...] = found[6:8, 0:24]
        grad_fc1_bias[...] = found[8:9, 0:96]

    finals = []
    scatters = {}
    for j, way in enumerate(SCATTER_FC2):
        scatters["f" + str(j)] = fc2_scatter(j, 96 // len(SCATTER_FC2), way)
    for j in range(2):
        scatters["h" + str(j)] = fc1_scatter(j)
    for name, j, start, size, way, chained in SCATTER_UNITS:
        if j < 3:
            ref, output, spot, first = s.g_qkv, grad_qkv, 384 + 384 * j, 768 * j
            natural = lambda side, t, j=j, start=start: piece(j, side, start + t)
        else:
            ref, output, spot, first = s.g_out, grad_out, 0, 0
            natural = lambda side, t, start=start: 384 * side + 128 * (start + t)
        columns = lambda side, first=first, start=start: first + 384 * side + 128 * start
        scatters[name] = column_scatter(
            ref, columns, natural, 128 * size, spot + 128 * start, output, way, chained
        )

    scatters["s0"] = Scatter(
        *columns_of(s.g_small, lambda side: 128 * side, 128),
        lambda levels, places: s.pr_small.at[levels, places],
        lambda levels: s.dx_small.at[levels],
        lambda levels: s.dx_small.at[levels],
        lambda levels: s.px_small.at[levels],
        lambda levels: s.py_small.at[levels],
        lambda i: s.pz_small.at[i],
        small_finish,
    )

    def weight_grad_fc2(j):
        size = 96 // len(SCATTER_FC2)
        rows = pl.ds(size * j, size)

        def body(turn, _):
            columns = lanes(384 * (turn * core + (1 - turn) * (1 - core)), 384)
            found = dot(s.active_t[:, rows, :].reshape(16 * size, 512), s.g_branch2[:, columns])
            s.g_fc2[:, :, :, rows, columns] = found.astype(BF16).reshape(4, 2, 2, size, 384)
            return 0

        lax.fori_loop(0, 2, body, 0)

    def column_grad(left, right, ref, columns):
        def body(turn, _):
            at = lanes(columns(turn * core + (1 - turn) * (1 - core)), 384)
            ref[:, :, :, at] = dot(left[...], right[:, at]).astype(BF16).reshape(4, 4, 48, 384)
            return 0

        lax.fori_loop(0, 2, body, 0)

    def feed_back(frame):
        tokens = pl.ds(256 * frame, 256)

        def body(part, _):
            columns = lanes(D * part, D)
            s.other[...] = dot_nt(s.g_branch2[tokens, :], s.w_fc2[pl.ds(2 * part, 2)].reshape(D, D))

            def slope(rows, sums):
                there = pl.ds(pl.multiple_of(rows.start + 256 * frame, ROWS), ROWS)
                found = (s.other[rows, :] * s.slope[there, columns]).astype(BF16)
                s.g_hidden[there, columns] = found
                return sums + jnp.sum(found.astype(F32), axis=0, keepdims=True)

            s.sums_fc1[frame : frame + 1, columns] = by_rows(slope, jnp.zeros((1, D), F32))
            return 0

        lax.fori_loop(0, 2, body, 0)

    def feed_out(frame):
        tokens = pl.ds(256 * frame, 256)
        s.total[...] = jnp.zeros((TOKENS, D), F32)

        def body(part, _):
            weight = s.w_fc2[pl.ds(2 * part, 2)].reshape(D, D)
            s.total[...] += dot(s.active[tokens, lanes(D * part, D)], weight)
            return 0

        lax.fori_loop(0, 2, body, 0)
        if frame:
            s.part_across[...] = s.total[...].astype(BF16)
        else:

            def add(rows, _):
                s.total[rows, :] = s.middle[rows, :] + (s.total[rows, :] + s.par[7:8, :])
                return 0

            by_rows(add, 0)
            s.base_send[...] = (valid * s.total[theirs_rows, :]).astype(BF16)

    def output():
        s.enc_send[0] = (valid * (s.total[ours_rows, :] + s.part_recv[...].astype(F32))).astype(BF16)
        part = valid_across * s.part_across[ours_rows, :].astype(F32)
        s.enc_send[1] = (s.base_recv[...].astype(F32) + part).astype(BF16)

        def body(rows, sums):
            return sums + jnp.sum(s.g_branch2[rows, :].astype(F32), axis=0, keepdims=True)

        s.sums[7:8, :] = by_rows(body, jnp.zeros((1, D), F32))

    def feed_back_rows(start, count):
        found = jnp.zeros((count, D), F32)
        for part in (0, 1):
            columns = slice(D * part, D * part + D)
            hidden = s.g_hidden[pl.ds(start, count), columns]
            found = found + dot_nt(hidden, s.w_fc1[:, :, :, columns].reshape(D, D))
        return found

    def feed_back_own():
        s.other[...] = feed_back_rows(0, 256)

    def feed_back_other():
        s.back_send[...] = feed_back_rows(256, 256).astype(BF16)

    def norm_back(upstream, found, scale, gain):
        weighted = upstream * gain
        return scale * (
            weighted
            - jnp.mean(weighted, axis=-1, keepdims=True)
            - found * jnp.mean(weighted * found, axis=-1, keepdims=True)
        )

    def column_sum(values):
        return jnp.sum(values, axis=0, keepdims=True)

    def second_norm_back(part):
        def rows_back(rows, sums):
            upstream = s.other[rows, :] + s.back_recv[rows, :].astype(F32)
            found, scale = standardized(s.middle[rows, :])
            middle = s.g_branch2[rows, :].astype(F32) + norm_back(upstream, found, scale, s.par[1:2, :])
            s.g_middle[rows, :] = middle
            branch = middle.astype(BF16)
            s.g_branch[rows, :] = branch
            return (
                sums[0] + column_sum(upstream * found),
                sums[1] + column_sum(upstream),
                sums[2] + column_sum(branch.astype(F32)),
            )

        before = [jnp.zeros((1, D), F32)] * 3
        if part:
            before = [s.sums[row : row + 1, :] for row in (1, 3, 6)]
        found = some_rows(rows_back, tuple(before), 128 * part, 128)
        s.sums[1:2, :], s.sums[3:4, :], s.sums[6:7, :] = found

    def attend_back(j):
        def body(i, _):
            spots = [lanes(at, 128) for at in pair_places(j, i)]
            natural = lanes(128 * (2 * j + i), 128)
            query, key, value = (s.mixed[:, spot] for spot in spots)
            upstream = s.g_attended[:, natural]
            g_query, g_key, g_value = (jnp.zeros((TOKENS, 128), F32) for _ in range(3))
            for mask in head_masks():
                probs = softmax(dot_nt(query * mask, key))
                g_probs = dot_nt(upstream * mask, value)
                g_value = g_value + dot_tn(probs.astype(BF16), upstream * mask)
                inner = jnp.sum(probs * g_probs, axis=-1, keepdims=True)
                g_scores = (probs * (g_probs - inner)).astype(BF16)
                g_query = g_query + dot(g_scores, key * mask)
                g_key = g_key + dot_tn(g_scores, query * mask)
            g_query = 0.125 * g_query.astype(BF16).astype(F32)
            g_value = g_value.astype(BF16)
            s.g_mixed[:, spots[0]] = g_query.astype(BF16)
            s.g_mixed[:, spots[1]] = g_key.astype(BF16)
            s.g_mixed[:, spots[2]] = g_value
            s.sums[4:5, natural] = column_sum(g_query)
            s.sums[5:6, natural] = column_sum(g_value.astype(F32))
            return 0

        lax.fori_loop(0, 2, body, 0)

    def first_norm_back():
        s.total[...] = jnp.zeros((TOKENS, D), F32)

        def body(level, _):
            columns = lanes(D * level, D)
            s.total[...] += dot_nt(s.g_mixed[:, columns], s.w_qkv[:, :, :, columns].reshape(D, D))
            return 0

        lax.fori_loop(0, 3, body, 0)

        def rows_back(rows, sums):
            upstream = s.total[rows, :]
            found, scale = standardized(s.rows_in[rows, :].astype(F32))
            result = s.g_middle[rows, :] + norm_back(upstream, found, scale, s.par[0:1, :])
            s.gx_send[rows, :] = result.astype(BF16)
            return (sums[0] + column_sum(upstream * found), sums[1] + column_sum(upstream))

        empty = jnp.zeros((1, D), F32)
        s.sums[0:1, :], s.sums[2:3, :] = by_rows(rows_back, (empty, empty))

    def pack_small():
        chips = lax.shift_right_logical(over((256, D), 0), 4)
        pieces = piece24(over((256, D), 1))
        spread = spread24()
        rows = jnp.broadcast_to(s.sums[...][None], (16, 16, D)).reshape(256, D)
        for side in (0, 1):
            placed = dot_nt(jnp.where(pieces == 2 * chips + side, rows, 0.0).astype(BF16), spread)
            s.g_small[:, :, :, 128 * side : 128 * side + 128] = placed.astype(BF16).reshape(4, 4, 16, 128)
        put = (over((256, 16), 0) == 16 * over((256, 16), 1) + 8).astype(F32).astype(BF16)
        spread = spread96()
        shape = (16, FF // 2)
        pieces = piece96(hidden_unit(over(shape, 1)))
        row = s.sums_fc1[0:1, :] + s.sums_fc1[1:2, :]
        for side in (0, 1):
            mine = pieces == 2 * over(shape, 0) + side
            placed = dot_nt(jnp.where(mine, row, 0.0).astype(BF16), spread).astype(BF16)
            here_ = s.g_small.at[:, :, :, pl.ds(128 * side, 128)]
            here_[...] = here_[...] + dot(put, placed).astype(BF16).reshape(4, 4, 16, 128)

    moved = {"rows": (rows_moved, s.rows_in.at[0:192, :])}

    cot_kept = {}

    def send_cotangent(frame):
        group, there = Group(), pl.ds(pl.multiple_of(64 * blk + 256 * frame, 64), 64)
        for py, pc in blk_peers:
            source = cotangent.at[2 * (1 - py if frame else py) + pc]
            remote(source, s.cot_in.at[there, :], (wide, 2 * py + pc), group)
        moved["cot" + str(frame)] = group, s.cot_in.at[256 * frame : 256 * frame + 192, :]
        cot_kept[frame] = Local(cotangent.at[across_y if frame else blk], s.cot_in.at[there, :])

    def received(name):
        group, ref = moved.pop(name)
        group.wait(ref)

    def start_norm():
        received("rows")
        taken[1].wait()
        first_norm()

    def start_cotangent(frame):
        received("cot" + str(frame))
        cot_kept[frame].wait()
        mask_cotangent(frame)

    def send_encoded():
        ours = pl.ds(pl.multiple_of(64 * core, 64), 64)
        theirs = pl.ds(pl.multiple_of(64 * (1 - core), 64), 64)
        group = Group()
        for i, frame in enumerate((blk, across_y)):
            remote(s.enc_send.at[i, theirs, :], encoded.at[frame], sibling, group)
        moved["enc"] = group, s.enc_send.at[0, :, :]
        Local(s.enc_send.at[0, ours, :], encoded.at[blk])
        Local(s.enc_send.at[1, ours, :], encoded.at[across_y])

    def send_grad_rows():
        group = Group()
        for py, pc in blk_peers:
            rows = pl.ds(pl.multiple_of(64 * (2 * py + pc), 64), 64)
            remote(s.gx_send.at[rows, :], s.gx_recv.at[blk], (wide, 2 * py + pc), group)
        moved["grad"] = group, s.gx_recv.at[THREE]
        s.gx_recv[blk] = s.gx_send[mine, :]

    def project_attended():
        s.g_attended[...] = dot_nt(s.g_branch[...], s.w_out[...].reshape(D, D)).astype(BF16)

    def across(name, source, target):
        moved[name] = Group(), target
        remote(source, target, y_peer, moved[name][0])

    def send_normed(part):
        start = 128 * part
        own, other = (s.normed2.at[at : at + 128, :] for at in (start, 256 + start))
        across("normed" + str(part), own, other)

    def take_normed(part):
        received("normed" + str(part))

    def transpose_other():
        s.normed2_t[:, 256:512] = s.normed2[256:512, :].T

    def send_part():
        across("part", s.part_across.at[theirs_rows, :], s.part_recv)

    def send_base():
        across("base", s.base_send, s.base_recv)

    def start_output():
        received("part")
        received("base")
        output()

    def send_back(part):
        rows = slice(128 * part, 128 * part + 128)
        across("back" + str(part), s.back_send.at[rows, :], s.back_recv.at[rows, :])

    def start_second(part):
        received("back" + str(part))
        second_norm_back(part)

    def grad_fc1_weight(j):
        column_grad(s.normed2_t, s.g_hidden, s.g_fc1, lambda side: 768 * side + 384 * j)

    def grad_out_weight():
        column_grad(s.attended_t, s.g_branch, s.g_out, lambda side: 384 * side)

    def grad_qkv_weight(j):
        column_grad(s.normed_t, s.g_mixed, s.g_qkv, lambda side: 768 * j + 384 * side)

    g, r = types.SimpleNamespace(**gathers), types.SimpleNamespace(**scatters)
    g.s0.z()
    assemble("q0")
    g.q0.z()
    assemble("q1")
    g.f1.x()
    assemble("h")
    g.q0.o()
    assemble("q2")
    g.q1.z()
    g.q2.z()
    g.s0.p()
    g.f2.x()
    assemble("o")
    g.q2.o()
    g.q1.o()
    g.q0.p()
    g.h0.y()
    g.h1.y()
    g.o0.z()
    g.o0.o()
    g.q1.p()
    g.q0.f()
    g.q0.g()
    g.s0.f()
    g.h0.z()
    g.q2.p()
    g.h1.z()
    g.s0.g()
    g.o0.p()
    g.q1.f()
    g.h0.w()
    g.q1.g()
    g.q0.l()
    g.h1.w()
    g.q2.f()
    g.h0.v()
    g.q2.g()
    g.s0.l()
    g.q0.d()
    g.f2.z()
    g.s0.d()
    g.o0.f()
    g.f0.z()
    g.h1.v()
    g.o0.g()
    send_cotangent(1)
    send_cotangent(0)
    unpack_small()
    g.f1.z()
    g.h0.x()
    start_norm()
    g.q2.l()
    project_qkv(0)
    g.f2.w()
    g.q1.l()
    attend(0)
    g.q1.d()
    project_qkv(1)
    g.o0.l()
    g.f0.w()
    g.q2.d()
    project_qkv(2)
    g.h1.x()
    attend(1)
    attend(2)
    g.f0.v()
    g.o0.d()
    g.f1.w()
    project_out(0)
    send_normed(0)
    project_out(1)
    start_cotangent(0)
    g.f2.v()
    g.f0.x()
    g.h0.l()
    transpose_out()
    g.f1.v()
    send_normed(1)
    start_cotangent(1)
    g.h0.d()
    feed_own(0)
    g.h1.l()
    take_normed(0)
    g.f2.l()
    feed_other(0, 0)
    g.h1.d()
    feed_own(1)
    feed_other(1, 0)
    g.f1.l()
    take_normed(1)
    feed_other(1, 1)
    feed_other(0, 1)
    g.f0.l()
    weight_grad_fc2(0)
    r.f0.s()
    weight_grad_fc2(2)
    r.f2.s()
    g.f2.d()
    g.f1.d()
    g.f0.d()
    feed_back(1)
    r.f0.z()
    feed_back_other()
    transpose_other()
    send_back(0)
    r.f2.x()
    feed_back(0)
    grad_fc1_weight(1)
    r.h1.s()
    weight_grad_fc2(1)
    r.f1.s()
    send_back(1)
    feed_back_own()
    r.h1.x()
    r.f1.z()
    feed_out(1)
    grad_fc1_weight(0)
    r.f2.z()
    send_part()
    r.h0.s()
    start_second(0)
    feed_out(0)
    r.h0.x()
    start_second(1)
    r.f0.w()
    send_base()
    grad_out_weight()
    project_attended()
    r.o0.s()
    attend_back(0)
    r.h1.z()
    r.f1.w()
    r.o0.p()
    grad_qkv_weight(0)
    r.q0.s()
    attend_back(1)
    grad_qkv_weight(1)
    r.h0.z()
    r.f2.w()
    r.q1.s()
    r.q0.p()
    attend_back(2)
    r.h1.w()
    r.f1.v()
    r.o0.f()
    r.o0.g()
    start_output()
    r.q1.p()
    first_norm_back()
    r.f2.v()
    r.h0.w()
    r.q0.f()
    r.q0.g()
    r.f0.v()
    r.o0.z()
    r.h1.v()
    grad_qkv_weight(2)
    r.q1.f()
    r.q2.s()
    r.q1.g()
    pack_small()
    r.s0.s()
    r.q2.p()
    r.s0.p()
    r.h0.v()
    r.q0.z()
    r.q1.z()
    r.q2.f()
    r.q2.g()
    r.h1.y()
    r.f1.x()
    r.s0.f()
    r.f2.l()
    r.s0.g()
    r.f0.x()
    r.h0.y()
    send_grad_rows()
    r.q2.z()
    send_encoded()
    r.s0.z()
    r.q0.l()
    r.f0.l()
    r.h0.l()
    r.f1.l()
    r.o0.l()
    r.q1.l()
    r.h1.l()
    r.q2.l()
    r.s0.l()
    received("grad")
    s.gx_out[...] = s.gx_recv[...].astype(F32)
    Local(s.gx_out, grad_patches)
    for name in list(moved):
        received(name)
    for arrived, ref in finals:
        if ref is None:
            arrived.wait_recv()
        else:
            arrived.wait(ref)
    for copy in kept:
        copy.wait()
    for spot in range(max(0, len(started) - SENDS), len(started)):
        leave(spot)


def emit_kernel(*refs):
    count = (len(refs) - 3) // 3
    given, made, held = refs[:count], refs[count : 2 * count], refs[2 * count : 3 * count]
    ordered, in_sem, out_sem = refs[3 * count :]
    arrive = [pltpu.make_async_copy(given[i], held[i], in_sem.at[i]) for i in range(count)]
    leave = [
        pltpu.make_async_copy(ordered if i == FC1_OUTPUT else held[i], made[i], out_sem.at[i]) for i in range(count)
    ]
    for copy in arrive:
        copy.start()
    for i in range(count):
        arrive[i].wait()
        if i == FC1_OUTPUT:
            for side in (0, 1):
                for k in range(8):
                    source = held[i][:, 1536 * side + 192 * k : 1536 * side + 192 * k + 192]
                    ordered[:, 384 * k + 192 * side : 384 * k + 192 * side + 192] = source
        leave[i].start()
    for copy in leave:
        copy.wait()


def emit(arrays):
    anywhere = pl.BlockSpec(memory_space=pl.ANY)
    count = len(arrays)
    return list(
        pl.pallas_call(
            emit_kernel,
            out_shape=[jax.ShapeDtypeStruct(a.shape, a.dtype) for a in arrays],
            in_specs=[anywhere] * count,
            out_specs=[anywhere] * count,
            scratch_shapes=[pltpu.VMEM(a.shape, a.dtype) for a in arrays]
            + [pltpu.VMEM(arrays[FC1_OUTPUT].shape, F32)]
            + [pltpu.SemaphoreType.DMA((count,))] * 2,
        )(*arrays)
    )


def fast(
    patches,
    norm_gain,
    norm_bias,
    qkv_weight,
    qv_bias,
    out_weight,
    fc1_weight,
    fc1_bias,
    fc2_weight,
    res_bias,
    cotangent,
    frame_valid,
):
    outputs = [
        ((4, 64, D), BF16),
        ((4, 64, D), F32),
        ((2, 24), F32),
        ((2, 24), F32),
        ((24, 3 * D), F32),
        ((2, 24), F32),
        ((24, D), F32),
        ((24, FF), F32),
        ((1, 96), F32),
        ((96, D), F32),
        ((2, 24), F32),
    ]
    vmem, anywhere = pl.BlockSpec(memory_space=pltpu.VMEM), pl.BlockSpec(memory_space=pl.ANY)
    found = list(pl.pallas_call(
        layer_kernel,
        out_shape=[jax.ShapeDtypeStruct(shape, dtype) for shape, dtype in outputs],
        in_specs=[anywhere if i in (0, 8, 10) else vmem for i in range(11)] + [pl.BlockSpec(memory_space=pltpu.SMEM)],
        out_specs=[anywhere if shape[0] > 2 else vmem for shape, _ in outputs],
        scratch_shapes=list(scratch_shapes().values()),
        compiler_params=pltpu.CompilerParams(
            collective_id=0, has_side_effects=True, vmem_limit_bytes=63 * 2**20
        ),
    )(
        patches,
        norm_gain,
        norm_bias,
        qkv_weight,
        qv_bias,
        out_weight,
        fc1_weight,
        fc1_bias.reshape(1, 96),
        fc2_weight,
        res_bias,
        cotangent,
        frame_valid,
    ))
    found = emit(found)
    found[8] = found[8].reshape(96)
    return tuple(found)


def solution(mesh):
    in_specs = (
        P("wide", "blk", None),
        P(None, ("wide", "blk")),
        P(None, ("wide", "blk")),
        P(("wide", "blk"), None),
        P(None, ("wide", "blk")),
        P(("wide", "blk"), None),
        P(("wide", "blk"), None),
        P(("wide", "blk")),
        P(("wide", "blk"), None),
        P(None, ("wide", "blk")),
        P("wide", "blk", None),
        P("wide"),
    )
    out_specs = (
        P("wide", "blk", None),
        P("wide", "blk", None),
        P(None, ("wide", "blk")),
        P(None, ("wide", "blk")),
        P(("wide", "blk"), None),
        P(None, ("wide", "blk")),
        P(("wide", "blk"), None),
        P(("wide", "blk"), None),
        P(("wide", "blk")),
        P(("wide", "blk"), None),
        P(None, ("wide", "blk")),
    )
    body = fast if dict(mesh.shape) == {"wide": 8, "blk": 4} else local
    return jax.shard_map(body, mesh=mesh, in_specs=in_specs, out_specs=out_specs, check_vma=False)
```

```python
from functools import partial
import math
import types

import jax
import jax.numpy as jnp
from jax import lax
from jax.experimental import pallas as pl
from jax.experimental.pallas import tpu as pltpu
from jax.sharding import PartitionSpec as P

D = 768
HEADS = 12
HEAD = 64


EPSILON = 1e-06


def layer_normalize(token_rows, norm_gain_vector, norm_bias_vector):
    row_average = jnp.mean(token_rows, axis=-1, keepdims=True)
    centered_rows = token_rows - row_average
    inverse_deviation_scale = lax.rsqrt(
        jnp.mean(centered_rows * centered_rows, axis=-1, keepdims=True) + EPSILON
    )
    standardized_rows = centered_rows * inverse_deviation_scale
    return (
        standardized_rows * norm_gain_vector + norm_bias_vector,
        standardized_rows,
        inverse_deviation_scale,
    )


def layer_normalize_backward(
    incoming_gradient, standardized_rows, inverse_deviation_scale, norm_gain_vector
):
    gain_weighted_gradient = incoming_gradient * norm_gain_vector
    inner_product_sum = (
        gain_weighted_gradient
        - jnp.mean(gain_weighted_gradient, axis=-1, keepdims=True)
        - standardized_rows
        * jnp.mean(gain_weighted_gradient * standardized_rows, axis=-1, keepdims=True)
    )
    return (
        inverse_deviation_scale * inner_product_sum,
        jnp.sum(incoming_gradient * standardized_rows, axis=0),
        jnp.sum(incoming_gradient, axis=0),
    )


def frame_groups(array, count):
    return array.reshape((array.shape[0] // count, count) + array.shape[1:])


def attend_forward(query, keys, values):
    scores = jnp.einsum("gqhe,gkhe->ghqk", query, keys, preferred_element_type=jnp.float32)
    top = jnp.max(scores, axis=-1, keepdims=True)
    expo = jnp.exp(scores - top)
    total = jnp.sum(expo, axis=-1, keepdims=True)
    probs = (expo / total).astype(jnp.bfloat16)
    attended = jnp.einsum("ghqk,gkhe->gqhe", probs, values, preferred_element_type=jnp.float32)
    return (attended, top + jnp.log(total))


def attend_back(query, keys, values, logsum, grad_out):
    scores = jnp.einsum("gqhe,gkhe->ghqk", query, keys, preferred_element_type=jnp.float32)
    probs = jnp.exp(scores - logsum)
    grad_probs = jnp.einsum("gqhe,gkhe->ghqk", grad_out, values, preferred_element_type=jnp.float32)
    grad_values = jnp.einsum(
        "ghqk,gqhe->gkhe", probs.astype(jnp.bfloat16), grad_out, preferred_element_type=jnp.float32
    )
    grad_scores = (
        probs * (grad_probs - jnp.sum(probs * grad_probs, axis=-1, keepdims=True))
    ).astype(jnp.bfloat16)
    grad_query = jnp.einsum(
        "ghqk,gkhe->gqhe", grad_scores, keys, preferred_element_type=jnp.float32
    )
    grad_keys = jnp.einsum(
        "ghqk,gqhe->gkhe", grad_scores, query, preferred_element_type=jnp.float32
    )
    return (grad_query, grad_keys, grad_values)


def local(
    patches,
    norm_gain,
    norm_bias,
    qkv_weight,
    qv_bias,
    out_weight,
    fc1_weight,
    fc1_bias,
    fc2_weight,
    res_bias,
    cotangent,
    frame_valid,
):
    frames, frame_rows, width = patches.shape
    count = frames * frame_rows
    group = math.gcd(frames, 8)
    params = (
        lax.all_gather(norm_gain, ("wide", "blk"), axis=1, tiled=True),
        lax.all_gather(norm_bias, ("wide", "blk"), axis=1, tiled=True),
        lax.all_gather(qkv_weight, ("wide", "blk"), axis=0, tiled=True),
        lax.all_gather(qv_bias, ("wide", "blk"), axis=1, tiled=True),
        lax.all_gather(out_weight, ("wide", "blk"), axis=0, tiled=True),
        lax.all_gather(fc1_weight, ("wide", "blk"), axis=0, tiled=True),
        lax.all_gather(fc1_bias, ("wide", "blk"), axis=0, tiled=True),
        lax.all_gather(fc2_weight, ("wide", "blk"), axis=0, tiled=True),
        lax.all_gather(res_bias, ("wide", "blk"), axis=1, tiled=True),
    )
    norm_gain_pair = params[0].astype(jnp.float32)
    norm_bias_pair = params[1].astype(jnp.float32)
    biases_qv = params[3].astype(jnp.float32)
    bias_fc1 = params[6].astype(jnp.float32)
    biases_res = params[8].astype(jnp.float32)
    token_rows = patches.reshape(count, width).astype(jnp.float32)
    valid = jnp.repeat(frame_valid.astype(jnp.float32), frame_rows)[:, None]
    first_branch, first_standardized_rows, first_norm_scale = layer_normalize(
        token_rows, norm_gain_pair[0], norm_bias_pair[0]
    )
    normed = first_branch.astype(jnp.bfloat16)
    mixed = jnp.dot(normed, params[2], preferred_element_type=jnp.float32)
    query = ((mixed[:, :D] + biases_qv[0]) * 0.125).astype(jnp.bfloat16)
    keys = mixed[:, D : 2 * D].astype(jnp.bfloat16).reshape(frames, frame_rows, width)
    values = (
        (mixed[:, 2 * D :] + biases_qv[1]).astype(jnp.bfloat16).reshape(frames, frame_rows, width)
    )
    keys_all, values_all = (
        lax.all_gather(keys, "blk", axis=1, tiled=True),
        lax.all_gather(values, "blk", axis=1, tiled=True),
    )
    query_heads = frame_groups(query.reshape(frames, frame_rows, HEADS, HEAD), group)
    keys_heads = frame_groups(keys_all.reshape(frames, -1, HEADS, HEAD), group)
    values_heads = frame_groups(values_all.reshape(frames, -1, HEADS, HEAD), group)
    attended, logsum = lax.map(
        lambda item: attend_forward(item[0], item[1], item[2]),
        (query_heads, keys_heads, values_heads),
    )
    attended = attended.reshape(count, width).astype(jnp.bfloat16)
    middle_activation = (
        token_rows
        + jnp.dot(attended, params[4], preferred_element_type=jnp.float32)
        + biases_res[0]
    )
    second_branch, second_standardized_rows, second_norm_scale = layer_normalize(
        middle_activation, norm_gain_pair[1], norm_bias_pair[1]
    )
    normed2 = second_branch.astype(jnp.bfloat16)
    hidden = jnp.dot(normed2, params[5], preferred_element_type=jnp.float32) + bias_fc1
    active = jax.nn.gelu(hidden, approximate=False).astype(jnp.bfloat16)
    branch2 = jnp.dot(active, params[7], preferred_element_type=jnp.float32) + biases_res[1]
    encoded = (
        ((middle_activation + branch2) * valid)
        .astype(jnp.bfloat16)
        .reshape(frames, frame_rows, width)
    )
    params = (
        lax.all_gather(norm_gain, ("wide", "blk"), axis=1, tiled=True),
        lax.all_gather(norm_bias, ("wide", "blk"), axis=1, tiled=True),
        lax.all_gather(qkv_weight, ("wide", "blk"), axis=0, tiled=True),
        lax.all_gather(qv_bias, ("wide", "blk"), axis=1, tiled=True),
        lax.all_gather(out_weight, ("wide", "blk"), axis=0, tiled=True),
        lax.all_gather(fc1_weight, ("wide", "blk"), axis=0, tiled=True),
        lax.all_gather(fc1_bias, ("wide", "blk"), axis=0, tiled=True),
        lax.all_gather(fc2_weight, ("wide", "blk"), axis=0, tiled=True),
        lax.all_gather(res_bias, ("wide", "blk"), axis=1, tiled=True),
    )
    grad_out = cotangent.reshape(count, width).astype(jnp.float32) * valid
    grad_branch2 = grad_out.astype(jnp.bfloat16)
    grad_fc2 = jnp.dot(active.T, grad_branch2, preferred_element_type=jnp.float32)
    grad_res_two = jnp.sum(grad_branch2.astype(jnp.float32), axis=0)
    grad_active = jnp.dot(grad_branch2, params[7].T, preferred_element_type=jnp.float32)
    gelu_back = jax.vjp(partial(jax.nn.gelu, approximate=False), hidden)[1]
    grad_hidden = gelu_back(grad_active)[0].astype(jnp.bfloat16)
    grad_fc1 = jnp.dot(normed2.T, grad_hidden, preferred_element_type=jnp.float32)
    grad_bias_fc1 = jnp.sum(grad_hidden.astype(jnp.float32), axis=0)
    normed_input_gradient2 = jnp.dot(grad_hidden, params[5].T, preferred_element_type=jnp.float32)
    second_norm_gradient, second_norm_gain, second_norm_bias = layer_normalize_backward(
        normed_input_gradient2, second_standardized_rows, second_norm_scale, norm_gain_pair[1]
    )
    grad_middle = grad_out + second_norm_gradient
    grad_branch = grad_middle.astype(jnp.bfloat16)
    grad_out_proj = jnp.dot(attended.T, grad_branch, preferred_element_type=jnp.float32)
    grad_res_one = jnp.sum(grad_branch.astype(jnp.float32), axis=0)
    grad_attended = jnp.dot(grad_branch, params[4].T, preferred_element_type=jnp.float32).astype(
        jnp.bfloat16
    )
    grad_heads = frame_groups(grad_attended.reshape(frames, frame_rows, HEADS, HEAD), group)
    grad_query, grad_keys, grad_values = lax.map(
        lambda item: attend_back(item[0], item[1], item[2], item[3], item[4]),
        (query_heads, keys_heads, values_heads, logsum, grad_heads),
    )
    grad_keys, grad_values = (
        lax.psum_scatter(
            grad_keys.reshape(frames, -1, width).astype(jnp.bfloat16),
            "blk",
            scatter_dimension=1,
            tiled=True,
        ).astype(jnp.float32),
        lax.psum_scatter(
            grad_values.reshape(frames, -1, width).astype(jnp.bfloat16),
            "blk",
            scatter_dimension=1,
            tiled=True,
        ).astype(jnp.float32),
    )
    grad_query = grad_query.reshape(count, width).astype(jnp.bfloat16) * 0.125
    grad_keys = grad_keys.reshape(count, width).astype(jnp.bfloat16)
    grad_values = grad_values.reshape(count, width).astype(jnp.bfloat16)
    grad_mixed = jnp.concatenate([grad_query, grad_keys, grad_values], axis=1)
    grad_qkv = jnp.dot(normed.T, grad_mixed, preferred_element_type=jnp.float32)
    grad_qv = jnp.stack(
        [
            jnp.sum(grad_query.astype(jnp.float32), axis=0),
            jnp.sum(grad_values.astype(jnp.float32), axis=0),
        ]
    )
    normed_input_gradient = jnp.dot(grad_mixed, params[2].T, preferred_element_type=jnp.float32)
    first_norm_gradient, first_norm_gain, first_norm_bias = layer_normalize_backward(
        normed_input_gradient, first_standardized_rows, first_norm_scale, norm_gain_pair[0]
    )
    grad_rows = (grad_middle + first_norm_gradient).reshape(frames, frame_rows, width)
    grad_gain = jnp.stack([first_norm_gain, second_norm_gain])
    grad_shift = jnp.stack([first_norm_bias, second_norm_bias])
    grad_res = jnp.stack([grad_res_one, grad_res_two])
    summed = (
        lax.psum_scatter(grad_gain, ("wide", "blk"), scatter_dimension=1, tiled=True),
        lax.psum_scatter(grad_shift, ("wide", "blk"), scatter_dimension=1, tiled=True),
        lax.psum_scatter(grad_qkv, ("wide", "blk"), scatter_dimension=0, tiled=True),
        lax.psum_scatter(grad_qv, ("wide", "blk"), scatter_dimension=1, tiled=True),
        lax.psum_scatter(grad_out_proj, ("wide", "blk"), scatter_dimension=0, tiled=True),
        lax.psum_scatter(grad_fc1, ("wide", "blk"), scatter_dimension=0, tiled=True),
        lax.psum_scatter(grad_bias_fc1, ("wide", "blk"), scatter_dimension=0, tiled=True),
        lax.psum_scatter(grad_fc2, ("wide", "blk"), scatter_dimension=0, tiled=True),
        lax.psum_scatter(grad_res, ("wide", "blk"), scatter_dimension=1, tiled=True),
    )
    return (
        encoded,
        grad_rows,
        summed[0],
        summed[1],
        summed[2],
        summed[3],
        summed[4],
        summed[5],
        summed[6],
        summed[7],
        summed[8],
    )


MESH_ID = pl.DeviceIdType.MESH
BF16 = jnp.bfloat16
F32 = jnp.float32
FF = 3072
TOKENS = 256
ROWS = 64
ALL, THREE, BOTH = pl.ds(0, 4), pl.ds(0, 3), pl.ds(0, 2)
GATHER_UNITS = (
    ("q0", 0, 0, 3, -1, 0),
    ("q1", 1, 0, 3, -2, 0),
    ("q2", 2, 0, 3, -2, 0),
    ("o0", 3, 0, 3, -1, 0),
)
SCATTER_UNITS = (
    ("o0", 3, 0, 3, 2, 0),
    ("q0", 0, 0, 3, 2, 0),
    ("q1a", 1, 0, 2, 2, 0),
    ("q1b", 1, 2, 1, 2, 0),
    ("q2a", 2, 0, 2, 2, 0),
    ("q2b", 2, 2, 1, 2, 0),
)
GATHER_FC2, SCATTER_FC2 = (1, 0, 0), (0, 0, 1)
GATHER_LINES = dict(h=(1, 1), f=(1, 1, 1))
SCATTER_LINES = dict(h=(1, 1), f=(1, 1, 1))
FIRST_UNIT = "q0"


PIECES = (((0, 12, 7), (6, 1, 13)), ((2, 14, 9), (8, 3, 15)), ((4, 16, 11), (10, 5, 17)))


def piece(j, side, t):
    first, second = PIECES[j][0][t], PIECES[j][1][t]
    return 128 * (first + side * (second - first))


def pair_places(j, i):
    return 768 * j + 512 * i, 768 * j + 384 - 128 * i, 768 * j + 128 + 512 * i


def dot(left, right):
    return lax.dot_general(left, right, (((1,), (0,)), ((), ())), preferred_element_type=F32)


def dot_nt(left, right):
    return lax.dot_general(left, right, (((1,), (1,)), ((), ())), preferred_element_type=F32)


def dot_tn(left, right):
    return lax.dot_general(left, right, (((0,), (0,)), ((), ())), preferred_element_type=F32)


SENDS, ARRIVALS, KEPT = 40, 145, 10
FC1_OUTPUT, ROWS_OUTPUT = 7, 1


def scratch_shapes():
    def vm(*shape, dtype=BF16):
        return pltpu.VMEM(shape, dtype)

    return dict(
        w_small=vm(4, 4, 16, 256),
        w_qkv=vm(4, 4, 48, 2304),
        w_out=vm(4, 4, 48, 768),
        w_fc1=vm(4, 4, 48, 1536),
        w_fc2=vm(4, 2, 2, 96, 768),
        fc1_other=vm(48, 768),
        own_small=vm(16, 128, dtype=F32),
        pair_rows=vm(48, 1536, dtype=F32),
        pair_send=vm(24, 1536, dtype=F32),
        pair_rows_h=vm(48, 1536, dtype=F32),
        pair_send_h=vm(24, 1536, dtype=F32),
        par=vm(16, 768, dtype=F32),
        par_fc1=vm(8, 1536, dtype=F32),
        rows_in=vm(256, 768),
        cot_in=vm(512, 768),
        normed=vm(256, 768),
        normed_t=vm(768, 256),
        mixed=vm(256, 2304),
        attended=vm(256, 768),
        attended_t=vm(768, 256),
        middle=vm(256, 768, dtype=F32),
        normed2=vm(512, 768),
        normed2_t=vm(768, 512),
        slope=vm(512, 1536, dtype=F32),
        active=vm(512, 1536),
        g_hidden=vm(512, 1536),
        active_t=vm(16, 96, 512),
        g_branch2=vm(512, 768),
        part_across=vm(256, 768),
        part_recv=vm(128, 768),
        base_send=vm(128, 768),
        base_recv=vm(128, 768),
        back_send=vm(256, 768),
        back_recv=vm(256, 768),
        other=vm(256, 768, dtype=F32),
        total=vm(256, 768, dtype=F32),
        g_middle=vm(256, 768, dtype=F32),
        g_branch=vm(256, 768),
        g_attended=vm(256, 768),
        g_mixed=vm(256, 2304),
        enc_send=vm(2, 128, 768),
        gx_send=vm(256, 768),
        sums=vm(16, 768, dtype=F32),
        sums_fc1=vm(8, 1536, dtype=F32),
        g_small=vm(4, 4, 16, 256),
        g_fc1=vm(4, 4, 48, 1536),
        g_fc2=vm(4, 2, 2, 96, 768),
        g_out=vm(4, 4, 48, 768),
        g_qkv=vm(4, 4, 48, 2304),
        pr_small=vm(4, 4, 16, 128),
        pr_a=vm(4, 4, 48, 1536),
        pr_fc1=vm(4, 4, 48, 768),
        pr_fc2=vm(4, 2, 2, 96, 384),
        dx_small=vm(4, 16, 128),
        dx_a=vm(4, 48, 1536),
        px_small=vm(4, 16, 128),
        px_a=vm(4, 48, 1536),
        px2_a=vm(4, 2, 48, 1536),
        send_a=vm(48, 1536),
        px_fc1=vm(4, 2, 48, 768),
        px_fc2=vm(4, 2, 96, 384),
        py_small=vm(4, 16, 128),
        py_a=vm(4, 48, 1536),
        py_fc1=vm(48, 768),
        pz_small=vm(3, 16, 128),
        pz_a=vm(3, 48, 1536),
        pz_fc1=vm(3, 2, 48, 768),
        pz_fc2=vm(3, 2, 96, 384),
        bz_a=vm(3, 4, 48, 1536),
        cz_a=vm(3, 4, 48, 1536),
        qz_a=vm(3, 48, 1536),
        qz_fc1=vm(3, 2, 48, 768),
        qz_fc2=vm(3, 2, 96, 384),
        bz_fc2=vm(3, 2, 2, 96, 384),
        cz_fc2=vm(3, 2, 2, 96, 384),
        last_a=vm(48, 1536, dtype=F32),
        last_fc1=vm(2, 48, 768, dtype=F32),
        send_fc1=vm(48, 768),
        last_fc2=vm(96, 384, dtype=F32),
        kept_fc2=vm(96, 384, dtype=F32),
        local_sem=pltpu.SemaphoreType.DMA((KEPT,)),
        send_sem=pltpu.SemaphoreType.DMA((SENDS,)),
        recv_sem=pltpu.SemaphoreType.DMA((ARRIVALS,)),
    )


def layer_kernel(
    patches,
    norm_gain,
    norm_bias,
    qkv_weight,
    qv_bias,
    out_weight,
    fc1_weight,
    fc1_bias,
    fc2_weight,
    res_bias,
    cotangent,
    frame_valid,
    encoded,
    grad_patches,
    grad_gain,
    grad_shift,
    grad_qkv,
    grad_qv,
    grad_out,
    grad_fc1,
    grad_fc1_bias,
    grad_fc2,
    grad_res,
    *scratch,
):
    s = types.SimpleNamespace(**dict(zip(scratch_shapes(), scratch)))
    wide, blk = lax.axis_index("wide"), lax.axis_index("blk")
    z, x = lax.div(wide, 2), lax.rem(wide, 2)
    y, core = lax.div(blk, 2), lax.rem(blk, 2)
    here, at_x, at_y, at_d = 2 * x + y, 2 * (1 - x) + y, 2 * x + 1 - y, 2 * (1 - x) + 1 - y
    sibling = (wide, 2 * y + 1 - core)
    x_peer = (2 * z + 1 - x, blk)
    y_peer = (wide, 2 * (1 - y) + core)
    d_peer = (2 * z + 1 - x, 2 * (1 - y) + core)
    y_cross = (wide, 2 * (1 - y) + 1 - core)
    z_of = [lax.rem(z + step, 4) for step in range(4)]
    z_peers = [(2 * z_of[step] + x, blk) for step in range(4)]
    z_order = (z_peers[1], z_peers[3], z_peers[2])
    inner, end = lax.rem(z + 1, 4) >= 2, lax.rem(z + 1, 4) < 2
    z_in, z_out = 1 + lax.rem(z, 2), 3 * lax.div(z, 2)
    in_peer, out_peer = (2 * z_in + x, blk), (2 * z_out + x, blk)
    blk_peers = [(y, 1 - core), (1 - y, core), (1 - y, 1 - core)]

    barrier = pltpu.get_barrier_semaphore()
    peers = [sibling, x_peer, y_peer, d_peer, y_cross] + z_peers[1:]
    for peer in peers:
        pl.semaphore_signal(barrier, inc=1, device_id=peer, device_id_type=MESH_ID)

    started, groups = [], []

    class Group:
        def __init__(self):
            self.sem = s.recv_sem.at[len(groups)]
            groups.append(self)

        def wait(self, ref):
            pltpu.make_async_copy(ref, ref, self.sem).wait()

    def leave(spot):
        copy, only = started[spot]
        if only is None:
            copy.wait_send()
        else:
            pl.when(only)(copy.wait_send)

    def prepare(source, target, peer, group=None, only=None):
        spot = len(started)
        if spot >= SENDS:
            leave(spot - SENDS)
        copy = pltpu.make_async_remote_copy(
            src_ref=source,
            dst_ref=target,
            send_sem=s.send_sem.at[spot % SENDS],
            recv_sem=(group or Group()).sem,
            device_id=peer,
            device_id_type=MESH_ID,
        )
        started.append((copy, only))
        return copy

    def remote(source, target, peer, group=None, only=None):
        copy = prepare(source, target, peer, group, only)
        if only is None:
            copy.start()
        else:
            pl.when(only)(copy.start)
        return copy

    kept = []

    class Local:
        def __init__(self, source, target):
            self.copy, self.waited = pltpu.make_async_copy(source, target, s.local_sem.at[len(kept)]), False
            self.copy.start()
            kept.append(self)

        def wait(self):
            if not self.waited:
                self.waited = True
                self.copy.wait()

    class Written:
        def __init__(self, ref):
            self.ref, self.arrived, self.copy = ref, Group(), None
            self.sem = s.local_sem.at[len(kept)]
            kept.append(self)

        def write(self, source, target):
            pltpu.make_async_copy(source, target, self.sem).start()

        def wait(self):
            self.arrived.wait(self.ref)
            pltpu.make_async_copy(self.ref, self.ref, self.sem).wait()

    def lanes(start, size):
        return pl.ds(pl.multiple_of(start, 128), size)

    mine = pl.ds(pl.multiple_of(64 * blk, 64), 64)
    taken = [Local(fc2_weight, s.w_fc2.at[z, x, core]), Local(patches.at[blk], s.rows_in.at[mine, :])]
    s.own_small[...] = jnp.zeros((16, 128), F32)
    s.sums[...] = jnp.zeros((16, D), F32)
    s.own_small[0:2, 0:24] = norm_gain[...].astype(F32)
    s.own_small[2:4, 0:24] = norm_bias[...].astype(F32)
    s.own_small[4:6, 0:24] = qv_bias[...].astype(F32)
    s.own_small[6:8, 0:24] = res_bias[...].astype(F32)
    s.own_small[8:9, 0:96] = fc1_bias[...].astype(F32)
    s.w_small[z, here, :, lanes(128 * core, 128)] = s.own_small[...].astype(BF16)
    own_rows = pl.ds(pl.multiple_of(24 * core, 8), 24)
    pairs = {}

    def prepare_rows(name):
        if name == "h":
            theirs = fc1_weight[:, lanes((1 - core) * 1536, 1536)].astype(F32)
            ours = fc1_weight[:, lanes(core * 1536, 1536)].astype(F32)
            for side in (0, 1):
                for k in range(4):
                    at, found = 768 * side + 192 * k, 384 * k + 192 * side
                    s.pair_send_h[:, at : at + 192] = theirs[:, found : found + 192]
                    s.pair_rows_h[own_rows, at : at + 192] = ours[:, found : found + 192]
            return
        j = 3 if name == "o" else int(name[1])
        for t in range(3):
            ref, at = (out_weight if name == "o" else qkv_weight), slice(384 * j + 128 * t, 384 * j + 128 * t + 128)
            columns = (lambda side: 384 * side + 128 * t) if name == "o" else partial(piece, j, t=t)
            s.pair_send[:, at] = ref[:, lanes(columns(1 - core), 128)].astype(F32)
            s.pair_rows[own_rows, at] = ref[:, lanes(columns(core), 128)].astype(F32)

    def send_pair(name):
        source, target = s.pair_send_h, s.pair_rows_h.at[own_rows, :]
        if name != "h":
            j = 3 if name == "o" else int(name[1])
            columns = slice(384 * j, 384 * j + 384)
            source, target = s.pair_send.at[:, columns], s.pair_rows.at[own_rows, columns]
        pairs[name] = remote(source, target, sibling)

    def exchange(name):
        prepare_rows(name)
        send_pair(name)

    prepare_rows(FIRST_UNIT)

    pl.semaphore_wait(barrier, len(peers))

    send_pair(FIRST_UNIT)


    class Direct:
        def __init__(self, block):
            self.block, self.arrived = block, Group()

        def start(self):
            own = self.block(z)
            for peer in z_order:
                remote(own, own, peer, self.arrived)

        def wait(self):
            self.arrived.wait(self.block(THREE))

    class Line:
        def __init__(self, block):
            self.block, self.first = block, len(groups)
            self.arrived = [Group() for _ in range(3)]

        def start(self):
            own = self.block(z)
            to_in = types.SimpleNamespace(sem=s.recv_sem.at[self.first + lax.div(lax.rem(z + 1, 4), 2)])
            remote(own, own, in_peer, to_in)
            remote(own, own, out_peer, self.arrived[0], inner)

        def pass_on(self):
            outer, other = self.block(z_out), self.block(z_in)
            inward = prepare(outer, outer, in_peer, self.arrived[2], inner)
            outward = prepare(other, other, out_peer, self.arrived[1], inner)

            @pl.when(inner)
            def _():
                self.arrived[0].wait(outer)
                inward.start()
                self.arrived[1].wait(other)
                outward.start()

        def pass_last(self):
            far = self.block(3 - z_out)
            outward = prepare(far, far, out_peer, self.arrived[2], inner)

            @pl.when(inner)
            def _():
                self.arrived[2].wait(far)
                outward.start()

        def wait(self):
            @pl.when(end)
            def _():
                for arrived, level in zip(self.arrived, (z_in, 3 - z_in, 3 - z)):
                    arrived.wait(self.block(level))

    class DirectSum:
        def __init__(self, own, parts, _):
            self.own, self.parts, self.arrived = own, parts, Group()

        def start(self):
            for step in (1, 3, 2):
                remote(self.own(z_of[step]), self.parts(step - 1), z_peers[step], self.arrived)

        def wait(self):
            self.arrived.wait(self.parts(THREE))

        def summed(self, view):
            found = view(self.own(z))[...].astype(F32)
            for i in range(3):
                found = found + view(self.parts(i))[...].astype(F32)
            return found

    class LineSum:
        def __init__(self, own, parts, more):
            self.own, self.parts, self.more = own, parts, more
            self.arrived = [Group() for _ in range(3)]

        def start(self):
            remote(self.own(pl.ds(1 - lax.div(z, 2), 3)), self.parts(THREE), in_peer, self.arrived[0], end)

        def pass_on(self):
            source = self.own(pl.ds(2 - 2 * lax.div(z, 2), 2))
            inward = prepare(source, self.more(BOTH), in_peer, self.arrived[1], inner)

            @pl.when(inner)
            def _():
                self.arrived[0].wait(self.parts(THREE))
                for level in (z_in, 3 - z_out):
                    ref = self.own(level)
                    ref[...] = ref[...] + self.parts(level - 1 + lax.div(z, 2))[...]
                inward.start()

        def pass_last(self):
            outward = prepare(self.own(z_out), self.more(2), out_peer, self.arrived[2], inner)

            @pl.when(inner)
            def _():
                self.arrived[1].wait(self.more(BOTH))
                base = 2 * lax.div(z, 2)
                ref = self.own(z_out)
                ref[...] = ref[...] + self.more(z_out - base)[...]
                outward.start()
                ref = self.own(z)
                found = ref[...].astype(F32) + self.parts(z - 1 + lax.div(z, 2))[...].astype(F32)
                ref[...] = (found + self.more(z - base)[...].astype(F32)).astype(BF16)

        def wait(self):
            @pl.when(end)
            def _():
                self.arrived[2].wait(self.more(2))
                ref = self.own(z)
                ref[...] = ref[...] + self.more(2)[...]

        def summed(self, view):
            return view(self.own(z))[...].astype(F32)

    def wait_fc2():
        taken[0].wait()

    class Steps:
        def w(self):
            self.line.pass_on()

        def v(self):
            self.line.pass_last()

    class Gather(Steps):
        def __init__(self, part, low, line):
            self.part, self.low, self.high = part, pl.ds(0, low), pl.ds(low, 4 - low)
            self.by_x, self.by_y, self.far, self.pair = (Group() for _ in range(4))
            self.line = line(lambda levels: part(levels, here))

        def z(self):
            self.line.start()

        def p(self):
            self.line.wait()
            self.share(self.part(ALL, here))

        def share(self, block):
            remote(block, block, x_peer, self.by_x)
            remote(block, block, y_peer, self.by_y)
            remote(block, block, sibling, self.pair)

        def f(self):
            column = self.part(ALL, at_x)
            self.by_x.wait(column)
            some = self.part(self.low, at_x)
            remote(some, some, y_peer, self.far)
            remote(column, column, sibling, self.pair)

        def g(self):
            column = self.part(ALL, at_y)
            self.by_y.wait(column)
            some = self.part(self.high, at_y)
            remote(some, some, x_peer, self.far)
            remote(column, column, sibling, self.pair)

        def l(self):
            column = self.part(ALL, at_d)
            self.far.wait(column)
            remote(column, column, sibling, self.pair)

        def d(self):
            self.pair.wait(self.part(ALL, ALL))

    class FineGather(Gather):
        def z(self):
            own = self.part(z, here)
            self.z_copies = [remote(own, own, peer) for peer in z_order]

        def o(self):
            self.share(self.part(z, here))

        def p(self):
            for step, copy in zip((1, 3, 2), self.z_copies):
                copy.wait_recv()
                self.share(self.part(z_of[4 - step], here))

    class SquareGather(Steps):
        def __init__(self, part, line):
            self.part, self.square, self.pair = part, Group(), Group()
            self.line = line(lambda levels: part(levels, ALL))

        def p(self):
            own = self.part(z, here)
            for peer in (x_peer, y_peer, d_peer):
                remote(own, own, peer, self.square)

        def z(self):
            self.square.wait(self.part(z, THREE))
            self.line.start()
            level = self.part(z, ALL)
            remote(level, level, sibling, self.pair)

        def l(self):
            self.line.wait()
            for step in (1, 2, 3):
                level = self.part(z_of[step], ALL)
                remote(level, level, sibling, self.pair)

        def d(self):
            self.pair.wait(self.part(ALL, ALL))

    class PlaneGather(Steps):
        def __init__(self, part, line, across=None):
            self.part, self.across, self.pair = part, across, Group()
            self.line = line(lambda levels: part(levels, x))

        def y(self):
            source, target = self.across
            self.y_copy = remote(source, target, y_peer)

        def z(self):
            if self.across:
                self.y_copy.wait_recv()
            else:
                wait_fc2()
            self.line.start()

        def x(self):
            self.line.wait()
            column = self.part(ALL, x)
            self.x_copy = remote(column, column, x_peer)
            remote(column, column, sibling, self.pair)

        def l(self):
            self.x_copy.wait_recv()
            column = self.part(ALL, 1 - x)
            remote(column, column, sibling, self.pair)

        def d(self):
            self.pair.wait(self.part(ALL, BOTH))

    class AcrossGather(Steps):
        def __init__(self, part, line):
            self.part, self.pair = part, Group()
            self.line = line(lambda levels: part(levels, BOTH))

        def x(self):
            wait_fc2()
            own = self.part(z, x)
            self.x_copy = remote(own, own, x_peer)

        def z(self):
            self.x_copy.wait_recv()
            self.line.start()
            level = self.part(z, BOTH)
            remote(level, level, sibling, self.pair)

        def l(self):
            self.line.wait()
            for step in (1, 2, 3):
                level = self.part(z_of[step], BOTH)
                remote(level, level, sibling, self.pair)

        def d(self):
            self.pair.wait(self.part(ALL, BOTH))

    def column_part(ref, start, size):
        return lambda levels, place: ref.at[levels, place, :, lanes(start, size)]

    def column_gather(ref, start, size, way, chained):
        part, line = column_part(ref, start, size), Line if chained else Direct
        if way == 9:
            own = part(z, here)
            sides = lambda levels, side: part(levels, ALL if side is BOTH else pl.ds(2 * side, 2))
            return PlaneGather(sides, line, (own, own))
        if way == 0:
            return SquareGather(part, line)
        return (Gather if way > 0 else FineGather)(part, abs(way), line)

    gathers = {"s0": column_gather(s.w_small, 128 * core, 128, 2, 0)}
    for name, j, start, size, way, chained in GATHER_UNITS:
        if j < 3:
            ref, first = s.w_qkv, 768 * j + 384 * core
        else:
            ref, first = s.w_out, 384 * core
        gathers[name] = column_gather(ref, first + 128 * start, 128 * size, way, chained)

    def fc1_gather(j):
        columns = lanes(768 * core + 384 * j, 384)
        return PlaneGather(
            lambda levels, side: s.w_fc1.at[levels, ALL if side is BOTH else pl.ds(2 * side, 2), :, columns],
            Line if GATHER_LINES["h"][j] else Direct,
            (s.fc1_other.at[:, 384 * j : 384 * j + 384], s.w_fc1.at[z, here, :, columns]),
        )

    def fc2_gather(j, size, way):
        rows = pl.ds(size * j, size)
        part = lambda levels, side: s.w_fc2.at[levels, side, core, rows, :]
        return (PlaneGather if way else AcrossGather)(part, Line if GATHER_LINES["f"][j] else Direct)

    for j in range(2):
        gathers["h" + str(j)] = fc1_gather(j)
    for j, way in enumerate(GATHER_FC2):
        gathers["f" + str(j)] = fc2_gather(j, 96 // len(GATHER_FC2), way)

    def assemble(name):
        pairs[name].wait_recv()
        if name == "h":
            halves = lanes(768 * y, 768), lanes(768 * (1 - y), 768)
            s.w_fc1[z, here, :, lanes(768 * core, 768)] = s.pair_rows_h[:, halves[0]].astype(BF16)
            s.fc1_other[...] = s.pair_rows_h[:, halves[1]].astype(BF16)
        elif name == "o":
            s.w_out[z, here, :, lanes(384 * core, 384)] = s.pair_rows[:, 1152:1536].astype(BF16)
        else:
            j = int(name[1])
            found = s.pair_rows[:, 384 * j : 384 * j + 384].astype(BF16)
            s.w_qkv[z, here, :, lanes(768 * j + 384 * core, 384)] = found


    def by_rows(body, carry=None):
        def step(i, held):
            return body(pl.ds(pl.multiple_of(ROWS * i, ROWS), ROWS), held)

        return lax.fori_loop(0, TOKENS // ROWS, step, carry)

    def over(shape, axis):
        return lax.broadcasted_iota(jnp.int32, shape, axis)

    def piece24(columns):
        return lax.shift_right_logical(columns * 43691, 20)

    def piece96(columns):
        return lax.shift_right_logical(columns * 10923, 20)

    def spread24():
        columns = over((128, D), 1)
        return (columns - 24 * piece24(columns) == over((128, D), 0)).astype(F32).astype(BF16)

    def hidden_unit(columns):
        return columns + 192 * lax.shift_right_logical(columns * 21846, 22) + 192 * y

    def spread96():
        columns = hidden_unit(over((128, FF // 2), 1))
        return (columns - 96 * piece96(columns) == over((128, FF // 2), 0)).astype(F32).astype(BF16)

    def unpack_small():
        flat = s.w_small[...].reshape(256, 256)
        chips = lax.shift_right_logical(over((256, D), 0), 4)
        pieces = piece24(over((256, D), 1))
        spread = spread24()
        found = jnp.zeros((16, D), F32)
        for side in (0, 1):
            wide_rows = dot(flat[:, 128 * side : 128 * side + 128], spread)
            wide_rows = jnp.where(pieces == 2 * chips + side, wide_rows, 0.0)
            found = found + jnp.sum(wide_rows.reshape(16, 16, D), axis=0)
        s.par[...] = found
        pick = (over((16, 256), 1) == 16 * over((16, 256), 0) + 8).astype(F32).astype(BF16)
        spread = spread96()
        shape = (16, FF // 2)
        pieces = piece96(hidden_unit(over(shape, 1)))
        found = jnp.zeros(shape, F32)
        for side in (0, 1):
            rows = dot(pick, flat[:, 128 * side : 128 * side + 128]).astype(BF16)
            found = found + jnp.where(pieces == 2 * over(shape, 0) + side, dot(rows, spread), 0.0)
        s.par_fc1[0:1, :] = jnp.sum(found, axis=0, keepdims=True)

    def standardized(rows):
        centered = rows - jnp.mean(rows, axis=-1, keepdims=True)
        scale = lax.rsqrt(jnp.mean(centered * centered, axis=-1, keepdims=True) + EPSILON)
        return centered * scale, scale

    def first_norm():
        def body(rows, _):
            found, _ = standardized(s.rows_in[rows, :].astype(F32))
            s.normed[rows, :] = (found * s.par[0:1, :] + s.par[2:3, :]).astype(BF16)
            return 0

        by_rows(body, 0)
        s.normed_t[...] = s.normed[...].T

    def project_qkv(j):
        found = dot(s.normed[...], s.w_qkv[:, :, :, 768 * j : 768 * j + 768].reshape(D, D))
        for i in (0, 1):
            query, key, value = (slice(at, at + 128) for at in pair_places(0, i))
            natural = slice(128 * (2 * j + i), 128 * (2 * j + i) + 128)
            parts = (
                (query, (found[:, query] + s.par[4:5, natural]) * 0.125),
                (key, found[:, key]),
                (value, found[:, value] + s.par[5:6, natural]),
            )
            for at, part in parts:
                s.mixed[:, 768 * j + at.start : 768 * j + at.stop] = part.astype(BF16)

    def head_masks():
        first = (over((TOKENS, 128), 1) < 64).astype(F32)
        return first.astype(BF16), (1.0 - first).astype(BF16)

    def softmax(scores):
        expo = jnp.exp(scores - jnp.max(scores, axis=-1, keepdims=True))
        return expo * (1.0 / jnp.sum(expo, axis=-1, keepdims=True))

    def attend(j):
        def body(i, _):
            query, key, value = (s.mixed[:, lanes(at, 128)] for at in pair_places(j, i))
            found = jnp.zeros((TOKENS, 128), F32)
            for mask in head_masks():
                probs = softmax(dot_nt(query * mask, key)).astype(BF16)
                found = found + dot(probs, value * mask)
            s.attended[:, lanes(128 * (2 * j + i), 128)] = found.astype(BF16)
            return 0

        lax.fori_loop(0, 2, body, 0)

    def some_rows(body, carry, start, count):
        def step(i, held):
            return body(pl.ds(pl.multiple_of(ROWS * i + start, ROWS), ROWS), held)

        return lax.fori_loop(0, count // ROWS, step, carry)

    def project_out(part):
        half = pl.ds(128 * part, 128)
        s.middle[half, :] = dot(s.attended[half, :], s.w_out[...].reshape(D, D))

        def body(rows, _):
            middle = s.rows_in[rows, :].astype(F32) + (s.middle[rows, :] + s.par[6:7, :])
            s.middle[rows, :] = middle
            found, _ = standardized(middle)
            s.normed2[rows, :] = (found * s.par[1:2, :] + s.par[3:4, :]).astype(BF16)
            return 0

        some_rows(body, 0, 128 * part, 128)

    def transpose_out():
        s.attended_t[...] = s.attended[...].T
        s.normed2_t[:, 0:256] = s.normed2[0:256, :].T

    def feed(j, start, count):
        def body(side, _):
            columns = lanes(768 * side + 384 * j, 384)
            tokens = pl.ds(start, count)
            s.other[0:count, 0:384] = dot(s.normed2[tokens, :], s.w_fc1[:, :, :, columns].reshape(D, 384))

            def gelu(rows, _):
                there = pl.ds(pl.multiple_of(rows.start + start, ROWS), ROWS)
                hidden = s.other[rows, 0:384] + s.par_fc1[0:1, columns]
                bell = jnp.exp(-0.5 * hidden * hidden)
                normal = 0.5 + 0.5 * lax.erf(hidden * (1.0 / math.sqrt(2.0)))
                s.slope[there, columns] = normal + hidden * (bell * (1.0 / math.sqrt(2.0 * math.pi)))
                s.active[there, columns] = (hidden * normal).astype(BF16)
                return 0

            some_rows(gelu, 0, 0, count)
            found = s.active[tokens, columns].T.reshape(4, 96, count)
            s.active_t[pl.ds(8 * side + 4 * j, 4), :, start : start + count] = found
            return 0

        lax.fori_loop(0, 2, body, 0)

    def feed_own(j):
        feed(j, 0, 256)

    def feed_other(j, part):
        feed(j, 256 + 128 * part, 128)

    ours_rows = pl.ds(pl.multiple_of(128 * y, 128), 128)
    theirs_rows = pl.ds(pl.multiple_of(128 * (1 - y), 128), 128)
    across_y = 2 * (1 - y) + core
    valid, valid_across = frame_valid[blk].astype(F32), frame_valid[across_y].astype(F32)

    def mask_cotangent(frame):
        def body(rows, _):
            there = pl.ds(pl.multiple_of(rows.start + 256 * frame, ROWS), ROWS)
            masked = s.cot_in[there, :].astype(F32) * (valid_across if frame else valid)
            s.g_branch2[there, :] = masked.astype(BF16)
            return 0

        by_rows(body, 0)


    class Scatter(Steps):
        every = ALL

        def view(self, ref):
            return ref

        def __init__(self, own, other, pr, dx, dy, px, py, pz, finish, low=2, line=DirectSum, more=None):
            self.own, self.other, self.finish = own, other, finish
            self.pr, self.dx, self.dy, self.px, self.py = pr, dx, dy, px, py
            self.line = line(lambda levels: own(levels, here), pz, more)
            self.square = Group()
            self.low, self.high = pl.ds(0, low), pl.ds(low, 4 - low)

        def s(self):
            self.pair = remote(self.other(), self.pr(ALL, self.every), sibling)

        def add_pair(self):
            self.pair.wait_recv()

            def add(level, _):
                ref = self.own(level, self.every)
                ref[...] = ref[...] + self.pr(level, self.every)[...]
                return 0

            lax.fori_loop(0, 4, add, 0)

        def p(self):
            self.add_pair()
            low, high = self.low, self.high
            self.a = remote(self.own(low, at_d), self.dx(low), x_peer)
            self.b = remote(self.own(high, at_d), self.dy(high), y_peer)
            remote(self.own(low, at_x), self.px(low), x_peer, self.square)
            remote(self.own(high, at_y), self.py(high), y_peer, self.square)

        def f(self):
            self.a.wait_recv()
            ref = self.own(self.low, at_y)
            ref[...] = ref[...] + self.dx(self.low)[...]
            remote(ref, self.py(self.low), y_peer, self.square)

        def g(self):
            self.b.wait_recv()
            ref = self.own(self.high, at_x)
            ref[...] = ref[...] + self.dy(self.high)[...]
            remote(ref, self.px(self.high), x_peer, self.square)

        def z(self):
            self.square.wait(self.own(ALL, BOTH))

            def add(level, _):
                ref = self.own(level, here)
                ref[...] = (
                    ref[...].astype(F32)
                    + self.px(level)[...].astype(F32)
                    + self.py(level)[...].astype(F32)
                ).astype(BF16)
                return 0

            lax.fori_loop(0, 4, add, 0)
            self.line.start()

        def l(self):
            self.line.wait()
            self.finish(self)

        def summed(self, view):
            return self.line.summed(view)

    class SquareScatter(Scatter):
        def __init__(self, own, other, pr, bz, pz, finish, line, more):
            self.own, self.other, self.finish = own, other, finish
            self.pr, self.pz, self.square = pr, pz, Group()
            self.line = line(lambda levels: own(levels, ALL), bz, more)

        def z(self):
            self.add_pair()
            self.line.start()

        def p(self):
            self.line.wait()
            if isinstance(self.line, DirectSum):
                self.own(z, ALL)[...] = self.line.summed(lambda ref: ref).astype(BF16)
            targets = ((at_x, x_peer), (at_y, y_peer), (at_d, d_peer))
            for i, (place, peer) in enumerate(targets):
                remote(self.own(z, place), self.pz(i), peer, self.square)

        def l(self):
            self.square.wait(self.pz(THREE))
            self.finish(self)

        def summed(self, view):
            found = view(self.own(z, here))[...].astype(F32)
            for i in range(3):
                found = found + view(self.pz(i))[...].astype(F32)
            return found

    class PlaneScatter(Scatter):
        def __init__(self, own, other, pr, px, pz, finish, line, more, across=None, view=None):
            self.own, self.other, self.finish, self.across, self.view = own, other, finish, across, view
            self.pr, self.px = pr, px
            self.line = line(lambda levels: own(levels, x), pz, more)

        def x(self):
            self.add_pair()
            self.x_copy = remote(self.own(ALL, 1 - x), self.px(ALL), x_peer)

        def z(self):
            self.x_copy.wait_recv()

            def add(level, _):
                ref = self.own(level, x)
                ref[...] = ref[...] + self.px(level)[...]
                return 0

            lax.fori_loop(0, 4, add, 0)
            self.line.start()

        def y(self):
            self.line.wait()
            source, target = self.across(self)
            self.y_copy = remote(source, target, y_peer)

        def l(self):
            if self.across:
                self.y_copy.wait_recv()
            else:
                self.line.wait()
            self.finish(self)

    class AcrossScatter(Scatter):
        def __init__(self, own, other, pr, bz, px, finish, line, more):
            self.own, self.other, self.finish = own, other, finish
            self.pr, self.px = pr, px
            self.line = line(lambda levels: own(levels, ALL), bz, more)

        def z(self):
            self.add_pair()
            self.line.start()

        def x(self):
            self.line.wait()
            if isinstance(self.line, DirectSum):
                self.own(z, ALL)[...] = self.line.summed(lambda ref: ref).astype(BF16)
            self.x_copy = remote(self.own(z, 1 - x), self.px(), x_peer)

        def l(self):
            self.x_copy.wait_recv()
            self.finish(self)

        def summed(self, view):
            return view(self.own(z, x))[...].astype(F32) + view(self.px())[...].astype(F32)

    def columns_of(ref, columns, size):
        def own(levels, places):
            return ref.at[levels, places, :, lanes(columns(core), size)]

        def other():
            return ref.at[:, :, :, lanes(columns(1 - core), size)]

        return own, other

    def column_scatter(ref, columns, natural, size, spot, output, way, chained):
        at = pl.ds(spot, size)

        def finish(scatter):
            total = scatter.summed(scatter.view)
            if way == 9:
                total = total + s.py_a[0, :, at].astype(F32)
            s.last_a[:, at] = total
            other_rows = pl.ds(pl.multiple_of(24 * (1 - core), 8), 24)
            for t in range(size // 128):
                some = slice(spot + 128 * t, spot + 128 * t + 128)
                target = lanes(natural(core, t), 128)
                remote(s.last_a.at[other_rows, some], output.at[:, target], sibling, columns_written.arrived)
                columns_written.write(s.last_a.at[own_rows, some], output.at[:, target])

        if way == 9:

            def across(scatter):
                s.send_a[:, at] = scatter.summed(lambda ref: ref.at[1 - y]).astype(BF16)
                return s.send_a.at[:, at], s.py_a.at[0, :, at]

            def sides(ref):
                return lambda levels, side: ref(levels, ALL if side is ALL else pl.ds(2 * side, 2))

            own, other = columns_of(ref, columns, size)
            return PlaneScatter(
                sides(own),
                other,
                lambda levels, places: s.pr_a.at[levels, places, :, at],
                lambda levels: s.px2_a.at[levels, :, :, at],
                lambda i: s.bz_a.at[i, BOTH, :, at],
                finish,
                LineSum if chained else DirectSum,
                lambda i: s.cz_a.at[i, BOTH, :, at],
                across,
                lambda ref: ref.at[y],
            )

        if not way:
            return SquareScatter(
                *columns_of(ref, columns, size),
                lambda levels, places: s.pr_a.at[levels, places, :, at],
                lambda i: s.bz_a.at[i, :, :, at],
                lambda i: s.pz_a.at[i, :, at],
                finish,
                LineSum if chained else DirectSum,
                lambda i: s.cz_a.at[i, :, :, at],
            )
        return Scatter(
            *columns_of(ref, columns, size),
            lambda levels, places: s.pr_a.at[levels, places, :, at],
            lambda levels: s.dx_a.at[levels, :, at],
            lambda levels: s.dx_a.at[levels, :, at],
            lambda levels: s.px_a.at[levels, :, at],
            lambda levels: s.py_a.at[levels, :, at],
            lambda i: s.pz_a.at[i, :, at],
            finish,
            way,
            LineSum if chained else DirectSum,
            lambda i: s.qz_a.at[i, :, at],
        )

    def fc1_scatter(j):
        at = slice(384 * j, 384 * j + 384)

        def own_columns(side):
            return lanes(768 * side + 384 * j, 384)

        def own(levels, side):
            places = ALL if side is ALL else pl.ds(2 * side, 2)
            return s.g_fc1.at[levels, places, :, own_columns(core)]

        def across(scatter):
            s.last_fc1[0, :, at] = scatter.summed(lambda ref: ref.at[y])
            s.send_fc1[:, at] = scatter.summed(lambda ref: ref.at[1 - y]).astype(BF16)
            return s.send_fc1.at[:, at], s.py_fc1.at[:, at]

        def finish(scatter):
            s.last_fc1[1, :, at] = s.py_fc1[:, at].astype(F32)
            other_rows = pl.ds(pl.multiple_of(24 * (1 - core), 8), 24)
            for i, half in enumerate((y, 1 - y)):
                target = lanes(1536 * half + 768 * core + 384 * j, 384)
                remote(s.last_fc1.at[i, other_rows, at], grad_fc1.at[:, target], sibling, fc1_written.arrived)
                fc1_written.write(s.last_fc1.at[i, own_rows, at], grad_fc1.at[:, target])

        return PlaneScatter(
            own,
            lambda: s.g_fc1.at[:, :, :, own_columns(1 - core)],
            lambda levels, places: s.pr_fc1.at[levels, places, :, at],
            lambda levels: s.px_fc1.at[levels, :, :, at],
            lambda i: s.pz_fc1.at[i, :, :, at],
            finish,
            LineSum if SCATTER_LINES["h"][j] else DirectSum,
            lambda i: s.qz_fc1.at[i, :, :, at],
            across,
        )

    def fc2_scatter(j, size, way):
        rows = pl.ds(size * j, size)
        half = lanes(384 * core, 384)

        def finish(scatter):
            s.last_fc2[rows, :] = scatter.summed(lambda ref: ref.at[1 - core])
            remote(s.last_fc2.at[rows, :], grad_fc2.at[rows, half], sibling, fc2_written.arrived)
            s.kept_fc2[rows, :] = scatter.summed(lambda ref: ref.at[core])
            fc2_written.write(s.kept_fc2.at[rows, :], grad_fc2.at[rows, half])

        def sides(side):
            return BOTH if side is ALL else side

        own = lambda levels, side: s.g_fc2.at[levels, sides(side), :, rows, half]
        other = lambda: s.g_fc2.at[:, :, :, rows, lanes(384 * (1 - core), 384)]
        pr = lambda levels, side: s.pr_fc2.at[levels, sides(side), :, rows, :]
        if not way:
            bz = lambda i: s.bz_fc2.at[i, :, :, rows, :]
            line = LineSum if SCATTER_LINES["f"][j] else DirectSum
            more = lambda i: s.cz_fc2.at[i, :, :, rows, :]
            return AcrossScatter(own, other, pr, bz, lambda: s.pz_fc2.at[0, :, rows, :], finish, line, more)
        return PlaneScatter(
            own,
            other,
            pr,
            lambda levels: s.px_fc2.at[levels, :, rows, :],
            lambda i: s.pz_fc2.at[i, :, rows, :],
            finish,
            LineSum if SCATTER_LINES["f"][j] else DirectSum,
            lambda i: s.qz_fc2.at[i, :, rows, :],
        )

    def small_finish(scatter):
        found = scatter.summed(lambda ref: ref)
        grad_gain[...] = found[0:2, 0:24]
        grad_shift[...] = found[2:4, 0:24]
        grad_qv[...] = found[4:6, 0:24]
        grad_res[...] = found[6:8, 0:24]
        grad_fc1_bias[...] = found[8:9, 0:96]

    columns_written, fc1_written = Written(s.last_a.at[own_rows, :]), Written(s.last_a.at[own_rows, :])
    fc2_written = Written(s.last_fc2)
    scatters = {}
    for j, way in enumerate(SCATTER_FC2):
        scatters["f" + str(j)] = fc2_scatter(j, 96 // len(SCATTER_FC2), way)
    for j in range(2):
        scatters["h" + str(j)] = fc1_scatter(j)
    for name, j, start, size, way, chained in SCATTER_UNITS:
        if j < 3:
            ref, output, spot, first = s.g_qkv, grad_qkv, 384 + 384 * j, 768 * j
            natural = lambda side, t, j=j, start=start: piece(j, side, start + t)
        else:
            ref, output, spot, first = s.g_out, grad_out, 0, 0
            natural = lambda side, t, start=start: 384 * side + 128 * (start + t)
        columns = lambda side, first=first, start=start: first + 384 * side + 128 * start
        scatters[name] = column_scatter(
            ref, columns, natural, 128 * size, spot + 128 * start, output, way, chained
        )

    scatters["s0"] = Scatter(
        *columns_of(s.g_small, lambda side: 128 * side, 128),
        lambda levels, places: s.pr_small.at[levels, places],
        lambda levels: s.dx_small.at[levels],
        lambda levels: s.dx_small.at[levels],
        lambda levels: s.px_small.at[levels],
        lambda levels: s.py_small.at[levels],
        lambda i: s.pz_small.at[i],
        small_finish,
    )

    def weight_grad_fc2(j):
        size = 96 // len(SCATTER_FC2)
        rows = pl.ds(size * j, size)

        def body(turn, _):
            columns = lanes(384 * (turn * core + (1 - turn) * (1 - core)), 384)
            found = dot(s.active_t[:, rows, :].reshape(16 * size, 512), s.g_branch2[:, columns])
            s.g_fc2[:, :, :, rows, columns] = found.astype(BF16).reshape(4, 2, 2, size, 384)
            return 0

        lax.fori_loop(0, 2, body, 0)

    def column_grad(left, right, ref, columns):
        def body(turn, _):
            at = lanes(columns(turn * core + (1 - turn) * (1 - core)), 384)
            ref[:, :, :, at] = dot(left[...], right[:, at]).astype(BF16).reshape(4, 4, 48, 384)
            return 0

        lax.fori_loop(0, 2, body, 0)

    def feed_back(frame):
        tokens = pl.ds(256 * frame, 256)

        def body(part, _):
            columns = lanes(D * part, D)
            s.other[...] = dot_nt(s.g_branch2[tokens, :], s.w_fc2[pl.ds(2 * part, 2)].reshape(D, D))

            def slope(rows, sums):
                there = pl.ds(pl.multiple_of(rows.start + 256 * frame, ROWS), ROWS)
                found = (s.other[rows, :] * s.slope[there, columns]).astype(BF16)
                s.g_hidden[there, columns] = found
                return sums + jnp.sum(found.astype(F32), axis=0, keepdims=True)

            s.sums_fc1[frame : frame + 1, columns] = by_rows(slope, jnp.zeros((1, D), F32))
            return 0

        lax.fori_loop(0, 2, body, 0)

    def feed_out(frame):
        tokens = pl.ds(256 * frame, 256)
        s.total[...] = jnp.zeros((TOKENS, D), F32)

        def body(part, _):
            weight = s.w_fc2[pl.ds(2 * part, 2)].reshape(D, D)
            s.total[...] += dot(s.active[tokens, lanes(D * part, D)], weight)
            return 0

        lax.fori_loop(0, 2, body, 0)
        if frame:
            s.part_across[...] = s.total[...].astype(BF16)
        else:

            def add(rows, _):
                s.total[rows, :] = s.middle[rows, :] + (s.total[rows, :] + s.par[7:8, :])
                return 0

            by_rows(add, 0)
            s.base_send[...] = (valid * s.total[theirs_rows, :]).astype(BF16)

    def output():
        s.enc_send[0] = (valid * (s.total[ours_rows, :] + s.part_recv[...].astype(F32))).astype(BF16)
        part = valid_across * s.part_across[ours_rows, :].astype(F32)
        s.enc_send[1] = (s.base_recv[...].astype(F32) + part).astype(BF16)

        def body(rows, sums):
            return sums + jnp.sum(s.g_branch2[rows, :].astype(F32), axis=0, keepdims=True)

        s.sums[7:8, :] = by_rows(body, jnp.zeros((1, D), F32))

    def feed_back_rows(start, count):
        found = jnp.zeros((count, D), F32)
        for part in (0, 1):
            columns = slice(D * part, D * part + D)
            hidden = s.g_hidden[pl.ds(start, count), columns]
            found = found + dot_nt(hidden, s.w_fc1[:, :, :, columns].reshape(D, D))
        return found

    def feed_back_own():
        s.other[...] = feed_back_rows(0, 256)

    def feed_back_other():
        s.back_send[...] = feed_back_rows(256, 256).astype(BF16)

    def norm_back(upstream, found, scale, gain):
        weighted = upstream * gain
        return scale * (
            weighted
            - jnp.mean(weighted, axis=-1, keepdims=True)
            - found * jnp.mean(weighted * found, axis=-1, keepdims=True)
        )

    def column_sum(values):
        return jnp.sum(values, axis=0, keepdims=True)

    def second_norm_back(part):
        def rows_back(rows, sums):
            upstream = s.other[rows, :] + s.back_recv[rows, :].astype(F32)
            found, scale = standardized(s.middle[rows, :])
            middle = s.g_branch2[rows, :].astype(F32) + norm_back(upstream, found, scale, s.par[1:2, :])
            s.g_middle[rows, :] = middle
            branch = middle.astype(BF16)
            s.g_branch[rows, :] = branch
            return (
                sums[0] + column_sum(upstream * found),
                sums[1] + column_sum(upstream),
                sums[2] + column_sum(branch.astype(F32)),
            )

        before = [jnp.zeros((1, D), F32)] * 3
        if part:
            before = [s.sums[row : row + 1, :] for row in (1, 3, 6)]
        found = some_rows(rows_back, tuple(before), 128 * part, 128)
        s.sums[1:2, :], s.sums[3:4, :], s.sums[6:7, :] = found

    def attend_back(j):
        def body(i, _):
            spots = [lanes(at, 128) for at in pair_places(j, i)]
            natural = lanes(128 * (2 * j + i), 128)
            query, key, value = (s.mixed[:, spot] for spot in spots)
            upstream = s.g_attended[:, natural]
            g_query, g_key, g_value = (jnp.zeros((TOKENS, 128), F32) for _ in range(3))
            for mask in head_masks():
                probs = softmax(dot_nt(query * mask, key))
                g_probs = dot_nt(upstream * mask, value)
                g_value = g_value + dot_tn(probs.astype(BF16), upstream * mask)
                inner = jnp.sum(probs * g_probs, axis=-1, keepdims=True)
                g_scores = (probs * (g_probs - inner)).astype(BF16)
                g_query = g_query + dot(g_scores, key * mask)
                g_key = g_key + dot_tn(g_scores, query * mask)
            g_query = 0.125 * g_query.astype(BF16).astype(F32)
            g_value = g_value.astype(BF16)
            s.g_mixed[:, spots[0]] = g_query.astype(BF16)
            s.g_mixed[:, spots[1]] = g_key.astype(BF16)
            s.g_mixed[:, spots[2]] = g_value
            s.sums[4:5, natural] = column_sum(g_query)
            s.sums[5:6, natural] = column_sum(g_value.astype(F32))
            return 0

        lax.fori_loop(0, 2, body, 0)

    def first_norm_back():
        s.total[...] = jnp.zeros((TOKENS, D), F32)

        def body(level, _):
            columns = lanes(D * level, D)
            s.total[...] += dot_nt(s.g_mixed[:, columns], s.w_qkv[:, :, :, columns].reshape(D, D))
            return 0

        lax.fori_loop(0, 3, body, 0)

        def rows_back(rows, sums):
            upstream = s.total[rows, :]
            found, scale = standardized(s.rows_in[rows, :].astype(F32))
            result = s.g_middle[rows, :] + norm_back(upstream, found, scale, s.par[0:1, :])
            s.gx_send[rows, :] = result.astype(BF16)
            return (sums[0] + column_sum(upstream * found), sums[1] + column_sum(upstream))

        empty = jnp.zeros((1, D), F32)
        s.sums[0:1, :], s.sums[2:3, :] = by_rows(rows_back, (empty, empty))

    def pack_small():
        chips = lax.shift_right_logical(over((256, D), 0), 4)
        pieces = piece24(over((256, D), 1))
        spread = spread24()
        rows = jnp.broadcast_to(s.sums[...][None], (16, 16, D)).reshape(256, D)
        for side in (0, 1):
            placed = dot_nt(jnp.where(pieces == 2 * chips + side, rows, 0.0).astype(BF16), spread)
            s.g_small[:, :, :, 128 * side : 128 * side + 128] = placed.astype(BF16).reshape(4, 4, 16, 128)
        put = (over((256, 16), 0) == 16 * over((256, 16), 1) + 8).astype(F32).astype(BF16)
        spread = spread96()
        shape = (16, FF // 2)
        pieces = piece96(hidden_unit(over(shape, 1)))
        row = s.sums_fc1[0:1, :] + s.sums_fc1[1:2, :]
        for side in (0, 1):
            mine = pieces == 2 * over(shape, 0) + side
            placed = dot_nt(jnp.where(mine, row, 0.0).astype(BF16), spread).astype(BF16)
            here_ = s.g_small.at[:, :, :, pl.ds(128 * side, 128)]
            here_[...] = here_[...] + dot(put, placed).astype(BF16).reshape(4, 4, 16, 128)

    moved = {}

    def send_rows():
        group = Group()
        for py, pc in blk_peers:
            remote(patches.at[2 * py + pc], s.rows_in.at[mine, :], (wide, 2 * py + pc), group)
        moved["rows"] = group, s.rows_in.at[0:192, :]

    cot_kept = {}

    def send_cotangent(frame):
        group, there = Group(), pl.ds(pl.multiple_of(64 * blk + 256 * frame, 64), 64)
        for py, pc in blk_peers:
            source = cotangent.at[2 * (1 - py if frame else py) + pc]
            remote(source, s.cot_in.at[there, :], (wide, 2 * py + pc), group)
        moved["cot" + str(frame)] = group, s.cot_in.at[256 * frame : 256 * frame + 192, :]
        cot_kept[frame] = Local(cotangent.at[across_y if frame else blk], s.cot_in.at[there, :])

    def received(name):
        group, ref = moved.pop(name)
        group.wait(ref)

    def start_norm():
        received("rows")
        taken[1].wait()
        first_norm()

    def start_cotangent(frame):
        received("cot" + str(frame))
        cot_kept[frame].wait()
        mask_cotangent(frame)

    def send_encoded():
        ours = pl.ds(pl.multiple_of(64 * core, 64), 64)
        theirs = pl.ds(pl.multiple_of(64 * (1 - core), 64), 64)
        group = Group()
        for i, frame in enumerate((blk, across_y)):
            remote(s.enc_send.at[i, theirs, :], encoded.at[frame], sibling, group)
        moved["enc"] = group, s.enc_send.at[0, :, :]
        Local(s.enc_send.at[0, ours, :], encoded.at[blk])
        Local(s.enc_send.at[1, ours, :], encoded.at[across_y])

    def send_grad_rows():
        group = Group()
        for py, pc in blk_peers:
            rows = pl.ds(pl.multiple_of(64 * (2 * py + pc), 64), 64)
            remote(s.gx_send.at[rows, :], grad_patches.at[blk], (wide, 2 * py + pc), group)
        moved["grad"] = group, s.gx_send.at[0:192, :]
        Local(s.gx_send.at[mine, :], grad_patches.at[blk])

    def project_attended():
        s.g_attended[...] = dot_nt(s.g_branch[...], s.w_out[...].reshape(D, D)).astype(BF16)

    def across(name, source, target):
        moved[name] = Group(), target
        remote(source, target, y_peer, moved[name][0])

    def send_normed(part):
        start = 128 * part
        own, other = (s.normed2.at[at : at + 128, :] for at in (start, 256 + start))
        across("normed" + str(part), own, other)

    def take_normed(part):
        received("normed" + str(part))

    def transpose_other():
        s.normed2_t[:, 256:512] = s.normed2[256:512, :].T

    def send_part():
        across("part", s.part_across.at[theirs_rows, :], s.part_recv)

    def send_base():
        across("base", s.base_send, s.base_recv)

    def start_output():
        received("part")
        received("base")
        output()

    def send_back(part):
        rows = slice(128 * part, 128 * part + 128)
        across("back" + str(part), s.back_send.at[rows, :], s.back_recv.at[rows, :])

    def start_second(part):
        received("back" + str(part))
        second_norm_back(part)

    def grad_fc1_weight(j):
        column_grad(s.normed2_t, s.g_hidden, s.g_fc1, lambda side: 768 * side + 384 * j)

    def grad_out_weight():
        column_grad(s.attended_t, s.g_branch, s.g_out, lambda side: 384 * side)

    def grad_qkv_weight(j):
        column_grad(s.normed_t, s.g_mixed, s.g_qkv, lambda side: 768 * j + 384 * side)

    g, r = types.SimpleNamespace(**gathers), types.SimpleNamespace(**scatters)
    send_rows()
    g.s0.z()
    exchange("q2")
    assemble("q0")
    g.q0.z()
    g.f1.x()
    g.f2.x()
    assemble("q2")
    g.q2.z()
    g.q0.o()
    exchange("h")
    exchange("q1")
    exchange("o")
    assemble("q1")
    g.s0.p()
    g.q1.z()
    assemble("o")
    g.o0.z()
    g.q2.o()
    g.o0.o()
    g.q0.p()
    assemble("h")
    g.h1.y()
    g.s0.f()
    g.q1.o()
    g.s0.g()
    g.q2.p()
    g.q0.f()
    g.q0.g()
    g.h0.y()
    g.s0.l()
    g.h1.z()
    g.q1.p()
    g.f2.z()
    g.o0.p()
    g.h1.w()
    g.h0.z()
    g.q2.f()
    g.s0.d()
    unpack_small()
    g.q0.l()
    g.q2.g()
    start_norm()
    g.q1.f()
    g.q1.g()
    g.h1.v()
    g.o0.f()
    send_cotangent(0)
    g.o0.g()
    g.q0.d()
    g.h0.w()
    g.f0.z()
    project_qkv(0)
    attend(0)
    g.h1.x()
    g.q2.l()
    g.q1.l()
    g.h0.v()
    g.q2.d()
    g.q1.d()
    send_cotangent(1)
    g.f0.w()
    g.f1.z()
    project_qkv(1)
    g.o0.l()
    attend(1)
    g.o0.d()
    project_qkv(2)
    g.h0.x()
    g.f2.w()
    attend(2)
    project_out(0)
    g.f0.v()
    send_normed(0)
    start_cotangent(0)
    g.f1.w()
    g.h1.l()
    g.f2.v()
    project_out(1)
    transpose_out()
    g.h1.d()
    send_normed(1)
    feed_own(1)
    g.f1.v()
    start_cotangent(1)
    g.f0.x()
    g.h0.l()
    take_normed(0)
    feed_other(1, 0)
    g.f2.l()
    g.h0.d()
    feed_own(0)
    feed_other(0, 0)
    g.f1.l()
    take_normed(1)
    feed_other(1, 1)
    g.f0.l()
    feed_other(0, 1)
    weight_grad_fc2(1)
    g.f2.d()
    r.f1.s()
    g.f1.d()
    weight_grad_fc2(2)
    g.f0.d()
    r.f2.s()
    feed_back(1)
    r.f1.z()
    feed_back_other()
    send_back(0)
    send_back(1)
    r.f2.x()
    transpose_other()
    feed_back(0)
    grad_fc1_weight(0)
    r.h0.s()
    weight_grad_fc2(0)
    r.f0.s()
    feed_back_own()
    r.h0.x()
    feed_out(1)
    r.f0.z()
    grad_fc1_weight(1)
    r.h1.s()
    start_second(0)
    send_part()
    feed_out(0)
    r.f2.z()
    r.h1.x()
    start_second(1)
    project_attended()
    r.f1.w()
    send_base()
    attend_back(0)
    r.h0.z()
    grad_qkv_weight(0)
    r.q0.s()
    r.f0.w()
    attend_back(1)
    r.q0.p()
    grad_qkv_weight(1)
    r.q1b.s()
    grad_out_weight()
    start_output()
    r.q1a.s()
    r.h1.z()
    r.f2.w()
    r.o0.s()
    r.q1b.p()
    r.q0.f()
    r.q0.g()
    r.f1.v()
    r.q1a.p()
    r.h0.w()
    r.o0.p()
    attend_back(2)
    r.f2.v()
    r.q0.z()
    grad_qkv_weight(2)
    r.q1a.f()
    r.q2b.s()
    r.q1a.g()
    r.h0.v()
    r.f0.v()
    r.q2a.s()
    r.q1b.f()
    r.h1.w()
    r.q2b.p()
    r.o0.f()
    r.o0.g()
    first_norm_back()
    r.q1a.z()
    r.q2b.f()
    r.q2a.p()
    pack_small()
    r.h1.v()
    r.q2b.g()
    r.s0.s()
    r.q0.l()
    r.o0.z()
    r.s0.p()
    r.q1b.g()
    r.q2a.f()
    r.h0.y()
    r.q2a.g()
    r.q2b.z()
    r.s0.f()
    r.h1.y()
    send_grad_rows()
    r.s0.g()
    r.q1b.z()
    r.f1.x()
    r.q2a.z()
    r.f0.x()
    r.q1a.l()
    r.o0.l()
    r.f2.l()
    r.h1.l()
    r.s0.z()
    r.q2b.l()
    r.f1.l()
    r.h0.l()
    r.f0.l()
    r.q1b.l()
    send_encoded()
    r.q2a.l()
    r.s0.l()
    for name in list(moved):
        received(name)
    for copy in kept:
        copy.wait()
    for spot in range(max(0, len(started) - SENDS), len(started)):
        leave(spot)


def emit_kernel(*refs):
    count = (len(refs) - 4) // 3
    given, made, held = refs[:count], refs[count : 2 * count], refs[2 * count : 3 * count]
    ordered, wide_rows, in_sem, out_sem = refs[3 * count :]
    ready = {FC1_OUTPUT: ordered, ROWS_OUTPUT: wide_rows}
    arrive = [pltpu.make_async_copy(given[i], held[i], in_sem.at[i]) for i in range(count)]
    leave = [pltpu.make_async_copy(ready.get(i, held[i]), made[i], out_sem.at[i]) for i in range(count)]
    for copy in arrive:
        copy.start()
    for i in range(count):
        arrive[i].wait()
        if i == ROWS_OUTPUT:
            wide_rows[...] = held[i][...].astype(F32)
        if i == FC1_OUTPUT:
            for side in (0, 1):
                for k in range(8):
                    source = held[i][:, 1536 * side + 192 * k : 1536 * side + 192 * k + 192]
                    ordered[:, 384 * k + 192 * side : 384 * k + 192 * side + 192] = source
        leave[i].start()
    for copy in leave:
        copy.wait()


def emit(arrays):
    anywhere = pl.BlockSpec(memory_space=pl.ANY)
    count = len(arrays)
    dtypes = [F32 if i == ROWS_OUTPUT else a.dtype for i, a in enumerate(arrays)]
    return list(
        pl.pallas_call(
            emit_kernel,
            out_shape=[jax.ShapeDtypeStruct(a.shape, dtype) for a, dtype in zip(arrays, dtypes)],
            in_specs=[anywhere] * count,
            out_specs=[anywhere] * count,
            scratch_shapes=[pltpu.VMEM(a.shape, a.dtype) for a in arrays]
            + [pltpu.VMEM(arrays[i].shape, F32) for i in (FC1_OUTPUT, ROWS_OUTPUT)]
            + [pltpu.SemaphoreType.DMA((count,))] * 2,
        )(*arrays)
    )


def fast(
    patches,
    norm_gain,
    norm_bias,
    qkv_weight,
    qv_bias,
    out_weight,
    fc1_weight,
    fc1_bias,
    fc2_weight,
    res_bias,
    cotangent,
    frame_valid,
):
    outputs = [
        ((4, 64, D), BF16),
        ((4, 64, D), BF16),
        ((2, 24), F32),
        ((2, 24), F32),
        ((24, 3 * D), F32),
        ((2, 24), F32),
        ((24, D), F32),
        ((24, FF), F32),
        ((1, 96), F32),
        ((96, D), F32),
        ((2, 24), F32),
    ]
    vmem, anywhere = pl.BlockSpec(memory_space=pltpu.VMEM), pl.BlockSpec(memory_space=pl.ANY)
    found = list(pl.pallas_call(
        layer_kernel,
        out_shape=[jax.ShapeDtypeStruct(shape, dtype) for shape, dtype in outputs],
        in_specs=[anywhere if i in (0, 8, 10) else vmem for i in range(11)] + [pl.BlockSpec(memory_space=pltpu.SMEM)],
        out_specs=[anywhere if shape[0] > 2 else vmem for shape, _ in outputs],
        scratch_shapes=list(scratch_shapes().values()),
        compiler_params=pltpu.CompilerParams(
            collective_id=0, has_side_effects=True, vmem_limit_bytes=63 * 2**20
        ),
    )(
        patches,
        norm_gain,
        norm_bias,
        qkv_weight,
        qv_bias,
        out_weight,
        fc1_weight,
        fc1_bias.reshape(1, 96),
        fc2_weight,
        res_bias,
        cotangent,
        frame_valid,
    ))
    found = emit(found)
    found[8] = found[8].reshape(96)
    return tuple(found)


def solution(mesh):
    in_specs = (
        P("wide", "blk", None),
        P(None, ("wide", "blk")),
        P(None, ("wide", "blk")),
        P(("wide", "blk"), None),
        P(None, ("wide", "blk")),
        P(("wide", "blk"), None),
        P(("wide", "blk"), None),
        P(("wide", "blk")),
        P(("wide", "blk"), None),
        P(None, ("wide", "blk")),
        P("wide", "blk", None),
        P("wide"),
    )
    out_specs = (
        P("wide", "blk", None),
        P("wide", "blk", None),
        P(None, ("wide", "blk")),
        P(None, ("wide", "blk")),
        P(("wide", "blk"), None),
        P(None, ("wide", "blk")),
        P(("wide", "blk"), None),
        P(("wide", "blk"), None),
        P(("wide", "blk")),
        P(("wide", "blk"), None),
        P(None, ("wide", "blk")),
    )
    body = fast if dict(mesh.shape) == {"wide": 8, "blk": 4} else local
    return jax.shard_map(body, mesh=mesh, in_specs=in_specs, out_specs=out_specs, check_vma=False)
```

```python
from functools import partial
import math
import types

import jax
import jax.numpy as jnp
from jax import lax
from jax.experimental import pallas as pl
from jax.experimental.pallas import tpu as pltpu
from jax.sharding import PartitionSpec as P

D = 768
HEADS = 12
HEAD = 64


EPSILON = 1e-06


def layer_normalize(token_rows, norm_gain_vector, norm_bias_vector):
    row_average = jnp.mean(token_rows, axis=-1, keepdims=True)
    centered_rows = token_rows - row_average
    inverse_deviation_scale = lax.rsqrt(
        jnp.mean(centered_rows * centered_rows, axis=-1, keepdims=True) + EPSILON
    )
    standardized_rows = centered_rows * inverse_deviation_scale
    return (
        standardized_rows * norm_gain_vector + norm_bias_vector,
        standardized_rows,
        inverse_deviation_scale,
    )


def layer_normalize_backward(
    incoming_gradient, standardized_rows, inverse_deviation_scale, norm_gain_vector
):
    gain_weighted_gradient = incoming_gradient * norm_gain_vector
    inner_product_sum = (
        gain_weighted_gradient
        - jnp.mean(gain_weighted_gradient, axis=-1, keepdims=True)
        - standardized_rows
        * jnp.mean(gain_weighted_gradient * standardized_rows, axis=-1, keepdims=True)
    )
    return (
        inverse_deviation_scale * inner_product_sum,
        jnp.sum(incoming_gradient * standardized_rows, axis=0),
        jnp.sum(incoming_gradient, axis=0),
    )


def frame_groups(array, count):
    return array.reshape((array.shape[0] // count, count) + array.shape[1:])


def attend_forward(query, keys, values):
    scores = jnp.einsum("gqhe,gkhe->ghqk", query, keys, preferred_element_type=jnp.float32)
    top = jnp.max(scores, axis=-1, keepdims=True)
    expo = jnp.exp(scores - top)
    total = jnp.sum(expo, axis=-1, keepdims=True)
    probs = (expo / total).astype(jnp.bfloat16)
    attended = jnp.einsum("ghqk,gkhe->gqhe", probs, values, preferred_element_type=jnp.float32)
    return (attended, top + jnp.log(total))


def attend_back(query, keys, values, logsum, grad_out):
    scores = jnp.einsum("gqhe,gkhe->ghqk", query, keys, preferred_element_type=jnp.float32)
    probs = jnp.exp(scores - logsum)
    grad_probs = jnp.einsum("gqhe,gkhe->ghqk", grad_out, values, preferred_element_type=jnp.float32)
    grad_values = jnp.einsum(
        "ghqk,gqhe->gkhe", probs.astype(jnp.bfloat16), grad_out, preferred_element_type=jnp.float32
    )
    grad_scores = (
        probs * (grad_probs - jnp.sum(probs * grad_probs, axis=-1, keepdims=True))
    ).astype(jnp.bfloat16)
    grad_query = jnp.einsum(
        "ghqk,gkhe->gqhe", grad_scores, keys, preferred_element_type=jnp.float32
    )
    grad_keys = jnp.einsum(
        "ghqk,gqhe->gkhe", grad_scores, query, preferred_element_type=jnp.float32
    )
    return (grad_query, grad_keys, grad_values)


def local(
    patches,
    norm_gain,
    norm_bias,
    qkv_weight,
    qv_bias,
    out_weight,
    fc1_weight,
    fc1_bias,
    fc2_weight,
    res_bias,
    cotangent,
    frame_valid,
):
    frames, frame_rows, width = patches.shape
    count = frames * frame_rows
    group = math.gcd(frames, 8)
    params = (
        lax.all_gather(norm_gain, ("wide", "blk"), axis=1, tiled=True),
        lax.all_gather(norm_bias, ("wide", "blk"), axis=1, tiled=True),
        lax.all_gather(qkv_weight, ("wide", "blk"), axis=0, tiled=True),
        lax.all_gather(qv_bias, ("wide", "blk"), axis=1, tiled=True),
        lax.all_gather(out_weight, ("wide", "blk"), axis=0, tiled=True),
        lax.all_gather(fc1_weight, ("wide", "blk"), axis=0, tiled=True),
        lax.all_gather(fc1_bias, ("wide", "blk"), axis=0, tiled=True),
        lax.all_gather(fc2_weight, ("wide", "blk"), axis=0, tiled=True),
        lax.all_gather(res_bias, ("wide", "blk"), axis=1, tiled=True),
    )
    norm_gain_pair = params[0].astype(jnp.float32)
    norm_bias_pair = params[1].astype(jnp.float32)
    biases_qv = params[3].astype(jnp.float32)
    bias_fc1 = params[6].astype(jnp.float32)
    biases_res = params[8].astype(jnp.float32)
    token_rows = patches.reshape(count, width).astype(jnp.float32)
    valid = jnp.repeat(frame_valid.astype(jnp.float32), frame_rows)[:, None]
    first_branch, first_standardized_rows, first_norm_scale = layer_normalize(
        token_rows, norm_gain_pair[0], norm_bias_pair[0]
    )
    normed = first_branch.astype(jnp.bfloat16)
    mixed = jnp.dot(normed, params[2], preferred_element_type=jnp.float32)
    query = ((mixed[:, :D] + biases_qv[0]) * 0.125).astype(jnp.bfloat16)
    keys = mixed[:, D : 2 * D].astype(jnp.bfloat16).reshape(frames, frame_rows, width)
    values = (
        (mixed[:, 2 * D :] + biases_qv[1]).astype(jnp.bfloat16).reshape(frames, frame_rows, width)
    )
    keys_all, values_all = (
        lax.all_gather(keys, "blk", axis=1, tiled=True),
        lax.all_gather(values, "blk", axis=1, tiled=True),
    )
    query_heads = frame_groups(query.reshape(frames, frame_rows, HEADS, HEAD), group)
    keys_heads = frame_groups(keys_all.reshape(frames, -1, HEADS, HEAD), group)
    values_heads = frame_groups(values_all.reshape(frames, -1, HEADS, HEAD), group)
    attended, logsum = lax.map(
        lambda item: attend_forward(item[0], item[1], item[2]),
        (query_heads, keys_heads, values_heads),
    )
    attended = attended.reshape(count, width).astype(jnp.bfloat16)
    middle_activation = (
        token_rows
        + jnp.dot(attended, params[4], preferred_element_type=jnp.float32)
        + biases_res[0]
    )
    second_branch, second_standardized_rows, second_norm_scale = layer_normalize(
        middle_activation, norm_gain_pair[1], norm_bias_pair[1]
    )
    normed2 = second_branch.astype(jnp.bfloat16)
    hidden = jnp.dot(normed2, params[5], preferred_element_type=jnp.float32) + bias_fc1
    active = jax.nn.gelu(hidden, approximate=False).astype(jnp.bfloat16)
    branch2 = jnp.dot(active, params[7], preferred_element_type=jnp.float32) + biases_res[1]
    encoded = (
        ((middle_activation + branch2) * valid)
        .astype(jnp.bfloat16)
        .reshape(frames, frame_rows, width)
    )
    params = (
        lax.all_gather(norm_gain, ("wide", "blk"), axis=1, tiled=True),
        lax.all_gather(norm_bias, ("wide", "blk"), axis=1, tiled=True),
        lax.all_gather(qkv_weight, ("wide", "blk"), axis=0, tiled=True),
        lax.all_gather(qv_bias, ("wide", "blk"), axis=1, tiled=True),
        lax.all_gather(out_weight, ("wide", "blk"), axis=0, tiled=True),
        lax.all_gather(fc1_weight, ("wide", "blk"), axis=0, tiled=True),
        lax.all_gather(fc1_bias, ("wide", "blk"), axis=0, tiled=True),
        lax.all_gather(fc2_weight, ("wide", "blk"), axis=0, tiled=True),
        lax.all_gather(res_bias, ("wide", "blk"), axis=1, tiled=True),
    )
    grad_out = cotangent.reshape(count, width).astype(jnp.float32) * valid
    grad_branch2 = grad_out.astype(jnp.bfloat16)
    grad_fc2 = jnp.dot(active.T, grad_branch2, preferred_element_type=jnp.float32)
    grad_res_two = jnp.sum(grad_branch2.astype(jnp.float32), axis=0)
    grad_active = jnp.dot(grad_branch2, params[7].T, preferred_element_type=jnp.float32)
    gelu_back = jax.vjp(partial(jax.nn.gelu, approximate=False), hidden)[1]
    grad_hidden = gelu_back(grad_active)[0].astype(jnp.bfloat16)
    grad_fc1 = jnp.dot(normed2.T, grad_hidden, preferred_element_type=jnp.float32)
    grad_bias_fc1 = jnp.sum(grad_hidden.astype(jnp.float32), axis=0)
    normed_input_gradient2 = jnp.dot(grad_hidden, params[5].T, preferred_element_type=jnp.float32)
    second_norm_gradient, second_norm_gain, second_norm_bias = layer_normalize_backward(
        normed_input_gradient2, second_standardized_rows, second_norm_scale, norm_gain_pair[1]
    )
    grad_middle = grad_out + second_norm_gradient
    grad_branch = grad_middle.astype(jnp.bfloat16)
    grad_out_proj = jnp.dot(attended.T, grad_branch, preferred_element_type=jnp.float32)
    grad_res_one = jnp.sum(grad_branch.astype(jnp.float32), axis=0)
    grad_attended = jnp.dot(grad_branch, params[4].T, preferred_element_type=jnp.float32).astype(
        jnp.bfloat16
    )
    grad_heads = frame_groups(grad_attended.reshape(frames, frame_rows, HEADS, HEAD), group)
    grad_query, grad_keys, grad_values = lax.map(
        lambda item: attend_back(item[0], item[1], item[2], item[3], item[4]),
        (query_heads, keys_heads, values_heads, logsum, grad_heads),
    )
    grad_keys, grad_values = (
        lax.psum_scatter(
            grad_keys.reshape(frames, -1, width).astype(jnp.bfloat16),
            "blk",
            scatter_dimension=1,
            tiled=True,
        ).astype(jnp.float32),
        lax.psum_scatter(
            grad_values.reshape(frames, -1, width).astype(jnp.bfloat16),
            "blk",
            scatter_dimension=1,
            tiled=True,
        ).astype(jnp.float32),
    )
    grad_query = grad_query.reshape(count, width).astype(jnp.bfloat16) * 0.125
    grad_keys = grad_keys.reshape(count, width).astype(jnp.bfloat16)
    grad_values = grad_values.reshape(count, width).astype(jnp.bfloat16)
    grad_mixed = jnp.concatenate([grad_query, grad_keys, grad_values], axis=1)
    grad_qkv = jnp.dot(normed.T, grad_mixed, preferred_element_type=jnp.float32)
    grad_qv = jnp.stack(
        [
            jnp.sum(grad_query.astype(jnp.float32), axis=0),
            jnp.sum(grad_values.astype(jnp.float32), axis=0),
        ]
    )
    normed_input_gradient = jnp.dot(grad_mixed, params[2].T, preferred_element_type=jnp.float32)
    first_norm_gradient, first_norm_gain, first_norm_bias = layer_normalize_backward(
        normed_input_gradient, first_standardized_rows, first_norm_scale, norm_gain_pair[0]
    )
    grad_rows = (grad_middle + first_norm_gradient).reshape(frames, frame_rows, width)
    grad_gain = jnp.stack([first_norm_gain, second_norm_gain])
    grad_shift = jnp.stack([first_norm_bias, second_norm_bias])
    grad_res = jnp.stack([grad_res_one, grad_res_two])
    summed = (
        lax.psum_scatter(grad_gain, ("wide", "blk"), scatter_dimension=1, tiled=True),
        lax.psum_scatter(grad_shift, ("wide", "blk"), scatter_dimension=1, tiled=True),
        lax.psum_scatter(grad_qkv, ("wide", "blk"), scatter_dimension=0, tiled=True),
        lax.psum_scatter(grad_qv, ("wide", "blk"), scatter_dimension=1, tiled=True),
        lax.psum_scatter(grad_out_proj, ("wide", "blk"), scatter_dimension=0, tiled=True),
        lax.psum_scatter(grad_fc1, ("wide", "blk"), scatter_dimension=0, tiled=True),
        lax.psum_scatter(grad_bias_fc1, ("wide", "blk"), scatter_dimension=0, tiled=True),
        lax.psum_scatter(grad_fc2, ("wide", "blk"), scatter_dimension=0, tiled=True),
        lax.psum_scatter(grad_res, ("wide", "blk"), scatter_dimension=1, tiled=True),
    )
    return (
        encoded,
        grad_rows,
        summed[0],
        summed[1],
        summed[2],
        summed[3],
        summed[4],
        summed[5],
        summed[6],
        summed[7],
        summed[8],
    )


MESH_ID = pl.DeviceIdType.MESH
BF16 = jnp.bfloat16
F32 = jnp.float32
FF = 3072
TOKENS = 256
ROWS = 64
ALL, THREE, BOTH = pl.ds(0, 4), pl.ds(0, 3), pl.ds(0, 2)
GATHER_UNITS = (
    ("q0", 0, 0, 3, -1, 0),
    ("q1", 1, 0, 3, -2, 0),
    ("q2", 2, 0, 3, -2, 0),
    ("o0", 3, 0, 3, -1, 0),
)
SCATTER_UNITS = (
    ("o0", 3, 0, 3, 2, 0),
    ("q0", 0, 0, 3, 2, 0),
    ("q1a", 1, 0, 2, 2, 0),
    ("q1b", 1, 2, 1, 2, 0),
    ("q2a", 2, 0, 2, 2, 0),
    ("q2b", 2, 2, 1, 2, 0),
)
GATHER_FC2, SCATTER_FC2 = (1, 0, 0), (0, 0, 1)
GATHER_LINES = dict(h=(1, 1), f=(1, 1, 1))
SCATTER_LINES = dict(h=(1, 1), f=(1, 1, 1))
FIRST_UNIT = "q0"


PIECES = (((0, 12, 7), (6, 1, 13)), ((2, 14, 9), (8, 3, 15)), ((4, 16, 11), (10, 5, 17)))


def piece(j, side, t):
    first, second = PIECES[j][0][t], PIECES[j][1][t]
    return 128 * (first + side * (second - first))


def pair_places(j, i):
    return 768 * j + 512 * i, 768 * j + 384 - 128 * i, 768 * j + 128 + 512 * i


def dot(left, right):
    return lax.dot_general(left, right, (((1,), (0,)), ((), ())), preferred_element_type=F32)


def dot_nt(left, right):
    return lax.dot_general(left, right, (((1,), (1,)), ((), ())), preferred_element_type=F32)


def dot_tn(left, right):
    return lax.dot_general(left, right, (((0,), (0,)), ((), ())), preferred_element_type=F32)


SENDS, ARRIVALS, KEPT = 40, 145, 10
FC1_OUTPUT, ROWS_OUTPUT = 7, 1


def scratch_shapes():
    def vm(*shape, dtype=BF16):
        return pltpu.VMEM(shape, dtype)

    return dict(
        w_small=vm(4, 4, 16, 256),
        w_qkv=vm(4, 4, 48, 2304),
        w_out=vm(4, 4, 48, 768),
        w_fc1=vm(4, 4, 48, 1536),
        w_fc2=vm(4, 2, 2, 96, 768),
        fc1_other=vm(48, 768),
        own_small=vm(16, 128, dtype=F32),
        pair_rows=vm(48, 1536, dtype=F32),
        pair_send=vm(24, 1536, dtype=F32),
        pair_rows_h=vm(48, 1536, dtype=F32),
        pair_send_h=vm(24, 1536, dtype=F32),
        par=vm(16, 768, dtype=F32),
        par_fc1=vm(8, 1536, dtype=F32),
        rows_in=vm(256, 768),
        cot_in=vm(512, 768),
        normed=vm(256, 768),
        normed_t=vm(768, 256),
        mixed=vm(256, 2304),
        attended=vm(256, 768),
        attended_t=vm(768, 256),
        middle=vm(256, 768, dtype=F32),
        normed2=vm(512, 768),
        normed2_t=vm(768, 512),
        slope=vm(512, 1536, dtype=F32),
        active=vm(512, 1536),
        g_hidden=vm(512, 1536),
        active_t=vm(16, 96, 512),
        g_branch2=vm(512, 768),
        part_across=vm(256, 768),
        part_recv=vm(128, 768),
        base_send=vm(128, 768),
        base_recv=vm(128, 768),
        back_send=vm(256, 768),
        back_recv=vm(256, 768),
        other=vm(256, 768, dtype=F32),
        total=vm(256, 768, dtype=F32),
        g_middle=vm(256, 768, dtype=F32),
        g_branch=vm(256, 768),
        g_attended=vm(256, 768),
        g_mixed=vm(256, 2304),
        enc_send=vm(2, 128, 768),
        gx_send=vm(256, 768),
        sums=vm(16, 768, dtype=F32),
        sums_fc1=vm(8, 1536, dtype=F32),
        g_small=vm(4, 4, 16, 256),
        g_fc1=vm(4, 4, 48, 1536),
        g_fc2=vm(4, 2, 2, 96, 768),
        g_out=vm(4, 4, 48, 768),
        g_qkv=vm(4, 4, 48, 2304),
        pr_small=vm(4, 4, 16, 128),
        pr_a=vm(4, 4, 48, 1536),
        pr_fc1=vm(4, 4, 48, 768),
        pr_fc2=vm(4, 2, 2, 96, 384),
        dx_small=vm(4, 16, 128),
        dx_a=vm(4, 48, 1536),
        px_small=vm(4, 16, 128),
        px_a=vm(4, 48, 1536),
        px2_a=vm(4, 2, 48, 1536),
        send_a=vm(48, 1536),
        px_fc1=vm(4, 2, 48, 768),
        px_fc2=vm(4, 2, 96, 384),
        py_small=vm(4, 16, 128),
        py_a=vm(4, 48, 1536),
        py_fc1=vm(48, 768),
        pz_small=vm(3, 16, 128),
        pz_a=vm(3, 48, 1536),
        pz_fc1=vm(3, 2, 48, 768),
        pz_fc2=vm(3, 2, 96, 384),
        bz_a=vm(3, 4, 48, 1536),
        cz_a=vm(3, 4, 48, 1536),
        qz_a=vm(3, 48, 1536),
        qz_fc1=vm(3, 2, 48, 768),
        qz_fc2=vm(3, 2, 96, 384),
        bz_fc2=vm(3, 2, 2, 96, 384),
        cz_fc2=vm(3, 2, 2, 96, 384),
        last_a=vm(48, 1536, dtype=F32),
        last_fc1=vm(2, 48, 768, dtype=F32),
        send_fc1=vm(48, 768),
        last_fc2=vm(96, 384, dtype=F32),
        kept_fc2=vm(96, 384, dtype=F32),
        local_sem=pltpu.SemaphoreType.DMA((KEPT,)),
        send_sem=pltpu.SemaphoreType.DMA((SENDS,)),
        recv_sem=pltpu.SemaphoreType.DMA((ARRIVALS,)),
    )


def layer_kernel(
    patches,
    norm_gain,
    norm_bias,
    qkv_weight,
    qv_bias,
    out_weight,
    fc1_weight,
    fc1_bias,
    fc2_weight,
    res_bias,
    cotangent,
    frame_valid,
    encoded,
    grad_patches,
    grad_gain,
    grad_shift,
    grad_qkv,
    grad_qv,
    grad_out,
    grad_fc1,
    grad_fc1_bias,
    grad_fc2,
    grad_res,
    *scratch,
):
    s = types.SimpleNamespace(**dict(zip(scratch_shapes(), scratch)))
    wide, blk = lax.axis_index("wide"), lax.axis_index("blk")
    z, x = lax.div(wide, 2), lax.rem(wide, 2)
    y, core = lax.div(blk, 2), lax.rem(blk, 2)
    here, at_x, at_y, at_d = 2 * x + y, 2 * (1 - x) + y, 2 * x + 1 - y, 2 * (1 - x) + 1 - y
    sibling = (wide, 2 * y + 1 - core)
    x_peer = (2 * z + 1 - x, blk)
    y_peer = (wide, 2 * (1 - y) + core)
    d_peer = (2 * z + 1 - x, 2 * (1 - y) + core)
    y_cross = (wide, 2 * (1 - y) + 1 - core)
    z_of = [lax.rem(z + step, 4) for step in range(4)]
    z_peers = [(2 * z_of[step] + x, blk) for step in range(4)]
    z_order = (z_peers[1], z_peers[3], z_peers[2])
    inner, end = lax.rem(z + 1, 4) >= 2, lax.rem(z + 1, 4) < 2
    z_in, z_out = 1 + lax.rem(z, 2), 3 * lax.div(z, 2)
    in_peer, out_peer = (2 * z_in + x, blk), (2 * z_out + x, blk)
    blk_peers = [(y, 1 - core), (1 - y, core), (1 - y, 1 - core)]

    barrier = pltpu.get_barrier_semaphore()
    peers = [sibling, x_peer, y_peer, y_cross] + z_peers[1:]
    if any(unit[4] == 0 for unit in GATHER_UNITS + SCATTER_UNITS):
        peers.append(d_peer)
    for peer in peers:
        pl.semaphore_signal(barrier, inc=1, device_id=peer, device_id_type=MESH_ID)

    started, groups = [], []

    class Group:
        def __init__(self):
            self.sem = s.recv_sem.at[len(groups)]
            groups.append(self)

        def wait(self, ref):
            pltpu.make_async_copy(ref, ref, self.sem).wait()

    def leave(spot):
        copy, only = started[spot]
        if only is None:
            copy.wait_send()
        else:
            pl.when(only)(copy.wait_send)

    def prepare(source, target, peer, group=None, only=None):
        spot = len(started)
        if spot >= SENDS:
            leave(spot - SENDS)
        copy = pltpu.make_async_remote_copy(
            src_ref=source,
            dst_ref=target,
            send_sem=s.send_sem.at[spot % SENDS],
            recv_sem=(group or Group()).sem,
            device_id=peer,
            device_id_type=MESH_ID,
        )
        started.append((copy, only))
        return copy

    def remote(source, target, peer, group=None, only=None):
        copy = prepare(source, target, peer, group, only)
        if only is None:
            copy.start()
        else:
            pl.when(only)(copy.start)
        return copy

    kept = []

    class Local:
        def __init__(self, source, target):
            self.copy, self.waited = pltpu.make_async_copy(source, target, s.local_sem.at[len(kept)]), False
            self.copy.start()
            kept.append(self)

        def wait(self):
            if not self.waited:
                self.waited = True
                self.copy.wait()

    class Written:
        def __init__(self, ref):
            self.ref, self.arrived, self.copy = ref, Group(), None
            self.sem = s.local_sem.at[len(kept)]
            kept.append(self)

        def write(self, source, target):
            pltpu.make_async_copy(source, target, self.sem).start()

        def wait(self):
            self.arrived.wait(self.ref)
            pltpu.make_async_copy(self.ref, self.ref, self.sem).wait()

    def lanes(start, size):
        return pl.ds(pl.multiple_of(start, 128), size)

    mine = pl.ds(pl.multiple_of(64 * blk, 64), 64)
    taken = [Local(fc2_weight, s.w_fc2.at[z, x, core]), Local(patches.at[blk], s.rows_in.at[mine, :])]
    own_rows = pl.ds(pl.multiple_of(24 * core, 8), 24)
    pairs = {}

    def prepare_rows(name):
        if name == "h":
            theirs = fc1_weight[:, lanes((1 - core) * 1536, 1536)].astype(F32)
            ours = fc1_weight[:, lanes(core * 1536, 1536)].astype(F32)
            for side in (0, 1):
                for k in range(4):
                    at, found = 768 * side + 192 * k, 384 * k + 192 * side
                    s.pair_send_h[:, at : at + 192] = theirs[:, found : found + 192]
                    s.pair_rows_h[own_rows, at : at + 192] = ours[:, found : found + 192]
            return
        j = 3 if name == "o" else int(name[1])
        for t in range(3):
            ref, at = (out_weight if name == "o" else qkv_weight), slice(384 * j + 128 * t, 384 * j + 128 * t + 128)
            columns = (lambda side: 384 * side + 128 * t) if name == "o" else partial(piece, j, t=t)
            s.pair_send[:, at] = ref[:, lanes(columns(1 - core), 128)].astype(F32)
            s.pair_rows[own_rows, at] = ref[:, lanes(columns(core), 128)].astype(F32)

    def send_pair(name):
        source, target = s.pair_send_h, s.pair_rows_h.at[own_rows, :]
        if name != "h":
            j = 3 if name == "o" else int(name[1])
            columns = slice(384 * j, 384 * j + 384)
            source, target = s.pair_send.at[:, columns], s.pair_rows.at[own_rows, columns]
        pairs[name] = remote(source, target, sibling)

    def exchange(name):
        prepare_rows(name)
        send_pair(name)

    prepare_rows(FIRST_UNIT)

    pl.semaphore_wait(barrier, len(peers))

    send_pair(FIRST_UNIT)


    class Direct:
        def __init__(self, block):
            self.block, self.arrived = block, Group()

        def start(self):
            own = self.block(z)
            for peer in z_order:
                remote(own, own, peer, self.arrived)

        def wait(self):
            self.arrived.wait(self.block(THREE))

    class Line:
        def __init__(self, block):
            self.block, self.first = block, len(groups)
            self.arrived = [Group() for _ in range(3)]

        def start(self):
            own = self.block(z)
            to_in = types.SimpleNamespace(sem=s.recv_sem.at[self.first + lax.div(lax.rem(z + 1, 4), 2)])
            remote(own, own, in_peer, to_in)
            remote(own, own, out_peer, self.arrived[0], inner)

        def pass_on(self):
            outer, other = self.block(z_out), self.block(z_in)
            inward = prepare(outer, outer, in_peer, self.arrived[2], inner)
            outward = prepare(other, other, out_peer, self.arrived[1], inner)

            @pl.when(inner)
            def _():
                self.arrived[0].wait(outer)
                inward.start()
                self.arrived[1].wait(other)
                outward.start()

        def pass_last(self):
            far = self.block(3 - z_out)
            outward = prepare(far, far, out_peer, self.arrived[2], inner)

            @pl.when(inner)
            def _():
                self.arrived[2].wait(far)
                outward.start()

        def wait(self):
            @pl.when(end)
            def _():
                for arrived, level in zip(self.arrived, (z_in, 3 - z_in, 3 - z)):
                    arrived.wait(self.block(level))

    class DirectSum:
        def __init__(self, own, parts, _):
            self.own, self.parts, self.arrived = own, parts, Group()

        def start(self):
            for step in (1, 3, 2):
                remote(self.own(z_of[step]), self.parts(step - 1), z_peers[step], self.arrived)

        def wait(self):
            self.arrived.wait(self.parts(THREE))

        def summed(self, view):
            found = view(self.own(z))[...].astype(F32)
            for i in range(3):
                found = found + view(self.parts(i))[...].astype(F32)
            return found

    class LineSum:
        def __init__(self, own, parts, more):
            self.own, self.parts, self.more = own, parts, more
            self.arrived = [Group() for _ in range(3)]

        def start(self):
            remote(self.own(pl.ds(1 - lax.div(z, 2), 3)), self.parts(THREE), in_peer, self.arrived[0], end)

        def pass_on(self):
            source = self.own(pl.ds(2 - 2 * lax.div(z, 2), 2))
            inward = prepare(source, self.more(BOTH), in_peer, self.arrived[1], inner)

            @pl.when(inner)
            def _():
                self.arrived[0].wait(self.parts(THREE))
                for level in (z_in, 3 - z_out):
                    ref = self.own(level)
                    ref[...] = ref[...] + self.parts(level - 1 + lax.div(z, 2))[...]
                inward.start()

        def pass_last(self):
            outward = prepare(self.own(z_out), self.more(2), out_peer, self.arrived[2], inner)

            @pl.when(inner)
            def _():
                self.arrived[1].wait(self.more(BOTH))
                base = 2 * lax.div(z, 2)
                ref = self.own(z_out)
                ref[...] = ref[...] + self.more(z_out - base)[...]
                outward.start()
                ref = self.own(z)
                found = ref[...].astype(F32) + self.parts(z - 1 + lax.div(z, 2))[...].astype(F32)
                ref[...] = (found + self.more(z - base)[...].astype(F32)).astype(BF16)

        def wait(self):
            @pl.when(end)
            def _():
                self.arrived[2].wait(self.more(2))
                ref = self.own(z)
                ref[...] = ref[...] + self.more(2)[...]

        def summed(self, view):
            return view(self.own(z))[...].astype(F32)

    def wait_fc2():
        taken[0].wait()

    class Steps:
        def w(self):
            self.line.pass_on()

        def v(self):
            self.line.pass_last()

    class Gather(Steps):
        def __init__(self, part, low, line):
            self.part, self.low, self.high = part, pl.ds(0, low), pl.ds(low, 4 - low)
            self.by_x, self.by_y, self.far, self.pair = (Group() for _ in range(4))
            self.line = line(lambda levels: part(levels, here))

        def z(self):
            self.line.start()

        def p(self):
            self.line.wait()
            self.share(self.part(ALL, here))

        def share(self, block):
            remote(block, block, x_peer, self.by_x)
            remote(block, block, y_peer, self.by_y)
            remote(block, block, sibling, self.pair)

        def f(self):
            column = self.part(ALL, at_x)
            self.by_x.wait(column)
            some = self.part(self.low, at_x)
            remote(some, some, y_peer, self.far)
            remote(column, column, sibling, self.pair)

        def g(self):
            column = self.part(ALL, at_y)
            self.by_y.wait(column)
            some = self.part(self.high, at_y)
            remote(some, some, x_peer, self.far)
            remote(column, column, sibling, self.pair)

        def l(self):
            column = self.part(ALL, at_d)
            self.far.wait(column)
            remote(column, column, sibling, self.pair)

        def d(self):
            self.pair.wait(self.part(ALL, ALL))

    class FineGather(Gather):
        def z(self):
            own = self.part(z, here)
            self.z_copies = [remote(own, own, peer) for peer in z_order]

        def o(self):
            self.share(self.part(z, here))

        def p(self):
            for step, copy in zip((1, 3, 2), self.z_copies):
                copy.wait_recv()
                self.share(self.part(z_of[4 - step], here))

    class SquareGather(Steps):
        def __init__(self, part, line):
            self.part, self.square, self.pair = part, Group(), Group()
            self.line = line(lambda levels: part(levels, ALL))

        def p(self):
            own = self.part(z, here)
            for peer in (x_peer, y_peer, d_peer):
                remote(own, own, peer, self.square)

        def z(self):
            self.square.wait(self.part(z, THREE))
            self.line.start()
            level = self.part(z, ALL)
            remote(level, level, sibling, self.pair)

        def l(self):
            self.line.wait()
            for step in (1, 2, 3):
                level = self.part(z_of[step], ALL)
                remote(level, level, sibling, self.pair)

        def d(self):
            self.pair.wait(self.part(ALL, ALL))

    class PlaneGather(Steps):
        def __init__(self, part, line, across=None):
            self.part, self.across, self.pair = part, across, Group()
            self.line = line(lambda levels: part(levels, x))

        def y(self):
            source, target = self.across
            self.y_copy = remote(source, target, y_peer)

        def z(self):
            if self.across:
                self.y_copy.wait_recv()
            else:
                wait_fc2()
            self.line.start()

        def x(self):
            self.line.wait()
            column = self.part(ALL, x)
            self.x_copy = remote(column, column, x_peer)
            remote(column, column, sibling, self.pair)

        def l(self):
            self.x_copy.wait_recv()
            column = self.part(ALL, 1 - x)
            remote(column, column, sibling, self.pair)

        def d(self):
            self.pair.wait(self.part(ALL, BOTH))

    class AcrossGather(Steps):
        def __init__(self, part, line):
            self.part, self.pair = part, Group()
            self.line = line(lambda levels: part(levels, BOTH))

        def x(self):
            wait_fc2()
            own = self.part(z, x)
            self.x_copy = remote(own, own, x_peer)

        def z(self):
            self.x_copy.wait_recv()
            self.line.start()
            level = self.part(z, BOTH)
            remote(level, level, sibling, self.pair)

        def l(self):
            self.line.wait()
            for step in (1, 2, 3):
                level = self.part(z_of[step], BOTH)
                remote(level, level, sibling, self.pair)

        def d(self):
            self.pair.wait(self.part(ALL, BOTH))

    def column_part(ref, start, size):
        return lambda levels, place: ref.at[levels, place, :, lanes(start, size)]

    def column_gather(ref, start, size, way, chained):
        part, line = column_part(ref, start, size), Line if chained else Direct
        if way == 9:
            own = part(z, here)
            sides = lambda levels, side: part(levels, ALL if side is BOTH else pl.ds(2 * side, 2))
            return PlaneGather(sides, line, (own, own))
        if way == 0:
            return SquareGather(part, line)
        return (Gather if way > 0 else FineGather)(part, abs(way), line)

    gathers = {"s0": column_gather(s.w_small, 128 * core, 128, 2, 0)}
    for name, j, start, size, way, chained in GATHER_UNITS:
        if j < 3:
            ref, first = s.w_qkv, 768 * j + 384 * core
        else:
            ref, first = s.w_out, 384 * core
        gathers[name] = column_gather(ref, first + 128 * start, 128 * size, way, chained)

    def fc1_gather(j):
        columns = lanes(768 * core + 384 * j, 384)
        return PlaneGather(
            lambda levels, side: s.w_fc1.at[levels, ALL if side is BOTH else pl.ds(2 * side, 2), :, columns],
            Line if GATHER_LINES["h"][j] else Direct,
            (s.fc1_other.at[:, 384 * j : 384 * j + 384], s.w_fc1.at[z, here, :, columns]),
        )

    def fc2_gather(j, size, way):
        rows = pl.ds(size * j, size)
        part = lambda levels, side: s.w_fc2.at[levels, side, core, rows, :]
        return (PlaneGather if way else AcrossGather)(part, Line if GATHER_LINES["f"][j] else Direct)

    for j in range(2):
        gathers["h" + str(j)] = fc1_gather(j)
    for j, way in enumerate(GATHER_FC2):
        gathers["f" + str(j)] = fc2_gather(j, 96 // len(GATHER_FC2), way)

    def assemble(name):
        pairs[name].wait_recv()
        if name == "h":
            halves = lanes(768 * y, 768), lanes(768 * (1 - y), 768)
            s.w_fc1[z, here, :, lanes(768 * core, 768)] = s.pair_rows_h[:, halves[0]].astype(BF16)
            s.fc1_other[...] = s.pair_rows_h[:, halves[1]].astype(BF16)
        elif name == "o":
            s.w_out[z, here, :, lanes(384 * core, 384)] = s.pair_rows[:, 1152:1536].astype(BF16)
        else:
            j = int(name[1])
            found = s.pair_rows[:, 384 * j : 384 * j + 384].astype(BF16)
            s.w_qkv[z, here, :, lanes(768 * j + 384 * core, 384)] = found


    def by_rows(body, carry=None):
        def step(i, held):
            return body(pl.ds(pl.multiple_of(ROWS * i, ROWS), ROWS), held)

        return lax.fori_loop(0, TOKENS // ROWS, step, carry)

    def over(shape, axis):
        return lax.broadcasted_iota(jnp.int32, shape, axis)

    def piece24(columns):
        return lax.shift_right_logical(columns * 43691, 20)

    def piece96(columns):
        return lax.shift_right_logical(columns * 10923, 20)

    def spread24():
        columns = over((128, D), 1)
        return (columns - 24 * piece24(columns) == over((128, D), 0)).astype(F32).astype(BF16)

    def hidden_unit(columns):
        return columns + 192 * lax.shift_right_logical(columns * 21846, 22) + 192 * y

    def spread96():
        columns = hidden_unit(over((128, FF // 2), 1))
        return (columns - 96 * piece96(columns) == over((128, FF // 2), 0)).astype(F32).astype(BF16)

    def unpack_small():
        flat = s.w_small[...].reshape(256, 256)
        chips = lax.shift_right_logical(over((256, D), 0), 4)
        pieces = piece24(over((256, D), 1))
        spread = spread24()
        found = jnp.zeros((16, D), F32)
        for side in (0, 1):
            wide_rows = dot(flat[:, 128 * side : 128 * side + 128], spread)
            wide_rows = jnp.where(pieces == 2 * chips + side, wide_rows, 0.0)
            found = found + jnp.sum(wide_rows.reshape(16, 16, D), axis=0)
        s.par[...] = found
        pick = (over((16, 256), 1) == 16 * over((16, 256), 0) + 8).astype(F32).astype(BF16)
        spread = spread96()
        shape = (16, FF // 2)
        pieces = piece96(hidden_unit(over(shape, 1)))
        found = jnp.zeros(shape, F32)
        for side in (0, 1):
            rows = dot(pick, flat[:, 128 * side : 128 * side + 128]).astype(BF16)
            found = found + jnp.where(pieces == 2 * over(shape, 0) + side, dot(rows, spread), 0.0)
        s.par_fc1[0:1, :] = jnp.sum(found, axis=0, keepdims=True)

    def standardized(rows):
        centered = rows - jnp.mean(rows, axis=-1, keepdims=True)
        scale = lax.rsqrt(jnp.mean(centered * centered, axis=-1, keepdims=True) + EPSILON)
        return centered * scale, scale

    def first_norm():
        def body(rows, _):
            found, _ = standardized(s.rows_in[rows, :].astype(F32))
            s.normed[rows, :] = (found * s.par[0:1, :] + s.par[2:3, :]).astype(BF16)
            return 0

        by_rows(body, 0)
        s.normed_t[...] = s.normed[...].T

    def project_qkv(j):
        found = dot(s.normed[...], s.w_qkv[:, :, :, 768 * j : 768 * j + 768].reshape(D, D))
        for i in (0, 1):
            query, key, value = (slice(at, at + 128) for at in pair_places(0, i))
            natural = slice(128 * (2 * j + i), 128 * (2 * j + i) + 128)
            parts = (
                (query, (found[:, query] + s.par[4:5, natural]) * 0.125),
                (key, found[:, key]),
                (value, found[:, value] + s.par[5:6, natural]),
            )
            for at, part in parts:
                s.mixed[:, 768 * j + at.start : 768 * j + at.stop] = part.astype(BF16)

    def head_masks():
        first = (over((TOKENS, 128), 1) < 64).astype(F32)
        return first.astype(BF16), (1.0 - first).astype(BF16)

    def softmax(scores):
        expo = jnp.exp(scores - jnp.max(scores, axis=-1, keepdims=True))
        return expo * (1.0 / jnp.sum(expo, axis=-1, keepdims=True))

    def attend(j):
        def body(i, _):
            query, key, value = (s.mixed[:, lanes(at, 128)] for at in pair_places(j, i))
            found = jnp.zeros((TOKENS, 128), F32)
            for mask in head_masks():
                probs = softmax(dot_nt(query * mask, key)).astype(BF16)
                found = found + dot(probs, value * mask)
            s.attended[:, lanes(128 * (2 * j + i), 128)] = found.astype(BF16)
            return 0

        lax.fori_loop(0, 2, body, 0)

    def some_rows(body, carry, start, count):
        def step(i, held):
            return body(pl.ds(pl.multiple_of(ROWS * i + start, ROWS), ROWS), held)

        return lax.fori_loop(0, count // ROWS, step, carry)

    def project_out(part):
        half = pl.ds(128 * part, 128)
        s.middle[half, :] = dot(s.attended[half, :], s.w_out[...].reshape(D, D))

        def body(rows, _):
            middle = s.rows_in[rows, :].astype(F32) + (s.middle[rows, :] + s.par[6:7, :])
            s.middle[rows, :] = middle
            found, _ = standardized(middle)
            s.normed2[rows, :] = (found * s.par[1:2, :] + s.par[3:4, :]).astype(BF16)
            return 0

        some_rows(body, 0, 128 * part, 128)

    def transpose_out():
        s.attended_t[...] = s.attended[...].T
        s.normed2_t[:, 0:256] = s.normed2[0:256, :].T

    def feed(j, start, count):
        def body(side, _):
            columns = lanes(768 * side + 384 * j, 384)
            tokens = pl.ds(start, count)
            s.other[0:count, 0:384] = dot(s.normed2[tokens, :], s.w_fc1[:, :, :, columns].reshape(D, 384))

            def gelu(rows, _):
                there = pl.ds(pl.multiple_of(rows.start + start, ROWS), ROWS)
                hidden = s.other[rows, 0:384] + s.par_fc1[0:1, columns]
                bell = jnp.exp(-0.5 * hidden * hidden)
                normal = 0.5 + 0.5 * lax.erf(hidden * (1.0 / math.sqrt(2.0)))
                s.slope[there, columns] = normal + hidden * (bell * (1.0 / math.sqrt(2.0 * math.pi)))
                s.active[there, columns] = (hidden * normal).astype(BF16)
                return 0

            some_rows(gelu, 0, 0, count)
            found = s.active[tokens, columns].T.reshape(4, 96, count)
            s.active_t[pl.ds(8 * side + 4 * j, 4), :, start : start + count] = found
            return 0

        lax.fori_loop(0, 2, body, 0)

    def feed_own(j):
        feed(j, 0, 256)

    def feed_other(j, part):
        feed(j, 256 + 128 * part, 128)

    ours_rows = pl.ds(pl.multiple_of(128 * y, 128), 128)
    theirs_rows = pl.ds(pl.multiple_of(128 * (1 - y), 128), 128)
    across_y = 2 * (1 - y) + core
    valid, valid_across = frame_valid[blk].astype(F32), frame_valid[across_y].astype(F32)

    def mask_cotangent(frame):
        def body(rows, _):
            there = pl.ds(pl.multiple_of(rows.start + 256 * frame, ROWS), ROWS)
            masked = s.cot_in[there, :].astype(F32) * (valid_across if frame else valid)
            s.g_branch2[there, :] = masked.astype(BF16)
            return 0

        by_rows(body, 0)


    class Scatter(Steps):
        every = ALL

        def view(self, ref):
            return ref

        def __init__(self, own, other, pr, dx, dy, px, py, pz, finish, low=2, line=DirectSum, more=None):
            self.own, self.other, self.finish = own, other, finish
            self.pr, self.dx, self.dy, self.px, self.py = pr, dx, dy, px, py
            self.line = line(lambda levels: own(levels, here), pz, more)
            self.square = Group()
            self.low, self.high = pl.ds(0, low), pl.ds(low, 4 - low)

        def s(self):
            self.pair = remote(self.other(), self.pr(ALL, self.every), sibling)

        def add_pair(self):
            self.pair.wait_recv()

            def add(level, _):
                ref = self.own(level, self.every)
                ref[...] = ref[...] + self.pr(level, self.every)[...]
                return 0

            lax.fori_loop(0, 4, add, 0)

        def p(self):
            self.add_pair()
            low, high = self.low, self.high
            self.a = remote(self.own(low, at_d), self.dx(low), x_peer)
            self.b = remote(self.own(high, at_d), self.dy(high), y_peer)
            remote(self.own(low, at_x), self.px(low), x_peer, self.square)
            remote(self.own(high, at_y), self.py(high), y_peer, self.square)

        def f(self):
            self.a.wait_recv()
            ref = self.own(self.low, at_y)
            ref[...] = ref[...] + self.dx(self.low)[...]
            remote(ref, self.py(self.low), y_peer, self.square)

        def g(self):
            self.b.wait_recv()
            ref = self.own(self.high, at_x)
            ref[...] = ref[...] + self.dy(self.high)[...]
            remote(ref, self.px(self.high), x_peer, self.square)

        def z(self):
            self.square.wait(self.own(ALL, BOTH))

            def add(level, _):
                ref = self.own(level, here)
                ref[...] = (
                    ref[...].astype(F32)
                    + self.px(level)[...].astype(F32)
                    + self.py(level)[...].astype(F32)
                ).astype(BF16)
                return 0

            lax.fori_loop(0, 4, add, 0)
            self.line.start()

        def l(self):
            self.line.wait()
            self.finish(self)

        def summed(self, view):
            return self.line.summed(view)

    class SquareScatter(Scatter):
        def __init__(self, own, other, pr, bz, pz, finish, line, more):
            self.own, self.other, self.finish = own, other, finish
            self.pr, self.pz, self.square = pr, pz, Group()
            self.line = line(lambda levels: own(levels, ALL), bz, more)

        def z(self):
            self.add_pair()
            self.line.start()

        def p(self):
            self.line.wait()
            if isinstance(self.line, DirectSum):
                self.own(z, ALL)[...] = self.line.summed(lambda ref: ref).astype(BF16)
            targets = ((at_x, x_peer), (at_y, y_peer), (at_d, d_peer))
            for i, (place, peer) in enumerate(targets):
                remote(self.own(z, place), self.pz(i), peer, self.square)

        def l(self):
            self.square.wait(self.pz(THREE))
            self.finish(self)

        def summed(self, view):
            found = view(self.own(z, here))[...].astype(F32)
            for i in range(3):
                found = found + view(self.pz(i))[...].astype(F32)
            return found

    class PlaneScatter(Scatter):
        def __init__(self, own, other, pr, px, pz, finish, line, more, across=None, view=None):
            self.own, self.other, self.finish, self.across, self.view = own, other, finish, across, view
            self.pr, self.px = pr, px
            self.line = line(lambda levels: own(levels, x), pz, more)

        def x(self):
            self.add_pair()
            self.x_copy = remote(self.own(ALL, 1 - x), self.px(ALL), x_peer)

        def z(self):
            self.x_copy.wait_recv()

            def add(level, _):
                ref = self.own(level, x)
                ref[...] = ref[...] + self.px(level)[...]
                return 0

            lax.fori_loop(0, 4, add, 0)
            self.line.start()

        def y(self):
            self.line.wait()
            source, target = self.across(self)
            self.y_copy = remote(source, target, y_peer)

        def l(self):
            if self.across:
                self.y_copy.wait_recv()
            else:
                self.line.wait()
            self.finish(self)

    class AcrossScatter(Scatter):
        def __init__(self, own, other, pr, bz, px, finish, line, more):
            self.own, self.other, self.finish = own, other, finish
            self.pr, self.px = pr, px
            self.line = line(lambda levels: own(levels, ALL), bz, more)

        def z(self):
            self.add_pair()
            self.line.start()

        def x(self):
            self.line.wait()
            if isinstance(self.line, DirectSum):
                self.own(z, ALL)[...] = self.line.summed(lambda ref: ref).astype(BF16)
            self.x_copy = remote(self.own(z, 1 - x), self.px(), x_peer)

        def l(self):
            self.x_copy.wait_recv()
            self.finish(self)

        def summed(self, view):
            return view(self.own(z, x))[...].astype(F32) + view(self.px())[...].astype(F32)

    def columns_of(ref, columns, size):
        def own(levels, places):
            return ref.at[levels, places, :, lanes(columns(core), size)]

        def other():
            return ref.at[:, :, :, lanes(columns(1 - core), size)]

        return own, other

    def column_scatter(ref, columns, natural, size, spot, output, way, chained):
        at = pl.ds(spot, size)

        def finish(scatter):
            total = scatter.summed(scatter.view)
            if way == 9:
                total = total + s.py_a[0, :, at].astype(F32)
            s.last_a[:, at] = total
            other_rows = pl.ds(pl.multiple_of(24 * (1 - core), 8), 24)
            for t in range(size // 128):
                some = slice(spot + 128 * t, spot + 128 * t + 128)
                target = lanes(natural(core, t), 128)
                remote(s.last_a.at[other_rows, some], output.at[:, target], sibling, columns_written.arrived)
                columns_written.write(s.last_a.at[own_rows, some], output.at[:, target])

        if way == 9:

            def across(scatter):
                s.send_a[:, at] = scatter.summed(lambda ref: ref.at[1 - y]).astype(BF16)
                return s.send_a.at[:, at], s.py_a.at[0, :, at]

            def sides(ref):
                return lambda levels, side: ref(levels, ALL if side is ALL else pl.ds(2 * side, 2))

            own, other = columns_of(ref, columns, size)
            return PlaneScatter(
                sides(own),
                other,
                lambda levels, places: s.pr_a.at[levels, places, :, at],
                lambda levels: s.px2_a.at[levels, :, :, at],
                lambda i: s.bz_a.at[i, BOTH, :, at],
                finish,
                LineSum if chained else DirectSum,
                lambda i: s.cz_a.at[i, BOTH, :, at],
                across,
                lambda ref: ref.at[y],
            )

        if not way:
            return SquareScatter(
                *columns_of(ref, columns, size),
                lambda levels, places: s.pr_a.at[levels, places, :, at],
                lambda i: s.bz_a.at[i, :, :, at],
                lambda i: s.pz_a.at[i, :, at],
                finish,
                LineSum if chained else DirectSum,
                lambda i: s.cz_a.at[i, :, :, at],
            )
        return Scatter(
            *columns_of(ref, columns, size),
            lambda levels, places: s.pr_a.at[levels, places, :, at],
            lambda levels: s.dx_a.at[levels, :, at],
            lambda levels: s.dx_a.at[levels, :, at],
            lambda levels: s.px_a.at[levels, :, at],
            lambda levels: s.py_a.at[levels, :, at],
            lambda i: s.pz_a.at[i, :, at],
            finish,
            way,
            LineSum if chained else DirectSum,
            lambda i: s.qz_a.at[i, :, at],
        )

    def fc1_scatter(j):
        at = slice(384 * j, 384 * j + 384)

        def own_columns(side):
            return lanes(768 * side + 384 * j, 384)

        def own(levels, side):
            places = ALL if side is ALL else pl.ds(2 * side, 2)
            return s.g_fc1.at[levels, places, :, own_columns(core)]

        def across(scatter):
            s.last_fc1[0, :, at] = scatter.summed(lambda ref: ref.at[y])
            s.send_fc1[:, at] = scatter.summed(lambda ref: ref.at[1 - y]).astype(BF16)
            return s.send_fc1.at[:, at], s.py_fc1.at[:, at]

        def finish(scatter):
            s.last_fc1[1, :, at] = s.py_fc1[:, at].astype(F32)
            other_rows = pl.ds(pl.multiple_of(24 * (1 - core), 8), 24)
            for i, half in enumerate((y, 1 - y)):
                target = lanes(1536 * half + 768 * core + 384 * j, 384)
                remote(s.last_fc1.at[i, other_rows, at], grad_fc1.at[:, target], sibling, fc1_written.arrived)
                fc1_written.write(s.last_fc1.at[i, own_rows, at], grad_fc1.at[:, target])

        return PlaneScatter(
            own,
            lambda: s.g_fc1.at[:, :, :, own_columns(1 - core)],
            lambda levels, places: s.pr_fc1.at[levels, places, :, at],
            lambda levels: s.px_fc1.at[levels, :, :, at],
            lambda i: s.pz_fc1.at[i, :, :, at],
            finish,
            LineSum if SCATTER_LINES["h"][j] else DirectSum,
            lambda i: s.qz_fc1.at[i, :, :, at],
            across,
        )

    def fc2_scatter(j, size, way):
        rows = pl.ds(size * j, size)
        half = lanes(384 * core, 384)

        def finish(scatter):
            s.last_fc2[rows, :] = scatter.summed(lambda ref: ref.at[1 - core])
            remote(s.last_fc2.at[rows, :], grad_fc2.at[rows, half], sibling, fc2_written.arrived)
            s.kept_fc2[rows, :] = scatter.summed(lambda ref: ref.at[core])
            fc2_written.write(s.kept_fc2.at[rows, :], grad_fc2.at[rows, half])

        def sides(side):
            return BOTH if side is ALL else side

        own = lambda levels, side: s.g_fc2.at[levels, sides(side), :, rows, half]
        other = lambda: s.g_fc2.at[:, :, :, rows, lanes(384 * (1 - core), 384)]
        pr = lambda levels, side: s.pr_fc2.at[levels, sides(side), :, rows, :]
        if not way:
            bz = lambda i: s.bz_fc2.at[i, :, :, rows, :]
            line = LineSum if SCATTER_LINES["f"][j] else DirectSum
            more = lambda i: s.cz_fc2.at[i, :, :, rows, :]
            return AcrossScatter(own, other, pr, bz, lambda: s.pz_fc2.at[0, :, rows, :], finish, line, more)
        return PlaneScatter(
            own,
            other,
            pr,
            lambda levels: s.px_fc2.at[levels, :, rows, :],
            lambda i: s.pz_fc2.at[i, :, rows, :],
            finish,
            LineSum if SCATTER_LINES["f"][j] else DirectSum,
            lambda i: s.qz_fc2.at[i, :, rows, :],
        )

    def small_finish(scatter):
        found = scatter.summed(lambda ref: ref)
        grad_gain[...] = found[0:2, 0:24]
        grad_shift[...] = found[2:4, 0:24]
        grad_qv[...] = found[4:6, 0:24]
        grad_res[...] = found[6:8, 0:24]
        grad_fc1_bias[...] = found[8:9, 0:96]

    columns_written, fc1_written = Written(s.last_a.at[own_rows, :]), Written(s.last_a.at[own_rows, :])
    fc2_written = Written(s.last_fc2)
    scatters = {}
    for j, way in enumerate(SCATTER_FC2):
        scatters["f" + str(j)] = fc2_scatter(j, 96 // len(SCATTER_FC2), way)
    for j in range(2):
        scatters["h" + str(j)] = fc1_scatter(j)
    for name, j, start, size, way, chained in SCATTER_UNITS:
        if j < 3:
            ref, output, spot, first = s.g_qkv, grad_qkv, 384 + 384 * j, 768 * j
            natural = lambda side, t, j=j, start=start: piece(j, side, start + t)
        else:
            ref, output, spot, first = s.g_out, grad_out, 0, 0
            natural = lambda side, t, start=start: 384 * side + 128 * (start + t)
        columns = lambda side, first=first, start=start: first + 384 * side + 128 * start
        scatters[name] = column_scatter(
            ref, columns, natural, 128 * size, spot + 128 * start, output, way, chained
        )

    scatters["s0"] = Scatter(
        *columns_of(s.g_small, lambda side: 128 * side, 128),
        lambda levels, places: s.pr_small.at[levels, places],
        lambda levels: s.dx_small.at[levels],
        lambda levels: s.dx_small.at[levels],
        lambda levels: s.px_small.at[levels],
        lambda levels: s.py_small.at[levels],
        lambda i: s.pz_small.at[i],
        small_finish,
    )

    def weight_grad_fc2(j):
        size = 96 // len(SCATTER_FC2)
        rows = pl.ds(size * j, size)

        def body(turn, _):
            columns = lanes(384 * (turn * core + (1 - turn) * (1 - core)), 384)
            found = dot(s.active_t[:, rows, :].reshape(16 * size, 512), s.g_branch2[:, columns])
            s.g_fc2[:, :, :, rows, columns] = found.astype(BF16).reshape(4, 2, 2, size, 384)
            return 0

        lax.fori_loop(0, 2, body, 0)

    def column_grad(left, right, ref, columns):
        def body(turn, _):
            at = lanes(columns(turn * core + (1 - turn) * (1 - core)), 384)
            ref[:, :, :, at] = dot(left[...], right[:, at]).astype(BF16).reshape(4, 4, 48, 384)
            return 0

        lax.fori_loop(0, 2, body, 0)

    def feed_back(frame):
        tokens = pl.ds(256 * frame, 256)

        def body(part, _):
            columns = lanes(D * part, D)
            s.other[...] = dot_nt(s.g_branch2[tokens, :], s.w_fc2[pl.ds(2 * part, 2)].reshape(D, D))

            def slope(rows, sums):
                there = pl.ds(pl.multiple_of(rows.start + 256 * frame, ROWS), ROWS)
                found = (s.other[rows, :] * s.slope[there, columns]).astype(BF16)
                s.g_hidden[there, columns] = found
                return sums + jnp.sum(found.astype(F32), axis=0, keepdims=True)

            s.sums_fc1[frame : frame + 1, columns] = by_rows(slope, jnp.zeros((1, D), F32))
            return 0

        lax.fori_loop(0, 2, body, 0)

    def feed_out(frame):
        tokens = pl.ds(256 * frame, 256)
        s.total[...] = jnp.zeros((TOKENS, D), F32)

        def body(part, _):
            weight = s.w_fc2[pl.ds(2 * part, 2)].reshape(D, D)
            s.total[...] += dot(s.active[tokens, lanes(D * part, D)], weight)
            return 0

        lax.fori_loop(0, 2, body, 0)
        if frame:
            s.part_across[...] = s.total[...].astype(BF16)
        else:

            def add(rows, _):
                s.total[rows, :] = s.middle[rows, :] + (s.total[rows, :] + s.par[7:8, :])
                return 0

            by_rows(add, 0)
            s.base_send[...] = (valid * s.total[theirs_rows, :]).astype(BF16)

    def output():
        s.enc_send[0] = (valid * (s.total[ours_rows, :] + s.part_recv[...].astype(F32))).astype(BF16)
        part = valid_across * s.part_across[ours_rows, :].astype(F32)
        s.enc_send[1] = (s.base_recv[...].astype(F32) + part).astype(BF16)

        def body(rows, sums):
            return sums + jnp.sum(s.g_branch2[rows, :].astype(F32), axis=0, keepdims=True)

        s.sums[7:8, :] = by_rows(body, jnp.zeros((1, D), F32))

    def feed_back_rows(start, count):
        found = jnp.zeros((count, D), F32)
        for part in (0, 1):
            columns = slice(D * part, D * part + D)
            hidden = s.g_hidden[pl.ds(start, count), columns]
            found = found + dot_nt(hidden, s.w_fc1[:, :, :, columns].reshape(D, D))
        return found

    def feed_back_own():
        s.other[...] = feed_back_rows(0, 256)

    def feed_back_other():
        s.back_send[...] = feed_back_rows(256, 256).astype(BF16)

    def norm_back(upstream, found, scale, gain):
        weighted = upstream * gain
        return scale * (
            weighted
            - jnp.mean(weighted, axis=-1, keepdims=True)
            - found * jnp.mean(weighted * found, axis=-1, keepdims=True)
        )

    def column_sum(values):
        return jnp.sum(values, axis=0, keepdims=True)

    def second_norm_back(part):
        def rows_back(rows, sums):
            upstream = s.other[rows, :] + s.back_recv[rows, :].astype(F32)
            found, scale = standardized(s.middle[rows, :])
            middle = s.g_branch2[rows, :].astype(F32) + norm_back(upstream, found, scale, s.par[1:2, :])
            s.g_middle[rows, :] = middle
            branch = middle.astype(BF16)
            s.g_branch[rows, :] = branch
            return (
                sums[0] + column_sum(upstream * found),
                sums[1] + column_sum(upstream),
                sums[2] + column_sum(branch.astype(F32)),
            )

        before = [jnp.zeros((1, D), F32)] * 3
        if part:
            before = [s.sums[row : row + 1, :] for row in (1, 3, 6)]
        found = some_rows(rows_back, tuple(before), 128 * part, 128)
        s.sums[1:2, :], s.sums[3:4, :], s.sums[6:7, :] = found

    def attend_back(j):
        def body(i, _):
            spots = [lanes(at, 128) for at in pair_places(j, i)]
            natural = lanes(128 * (2 * j + i), 128)
            query, key, value = (s.mixed[:, spot] for spot in spots)
            upstream = s.g_attended[:, natural]
            g_query, g_key, g_value = (jnp.zeros((TOKENS, 128), F32) for _ in range(3))
            for mask in head_masks():
                probs = softmax(dot_nt(query * mask, key))
                g_probs = dot_nt(upstream * mask, value)
                g_value = g_value + dot_tn(probs.astype(BF16), upstream * mask)
                inner = jnp.sum(probs * g_probs, axis=-1, keepdims=True)
                g_scores = (probs * (g_probs - inner)).astype(BF16)
                g_query = g_query + dot(g_scores, key * mask)
                g_key = g_key + dot_tn(g_scores, query * mask)
            g_query = 0.125 * g_query.astype(BF16).astype(F32)
            g_value = g_value.astype(BF16)
            s.g_mixed[:, spots[0]] = g_query.astype(BF16)
            s.g_mixed[:, spots[1]] = g_key.astype(BF16)
            s.g_mixed[:, spots[2]] = g_value
            s.sums[4:5, natural] = column_sum(g_query)
            s.sums[5:6, natural] = column_sum(g_value.astype(F32))
            return 0

        lax.fori_loop(0, 2, body, 0)

    def first_norm_back():
        s.total[...] = jnp.zeros((TOKENS, D), F32)

        def body(level, _):
            columns = lanes(D * level, D)
            s.total[...] += dot_nt(s.g_mixed[:, columns], s.w_qkv[:, :, :, columns].reshape(D, D))
            return 0

        lax.fori_loop(0, 3, body, 0)

        def rows_back(rows, sums):
            upstream = s.total[rows, :]
            found, scale = standardized(s.rows_in[rows, :].astype(F32))
            result = s.g_middle[rows, :] + norm_back(upstream, found, scale, s.par[0:1, :])
            s.gx_send[rows, :] = result.astype(BF16)
            return (sums[0] + column_sum(upstream * found), sums[1] + column_sum(upstream))

        empty = jnp.zeros((1, D), F32)
        s.sums[0:1, :], s.sums[2:3, :] = by_rows(rows_back, (empty, empty))

    def pack_small():
        chips = lax.shift_right_logical(over((256, D), 0), 4)
        pieces = piece24(over((256, D), 1))
        spread = spread24()
        rows = jnp.broadcast_to(s.sums[...][None], (16, 16, D)).reshape(256, D)
        for side in (0, 1):
            placed = dot_nt(jnp.where(pieces == 2 * chips + side, rows, 0.0).astype(BF16), spread)
            s.g_small[:, :, :, 128 * side : 128 * side + 128] = placed.astype(BF16).reshape(4, 4, 16, 128)
        put = (over((256, 16), 0) == 16 * over((256, 16), 1) + 8).astype(F32).astype(BF16)
        spread = spread96()
        shape = (16, FF // 2)
        pieces = piece96(hidden_unit(over(shape, 1)))
        row = s.sums_fc1[0:1, :] + s.sums_fc1[1:2, :]
        for side in (0, 1):
            mine = pieces == 2 * over(shape, 0) + side
            placed = dot_nt(jnp.where(mine, row, 0.0).astype(BF16), spread).astype(BF16)
            here_ = s.g_small.at[:, :, :, pl.ds(128 * side, 128)]
            here_[...] = here_[...] + dot(put, placed).astype(BF16).reshape(4, 4, 16, 128)

    moved = {}

    def send_rows():
        group = Group()
        for py, pc in blk_peers:
            remote(patches.at[2 * py + pc], s.rows_in.at[mine, :], (wide, 2 * py + pc), group)
        moved["rows"] = group, s.rows_in.at[0:192, :]

    cot_kept = {}

    def send_cotangent(frame):
        group, there = Group(), pl.ds(pl.multiple_of(64 * blk + 256 * frame, 64), 64)
        for py, pc in blk_peers:
            source = cotangent.at[2 * (1 - py if frame else py) + pc]
            remote(source, s.cot_in.at[there, :], (wide, 2 * py + pc), group)
        moved["cot" + str(frame)] = group, s.cot_in.at[256 * frame : 256 * frame + 192, :]
        cot_kept[frame] = Local(cotangent.at[across_y if frame else blk], s.cot_in.at[there, :])

    def received(name):
        group, ref = moved.pop(name)
        group.wait(ref)

    def start_norm():
        received("rows")
        taken[1].wait()
        first_norm()

    def start_cotangent(frame):
        received("cot" + str(frame))
        cot_kept[frame].wait()
        mask_cotangent(frame)

    def send_encoded():
        ours = pl.ds(pl.multiple_of(64 * core, 64), 64)
        theirs = pl.ds(pl.multiple_of(64 * (1 - core), 64), 64)
        group = Group()
        for i, frame in enumerate((blk, across_y)):
            remote(s.enc_send.at[i, theirs, :], encoded.at[frame], sibling, group)
        moved["enc"] = group, s.enc_send.at[0, :, :]
        Local(s.enc_send.at[0, ours, :], encoded.at[blk])
        Local(s.enc_send.at[1, ours, :], encoded.at[across_y])

    def send_grad_rows():
        group = Group()
        for py, pc in blk_peers:
            rows = pl.ds(pl.multiple_of(64 * (2 * py + pc), 64), 64)
            remote(s.gx_send.at[rows, :], grad_patches.at[blk], (wide, 2 * py + pc), group)
        moved["grad"] = group, s.gx_send.at[0:192, :]
        Local(s.gx_send.at[mine, :], grad_patches.at[blk])

    def project_attended():
        s.g_attended[...] = dot_nt(s.g_branch[...], s.w_out[...].reshape(D, D)).astype(BF16)

    def across(name, source, target):
        moved[name] = Group(), target
        remote(source, target, y_peer, moved[name][0])

    def send_normed(part):
        start = 128 * part
        own, other = (s.normed2.at[at : at + 128, :] for at in (start, 256 + start))
        across("normed" + str(part), own, other)

    def take_normed(part):
        received("normed" + str(part))

    def transpose_other():
        s.normed2_t[:, 256:512] = s.normed2[256:512, :].T

    def send_part():
        across("part", s.part_across.at[theirs_rows, :], s.part_recv)

    def send_base():
        across("base", s.base_send, s.base_recv)

    def start_output():
        received("part")
        received("base")
        output()

    def send_back(part):
        rows = slice(128 * part, 128 * part + 128)
        across("back" + str(part), s.back_send.at[rows, :], s.back_recv.at[rows, :])

    def start_second(part):
        received("back" + str(part))
        second_norm_back(part)

    def grad_fc1_weight(j):
        column_grad(s.normed2_t, s.g_hidden, s.g_fc1, lambda side: 768 * side + 384 * j)

    def grad_out_weight():
        column_grad(s.attended_t, s.g_branch, s.g_out, lambda side: 384 * side)

    def grad_qkv_weight(j):
        column_grad(s.normed_t, s.g_mixed, s.g_qkv, lambda side: 768 * j + 384 * side)

    g, r = types.SimpleNamespace(**gathers), types.SimpleNamespace(**scatters)
    send_rows()
    s.own_small[...] = jnp.zeros((16, 128), F32)
    s.sums[...] = jnp.zeros((16, D), F32)
    s.own_small[0:2, 0:24] = norm_gain[...].astype(F32)
    s.own_small[2:4, 0:24] = norm_bias[...].astype(F32)
    s.own_small[4:6, 0:24] = qv_bias[...].astype(F32)
    s.own_small[6:8, 0:24] = res_bias[...].astype(F32)
    s.own_small[8:9, 0:96] = fc1_bias[...].astype(F32)
    s.w_small[z, here, :, lanes(128 * core, 128)] = s.own_small[...].astype(BF16)
    g.s0.z()
    exchange("q2")
    assemble("q0")
    g.q0.z()
    g.f1.x()
    g.f2.x()
    assemble("q2")
    g.q2.z()
    g.q0.o()
    exchange("h")
    exchange("q1")
    exchange("o")
    assemble("q1")
    g.s0.p()
    g.q1.z()
    assemble("o")
    g.o0.z()
    g.q2.o()
    g.o0.o()
    g.q0.p()
    assemble("h")
    g.h1.y()
    g.s0.f()
    g.q1.o()
    g.s0.g()
    g.q2.p()
    g.q0.f()
    g.q0.g()
    g.h0.y()
    g.s0.l()
    g.h1.z()
    g.q1.p()
    g.f2.z()
    g.o0.p()
    g.h1.w()
    g.h0.z()
    g.q2.f()
    g.s0.d()
    unpack_small()
    g.q0.l()
    g.q2.g()
    start_norm()
    g.q1.f()
    g.q1.g()
    g.h1.v()
    g.o0.f()
    send_cotangent(0)
    g.o0.g()
    g.q0.d()
    g.h0.w()
    g.f0.z()
    project_qkv(0)
    attend(0)
    g.h1.x()
    g.q2.l()
    g.q1.l()
    g.h0.v()
    g.q2.d()
    g.q1.d()
    send_cotangent(1)
    g.f0.w()
    g.f1.z()
    project_qkv(1)
    g.o0.l()
    attend(1)
    g.o0.d()
    project_qkv(2)
    g.h0.x()
    g.f2.w()
    attend(2)
    project_out(0)
    g.f0.v()
    send_normed(0)
    start_cotangent(0)
    g.f1.w()
    g.h1.l()
    g.f2.v()
    project_out(1)
    transpose_out()
    g.h1.d()
    send_normed(1)
    feed_own(1)
    g.f1.v()
    start_cotangent(1)
    g.f0.x()
    g.h0.l()
    take_normed(0)
    feed_other(1, 0)
    g.f2.l()
    g.h0.d()
    feed_own(0)
    feed_other(0, 0)
    g.f1.l()
    take_normed(1)
    feed_other(1, 1)
    g.f0.l()
    feed_other(0, 1)
    weight_grad_fc2(1)
    g.f2.d()
    r.f1.s()
    g.f1.d()
    weight_grad_fc2(2)
    g.f0.d()
    r.f2.s()
    feed_back(1)
    r.f1.z()
    feed_back_other()
    send_back(0)
    send_back(1)
    r.f2.x()
    transpose_other()
    feed_back(0)
    grad_fc1_weight(0)
    r.h0.s()
    weight_grad_fc2(0)
    r.f0.s()
    feed_back_own()
    r.h0.x()
    feed_out(1)
    r.f0.z()
    grad_fc1_weight(1)
    r.h1.s()
    start_second(0)
    send_part()
    feed_out(0)
    r.f2.z()
    r.h1.x()
    start_second(1)
    project_attended()
    r.f1.w()
    send_base()
    attend_back(0)
    r.h0.z()
    grad_qkv_weight(0)
    r.q0.s()
    r.f0.w()
    attend_back(1)
    r.q0.p()
    grad_qkv_weight(1)
    r.q1b.s()
    grad_out_weight()
    start_output()
    r.q1a.s()
    r.h1.z()
    r.f2.w()
    r.o0.s()
    r.q1b.p()
    r.q0.f()
    r.q0.g()
    r.f1.v()
    r.q1a.p()
    r.h0.w()
    r.o0.p()
    attend_back(2)
    r.f2.v()
    r.q0.z()
    grad_qkv_weight(2)
    r.q1a.f()
    r.q2b.s()
    r.q1a.g()
    r.h0.v()
    r.f0.v()
    r.q2a.s()
    r.q1b.f()
    r.h1.w()
    r.q2b.p()
    r.o0.f()
    r.o0.g()
    first_norm_back()
    r.q1a.z()
    r.q2b.f()
    r.q2a.p()
    pack_small()
    r.h1.v()
    r.q2b.g()
    r.s0.s()
    r.q0.l()
    r.o0.z()
    r.s0.p()
    r.q1b.g()
    r.q2a.f()
    r.h0.y()
    r.q2a.g()
    r.q2b.z()
    r.s0.f()
    r.h1.y()
    send_grad_rows()
    r.s0.g()
    r.q1b.z()
    r.f1.x()
    r.q2a.z()
    r.f0.x()
    r.q1a.l()
    r.o0.l()
    r.f2.l()
    r.h1.l()
    r.s0.z()
    r.q2b.l()
    r.f1.l()
    r.h0.l()
    r.f0.l()
    r.q1b.l()
    send_encoded()
    r.q2a.l()
    r.s0.l()
    for name in list(moved):
        received(name)
    for copy in kept:
        copy.wait()
    for spot in range(max(0, len(started) - SENDS), len(started)):
        leave(spot)


def emit_kernel(*refs):
    count = (len(refs) - 4) // 3
    given, made, held = refs[:count], refs[count : 2 * count], refs[2 * count : 3 * count]
    ordered, wide_rows, in_sem, out_sem = refs[3 * count :]
    ready = {FC1_OUTPUT: ordered, ROWS_OUTPUT: wide_rows}
    arrive = [pltpu.make_async_copy(given[i], held[i], in_sem.at[i]) for i in range(count)]
    leave = [pltpu.make_async_copy(ready.get(i, held[i]), made[i], out_sem.at[i]) for i in range(count)]
    for copy in arrive:
        copy.start()
    for i in range(count):
        arrive[i].wait()
        if i == ROWS_OUTPUT:
            wide_rows[...] = held[i][...].astype(F32)
        if i == FC1_OUTPUT:
            for side in (0, 1):
                for k in range(8):
                    source = held[i][:, 1536 * side + 192 * k : 1536 * side + 192 * k + 192]
                    ordered[:, 384 * k + 192 * side : 384 * k + 192 * side + 192] = source
        leave[i].start()
    for copy in leave:
        copy.wait()


def emit(arrays):
    anywhere = pl.BlockSpec(memory_space=pl.ANY)
    count = len(arrays)
    dtypes = [F32 if i == ROWS_OUTPUT else a.dtype for i, a in enumerate(arrays)]
    return list(
        pl.pallas_call(
            emit_kernel,
            out_shape=[jax.ShapeDtypeStruct(a.shape, dtype) for a, dtype in zip(arrays, dtypes)],
            in_specs=[anywhere] * count,
            out_specs=[anywhere] * count,
            scratch_shapes=[pltpu.VMEM(a.shape, a.dtype) for a in arrays]
            + [pltpu.VMEM(arrays[i].shape, F32) for i in (FC1_OUTPUT, ROWS_OUTPUT)]
            + [pltpu.SemaphoreType.DMA((count,))] * 2,
        )(*arrays)
    )


def fast(
    patches,
    norm_gain,
    norm_bias,
    qkv_weight,
    qv_bias,
    out_weight,
    fc1_weight,
    fc1_bias,
    fc2_weight,
    res_bias,
    cotangent,
    frame_valid,
):
    outputs = [
        ((4, 64, D), BF16),
        ((4, 64, D), BF16),
        ((2, 24), F32),
        ((2, 24), F32),
        ((24, 3 * D), F32),
        ((2, 24), F32),
        ((24, D), F32),
        ((24, FF), F32),
        ((1, 96), F32),
        ((96, D), F32),
        ((2, 24), F32),
    ]
    vmem, anywhere = pl.BlockSpec(memory_space=pltpu.VMEM), pl.BlockSpec(memory_space=pl.ANY)
    found = list(pl.pallas_call(
        layer_kernel,
        out_shape=[jax.ShapeDtypeStruct(shape, dtype) for shape, dtype in outputs],
        in_specs=[anywhere if i in (0, 8, 10) else vmem for i in range(11)] + [pl.BlockSpec(memory_space=pltpu.SMEM)],
        out_specs=[anywhere if shape[0] > 2 else vmem for shape, _ in outputs],
        scratch_shapes=list(scratch_shapes().values()),
        compiler_params=pltpu.CompilerParams(
            collective_id=0, has_side_effects=True, vmem_limit_bytes=63 * 2**20
        ),
    )(
        patches,
        norm_gain,
        norm_bias,
        qkv_weight,
        qv_bias,
        out_weight,
        fc1_weight,
        fc1_bias.reshape(1, 96),
        fc2_weight,
        res_bias,
        cotangent,
        frame_valid,
    ))
    found = emit(found)
    found[8] = found[8].reshape(96)
    return tuple(found)


def solution(mesh):
    in_specs = (
        P("wide", "blk", None),
        P(None, ("wide", "blk")),
        P(None, ("wide", "blk")),
        P(("wide", "blk"), None),
        P(None, ("wide", "blk")),
        P(("wide", "blk"), None),
        P(("wide", "blk"), None),
        P(("wide", "blk")),
        P(("wide", "blk"), None),
        P(None, ("wide", "blk")),
        P("wide", "blk", None),
        P("wide"),
    )
    out_specs = (
        P("wide", "blk", None),
        P("wide", "blk", None),
        P(None, ("wide", "blk")),
        P(None, ("wide", "blk")),
        P(("wide", "blk"), None),
        P(None, ("wide", "blk")),
        P(("wide", "blk"), None),
        P(("wide", "blk"), None),
        P(("wide", "blk")),
        P(("wide", "blk"), None),
        P(None, ("wide", "blk")),
    )
    body = fast if dict(mesh.shape) == {"wide": 8, "blk": 4} else local
    return jax.shard_map(body, mesh=mesh, in_specs=in_specs, out_specs=out_specs, check_vma=False)
```
